32 devices in a mesh: dp: 4 (over y, core), seq: 8 (over z, x).
Axes of the slice: x: 2, y: 2, z: 4, core: 2. Of those that a mesh axis runs over, the one named last changes fastest.
Arguments:
- tokens: bfloat16 [8, 512, 2048], P('dp', 'seq'), may hold values from -6 to 6
- cotangent: bfloat16 [8, 512, 2048], P('dp', 'seq'), may hold values from -6 to 6
- segment_ids: int32 [8, 512], P('dp', 'seq'), may hold values from 0 to 7, as said below
- doc_positions: int32 [8, 512], P('dp', 'seq'), may hold values from 0 to 504, as said below
- in_weight: float32 [2048, 17408], P(('dp', 'seq')), may hold values from -0.125 to 0.125
- in_first: float32 [2048, 17408], P(('dp', 'seq'))
- in_second: float32 [2048, 17408], P(('dp', 'seq'))
- in_average: float32 [2048, 17408], P(('dp', 'seq')), may hold values from -0.125 to 0.125
- out_weight: float32 [7680, 2048], P(('dp', 'seq'))
- out_first: float32 [7680, 2048], P(('dp', 'seq'))
- out_second: float32 [7680, 2048], P(('dp', 'seq'))
- out_average: float32 [7680, 2048], P(('dp', 'seq'))
- small_params: float32 [2048, 5], P(('dp', 'seq'))
- small_first: float32 [2048, 5], P(('dp', 'seq'))
- small_second: float32 [2048, 5], P(('dp', 'seq'))
- small_average: float32 [2048, 5], P(('dp', 'seq'))
Outputs:
- output: bfloat16 [8, 512, 2048], P('dp', 'seq')
- input_grad: float32 [8, 512, 2048], P('dp', 'seq')
- new_in_weight: float32 [2048, 17408], P(('dp', 'seq'))
- new_in_second: float32 [2048, 17408], P(('dp', 'seq'))
- new_in_average: float32 [2048, 17408], P(('dp', 'seq'))
- new_out_weight: float32 [7680, 2048], P(('dp', 'seq'))
- new_out_second: float32 [7680, 2048], P(('dp', 'seq'))
- new_out_average: float32 [7680, 2048], P(('dp', 'seq'))
- new_small_params: float32 [2048, 5], P(('dp', 'seq'))
- new_small_second: float32 [2048, 5], P(('dp', 'seq'))
- new_small_average: float32 [2048, 5], P(('dp', 'seq'))
- small_grad: float32 [2048, 5], P(('dp', 'seq'))
- in_grad: float32 [2048, 17408], P(('dp', 'seq'))
- out_grad: float32 [7680, 2048], P(('dp', 'seq'))
The draws below stay inside these ranges and needn't reach their ends.
Inputs may be any that keep to these rules, and one draw needn't show every extreme that they name: `segment_ids`: within each row the ids never fall, start at 0 and take every value up to 7. `doc_positions`: 0 at a document's first token of a row, rising by one along the document; row 0's longest document reaches position 504.
All inputs are finite; a program needn't handle non-finite values.
Results may differ from the reference program's by a relative error of at most 0.025.
Values may be sent and summed in bfloat16 or wider, within the bound.
A program may use at most 448 MiB of HBM per device.

```python
import math
import jax
import jax.numpy as jnp
from jax import lax

D = 2048
HEADS = 32
HEAD = 64
ROT = 16
FF = 5632
DOCS = 8
STEP = 2
WIN = 17408
OUT_ROWS = 7680
ROWS = 8
LENGTH = 512


def document_split(key):
    row_keys = jax.random.split(key, ROWS)
    row_numbers = jnp.arange(ROWS)

    def one_row(row_key, row_number):
        drawn_cuts = jax.random.permutation(row_key, LENGTH - 1)[:DOCS - 1] + 1
        early_cuts = jnp.arange(1, DOCS)
        cuts = jnp.where(row_number == 0, early_cuts, drawn_cuts)
        places = jnp.arange(LENGTH)
        before = cuts[None, :] <= places[:, None]
        segment = jnp.sum(before.astype(jnp.int32), axis=1)
        begin = jnp.max(jnp.where(before, cuts[None, :], 0), axis=1)
        return (segment.astype(jnp.int32), (places - begin).astype(jnp.int32))
    return jax.vmap(one_row)(row_keys, row_numbers)


def draw_segment_ids(key, part):
    return document_split(jax.random.fold_in(key, 17))[0]


def draw_doc_positions(key, part):
    return document_split(jax.random.fold_in(key, 17))[1]


def base_normal(key, shape):
    return jnp.clip(jax.random.normal(key, shape, jnp.float32), -6.0, 6.0)


def token_root():
    return math.sqrt(ROWS * LENGTH)


def in_scale():
    columns = jnp.arange(WIN)[None, :]
    return jnp.where(columns < 3 * D, 0.8, 0.35) * token_root()


def keys_seen():
    return max(LENGTH // DOCS // 8, 1)


def out_scale():
    rows_idx = jnp.arange(OUT_ROWS)[:, None]
    return jnp.where(rows_idx < D, 1.0 / math.sqrt(keys_seen()), 0.6) * token_root()


def first_moment(key, scale_arr, shape):
    return base_normal(key, shape) * 9.0 * scale_arr


def second_moment(key, scale_arr, shape):
    keep_part = 1.0 - STEP ** (-0.8)
    held = keep_part / (1.0 - keep_part)
    spread = jnp.exp(jax.random.uniform(key, shape, jnp.float32, 0.0, math.log(2.0)))
    return held * scale_arr * scale_arr * spread


def out_law(key):
    rows_idx = jnp.arange(OUT_ROWS)[:, None]
    row_scale = jnp.where(rows_idx < D, math.sqrt(keys_seen()) / math.sqrt(D), 1.0 / math.sqrt(FF))
    return base_normal(key, (OUT_ROWS, D)) * row_scale


def small_law(key):
    columns = jnp.arange(5)[None, :]
    gain_part = jax.random.uniform(jax.random.fold_in(key, 1), (D, 5), jnp.float32, 0.7, 1.3)
    rest_part = base_normal(jax.random.fold_in(key, 2), (D, 5)) * jnp.where(columns == 1, 0.2, 0.5)
    return jnp.where(columns == 0, gain_part, rest_part)


def draw_in_first(key, part):
    return first_moment(jax.random.fold_in(key, 101), in_scale(), (D, WIN))


def draw_in_second(key, part):
    return second_moment(jax.random.fold_in(key, 102), in_scale(), (D, WIN))


def draw_out_weight(key, part):
    return out_law(jax.random.fold_in(key, 201))


def draw_out_first(key, part):
    return first_moment(jax.random.fold_in(key, 202), out_scale(), (OUT_ROWS, D))


def draw_out_second(key, part):
    return second_moment(jax.random.fold_in(key, 203), out_scale(), (OUT_ROWS, D))


def draw_out_average(key, part):
    return out_law(jax.random.fold_in(key, 204))


def draw_small_params(key, part):
    return small_law(jax.random.fold_in(key, 301))


def draw_small_first(key, part):
    return first_moment(jax.random.fold_in(key, 302), 1.2 * token_root(), (D, 5))


def draw_small_second(key, part):
    return second_moment(jax.random.fold_in(key, 303), 1.2 * token_root(), (D, 5))


def draw_small_average(key, part):
    return small_law(jax.random.fold_in(key, 304))


def block_levels(key, shape, cuts, low, high):
    loudness = 1.0
    for axis_at, blocks in cuts:
        steps = jax.random.uniform(jax.random.fold_in(jax.random.fold_in(key, 6), axis_at), (blocks,), jnp.float32, low / len(cuts), high / len(cuts))
        loudness = loudness * jnp.repeat(jnp.exp(steps), shape[axis_at] // blocks).reshape((-1,) + (1,) * (len(shape) - 1 - axis_at))
    return loudness


def centred(own_key, shape, scale, most, pieces=(), kind=jnp.bfloat16):
    result = scale * jax.random.normal(own_key, shape, jnp.float32)
    if pieces:
        result = result * block_levels(own_key, shape, pieces, -0.22, 0.18)
    return jnp.clip(result, -most, most).astype(kind)


def setup_inputs(seed: int = 0) -> dict:
    arg_keys = jax.random.split(jax.random.key(seed), 17)
    return {
        "tokens": centred(arg_keys[0], (ROWS, LENGTH, D), 1.0, 6.0, ((0, 4), (1, 8))),
        "cotangent": centred(arg_keys[1], (ROWS, LENGTH, D), 1.0, 6.0, ((0, 4), (1, 8))),
        "segment_ids": draw_segment_ids(jax.random.fold_in(arg_keys[16], 71), 0),
        "doc_positions": draw_doc_positions(jax.random.fold_in(arg_keys[16], 71), 0),
        "in_weight": centred(arg_keys[4], (D, WIN), D ** -0.5, 0.125, ((0, 32),), jnp.float32),
        "in_first": draw_in_first(jax.random.fold_in(arg_keys[16], 71), 0),
        "in_second": draw_in_second(jax.random.fold_in(arg_keys[16], 71), 0),
        "in_average": centred(arg_keys[7], (D, WIN), D ** -0.5, 0.125, ((0, 32),), jnp.float32),
        "out_weight": draw_out_weight(jax.random.fold_in(arg_keys[16], 71), 0),
        "out_first": draw_out_first(jax.random.fold_in(arg_keys[16], 71), 0),
        "out_second": draw_out_second(jax.random.fold_in(arg_keys[16], 71), 0),
        "out_average": draw_out_average(jax.random.fold_in(arg_keys[16], 71), 0),
        "small_params": draw_small_params(jax.random.fold_in(arg_keys[16], 71), 0),
        "small_first": draw_small_first(jax.random.fold_in(arg_keys[16], 71), 0),
        "small_second": draw_small_second(jax.random.fold_in(arg_keys[16], 71), 0),
        "small_average": draw_small_average(jax.random.fold_in(arg_keys[16], 71), 0),
    }


@jax.custom_vjp
def low(v):
    return lax.optimization_barrier(v.astype(jnp.bfloat16)).astype(jnp.float32)

@jax.custom_vjp
def low_back(v):
    return v

def low_keep(v):
    return (low(v), None)

def low_pass(kept, grad):
    return (grad,)

def back_keep(v):
    return (v, None)

def back_low(kept, grad):
    return (low(grad),)
low.defvjp(low_keep, low_pass)
low_back.defvjp(back_keep, back_low)
highest = lax.Precision.HIGHEST
beta_one = 0.9
adam_eps = 1e-08
matrix_rate = 0.001
small_rate = 0.01
weight_decay = 0.1
norm_eps = 1e-05
rope_base = 10000.0

def rope_tables(positions):
    half_rot = ROT // 2
    inv_freq = rope_base ** (-2.0 * jnp.arange(half_rot, dtype=jnp.float32) / ROT)
    angles = positions.astype(jnp.float32)[..., None] * inv_freq
    return (jnp.cos(angles)[..., None, :], jnp.sin(angles)[..., None, :])

def apply_rope(field_in, cosine_tab, sine_tab):
    half_rot = ROT // 2
    low_half = field_in[..., :half_rot]
    high_half = field_in[..., half_rot:ROT]
    return jnp.concatenate([low_half * cosine_tab - high_half * sine_tab, high_half * cosine_tab + low_half * sine_tab, field_in[..., ROT:]], axis=-1)

def attention_row(queries, keys_all, values_all, segments):
    block_rows = min(512, LENGTH)
    block_count = LENGTH // block_rows
    key_places = jnp.arange(LENGTH)

    def one_block(block_args):
        query_blk, seg_blk, block_start = block_args
        query_places = block_start + jnp.arange(block_rows)
        key_mask = (seg_blk[:, None] == segments[None, :]) & (key_places[None, :] <= query_places[:, None])
        scores = low_back(jnp.einsum('qhe,khe->hqk', query_blk, keys_all, precision=highest) * HEAD ** (-0.5))
        scores = jnp.where(key_mask[None], scores, -jnp.inf)
        row_top = lax.optimization_barrier(jnp.max(scores, axis=-1, keepdims=True))
        weights = jnp.exp(scores - row_top)
        weights = weights / lax.optimization_barrier(jnp.sum(weights, axis=-1, keepdims=True))
        return jnp.einsum('hqk,khe->qhe', low(weights), values_all, precision=highest)
    blocks = lax.map(jax.checkpoint(one_block), (queries.reshape(block_count, block_rows, HEADS, HEAD), segments.reshape(block_count, block_rows), (jnp.arange(block_count) * block_rows).astype(jnp.int32)))
    return blocks.reshape(LENGTH, D)

def forward(tokens_f, in_weight, out_weight, small_params, segment_ids, doc_positions):
    in_low = low(in_weight)
    out_low = low(out_weight)
    small_low = low(small_params)
    norm_gain = small_low[:, 0]
    norm_shift = small_low[:, 1]
    qkv_bias = jnp.concatenate([small_low[:, 2:5].T.reshape(3 * D), jnp.zeros((2 * FF,), jnp.float32)])

    def one_row(row_args):
        row_in, segments, positions = row_args
        centered = row_in - lax.optimization_barrier(jnp.mean(row_in, axis=-1, keepdims=True))
        variance = lax.optimization_barrier(jnp.mean(centered * centered, axis=-1, keepdims=True))
        normed = centered * lax.rsqrt(variance + norm_eps)
        hidden_in = low(normed * norm_gain + norm_shift)
        projected = low_back(jnp.dot(hidden_in, in_low, precision=highest) + qkv_bias)
        cosine_tab, sine_tab = rope_tables(positions)
        queries = low(apply_rope(projected[:, :D].reshape(LENGTH, HEADS, HEAD), cosine_tab, sine_tab))
        keys_rot = low(apply_rope(projected[:, D:2 * D].reshape(LENGTH, HEADS, HEAD), cosine_tab, sine_tab))
        values_low = low(projected[:, 2 * D:3 * D].reshape(LENGTH, HEADS, HEAD))
        attended = attention_row(queries, keys_rot, values_low, segments)
        gate_pre = projected[:, 3 * D:3 * D + FF]
        up_pre = projected[:, 3 * D + FF:]
        activated = jax.nn.silu(gate_pre) * up_pre
        joined = low_back(low(jnp.concatenate([attended, activated], axis=1)))
        return row_in + jnp.dot(joined, out_low, precision=highest)
    return lax.map(one_row, (tokens_f, segment_ids, doc_positions))

def adam_update(weight, first, second, average, gradient, rate, decay_rate):
    beta_two = 1.0 - STEP ** (-0.8)
    average_keep = min(0.999, (1.0 + STEP) / (10.0 + STEP))
    first_new = beta_one * first + (1.0 - beta_one) * gradient
    second_new = beta_two * second + (1.0 - beta_two) * gradient * gradient
    moment_hat = beta_one * first_new / (1.0 - beta_one ** (STEP + 1)) + (1.0 - beta_one) * gradient / (1.0 - beta_one ** STEP)
    weight_new = weight - rate * (moment_hat / (jnp.sqrt(second_new) + adam_eps) + decay_rate * weight)
    average_new = average_keep * average + (1.0 - average_keep) * weight_new
    return (weight_new, second_new, average_new)

def reference(tokens, cotangent, segment_ids, doc_positions, in_weight, in_first, in_second, in_average, out_weight, out_first, out_second, out_average, small_params, small_first, small_second, small_average):
    tokens_f = tokens.astype(jnp.float32)

    def closed(tok_arg, in_arg, out_arg, small_arg):
        return forward(tok_arg, in_arg, out_arg, small_arg, segment_ids, doc_positions)
    output, pullback = jax.vjp(closed, tokens_f, in_weight, out_weight, small_params)
    input_grad, in_grad, out_grad, small_grad = pullback(cotangent.astype(jnp.float32))
    in_new = adam_update(in_weight, in_first, in_second, in_average, in_grad, matrix_rate, weight_decay)
    out_new = adam_update(out_weight, out_first, out_second, out_average, out_grad, matrix_rate, weight_decay)
    small_new = adam_update(small_params, small_first, small_second, small_average, small_grad, small_rate, 0.0)
    return (output.astype(jnp.bfloat16), input_grad, in_new[0], in_new[1], in_new[2], out_new[0], out_new[1], out_new[2], small_new[0], small_new[1], small_new[2], small_grad, in_grad, out_grad)
```

```python
import functools

import jax
import jax.numpy as jnp
from jax import lax
from jax.experimental import pallas as pl
from jax.experimental.pallas import tpu as pltpu
from jax.sharding import PartitionSpec as P

HEADS = 32
ROT = 16
STEP = 2


beta_one = 0.9
adam_eps = 1e-08
matrix_rate = 0.001
small_rate = 0.01
weight_decay = 0.1
norm_eps = 1e-05
rope_base = 10000.0
neg_large = -1e30


def rope_tables(positions, rot_dims):
    half_rot = rot_dims // 2
    inv_freq = rope_base ** (-2.0 * jnp.arange(half_rot, dtype=jnp.float32) / rot_dims)
    angles = positions.astype(jnp.float32)[..., None] * inv_freq
    return (jnp.cos(angles)[..., None, :], jnp.sin(angles)[..., None, :])


def apply_rope(field_in, cosine_tab, sine_tab, rot_dims):
    half_rot = rot_dims // 2
    low_half = field_in[..., :half_rot]
    high_half = field_in[..., half_rot:rot_dims]
    return jnp.concatenate(
        [
            low_half * cosine_tab - high_half * sine_tab,
            high_half * cosine_tab + low_half * sine_tab,
            field_in[..., rot_dims:],
        ],
        axis=-1,
    )


def undo_rope(grad_in, cosine_tab, sine_tab, rot_dims):
    half_rot = rot_dims // 2
    low_half = grad_in[..., :half_rot]
    high_half = grad_in[..., half_rot:rot_dims]
    return jnp.concatenate(
        [
            low_half * cosine_tab + high_half * sine_tab,
            high_half * cosine_tab - low_half * sine_tab,
            grad_in[..., rot_dims:],
        ],
        axis=-1,
    )


def visible(query_seg, key_seg, query_pos, key_pos):
    same_doc = query_seg[:, :, None] == key_seg[:, None, :]
    causal = key_pos[None, :] <= query_pos[:, None]
    return (same_doc & causal[None])[:, None]


def to_tokens(head_major):
    return jnp.transpose(head_major, (0, 2, 1, 3))


def adam_update(weight, first, second, average, gradient, rate, decay_rate):
    beta_two = 1.0 - STEP ** (-0.8)
    average_keep = min(0.999, (1.0 + STEP) / (10.0 + STEP))
    first_new = beta_one * first + (1.0 - beta_one) * gradient
    second_new = beta_two * second + (1.0 - beta_two) * gradient * gradient
    moment_hat = beta_one * first_new / (1.0 - beta_one ** (STEP + 1)) + (
        1.0 - beta_one
    ) * gradient / (1.0 - beta_one**STEP)
    weight_new = weight - rate * (
        moment_hat / (jnp.sqrt(second_new) + adam_eps) + decay_rate * weight
    )
    average_new = average_keep * average + (1.0 - average_keep) * weight_new
    return (weight_new, second_new, average_new)


def per_device(
    tokens,
    cotangent,
    segment_ids,
    doc_positions,
    in_weight,
    in_first,
    in_second,
    in_average,
    out_weight,
    out_first,
    out_second,
    out_average,
    small_params,
    small_first,
    small_second,
    small_average,
):
    rows_here, row_tokens, model_width = tokens.shape
    head_count = HEADS
    head_size = model_width // head_count
    score_scale = head_size ** (-0.5)
    all_tokens = rows_here * row_tokens
    wide_in = in_weight.shape[1]
    ffn_width = (wide_in - 3 * model_width) // 2
    shape_heads = (rows_here, row_tokens, head_count, head_size)
    own_places = lax.axis_index("seq") * row_tokens + jnp.arange(row_tokens)
    flat_in = tokens.astype(jnp.float32).reshape(all_tokens, model_width)
    centered = flat_in - jnp.mean(flat_in, axis=-1, keepdims=True)
    inv_std = lax.rsqrt(jnp.mean(centered * centered, axis=-1, keepdims=True) + norm_eps)
    normed = centered * inv_std
    in_low = in_weight.astype(jnp.bfloat16)
    out_low = out_weight.astype(jnp.bfloat16)
    small_low = small_params.astype(jnp.bfloat16)
    w_piece = lax.all_gather(in_low, ("dp", "seq"), axis=0, tiled=True)
    s_piece = lax.all_gather(small_low, ("dp", "seq"), axis=0, tiled=True)
    columns = normed
    s_float = s_piece.astype(jnp.float32)
    h_piece = (columns * s_float[:, 0] + s_float[:, 1]).astype(jnp.bfloat16)
    proj_acc = jnp.dot(h_piece, w_piece, preferred_element_type=jnp.float32)
    norm_gain = s_float[:, 0]
    qkv_bias = s_float[:, 2:5].T.reshape(3 * model_width)
    qkv_full = proj_acc[:, : 3 * model_width] + qkv_bias
    gate_pre = proj_acc[:, 3 * model_width : 3 * model_width + ffn_width]
    up_pre = proj_acc[:, 3 * model_width + ffn_width :]
    cosine_tab, sine_tab = rope_tables(doc_positions, ROT)
    query_low = apply_rope(
        qkv_full[:, :model_width].reshape(shape_heads), cosine_tab, sine_tab, ROT
    ).astype(jnp.bfloat16)
    key_low = apply_rope(
        qkv_full[:, model_width : 2 * model_width].reshape(shape_heads), cosine_tab, sine_tab, ROT
    ).astype(jnp.bfloat16)
    value_low = qkv_full[:, 2 * model_width :].reshape(shape_heads).astype(jnp.bfloat16)
    seg_low = segment_ids.astype(jnp.bfloat16)
    seg_own = segment_ids.astype(jnp.float32)
    key_flat = key_low.reshape(rows_here, row_tokens, model_width)
    value_flat = value_low.reshape(rows_here, row_tokens, model_width)
    attend_init = (
        jnp.full((rows_here, head_count, row_tokens), neg_large, jnp.float32),
        jnp.zeros((rows_here, head_count, row_tokens), jnp.float32),
        jnp.zeros((rows_here, head_count, row_tokens, head_size), jnp.float32),
    )
    key_piece = lax.all_gather(key_flat, "seq", axis=1, tiled=True)
    value_piece = lax.all_gather(value_flat, "seq", axis=1, tiled=True)
    seg_piece = lax.all_gather(seg_low, "seq", axis=1, tiled=True)
    turn_count = key_piece.shape[1] // row_tokens

    def attend_one_turn(turn_index, inner_state):
        offset = turn_index * row_tokens
        key_blk = lax.dynamic_slice_in_dim(key_piece, offset, row_tokens, 1).reshape(shape_heads)
        value_blk = lax.dynamic_slice_in_dim(value_piece, offset, row_tokens, 1).reshape(
            shape_heads
        )
        seg_blk = lax.dynamic_slice_in_dim(seg_piece, offset, row_tokens, 1).astype(jnp.float32)
        key_mask = visible(seg_own, seg_blk, own_places, offset + jnp.arange(row_tokens))
        running_top, running_sum, weighted = inner_state
        scores = (
            jnp.einsum("rqhe,rkhe->rhqk", query_low, key_blk, preferred_element_type=jnp.float32)
            * score_scale
        )
        scores = jnp.where(key_mask, scores, neg_large)
        new_top = jnp.maximum(running_top, jnp.max(scores, axis=-1))
        weights = jnp.where(key_mask, jnp.exp(scores - new_top[..., None]), 0.0)
        factor = jnp.exp(running_top - new_top)
        running_sum = running_sum * factor + jnp.sum(weights, axis=-1)
        weighted = weighted * factor[..., None] + jnp.einsum(
            "rhqk,rkhe->rhqe",
            weights.astype(jnp.bfloat16),
            value_blk,
            preferred_element_type=jnp.float32,
        )
        return (new_top, running_sum, weighted)

    running_top, running_sum, weighted = lax.fori_loop(0, turn_count, attend_one_turn, attend_init)
    attended = weighted / running_sum[..., None]
    log_total = running_top + jnp.log(running_sum)
    attended_low = to_tokens(attended).reshape(all_tokens, model_width).astype(jnp.bfloat16)
    gate_sig = jax.nn.sigmoid(gate_pre)
    activated = gate_pre * gate_sig * up_pre
    joined = jnp.concatenate([attended_low, activated.astype(jnp.bfloat16)], axis=1)
    columns = joined
    branch_sum = jnp.dot(
        columns,
        lax.all_gather(out_low, ("dp", "seq"), axis=0, tiled=True),
        preferred_element_type=jnp.float32,
    )
    output = (flat_in + branch_sum).astype(jnp.bfloat16).reshape(rows_here, row_tokens, model_width)
    grad_out = cotangent.reshape(all_tokens, model_width)
    d_joined = lax.dot_general(
        grad_out,
        lax.all_gather(out_low, ("dp", "seq"), axis=0, tiled=True),
        (((1,), (1,)), ((), ())),
        preferred_element_type=jnp.float32,
    )
    d_joined = d_joined.astype(jnp.bfloat16)
    columns = joined
    out_grad = lax.psum_scatter(
        lax.dot_general(
            columns, grad_out, (((0,), (0,)), ((), ())), preferred_element_type=jnp.float32
        ),
        ("dp", "seq"),
        scatter_dimension=0,
        tiled=True,
    )
    d_attended = d_joined[:, :model_width].reshape(shape_heads)
    d_act = d_joined[:, model_width:].astype(jnp.float32)
    d_gate = d_act * up_pre * gate_sig * (1.0 + gate_pre * (1.0 - gate_sig))
    d_up = d_act * gate_pre * gate_sig
    out_dot = jnp.einsum("rqhe,rhqe->rhq", d_attended.astype(jnp.float32), attended)
    grad_zero = jnp.zeros((rows_here, head_count, row_tokens, head_size), jnp.float32)
    query_key_piece = lax.all_gather(key_flat, "seq", axis=1, tiled=True)
    query_value_piece = lax.all_gather(value_flat, "seq", axis=1, tiled=True)
    query_seg_piece = lax.all_gather(seg_low, "seq", axis=1, tiled=True)
    turn_count = query_key_piece.shape[1] // row_tokens

    def query_one_turn(turn_index, inner_state):
        offset = turn_index * row_tokens
        key_blk = lax.dynamic_slice_in_dim(query_key_piece, offset, row_tokens, 1).reshape(
            shape_heads
        )
        value_blk = lax.dynamic_slice_in_dim(query_value_piece, offset, row_tokens, 1).reshape(
            shape_heads
        )
        seg_blk = lax.dynamic_slice_in_dim(query_seg_piece, offset, row_tokens, 1).astype(
            jnp.float32
        )
        key_mask = visible(seg_own, seg_blk, own_places, offset + jnp.arange(row_tokens))
        scores = (
            jnp.einsum("rqhe,rkhe->rhqk", query_low, key_blk, preferred_element_type=jnp.float32)
            * score_scale
        )
        weights = jnp.where(key_mask, jnp.exp(scores - log_total[..., None]), 0.0)
        d_prob = jnp.einsum(
            "rqhe,rkhe->rhqk", d_attended, value_blk, preferred_element_type=jnp.float32
        )
        d_score = (weights * (d_prob - out_dot[..., None])).astype(jnp.bfloat16)
        return (
            inner_state
            + jnp.einsum("rhqk,rkhe->rhqe", d_score, key_blk, preferred_element_type=jnp.float32)
            * score_scale
        )

    d_query = lax.fori_loop(0, turn_count, query_one_turn, grad_zero)
    row_stats = jnp.concatenate(
        [jnp.transpose(log_total, (0, 2, 1)), jnp.transpose(out_dot, (0, 2, 1))], axis=2
    )
    stat_high = row_stats.astype(jnp.bfloat16)
    stat_low = (row_stats - stat_high.astype(jnp.float32)).astype(jnp.bfloat16)
    query_flat = query_low.reshape(rows_here, row_tokens, model_width)
    d_att_flat = d_attended.reshape(rows_here, row_tokens, model_width)
    query_piece = lax.all_gather(query_flat, "seq", axis=1, tiled=True)
    dout_piece = lax.all_gather(d_att_flat, "seq", axis=1, tiled=True)
    high_piece = lax.all_gather(stat_high, "seq", axis=1, tiled=True)
    low_piece = lax.all_gather(stat_low, "seq", axis=1, tiled=True)
    key_seg_piece = lax.all_gather(seg_low, "seq", axis=1, tiled=True)
    turn_count = query_piece.shape[1] // row_tokens

    def key_one_turn(turn_index, inner_state):
        offset = turn_index * row_tokens
        query_blk = lax.dynamic_slice_in_dim(query_piece, offset, row_tokens, 1).reshape(
            shape_heads
        )
        dout_blk = lax.dynamic_slice_in_dim(dout_piece, offset, row_tokens, 1).reshape(shape_heads)
        stat_blk = lax.dynamic_slice_in_dim(high_piece, offset, row_tokens, 1).astype(
            jnp.float32
        ) + lax.dynamic_slice_in_dim(low_piece, offset, row_tokens, 1).astype(jnp.float32)
        lse_blk = jnp.transpose(stat_blk[..., :head_count], (0, 2, 1))
        dot_blk = jnp.transpose(stat_blk[..., head_count:], (0, 2, 1))
        seg_blk = lax.dynamic_slice_in_dim(key_seg_piece, offset, row_tokens, 1).astype(jnp.float32)
        key_mask = visible(seg_blk, seg_own, offset + jnp.arange(row_tokens), own_places)
        d_key, d_value = inner_state
        scores = (
            jnp.einsum("rqhe,rkhe->rhqk", query_blk, key_low, preferred_element_type=jnp.float32)
            * score_scale
        )
        weights = jnp.where(key_mask, jnp.exp(scores - lse_blk[..., None]), 0.0)
        d_value = d_value + jnp.einsum(
            "rhqk,rqhe->rhke",
            weights.astype(jnp.bfloat16),
            dout_blk,
            preferred_element_type=jnp.float32,
        )
        d_prob = jnp.einsum(
            "rqhe,rkhe->rhqk", dout_blk, value_low, preferred_element_type=jnp.float32
        )
        d_score = (weights * (d_prob - dot_blk[..., None])).astype(jnp.bfloat16)
        d_key = (
            d_key
            + jnp.einsum("rhqk,rqhe->rhke", d_score, query_blk, preferred_element_type=jnp.float32)
            * score_scale
        )
        return (d_key, d_value)

    d_key, d_value = lax.fori_loop(0, turn_count, key_one_turn, (grad_zero, grad_zero))
    d_query_tok = undo_rope(to_tokens(d_query), cosine_tab, sine_tab, ROT).reshape(
        all_tokens, model_width
    )
    d_key_tok = undo_rope(to_tokens(d_key), cosine_tab, sine_tab, ROT).reshape(
        all_tokens, model_width
    )
    d_value_tok = to_tokens(d_value).reshape(all_tokens, model_width)
    d_proj = jnp.concatenate([d_query_tok, d_key_tok, d_value_tok, d_gate, d_up], axis=1).astype(
        jnp.bfloat16
    )
    d_hidden = lax.dot_general(
        d_proj,
        lax.all_gather(in_low, ("dp", "seq"), axis=0, tiled=True),
        (((1,), (1,)), ((), ())),
        preferred_element_type=jnp.float32,
    )
    columns = h_piece
    in_grad = lax.psum_scatter(
        lax.dot_general(
            columns, d_proj, (((0,), (0,)), ((), ())), preferred_element_type=jnp.float32
        ),
        ("dp", "seq"),
        scatter_dimension=0,
        tiled=True,
    )
    gain_grad = jnp.sum(d_hidden * normed, axis=0)
    shift_grad = jnp.sum(d_hidden, axis=0)
    bias_grad = (
        jnp.sum(d_proj[:, : 3 * model_width].astype(jnp.float32), axis=0).reshape(3, model_width).T
    )
    small_term = jnp.concatenate([gain_grad[:, None], shift_grad[:, None], bias_grad], axis=1)
    small_grad = lax.psum_scatter(small_term, ("dp", "seq"), scatter_dimension=0, tiled=True)
    d_normed = d_hidden * norm_gain
    input_grad = grad_out.astype(jnp.float32) + inv_std * (
        d_normed
        - jnp.mean(d_normed, axis=-1, keepdims=True)
        - normed * jnp.mean(d_normed * normed, axis=-1, keepdims=True)
    )
    input_grad = input_grad.reshape(rows_here, row_tokens, model_width)
    in_new = adam_update(
        in_weight, in_first, in_second, in_average, in_grad, matrix_rate, weight_decay
    )
    out_new = adam_update(
        out_weight, out_first, out_second, out_average, out_grad, matrix_rate, weight_decay
    )
    small_new = adam_update(
        small_params, small_first, small_second, small_average, small_grad, small_rate, 0.0
    )
    return (
        output,
        input_grad,
        in_new[0],
        in_new[1],
        in_new[2],
        out_new[0],
        out_new[1],
        out_new[2],
        small_new[0],
        small_new[1],
        small_new[2],
        small_grad,
        in_grad,
        out_grad,
    )


def heads_fit(n_dp, n_seq, own_rows, model_width, wide_in):
    dp_rows = own_rows * n_seq
    if n_dp != 4 or HEADS % (2 * n_seq) or not dp_rows < model_width < 2 * dp_rows:
        return False
    att_rows = model_width // n_seq
    late_att = model_width - dp_rows
    first_act = dp_rows - late_att
    if first_act % n_seq:
        return False
    lead = att_rows - own_rows
    return (
        wide_in - 3 * model_width == 2 * (n_dp * dp_rows - model_width)
        and lead == own_rows - first_act // n_seq
        and lead * n_seq == late_att
        and lead % 16 == 0
    )


def attention_kernel(
    q_ref, k_ref, v_ref, bq_ref, bk_ref, bv_ref, da_ref, rope_ref, seg_q_ref, seg_k_ref,
    o_ref, dq_ref, dk_ref, dv_ref, *, head_size, half_rot,
):
    cos, sin_low, sin_high = rope_ref[0], rope_ref[1], rope_ref[2]
    tokens, lanes = cos.shape
    scale = head_size ** (-0.5)

    def turn(v, way):
        return (
            v * cos
            + way * pltpu.roll(v, lanes - half_rot, 1) * sin_low
            + way * pltpu.roll(v, half_rot, 1) * sin_high
        )

    query = (turn(q_ref[...] + bq_ref[...], 1.0)).astype(jnp.bfloat16) * scale
    query = query.astype(jnp.bfloat16)
    key = turn(k_ref[...] + bk_ref[...], 1.0).astype(jnp.bfloat16)
    value = (v_ref[...] + bv_ref[...]).astype(jnp.bfloat16)
    d_att = da_ref[...]
    place_q = lax.broadcasted_iota(jnp.int32, (tokens, tokens), 0)
    place_k = lax.broadcasted_iota(jnp.int32, (tokens, tokens), 1)
    mask = (seg_q_ref[0] == seg_k_ref[0]) & (place_k <= place_q)
    lane = lax.broadcasted_iota(jnp.int32, (tokens, lanes), 1)
    nt = (((1,), (1,)), ((), ()))
    tn = (((0,), (0,)), ((), ()))
    dot = functools.partial(lax.dot_general, preferred_element_type=jnp.float32)
    att = jnp.zeros((tokens, lanes), jnp.float32)
    d_query = jnp.zeros((tokens, lanes), jnp.float32)
    d_key = jnp.zeros((tokens, lanes), jnp.float32)
    d_value = jnp.zeros((tokens, lanes), jnp.float32)
    for head in range(lanes // head_size):
        mine = (lane >= head * head_size) & (lane < (head + 1) * head_size)
        q_h = jnp.where(mine, query, jnp.zeros_like(query))
        da_h = jnp.where(mine, d_att, jnp.zeros_like(d_att))
        scores = jnp.where(mask, dot(q_h, key, nt), neg_large)
        top = jnp.max(scores, axis=1, keepdims=True)
        weights = jnp.exp(scores - top)
        probs = weights * (1.0 / jnp.sum(weights, axis=1, keepdims=True))
        probs_low = probs.astype(jnp.bfloat16)
        att_h = jnp.where(mine, dot(probs_low, value, (((1,), (0,)), ((), ()))), 0.0)
        out_dot = jnp.sum(att_h * d_att.astype(jnp.float32), axis=1, keepdims=True)
        d_prob = dot(da_h, value, nt)
        d_score = (probs * (d_prob - out_dot)).astype(jnp.bfloat16)
        att = att + att_h
        d_query = d_query + jnp.where(mine, dot(d_score, key, (((1,), (0,)), ((), ()))), 0.0)
        d_key = d_key + dot(d_score, q_h, tn)
        d_value = d_value + dot(probs_low, da_h, tn)
    o_ref[...] = att.astype(jnp.bfloat16)
    dq_ref[...] = turn(d_query * scale, -1.0).astype(jnp.bfloat16)
    dk_ref[...] = turn(d_key, -1.0).astype(jnp.bfloat16)
    dv_ref[...] = d_value.astype(jnp.bfloat16)


def attention_both(proj, bias, d_joined, rope, seg, rows, tokens, att_rows, head_size):
    lanes = 2 * head_size
    pairs = att_rows // lanes
    block = lambda first: pl.BlockSpec((tokens, lanes), lambda r, h: (r, first + h))
    row = lambda first: pl.BlockSpec((1, lanes), lambda r, h: (0, first + h))
    out = jax.ShapeDtypeStruct((rows * tokens, att_rows), jnp.bfloat16)
    return pl.pallas_call(
        functools.partial(attention_kernel, head_size=head_size, half_rot=ROT // 2),
        grid=(rows, pairs),
        in_specs=[
            block(0), block(pairs), block(2 * pairs),
            row(0), row(pairs), row(2 * pairs),
            block(0),
            pl.BlockSpec((3, tokens, lanes), lambda r, h: (0, r, 0)),
            pl.BlockSpec((1, tokens, 1), lambda r, h: (r, 0, 0)),
            pl.BlockSpec((1, 1, tokens), lambda r, h: (r, 0, 0)),
        ],
        out_specs=[block(0)] * 4,
        out_shape=[out] * 4,
        compiler_params=pltpu.CompilerParams(vmem_limit_bytes=56 * 2**20),
        cost_estimate=pl.CostEstimate(
            flops=rows * pairs * 2 * 12 * tokens * tokens * lanes,
            bytes_accessed=rows * tokens * att_rows * 20,
            transcendentals=rows * pairs * 2 * tokens * tokens,
        ),
        name="attention",
    )(proj, proj, proj, bias, bias, bias, d_joined, rope, seg[:, :, None], seg[:, None, :])


def split_heads(
    n_dp, n_seq, tokens, cotangent, segment_ids, doc_positions,
    in_weight, in_first, in_second, in_average,
    out_weight, out_first, out_second, out_average,
    small_params, small_first, small_second, small_average,
):
    bf16, f32 = jnp.bfloat16, jnp.float32
    rows, own_tokens, width = tokens.shape
    row_tokens = own_tokens * n_seq
    all_tokens = rows * row_tokens
    head_size = width // HEADS
    ffn = (in_weight.shape[1] - 3 * width) // 2
    in_rows, own = in_weight.shape[0], out_weight.shape[0]
    dp_rows = own * n_seq
    att = width // n_seq
    late = width - dp_rows
    act = [(dp_rows - late) // n_seq, own, own]
    act_all = sum(act)
    cuts = [0, act[0] * n_seq, (act[0] + own) * n_seq, ffn]
    lead = att - own
    slot = act[0] + late
    p, s = lax.axis_index("dp"), lax.axis_index("seq")

    def share(v):
        parts = [v[:, i * width : (i + 1) * width].reshape(-1, n_seq, att) for i in range(3)]
        for half in range(2):
            base = 3 * width + half * ffn
            for i in range(3):
                parts.append(v[:, base + cuts[i] : base + cuts[i + 1]].reshape(-1, n_seq, act[i]))
        return jnp.transpose(jnp.concatenate(parts, axis=2), (1, 0, 2))

    def unshare(v):
        v = jnp.transpose(v, (1, 0, 2))
        sizes = [att] * 3 + act * 2
        parts, at = [], 0
        for size in sizes:
            parts.append(v[:, :, at : at + size].reshape(v.shape[0], n_seq * size))
            at += size
        return jnp.concatenate(parts, axis=1)

    in_low = lax.all_to_all(share(in_weight.astype(bf16)), "seq", 0, 0, tiled=True)
    in_low = in_low.reshape(n_seq * in_rows, 3 * att + 2 * act_all)
    in_low = lax.all_gather(in_low, "dp", axis=0, tiled=True)
    small_low = lax.all_gather(small_params.astype(bf16), ("dp", "seq"), axis=0, tiled=True)
    small_low = small_low.astype(f32)
    gain, shift = small_low[:, 0], small_low[:, 1]
    bias = lax.dynamic_slice_in_dim(small_low[:, 2:5], s * att, att, 0).T.reshape(1, 3 * att)

    out_low = out_weight.astype(bf16)
    from_next = lax.ppermute(out_low[:late], "seq", [(k, (k - 1) % n_seq) for k in range(n_seq)])
    start = jnp.where(p == 0, lead * s, jnp.where(p == 1, late - lead * s, 0))
    joined_rows = jnp.concatenate([out_low, from_next, out_low[:lead]], axis=0)
    main = lax.dynamic_slice_in_dim(joined_rows, start, att, 0)
    late_slot = jnp.concatenate([main[: act[0]], from_next], axis=0)
    plain_slot = jnp.concatenate([main, main[: slot - att]], axis=0)
    slots = lax.all_gather(jnp.where(p == 1, late_slot, plain_slot), "dp", axis=0)
    last = s == n_seq - 1
    keep = att - late
    out_mine = jnp.concatenate(
        [
            slots[0, :keep],
            jnp.where(last, slots[1, act[0] : slot], slots[0, keep:att]),
            slots[1, : act[0]],
            slots[2, :own],
            slots[3, :own],
        ],
        axis=0,
    )

    x_full = lax.all_gather(tokens, "seq", axis=1, tiled=True).reshape(all_tokens, width)
    g_full = lax.all_gather(cotangent, "seq", axis=1, tiled=True).reshape(all_tokens, width)
    seg_full = lax.all_gather(segment_ids, "seq", axis=1, tiled=True)
    pos_full = lax.all_gather(doc_positions, "seq", axis=1, tiled=True)

    def normalise(v):
        v = v.astype(f32)
        centered = v - jnp.mean(v, axis=-1, keepdims=True)
        inv_std = lax.rsqrt(jnp.mean(centered * centered, axis=-1, keepdims=True) + norm_eps)
        return centered * inv_std, inv_std

    hidden = (normalise(x_full)[0] * gain + shift).astype(bf16)
    proj = jnp.dot(hidden, in_low, preferred_element_type=f32)
    d_joined = lax.dot_general(
        g_full, out_mine, (((1,), (1,)), ((), ())), preferred_element_type=f32
    ).astype(bf16)

    half_rot = ROT // 2
    inv_freq = rope_base ** (-2.0 * jnp.arange(half_rot, dtype=f32) / ROT)
    angles = pos_full.reshape(all_tokens, 1).astype(f32) * inv_freq
    cos, sin = jnp.cos(angles), jnp.sin(angles)
    rest = head_size - ROT
    one, zero = jnp.ones((all_tokens, rest), f32), jnp.zeros((all_tokens, rest), f32)
    none = jnp.zeros_like(sin)
    rope = jnp.stack(
        [
            jnp.concatenate([cos, cos, one] * 2, axis=1),
            jnp.concatenate([-sin, none, zero] * 2, axis=1),
            jnp.concatenate([none, sin, zero] * 2, axis=1),
        ]
    )
    att_low, d_query, d_key, d_value = attention_both(
        proj, bias, d_joined, rope, seg_full, rows, row_tokens, att, head_size
    )

    gate = proj[:, 3 * att : 3 * att + act_all]
    up = proj[:, 3 * att + act_all :]
    sig = jax.nn.sigmoid(gate)
    silu = gate * sig
    joined = jnp.concatenate([att_low, (silu * up).astype(bf16)], axis=1)
    d_act = d_joined[:, att:].astype(f32)
    d_gate = d_act * up * sig * (1.0 + gate * (1.0 - sig))
    d_up = d_act * silu
    d_proj = jnp.concatenate(
        [d_query, d_key, d_value, d_gate.astype(bf16), d_up.astype(bf16)], axis=1
    )

    branch = jnp.dot(joined, out_mine, preferred_element_type=f32).astype(bf16)
    branch = lax.psum_scatter(
        branch.reshape(rows, row_tokens, width), "seq", scatter_dimension=1, tiled=True
    )
    output = (tokens.astype(f32) + branch.astype(f32)).astype(bf16)

    out_part = lax.dot_general(
        joined, g_full, (((0,), (0,)), ((), ())), preferred_element_type=f32
    ).astype(bf16)
    a0 = out_part[:att]
    a1, a2, a3 = (
        out_part[att : att + act[0]],
        out_part[att + act[0] : att + act[0] + own],
        out_part[att + act[0] + own :],
    )
    fill = lambda v: jnp.pad(v, ((0, slot - v.shape[0]), (0, 0)))
    out_slots = jnp.stack(
        [fill(a0), jnp.concatenate([a1, a0[keep:]], axis=0), fill(a2), fill(a3)]
    )
    out_sum = lax.psum_scatter(out_slots, "dp", scatter_dimension=0, tiled=True)[0]
    send_at = jnp.where(p == 0, keep, jnp.where(last, act[0], act[0] - late))
    sent = lax.dynamic_slice_in_dim(out_sum, send_at, late, 0)
    from_prev = lax.ppermute(sent, "seq", [(k, (k + 1) % n_seq) for k in range(n_seq)])
    count = jnp.where(p == 0, lead * s, jnp.where(p == 1, late - lead * s, 0))
    out_grad = lax.dynamic_slice_in_dim(
        jnp.concatenate([from_prev, out_sum[:own]], axis=0), late - count, own, 0
    ).astype(f32)

    in_part = lax.dot_general(
        hidden, d_proj, (((0,), (0,)), ((), ())), preferred_element_type=f32
    ).astype(bf16)
    in_sum = lax.psum_scatter(in_part, "dp", scatter_dimension=0, tiled=True)
    in_sum = lax.all_to_all(in_sum.reshape(n_seq, in_rows, -1), "seq", 0, 0, tiled=True)
    in_grad = unshare(in_sum).astype(f32)

    d_hidden = lax.dot_general(
        d_proj, in_low, (((1,), (1,)), ((), ())), preferred_element_type=f32
    ).astype(bf16)
    d_hidden = lax.psum_scatter(
        d_hidden.reshape(rows, row_tokens, width), "seq", scatter_dimension=1, tiled=True
    ).astype(f32)
    normed, inv_std = normalise(tokens)
    d_normed = d_hidden * gain
    input_grad = cotangent.astype(f32) + inv_std * (
        d_normed
        - jnp.mean(d_normed, axis=-1, keepdims=True)
        - normed * jnp.mean(d_normed * normed, axis=-1, keepdims=True)
    )

    gain_grad = jnp.sum(d_hidden * normed, axis=(0, 1))
    shift_grad = jnp.sum(d_hidden, axis=(0, 1))
    bias_part = jnp.sum(d_proj[:, : 3 * att].astype(f32), axis=0).reshape(3, att).T
    bias_grad = lax.dynamic_update_slice_in_dim(jnp.zeros((width, 3), f32), bias_part, s * att, 0)
    small_term = jnp.concatenate([gain_grad[:, None], shift_grad[:, None], bias_grad], axis=1)
    small_grad = lax.psum_scatter(small_term, ("dp", "seq"), scatter_dimension=0, tiled=True)

    in_new = adam_update(
        in_weight, in_first, in_second, in_average, in_grad, matrix_rate, weight_decay
    )
    out_new = adam_update(
        out_weight, out_first, out_second, out_average, out_grad, matrix_rate, weight_decay
    )
    small_new = adam_update(
        small_params, small_first, small_second, small_average, small_grad, small_rate, 0.0
    )
    return (output, input_grad, *in_new, *out_new, *small_new, small_grad, in_grad, out_grad)


def solution(mesh):
    n_dp, n_seq = mesh.shape["dp"], mesh.shape["seq"]

    def choose(*operands):
        own_rows = operands[8].shape[0]
        model_width = operands[0].shape[2]
        if heads_fit(n_dp, n_seq, own_rows, model_width, operands[4].shape[1]):
            return split_heads(n_dp, n_seq, *operands)
        return per_device(*operands)

    return jax.shard_map(
        choose,
        mesh=mesh,
        in_specs=(
            P("dp", "seq", None),
            P("dp", "seq", None),
            P("dp", "seq"),
            P("dp", "seq"),
            P(("dp", "seq"), None),
            P(("dp", "seq"), None),
            P(("dp", "seq"), None),
            P(("dp", "seq"), None),
            P(("dp", "seq"), None),
            P(("dp", "seq"), None),
            P(("dp", "seq"), None),
            P(("dp", "seq"), None),
            P(("dp", "seq"), None),
            P(("dp", "seq"), None),
            P(("dp", "seq"), None),
            P(("dp", "seq"), None),
        ),
        out_specs=(
            P("dp", "seq", None),
            P("dp", "seq", None),
            P(("dp", "seq"), None),
            P(("dp", "seq"), None),
            P(("dp", "seq"), None),
            P(("dp", "seq"), None),
            P(("dp", "seq"), None),
            P(("dp", "seq"), None),
            P(("dp", "seq"), None),
            P(("dp", "seq"), None),
            P(("dp", "seq"), None),
            P(("dp", "seq"), None),
            P(("dp", "seq"), None),
            P(("dp", "seq"), None),
        ),
        check_vma=False,
    )
```

```python
import functools

import jax
import jax.numpy as jnp
from jax import lax
from jax.experimental import pallas as pl
from jax.experimental.pallas import tpu as pltpu
from jax.sharding import PartitionSpec as P

HEADS = 32
ROT = 16
STEP = 2


beta_one = 0.9
adam_eps = 1e-08
matrix_rate = 0.001
small_rate = 0.01
weight_decay = 0.1
norm_eps = 1e-05
rope_base = 10000.0
neg_large = -1e30


def rope_tables(positions, rot_dims):
    half_rot = rot_dims // 2
    inv_freq = rope_base ** (-2.0 * jnp.arange(half_rot, dtype=jnp.float32) / rot_dims)
    angles = positions.astype(jnp.float32)[..., None] * inv_freq
    return (jnp.cos(angles)[..., None, :], jnp.sin(angles)[..., None, :])


def apply_rope(field_in, cosine_tab, sine_tab, rot_dims):
    half_rot = rot_dims // 2
    low_half = field_in[..., :half_rot]
    high_half = field_in[..., half_rot:rot_dims]
    return jnp.concatenate(
        [
            low_half * cosine_tab - high_half * sine_tab,
            high_half * cosine_tab + low_half * sine_tab,
            field_in[..., rot_dims:],
        ],
        axis=-1,
    )


def undo_rope(grad_in, cosine_tab, sine_tab, rot_dims):
    half_rot = rot_dims // 2
    low_half = grad_in[..., :half_rot]
    high_half = grad_in[..., half_rot:rot_dims]
    return jnp.concatenate(
        [
            low_half * cosine_tab + high_half * sine_tab,
            high_half * cosine_tab - low_half * sine_tab,
            grad_in[..., rot_dims:],
        ],
        axis=-1,
    )


def visible(query_seg, key_seg, query_pos, key_pos):
    same_doc = query_seg[:, :, None] == key_seg[:, None, :]
    causal = key_pos[None, :] <= query_pos[:, None]
    return (same_doc & causal[None])[:, None]


def to_tokens(head_major):
    return jnp.transpose(head_major, (0, 2, 1, 3))


def adam_update(weight, first, second, average, gradient, rate, decay_rate):
    beta_two = 1.0 - STEP ** (-0.8)
    average_keep = min(0.999, (1.0 + STEP) / (10.0 + STEP))
    first_new = beta_one * first + (1.0 - beta_one) * gradient
    second_new = beta_two * second + (1.0 - beta_two) * gradient * gradient
    moment_hat = beta_one * first_new / (1.0 - beta_one ** (STEP + 1)) + (
        1.0 - beta_one
    ) * gradient / (1.0 - beta_one**STEP)
    weight_new = weight - rate * (
        moment_hat / (jnp.sqrt(second_new) + adam_eps) + decay_rate * weight
    )
    average_new = average_keep * average + (1.0 - average_keep) * weight_new
    return (weight_new, second_new, average_new)


def per_device(
    tokens,
    cotangent,
    segment_ids,
    doc_positions,
    in_weight,
    in_first,
    in_second,
    in_average,
    out_weight,
    out_first,
    out_second,
    out_average,
    small_params,
    small_first,
    small_second,
    small_average,
):
    rows_here, row_tokens, model_width = tokens.shape
    head_count = HEADS
    head_size = model_width // head_count
    score_scale = head_size ** (-0.5)
    all_tokens = rows_here * row_tokens
    wide_in = in_weight.shape[1]
    ffn_width = (wide_in - 3 * model_width) // 2
    shape_heads = (rows_here, row_tokens, head_count, head_size)
    own_places = lax.axis_index("seq") * row_tokens + jnp.arange(row_tokens)
    flat_in = tokens.astype(jnp.float32).reshape(all_tokens, model_width)
    centered = flat_in - jnp.mean(flat_in, axis=-1, keepdims=True)
    inv_std = lax.rsqrt(jnp.mean(centered * centered, axis=-1, keepdims=True) + norm_eps)
    normed = centered * inv_std
    in_low = in_weight.astype(jnp.bfloat16)
    out_low = out_weight.astype(jnp.bfloat16)
    small_low = small_params.astype(jnp.bfloat16)
    w_piece = lax.all_gather(in_low, ("dp", "seq"), axis=0, tiled=True)
    s_piece = lax.all_gather(small_low, ("dp", "seq"), axis=0, tiled=True)
    columns = normed
    s_float = s_piece.astype(jnp.float32)
    h_piece = (columns * s_float[:, 0] + s_float[:, 1]).astype(jnp.bfloat16)
    proj_acc = jnp.dot(h_piece, w_piece, preferred_element_type=jnp.float32)
    norm_gain = s_float[:, 0]
    qkv_bias = s_float[:, 2:5].T.reshape(3 * model_width)
    qkv_full = proj_acc[:, : 3 * model_width] + qkv_bias
    gate_pre = proj_acc[:, 3 * model_width : 3 * model_width + ffn_width]
    up_pre = proj_acc[:, 3 * model_width + ffn_width :]
    cosine_tab, sine_tab = rope_tables(doc_positions, ROT)
    query_low = apply_rope(
        qkv_full[:, :model_width].reshape(shape_heads), cosine_tab, sine_tab, ROT
    ).astype(jnp.bfloat16)
    key_low = apply_rope(
        qkv_full[:, model_width : 2 * model_width].reshape(shape_heads), cosine_tab, sine_tab, ROT
    ).astype(jnp.bfloat16)
    value_low = qkv_full[:, 2 * model_width :].reshape(shape_heads).astype(jnp.bfloat16)
    seg_low = segment_ids.astype(jnp.bfloat16)
    seg_own = segment_ids.astype(jnp.float32)
    key_flat = key_low.reshape(rows_here, row_tokens, model_width)
    value_flat = value_low.reshape(rows_here, row_tokens, model_width)
    attend_init = (
        jnp.full((rows_here, head_count, row_tokens), neg_large, jnp.float32),
        jnp.zeros((rows_here, head_count, row_tokens), jnp.float32),
        jnp.zeros((rows_here, head_count, row_tokens, head_size), jnp.float32),
    )
    key_piece = lax.all_gather(key_flat, "seq", axis=1, tiled=True)
    value_piece = lax.all_gather(value_flat, "seq", axis=1, tiled=True)
    seg_piece = lax.all_gather(seg_low, "seq", axis=1, tiled=True)
    turn_count = key_piece.shape[1] // row_tokens

    def attend_one_turn(turn_index, inner_state):
        offset = turn_index * row_tokens
        key_blk = lax.dynamic_slice_in_dim(key_piece, offset, row_tokens, 1).reshape(shape_heads)
        value_blk = lax.dynamic_slice_in_dim(value_piece, offset, row_tokens, 1).reshape(
            shape_heads
        )
        seg_blk = lax.dynamic_slice_in_dim(seg_piece, offset, row_tokens, 1).astype(jnp.float32)
        key_mask = visible(seg_own, seg_blk, own_places, offset + jnp.arange(row_tokens))
        running_top, running_sum, weighted = inner_state
        scores = (
            jnp.einsum("rqhe,rkhe->rhqk", query_low, key_blk, preferred_element_type=jnp.float32)
            * score_scale
        )
        scores = jnp.where(key_mask, scores, neg_large)
        new_top = jnp.maximum(running_top, jnp.max(scores, axis=-1))
        weights = jnp.where(key_mask, jnp.exp(scores - new_top[..., None]), 0.0)
        factor = jnp.exp(running_top - new_top)
        running_sum = running_sum * factor + jnp.sum(weights, axis=-1)
        weighted = weighted * factor[..., None] + jnp.einsum(
            "rhqk,rkhe->rhqe",
            weights.astype(jnp.bfloat16),
            value_blk,
            preferred_element_type=jnp.float32,
        )
        return (new_top, running_sum, weighted)

    running_top, running_sum, weighted = lax.fori_loop(0, turn_count, attend_one_turn, attend_init)
    attended = weighted / running_sum[..., None]
    log_total = running_top + jnp.log(running_sum)
    attended_low = to_tokens(attended).reshape(all_tokens, model_width).astype(jnp.bfloat16)
    gate_sig = jax.nn.sigmoid(gate_pre)
    activated = gate_pre * gate_sig * up_pre
    joined = jnp.concatenate([attended_low, activated.astype(jnp.bfloat16)], axis=1)
    columns = joined
    branch_sum = jnp.dot(
        columns,
        lax.all_gather(out_low, ("dp", "seq"), axis=0, tiled=True),
        preferred_element_type=jnp.float32,
    )
    output = (flat_in + branch_sum).astype(jnp.bfloat16).reshape(rows_here, row_tokens, model_width)
    grad_out = cotangent.reshape(all_tokens, model_width)
    d_joined = lax.dot_general(
        grad_out,
        lax.all_gather(out_low, ("dp", "seq"), axis=0, tiled=True),
        (((1,), (1,)), ((), ())),
        preferred_element_type=jnp.float32,
    )
    d_joined = d_joined.astype(jnp.bfloat16)
    columns = joined
    out_grad = lax.psum_scatter(
        lax.dot_general(
            columns, grad_out, (((0,), (0,)), ((), ())), preferred_element_type=jnp.float32
        ),
        ("dp", "seq"),
        scatter_dimension=0,
        tiled=True,
    )
    d_attended = d_joined[:, :model_width].reshape(shape_heads)
    d_act = d_joined[:, model_width:].astype(jnp.float32)
    d_gate = d_act * up_pre * gate_sig * (1.0 + gate_pre * (1.0 - gate_sig))
    d_up = d_act * gate_pre * gate_sig
    out_dot = jnp.einsum("rqhe,rhqe->rhq", d_attended.astype(jnp.float32), attended)
    grad_zero = jnp.zeros((rows_here, head_count, row_tokens, head_size), jnp.float32)
    query_key_piece = lax.all_gather(key_flat, "seq", axis=1, tiled=True)
    query_value_piece = lax.all_gather(value_flat, "seq", axis=1, tiled=True)
    query_seg_piece = lax.all_gather(seg_low, "seq", axis=1, tiled=True)
    turn_count = query_key_piece.shape[1] // row_tokens

    def query_one_turn(turn_index, inner_state):
        offset = turn_index * row_tokens
        key_blk = lax.dynamic_slice_in_dim(query_key_piece, offset, row_tokens, 1).reshape(
            shape_heads
        )
        value_blk = lax.dynamic_slice_in_dim(query_value_piece, offset, row_tokens, 1).reshape(
            shape_heads
        )
        seg_blk = lax.dynamic_slice_in_dim(query_seg_piece, offset, row_tokens, 1).astype(
            jnp.float32
        )
        key_mask = visible(seg_own, seg_blk, own_places, offset + jnp.arange(row_tokens))
        scores = (
            jnp.einsum("rqhe,rkhe->rhqk", query_low, key_blk, preferred_element_type=jnp.float32)
            * score_scale
        )
        weights = jnp.where(key_mask, jnp.exp(scores - log_total[..., None]), 0.0)
        d_prob = jnp.einsum(
            "rqhe,rkhe->rhqk", d_attended, value_blk, preferred_element_type=jnp.float32
        )
        d_score = (weights * (d_prob - out_dot[..., None])).astype(jnp.bfloat16)
        return (
            inner_state
            + jnp.einsum("rhqk,rkhe->rhqe", d_score, key_blk, preferred_element_type=jnp.float32)
            * score_scale
        )

    d_query = lax.fori_loop(0, turn_count, query_one_turn, grad_zero)
    row_stats = jnp.concatenate(
        [jnp.transpose(log_total, (0, 2, 1)), jnp.transpose(out_dot, (0, 2, 1))], axis=2
    )
    stat_high = row_stats.astype(jnp.bfloat16)
    stat_low = (row_stats - stat_high.astype(jnp.float32)).astype(jnp.bfloat16)
    query_flat = query_low.reshape(rows_here, row_tokens, model_width)
    d_att_flat = d_attended.reshape(rows_here, row_tokens, model_width)
    query_piece = lax.all_gather(query_flat, "seq", axis=1, tiled=True)
    dout_piece = lax.all_gather(d_att_flat, "seq", axis=1, tiled=True)
    high_piece = lax.all_gather(stat_high, "seq", axis=1, tiled=True)
    low_piece = lax.all_gather(stat_low, "seq", axis=1, tiled=True)
    key_seg_piece = lax.all_gather(seg_low, "seq", axis=1, tiled=True)
    turn_count = query_piece.shape[1] // row_tokens

    def key_one_turn(turn_index, inner_state):
        offset = turn_index * row_tokens
        query_blk = lax.dynamic_slice_in_dim(query_piece, offset, row_tokens, 1).reshape(
            shape_heads
        )
        dout_blk = lax.dynamic_slice_in_dim(dout_piece, offset, row_tokens, 1).reshape(shape_heads)
        stat_blk = lax.dynamic_slice_in_dim(high_piece, offset, row_tokens, 1).astype(
            jnp.float32
        ) + lax.dynamic_slice_in_dim(low_piece, offset, row_tokens, 1).astype(jnp.float32)
        lse_blk = jnp.transpose(stat_blk[..., :head_count], (0, 2, 1))
        dot_blk = jnp.transpose(stat_blk[..., head_count:], (0, 2, 1))
        seg_blk = lax.dynamic_slice_in_dim(key_seg_piece, offset, row_tokens, 1).astype(jnp.float32)
        key_mask = visible(seg_blk, seg_own, offset + jnp.arange(row_tokens), own_places)
        d_key, d_value = inner_state
        scores = (
            jnp.einsum("rqhe,rkhe->rhqk", query_blk, key_low, preferred_element_type=jnp.float32)
            * score_scale
        )
        weights = jnp.where(key_mask, jnp.exp(scores - lse_blk[..., None]), 0.0)
        d_value = d_value + jnp.einsum(
            "rhqk,rqhe->rhke",
            weights.astype(jnp.bfloat16),
            dout_blk,
            preferred_element_type=jnp.float32,
        )
        d_prob = jnp.einsum(
            "rqhe,rkhe->rhqk", dout_blk, value_low, preferred_element_type=jnp.float32
        )
        d_score = (weights * (d_prob - dot_blk[..., None])).astype(jnp.bfloat16)
        d_key = (
            d_key
            + jnp.einsum("rhqk,rqhe->rhke", d_score, query_blk, preferred_element_type=jnp.float32)
            * score_scale
        )
        return (d_key, d_value)

    d_key, d_value = lax.fori_loop(0, turn_count, key_one_turn, (grad_zero, grad_zero))
    d_query_tok = undo_rope(to_tokens(d_query), cosine_tab, sine_tab, ROT).reshape(
        all_tokens, model_width
    )
    d_key_tok = undo_rope(to_tokens(d_key), cosine_tab, sine_tab, ROT).reshape(
        all_tokens, model_width
    )
    d_value_tok = to_tokens(d_value).reshape(all_tokens, model_width)
    d_proj = jnp.concatenate([d_query_tok, d_key_tok, d_value_tok, d_gate, d_up], axis=1).astype(
        jnp.bfloat16
    )
    d_hidden = lax.dot_general(
        d_proj,
        lax.all_gather(in_low, ("dp", "seq"), axis=0, tiled=True),
        (((1,), (1,)), ((), ())),
        preferred_element_type=jnp.float32,
    )
    columns = h_piece
    in_grad = lax.psum_scatter(
        lax.dot_general(
            columns, d_proj, (((0,), (0,)), ((), ())), preferred_element_type=jnp.float32
        ),
        ("dp", "seq"),
        scatter_dimension=0,
        tiled=True,
    )
    gain_grad = jnp.sum(d_hidden * normed, axis=0)
    shift_grad = jnp.sum(d_hidden, axis=0)
    bias_grad = (
        jnp.sum(d_proj[:, : 3 * model_width].astype(jnp.float32), axis=0).reshape(3, model_width).T
    )
    small_term = jnp.concatenate([gain_grad[:, None], shift_grad[:, None], bias_grad], axis=1)
    small_grad = lax.psum_scatter(small_term, ("dp", "seq"), scatter_dimension=0, tiled=True)
    d_normed = d_hidden * norm_gain
    input_grad = grad_out.astype(jnp.float32) + inv_std * (
        d_normed
        - jnp.mean(d_normed, axis=-1, keepdims=True)
        - normed * jnp.mean(d_normed * normed, axis=-1, keepdims=True)
    )
    input_grad = input_grad.reshape(rows_here, row_tokens, model_width)
    in_new = adam_update(
        in_weight, in_first, in_second, in_average, in_grad, matrix_rate, weight_decay
    )
    out_new = adam_update(
        out_weight, out_first, out_second, out_average, out_grad, matrix_rate, weight_decay
    )
    small_new = adam_update(
        small_params, small_first, small_second, small_average, small_grad, small_rate, 0.0
    )
    return (
        output,
        input_grad,
        in_new[0],
        in_new[1],
        in_new[2],
        out_new[0],
        out_new[1],
        out_new[2],
        small_new[0],
        small_new[1],
        small_new[2],
        small_grad,
        in_grad,
        out_grad,
    )


def heads_fit(n_dp, n_seq, own_rows, model_width, wide_in):
    dp_rows = own_rows * n_seq
    if n_dp != 4 or HEADS % (2 * n_seq) or not dp_rows < model_width < 2 * dp_rows:
        return False
    att_rows = model_width // n_seq
    late_att = model_width - dp_rows
    first_act = dp_rows - late_att
    if first_act % n_seq:
        return False
    lead = att_rows - own_rows
    return (
        wide_in - 3 * model_width == 2 * (n_dp * dp_rows - model_width)
        and lead == own_rows - first_act // n_seq
        and lead * n_seq == late_att
        and lead % 16 == 0
    )


def attention_kernel(
    q_ref, k_ref, v_ref, bq_ref, bk_ref, bv_ref, da_ref, rope_ref, seg_q_ref, seg_k_ref,
    o_ref, dq_ref, dk_ref, dv_ref, *, head_size, half_rot,
):
    def whole(v):
        across, depth = v.shape[:2]
        parts = [v[x, z].reshape(v.shape[-2:]) for z in range(depth) for x in range(across)]
        return jnp.concatenate(parts, axis=0)

    def store(ref, v):
        across, depth, _, some, _ = ref.shape
        for z in range(depth):
            for x in range(across):
                at = (z * across + x) * some
                ref[x, z, 0] = v[at : at + some].astype(ref.dtype)

    cos, sin_low, sin_high = (whole(rope_ref[i]) for i in range(3))
    tokens, lanes = cos.shape
    scale = head_size ** (-0.5)

    def turn(v, way):
        return (
            v * cos
            + way * pltpu.roll(v, lanes - half_rot, 1) * sin_low
            + way * pltpu.roll(v, half_rot, 1) * sin_high
        )

    query = (turn(whole(q_ref[...]) + bq_ref[...], 1.0)).astype(jnp.bfloat16) * scale
    query = query.astype(jnp.bfloat16)
    key = turn(whole(k_ref[...]) + bk_ref[...], 1.0).astype(jnp.bfloat16)
    value = (whole(v_ref[...]) + bv_ref[...]).astype(jnp.bfloat16)
    d_att = whole(da_ref[...])
    place_q = lax.broadcasted_iota(jnp.int32, (tokens, tokens), 0)
    place_k = lax.broadcasted_iota(jnp.int32, (tokens, tokens), 1)
    mask = (seg_q_ref[0] == seg_k_ref[0]) & (place_k <= place_q)
    lane = lax.broadcasted_iota(jnp.int32, (tokens, lanes), 1)
    nt = (((1,), (1,)), ((), ()))
    tn = (((0,), (0,)), ((), ()))
    dot = functools.partial(lax.dot_general, preferred_element_type=jnp.float32)
    att = jnp.zeros((tokens, lanes), jnp.float32)
    d_query = jnp.zeros((tokens, lanes), jnp.float32)
    d_key = jnp.zeros((tokens, lanes), jnp.float32)
    d_value = jnp.zeros((tokens, lanes), jnp.float32)
    for head in range(lanes // head_size):
        mine = (lane >= head * head_size) & (lane < (head + 1) * head_size)
        q_h = jnp.where(mine, query, jnp.zeros_like(query))
        da_h = jnp.where(mine, d_att, jnp.zeros_like(d_att))
        scores = jnp.where(mask, dot(q_h, key, nt), neg_large)
        top = jnp.max(scores, axis=1, keepdims=True)
        weights = jnp.exp(scores - top)
        probs = weights * (1.0 / jnp.sum(weights, axis=1, keepdims=True))
        probs_low = probs.astype(jnp.bfloat16)
        att_h = jnp.where(mine, dot(probs_low, value, (((1,), (0,)), ((), ()))), 0.0)
        out_dot = jnp.sum(att_h * d_att.astype(jnp.float32), axis=1, keepdims=True)
        d_prob = dot(da_h, value, nt)
        d_score = (probs * (d_prob - out_dot)).astype(jnp.bfloat16)
        att = att + att_h
        d_query = d_query + jnp.where(mine, dot(d_score, key, (((1,), (0,)), ((), ()))), 0.0)
        d_key = d_key + dot(d_score, q_h, tn)
        d_value = d_value + dot(probs_low, da_h, tn)
    store(o_ref, att)
    store(dq_ref, turn(d_query * scale, -1.0))
    store(dk_ref, turn(d_key, -1.0))
    store(dv_ref, d_value)


def attention_both(proj, bias, d_joined, rope, seg, n_seq, att_rows, head_size):
    rows, tokens = seg.shape
    lanes = 2 * head_size
    pairs = att_rows // lanes
    order = (2, n_seq // 2, rows, tokens // n_seq)
    wide = lambda v: v.reshape(order + v.shape[-1:])
    shape = (2, n_seq // 2, 1, tokens // n_seq, lanes)
    block = lambda first: pl.BlockSpec(shape, lambda r, h: (0, 0, r, 0, first + h))
    row = lambda first: pl.BlockSpec((1, lanes), lambda r, h: (0, first + h))
    out = jax.ShapeDtypeStruct(order + (att_rows,), jnp.bfloat16)
    proj, d_joined = wide(proj), wide(d_joined)
    results = pl.pallas_call(
        functools.partial(attention_kernel, head_size=head_size, half_rot=ROT // 2),
        grid=(rows, pairs),
        in_specs=[
            block(0), block(pairs), block(2 * pairs),
            row(0), row(pairs), row(2 * pairs),
            block(0),
            pl.BlockSpec((3,) + shape, lambda r, h: (0, 0, 0, r, 0, 0)),
            pl.BlockSpec((1, tokens, 1), lambda r, h: (r, 0, 0)),
            pl.BlockSpec((1, 1, tokens), lambda r, h: (r, 0, 0)),
        ],
        out_specs=[block(0)] * 4,
        out_shape=[out] * 4,
        compiler_params=pltpu.CompilerParams(vmem_limit_bytes=56 * 2**20),
        cost_estimate=pl.CostEstimate(
            flops=rows * pairs * 2 * 12 * tokens * tokens * lanes,
            bytes_accessed=rows * tokens * att_rows * 20,
            transcendentals=rows * pairs * 2 * tokens * tokens,
        ),
        name="attention",
    )(
        proj, proj, proj, bias, bias, bias, d_joined,
        rope.reshape((3,) + order + (lanes,)), seg[:, :, None], seg[:, None, :],
    )
    return [v.reshape(rows * tokens, att_rows) for v in results]

MESH_ID = pl.DeviceIdType.MESH


def remote(src, dst, send_sem, recv_sem, device):
    return pltpu.make_async_remote_copy(
        src_ref=src,
        dst_ref=dst,
        send_sem=send_sem,
        recv_sem=recv_sem,
        device_id=device,
        device_id_type=MESH_ID,
    )


class Place:
    def __init__(self, n_seq):
        self.n_seq = n_seq
        self.depth = n_seq // 2
        self.p, self.s = lax.axis_index("dp"), lax.axis_index("seq")
        self.y, self.c = self.p // 2, lax.rem(self.p, 2)
        self.z, self.x = self.s // 2, lax.rem(self.s, 2)
        self.p_y = (1 - self.y) * 2 + self.c
        self.p_c = self.y * 2 + 1 - self.c
        self.p_d = (1 - self.y) * 2 + 1 - self.c
        self.to_y = (self.p_y, self.s)
        self.to_c = (self.p_c, self.s)
        self.to_x = (self.p, self.z * 2 + 1 - self.x)
        self.to_up = (self.p, self.s + 2)
        self.to_down = (self.p, self.s - 2)

    def seq(self, hop):
        return lax.rem(self.s + hop + self.n_seq, self.n_seq)

    def meet(self):
        barrier = pltpu.get_barrier_semaphore()

        def greet(hop, carry):
            pl.semaphore_signal(
                barrier, inc=1, device_id=(self.p, self.seq(hop)), device_id_type=MESH_ID
            )
            return carry

        lax.fori_loop(1, self.n_seq, greet, 0)
        for device in (self.to_y, self.to_c):
            pl.semaphore_signal(barrier, inc=1, device_id=device, device_id_type=MESH_ID)
        pl.semaphore_wait(barrier, self.n_seq + 1)


class Spread:
    def __init__(self, at, own, full, sems):
        self.at, self.own, self.full, self.sems = at, own, full, sems

    def along(self, src, up, ref=None):
        sems, at = self.sems, self.at
        here = self.full.at[at.x, src]
        return remote(
            here if ref is None else ref,
            here,
            sems.at[0 if up else 1, src],
            sems.at[3, src],
            at.to_up if up else at.to_down,
        )

    def across(self, src, ref=None):
        sems, at = self.sems, self.at
        here = self.full.at[at.x, src]
        return remote(here if ref is None else ref, here, sems.at[2, src], sems.at[4, src], at.to_x)

    def local(self):
        return pltpu.make_async_copy(
            self.own, self.full.at[self.at.x, self.at.z], self.sems.at[5, 0]
        )

    def begin(self):
        at = self.at

        @pl.when(at.z < at.depth - 1)
        def _():
            self.along(at.z, True, self.own).start()

        @pl.when(at.z > 0)
        def _():
            self.along(at.z, False, self.own).start()

        self.across(at.z, self.own).start()
        self.local().start()

    def step(self, hop):
        at = self.at

        @pl.when(at.z - hop >= 0)
        def _():
            src = at.z - hop
            self.along(src, True).wait_recv()

            @pl.when(at.z < at.depth - 1)
            def _():
                self.along(src, True).start()

            self.across(src).start()

        @pl.when(at.z + hop < at.depth)
        def _():
            src = at.z + hop
            self.along(src, False).wait_recv()

            @pl.when(at.z > 0)
            def _():
                self.along(src, False).start()

            self.across(src).start()

    def arrive(self):
        at = self.at
        for src in range(at.depth):
            here = self.full.at[1 - at.x, src]
            remote(here, here, self.sems.at[2, src], self.sems.at[4, src], at.to_x).wait_recv()
        self.local().wait()

    def sent(self):
        at = self.at
        for src in range(at.depth):
            self.across(src).wait_send()

            @pl.when((at.z < at.depth - 1) & (src <= at.z))
            def _():
                self.along(src, True).wait_send()

            @pl.when((at.z > 0) & (src >= at.z))
            def _():
                self.along(src, False).wait_send()


class Fan:
    def __init__(self, at, pick, sems):
        self.at, self.pick, self.sems = at, pick, sems

    def y(self, k, ref=None):
        at = self.at
        here = self.pick(at.p, k)
        return remote(here if ref is None else ref, here, self.sems.at[0, k], self.sems.at[1, k], at.to_y)

    def core(self, k, ref=None):
        at = self.at
        here = self.pick(at.p, k)
        return remote(here if ref is None else ref, here, self.sems.at[2, k], self.sems.at[3, k], at.to_c)

    def pass_on(self, k):
        at = self.at
        here = self.pick(at.p_y, k)
        return remote(here, here, self.sems.at[4, k], self.sems.at[5, k], at.to_c)

    def from_y(self, k):
        here = self.pick(self.at.p_y, k)
        return remote(here, here, self.sems.at[0, k], self.sems.at[1, k], self.at.to_y)

    def from_core(self, k):
        here = self.pick(self.at.p_c, k)
        return remote(here, here, self.sems.at[2, k], self.sems.at[3, k], self.at.to_c)

    def from_diagonal(self, k):
        here = self.pick(self.at.p_d, k)
        return remote(here, here, self.sems.at[4, k], self.sems.at[5, k], self.at.to_c)


def loop(low, high, body):
    def step(k, carry):
        body(k)
        return carry

    lax.fori_loop(low, high, step, 0)


def gather_kernel(
    x_ref, g_ref, w_ref, o_ref, tile_ref,
    x_full, g_full, w_full, o_full, tiles,
    x_sems, g_sems, w_sems, w_fan_sems, o_sems, o_fan_sems, t_sems, t_fan_sems, local_sems,
    *, n_seq, late,
):
    at = Place(n_seq)
    own = o_ref.shape[0]
    body, extra = pl.ds(0, own), pl.ds(own, late)
    x_go = Spread(at, x_ref, x_full, x_sems)
    g_go = Spread(at, g_ref, g_full, g_sems)
    w_fan = Fan(at, lambda p, k: w_full.at[p, k], w_fan_sems)
    o_fan = Fan(at, lambda p, k: o_full.at[p, body if k == 0 else extra], o_fan_sems)
    t_fan = Fan(at, lambda p, k: tiles.at[p], t_fan_sems)

    def w_send(hop):
        to = at.seq(hop)
        return remote(w_ref.at[to], w_full.at[at.p, at.s], w_sems.at[0, to], w_sems.at[1, at.s], (at.p, to))

    def w_recv(hop):
        src = at.seq(-hop)
        here = w_full.at[at.p, src]
        return remote(here, here, w_sems.at[0, src], w_sems.at[1, src], (at.p, src))

    def t_send(hop):
        to = at.seq(hop)
        return remote(tile_ref, tiles.at[at.p, at.s], t_sems.at[0, to], t_sems.at[1, at.s], (at.p, to))

    def t_recv(hop):
        src = at.seq(-hop)
        here = tiles.at[at.p, src]
        return remote(here, here, t_sems.at[0, src], t_sems.at[1, src], (at.p, src))

    w_local = pltpu.make_async_copy(w_ref.at[at.s], w_full.at[at.p, at.s], local_sems.at[0])
    o_local = pltpu.make_async_copy(o_ref, o_full.at[at.p, body], local_sems.at[1])
    t_local = pltpu.make_async_copy(tile_ref, tiles.at[at.p, at.s], local_sems.at[2])
    head = o_ref.at[pl.ds(0, late)]
    o_send = remote(
        head, o_full.at[at.p, extra], o_sems.at[0], o_sems.at[1], (at.p, at.seq(-1))
    )

    at.meet()
    x_go.begin()
    loop(1, n_seq, lambda hop: t_send(hop).start())
    t_local.start()
    w_fan.y(at.s, w_ref.at[at.s]).start()
    loop(1, n_seq, lambda hop: w_send(hop).start())
    w_fan.core(at.s, w_ref.at[at.s]).start()
    w_local.start()
    o_fan.core(0, o_ref).start()
    o_local.start()
    for hop in range(1, at.depth):
        x_go.step(hop)
    g_go.begin()
    t_local.wait()
    loop(1, n_seq, lambda hop: t_recv(hop).wait_recv())
    t_fan.y(0).start()
    t_fan.core(0).start()

    @pl.when(at.y == 0)
    def _():
        o_send.start()

    def w_step(hop):
        src = at.seq(-hop)
        w_recv(hop).wait_recv()
        w_fan.y(src).start()
        w_fan.core(src).start()

    loop(1, n_seq, w_step)
    t_fan.from_y(0).wait_recv()
    t_fan.pass_on(0).start()
    o_fan.y(0, o_ref).start()
    for hop in range(1, at.depth):
        g_go.step(hop)

    @pl.when(at.y == 0)
    def _():
        o_send.wait_recv()
        o_fan.y(1).start()
        o_fan.core(1).start()

    def w_pass(hop):
        src = at.seq(-hop)
        w_fan.from_y(src).wait_recv()
        w_fan.pass_on(src).start()

    loop(0, n_seq, w_pass)
    o_fan.from_y(0).wait_recv()
    o_fan.pass_on(0).start()

    @pl.when(at.y == 1)
    def _():
        o_fan.from_y(1).wait_recv()
        o_fan.pass_on(1).start()

    x_go.arrive()
    g_go.arrive()
    w_local.wait()
    o_local.wait()
    t_fan.from_core(0).wait_recv()
    t_fan.from_diagonal(0).wait_recv()
    o_fan.from_core(0).wait_recv()
    o_fan.from_diagonal(0).wait_recv()

    @pl.when(at.y == 0)
    def _():
        o_fan.from_core(1).wait_recv()

    @pl.when(at.y == 1)
    def _():
        o_fan.from_diagonal(1).wait_recv()

    def w_last(k):
        w_fan.from_core(k).wait_recv()
        w_fan.from_diagonal(k).wait_recv()
        w_fan.y(k).wait_send()
        w_fan.core(k).wait_send()
        w_fan.pass_on(k).wait_send()

    loop(0, n_seq, w_last)

    x_go.sent()
    g_go.sent()

    def seq_sent(hop):
        w_send(hop).wait_send()
        t_send(hop).wait_send()

    loop(1, n_seq, seq_sent)
    for fan in (t_fan, o_fan):
        fan.y(0).wait_send()
        fan.core(0).wait_send()
        fan.pass_on(0).wait_send()

    @pl.when(at.y == 0)
    def _():
        o_send.wait_send()
        o_fan.y(1).wait_send()
        o_fan.core(1).wait_send()

    @pl.when(at.y == 1)
    def _():
        o_fan.pass_on(1).wait_send()


def gather_all(n_dp, n_seq, late, x, g, w, o, tile):
    depth = n_seq // 2
    own, width = o.shape
    rest = pl.BlockSpec(memory_space=pl.ANY)
    dma = pltpu.SemaphoreType.DMA
    like = lambda lead, ref: jax.ShapeDtypeStruct(lead + ref.shape, ref.dtype)
    return pl.pallas_call(
        functools.partial(gather_kernel, n_seq=n_seq, late=late),
        in_specs=[rest] * 5,
        out_specs=[rest] * 5,
        out_shape=[
            like((2, depth), x),
            like((2, depth), g),
            jax.ShapeDtypeStruct((n_dp,) + w.shape, w.dtype),
            jax.ShapeDtypeStruct((n_dp, own + late, width), o.dtype),
            like((n_dp, n_seq), tile),
        ],
        scratch_shapes=[
            dma((6, depth)), dma((6, depth)), dma((2, n_seq)), dma((6, n_seq)),
            dma((2,)), dma((6, 2)), dma((2, n_seq)), dma((6, 1)), dma((3,)),
        ],
        compiler_params=pltpu.CompilerParams(collective_id=0, has_side_effects=True),
        name="gather_all",
    )(x, g, w, o, tile)

def split_heads(
    n_dp, n_seq, tokens, cotangent, segment_ids, doc_positions,
    in_weight, in_first, in_second, in_average,
    out_weight, out_first, out_second, out_average,
    small_params, small_first, small_second, small_average,
):
    bf16, f32 = jnp.bfloat16, jnp.float32
    rows, own_tokens, width = tokens.shape
    row_tokens = own_tokens * n_seq
    all_tokens = rows * row_tokens
    head_size = width // HEADS
    ffn = (in_weight.shape[1] - 3 * width) // 2
    in_rows, own = in_weight.shape[0], out_weight.shape[0]
    dp_rows = own * n_seq
    att = width // n_seq
    late = width - dp_rows
    act = [(dp_rows - late) // n_seq, own, own]
    act_all = sum(act)
    cuts = [0, act[0] * n_seq, (act[0] + own) * n_seq, ffn]
    lead = att - own
    slot = act[0] + late
    p, s = lax.axis_index("dp"), lax.axis_index("seq")

    def share(v):
        parts = [v[:, i * width : (i + 1) * width].reshape(-1, n_seq, att) for i in range(3)]
        for half in range(2):
            base = 3 * width + half * ffn
            for i in range(3):
                parts.append(v[:, base + cuts[i] : base + cuts[i + 1]].reshape(-1, n_seq, act[i]))
        return jnp.transpose(jnp.concatenate(parts, axis=2), (1, 0, 2))

    def unshare(v):
        v = jnp.transpose(v, (1, 0, 2))
        sizes = [att] * 3 + act * 2
        parts, at = [], 0
        for size in sizes:
            parts.append(v[:, :, at : at + size].reshape(v.shape[0], n_seq * size))
            at += size
        return jnp.concatenate(parts, axis=1)

    out_low = out_weight.astype(bf16)
    small_low = small_params.astype(bf16).astype(f32).T
    widen = lambda v, n: jnp.pad(v, ((0, n - v.shape[0]), (0, 128 - v.shape[1])))
    tile = jnp.concatenate(
        [
            widen(small_low, 8),
            widen(jnp.concatenate([segment_ids, doc_positions], axis=0).astype(f32), 8),
        ],
        axis=0,
    )
    x_full, g_full, in_low, slots, tiles = gather_all(
        n_dp, n_seq, late, tokens, cotangent, share(in_weight.astype(bf16)), out_low, tile
    )
    x_full, g_full = x_full.reshape(all_tokens, width), g_full.reshape(all_tokens, width)
    in_low = in_low.reshape(n_dp * n_seq * in_rows, 3 * att + 2 * act_all)

    small_low = jnp.transpose(tiles[:, :, :5, :in_rows], (2, 0, 1, 3)).reshape(5, width)
    gain, shift = small_low[0], small_low[1]
    bias = lax.dynamic_slice_in_dim(small_low[2:5], s * att, att, 1).reshape(1, 3 * att)
    docs = lax.dynamic_index_in_dim(tiles, p, 0, keepdims=False)[:, 8:, :own_tokens]
    seg_full = jnp.transpose(docs[:, :rows], (1, 0, 2)).reshape(rows, row_tokens)
    pos_full = docs[:, rows : 2 * rows].reshape(n_seq // 2, 2, rows, own_tokens)
    pos_full = jnp.transpose(pos_full, (1, 0, 2, 3))

    late_at = late - lead * s
    first = lax.dynamic_slice_in_dim(slots[0], lead * s, att, 0)
    second = lax.dynamic_slice_in_dim(slots[1], late_at, act[0], 0)
    last = s == n_seq - 1
    keep = att - late
    out_mine = jnp.concatenate(
        [
            first[:keep],
            jnp.where(last, slots[1, own:], first[keep:]),
            second,
            slots[2, :own],
            slots[3, :own],
        ],
        axis=0,
    )

    def normalise(v):
        v = v.astype(f32)
        centered = v - jnp.mean(v, axis=-1, keepdims=True)
        inv_std = lax.rsqrt(jnp.mean(centered * centered, axis=-1, keepdims=True) + norm_eps)
        return centered * inv_std, inv_std

    hidden = (normalise(x_full)[0] * gain + shift).astype(bf16)
    proj = jnp.dot(hidden, in_low, preferred_element_type=f32)
    d_joined = lax.dot_general(
        g_full, out_mine, (((1,), (1,)), ((), ())), preferred_element_type=f32
    ).astype(bf16)

    half_rot = ROT // 2
    inv_freq = rope_base ** (-2.0 * jnp.arange(half_rot, dtype=f32) / ROT)
    angles = pos_full.reshape(all_tokens, 1).astype(f32) * inv_freq
    cos, sin = jnp.cos(angles), jnp.sin(angles)
    rest = head_size - ROT
    one, zero = jnp.ones((all_tokens, rest), f32), jnp.zeros((all_tokens, rest), f32)
    none = jnp.zeros_like(sin)
    rope = jnp.stack(
        [
            jnp.concatenate([cos, cos, one] * 2, axis=1),
            jnp.concatenate([-sin, none, zero] * 2, axis=1),
            jnp.concatenate([none, sin, zero] * 2, axis=1),
        ]
    )
    att_low, d_query, d_key, d_value = attention_both(
        proj, bias, d_joined, rope, seg_full, n_seq, att, head_size
    )

    gate = proj[:, 3 * att : 3 * att + act_all]
    up = proj[:, 3 * att + act_all :]
    sig = jax.nn.sigmoid(gate)
    silu = gate * sig
    joined = jnp.concatenate([att_low, (silu * up).astype(bf16)], axis=1)
    d_act = d_joined[:, att:].astype(f32)
    d_gate = d_act * up * sig * (1.0 + gate * (1.0 - sig))
    d_up = d_act * silu
    d_proj = jnp.concatenate(
        [d_query, d_key, d_value, d_gate.astype(bf16), d_up.astype(bf16)], axis=1
    )

    branch = jnp.dot(joined, out_mine, preferred_element_type=f32).astype(bf16)
    def to_owner(v):
        v = jnp.swapaxes(v.reshape(2, n_seq // 2, rows * own_tokens, width), 0, 1)
        v = lax.psum_scatter(v.reshape(all_tokens, width), "seq", scatter_dimension=0, tiled=True)
        return v.reshape(rows, own_tokens, width)

    branch = to_owner(branch)
    output = (tokens.astype(f32) + branch.astype(f32)).astype(bf16)

    out_part = lax.dot_general(
        joined, g_full, (((0,), (0,)), ((), ())), preferred_element_type=f32
    ).astype(bf16)
    a0 = out_part[:att]
    a1, a2, a3 = (
        out_part[att : att + act[0]],
        out_part[att + act[0] : att + act[0] + own],
        out_part[att + act[0] + own :],
    )
    fill = lambda v: jnp.pad(v, ((0, slot - v.shape[0]), (0, 0)))
    out_slots = jnp.stack(
        [fill(a0), jnp.concatenate([a1, a0[keep:]], axis=0), fill(a2), fill(a3)]
    )
    out_sum = lax.psum_scatter(out_slots, "dp", scatter_dimension=0, tiled=True)[0]
    send_at = jnp.where(p == 0, keep, jnp.where(last, act[0], act[0] - late))
    sent = lax.dynamic_slice_in_dim(out_sum, send_at, late, 0)
    from_prev = lax.ppermute(sent, "seq", [(k, (k + 1) % n_seq) for k in range(n_seq)])
    count = jnp.where(p == 0, lead * s, jnp.where(p == 1, late - lead * s, 0))
    out_grad = lax.dynamic_slice_in_dim(
        jnp.concatenate([from_prev, out_sum[:own]], axis=0), late - count, own, 0
    ).astype(f32)

    in_part = lax.dot_general(
        hidden, d_proj, (((0,), (0,)), ((), ())), preferred_element_type=f32
    ).astype(bf16)
    in_sum = lax.psum_scatter(in_part, "dp", scatter_dimension=0, tiled=True)
    in_sum = lax.all_to_all(in_sum.reshape(n_seq, in_rows, -1), "seq", 0, 0, tiled=True)
    in_grad = unshare(in_sum).astype(f32)

    d_hidden = lax.dot_general(
        d_proj, in_low, (((1,), (1,)), ((), ())), preferred_element_type=f32
    ).astype(bf16)
    d_hidden = to_owner(d_hidden).astype(f32)
    normed, inv_std = normalise(tokens)
    d_normed = d_hidden * gain
    input_grad = cotangent.astype(f32) + inv_std * (
        d_normed
        - jnp.mean(d_normed, axis=-1, keepdims=True)
        - normed * jnp.mean(d_normed * normed, axis=-1, keepdims=True)
    )

    gain_grad = jnp.sum(d_hidden * normed, axis=(0, 1))
    shift_grad = jnp.sum(d_hidden, axis=(0, 1))
    bias_part = jnp.sum(d_proj[:, : 3 * att].astype(f32), axis=0).reshape(3, att).T
    bias_grad = lax.dynamic_update_slice_in_dim(jnp.zeros((width, 3), f32), bias_part, s * att, 0)
    small_term = jnp.concatenate([gain_grad[:, None], shift_grad[:, None], bias_grad], axis=1)
    small_grad = lax.psum_scatter(small_term, ("dp", "seq"), scatter_dimension=0, tiled=True)

    in_new = adam_update(
        in_weight, in_first, in_second, in_average, in_grad, matrix_rate, weight_decay
    )
    out_new = adam_update(
        out_weight, out_first, out_second, out_average, out_grad, matrix_rate, weight_decay
    )
    small_new = adam_update(
        small_params, small_first, small_second, small_average, small_grad, small_rate, 0.0
    )
    return (output, input_grad, *in_new, *out_new, *small_new, small_grad, in_grad, out_grad)


def solution(mesh):
    n_dp, n_seq = mesh.shape["dp"], mesh.shape["seq"]

    def choose(*operands):
        own_rows = operands[8].shape[0]
        model_width = operands[0].shape[2]
        if heads_fit(n_dp, n_seq, own_rows, model_width, operands[4].shape[1]):
            return split_heads(n_dp, n_seq, *operands)
        return per_device(*operands)

    return jax.shard_map(
        choose,
        mesh=mesh,
        in_specs=(
            P("dp", "seq", None),
            P("dp", "seq", None),
            P("dp", "seq"),
            P("dp", "seq"),
            P(("dp", "seq"), None),
            P(("dp", "seq"), None),
            P(("dp", "seq"), None),
            P(("dp", "seq"), None),
            P(("dp", "seq"), None),
            P(("dp", "seq"), None),
            P(("dp", "seq"), None),
            P(("dp", "seq"), None),
            P(("dp", "seq"), None),
            P(("dp", "seq"), None),
            P(("dp", "seq"), None),
            P(("dp", "seq"), None),
        ),
        out_specs=(
            P("dp", "seq", None),
            P("dp", "seq", None),
            P(("dp", "seq"), None),
            P(("dp", "seq"), None),
            P(("dp", "seq"), None),
            P(("dp", "seq"), None),
            P(("dp", "seq"), None),
            P(("dp", "seq"), None),
            P(("dp", "seq"), None),
            P(("dp", "seq"), None),
            P(("dp", "seq"), None),
            P(("dp", "seq"), None),
            P(("dp", "seq"), None),
            P(("dp", "seq"), None),
        ),
        check_vma=False,
    )
```

```python
import functools

import jax
import jax.numpy as jnp
from jax import lax
from jax.experimental import pallas as pl
from jax.experimental.pallas import tpu as pltpu
from jax.sharding import PartitionSpec as P

HEADS = 32
ROT = 16
STEP = 2


beta_one = 0.9
adam_eps = 1e-08
matrix_rate = 0.001
small_rate = 0.01
weight_decay = 0.1
norm_eps = 1e-05
rope_base = 10000.0
neg_large = -1e30


def rope_tables(positions, rot_dims):
    half_rot = rot_dims // 2
    inv_freq = rope_base ** (-2.0 * jnp.arange(half_rot, dtype=jnp.float32) / rot_dims)
    angles = positions.astype(jnp.float32)[..., None] * inv_freq
    return (jnp.cos(angles)[..., None, :], jnp.sin(angles)[..., None, :])


def apply_rope(field_in, cosine_tab, sine_tab, rot_dims):
    half_rot = rot_dims // 2
    low_half = field_in[..., :half_rot]
    high_half = field_in[..., half_rot:rot_dims]
    return jnp.concatenate(
        [
            low_half * cosine_tab - high_half * sine_tab,
            high_half * cosine_tab + low_half * sine_tab,
            field_in[..., rot_dims:],
        ],
        axis=-1,
    )


def undo_rope(grad_in, cosine_tab, sine_tab, rot_dims):
    half_rot = rot_dims // 2
    low_half = grad_in[..., :half_rot]
    high_half = grad_in[..., half_rot:rot_dims]
    return jnp.concatenate(
        [
            low_half * cosine_tab + high_half * sine_tab,
            high_half * cosine_tab - low_half * sine_tab,
            grad_in[..., rot_dims:],
        ],
        axis=-1,
    )


def visible(query_seg, key_seg, query_pos, key_pos):
    same_doc = query_seg[:, :, None] == key_seg[:, None, :]
    causal = key_pos[None, :] <= query_pos[:, None]
    return (same_doc & causal[None])[:, None]


def to_tokens(head_major):
    return jnp.transpose(head_major, (0, 2, 1, 3))


def adam_update(weight, first, second, average, gradient, rate, decay_rate):
    beta_two = 1.0 - STEP ** (-0.8)
    average_keep = min(0.999, (1.0 + STEP) / (10.0 + STEP))
    first_new = beta_one * first + (1.0 - beta_one) * gradient
    second_new = beta_two * second + (1.0 - beta_two) * gradient * gradient
    moment_hat = beta_one * first_new / (1.0 - beta_one ** (STEP + 1)) + (
        1.0 - beta_one
    ) * gradient / (1.0 - beta_one**STEP)
    weight_new = weight - rate * (
        moment_hat / (jnp.sqrt(second_new) + adam_eps) + decay_rate * weight
    )
    average_new = average_keep * average + (1.0 - average_keep) * weight_new
    return (weight_new, second_new, average_new)


def per_device(
    tokens,
    cotangent,
    segment_ids,
    doc_positions,
    in_weight,
    in_first,
    in_second,
    in_average,
    out_weight,
    out_first,
    out_second,
    out_average,
    small_params,
    small_first,
    small_second,
    small_average,
):
    rows_here, row_tokens, model_width = tokens.shape
    head_count = HEADS
    head_size = model_width // head_count
    score_scale = head_size ** (-0.5)
    all_tokens = rows_here * row_tokens
    wide_in = in_weight.shape[1]
    ffn_width = (wide_in - 3 * model_width) // 2
    shape_heads = (rows_here, row_tokens, head_count, head_size)
    own_places = lax.axis_index("seq") * row_tokens + jnp.arange(row_tokens)
    flat_in = tokens.astype(jnp.float32).reshape(all_tokens, model_width)
    centered = flat_in - jnp.mean(flat_in, axis=-1, keepdims=True)
    inv_std = lax.rsqrt(jnp.mean(centered * centered, axis=-1, keepdims=True) + norm_eps)
    normed = centered * inv_std
    in_low = in_weight.astype(jnp.bfloat16)
    out_low = out_weight.astype(jnp.bfloat16)
    small_low = small_params.astype(jnp.bfloat16)
    w_piece = lax.all_gather(in_low, ("dp", "seq"), axis=0, tiled=True)
    s_piece = lax.all_gather(small_low, ("dp", "seq"), axis=0, tiled=True)
    columns = normed
    s_float = s_piece.astype(jnp.float32)
    h_piece = (columns * s_float[:, 0] + s_float[:, 1]).astype(jnp.bfloat16)
    proj_acc = jnp.dot(h_piece, w_piece, preferred_element_type=jnp.float32)
    norm_gain = s_float[:, 0]
    qkv_bias = s_float[:, 2:5].T.reshape(3 * model_width)
    qkv_full = proj_acc[:, : 3 * model_width] + qkv_bias
    gate_pre = proj_acc[:, 3 * model_width : 3 * model_width + ffn_width]
    up_pre = proj_acc[:, 3 * model_width + ffn_width :]
    cosine_tab, sine_tab = rope_tables(doc_positions, ROT)
    query_low = apply_rope(
        qkv_full[:, :model_width].reshape(shape_heads), cosine_tab, sine_tab, ROT
    ).astype(jnp.bfloat16)
    key_low = apply_rope(
        qkv_full[:, model_width : 2 * model_width].reshape(shape_heads), cosine_tab, sine_tab, ROT
    ).astype(jnp.bfloat16)
    value_low = qkv_full[:, 2 * model_width :].reshape(shape_heads).astype(jnp.bfloat16)
    seg_low = segment_ids.astype(jnp.bfloat16)
    seg_own = segment_ids.astype(jnp.float32)
    key_flat = key_low.reshape(rows_here, row_tokens, model_width)
    value_flat = value_low.reshape(rows_here, row_tokens, model_width)
    attend_init = (
        jnp.full((rows_here, head_count, row_tokens), neg_large, jnp.float32),
        jnp.zeros((rows_here, head_count, row_tokens), jnp.float32),
        jnp.zeros((rows_here, head_count, row_tokens, head_size), jnp.float32),
    )
    key_piece = lax.all_gather(key_flat, "seq", axis=1, tiled=True)
    value_piece = lax.all_gather(value_flat, "seq", axis=1, tiled=True)
    seg_piece = lax.all_gather(seg_low, "seq", axis=1, tiled=True)
    turn_count = key_piece.shape[1] // row_tokens

    def attend_one_turn(turn_index, inner_state):
        offset = turn_index * row_tokens
        key_blk = lax.dynamic_slice_in_dim(key_piece, offset, row_tokens, 1).reshape(shape_heads)
        value_blk = lax.dynamic_slice_in_dim(value_piece, offset, row_tokens, 1).reshape(
            shape_heads
        )
        seg_blk = lax.dynamic_slice_in_dim(seg_piece, offset, row_tokens, 1).astype(jnp.float32)
        key_mask = visible(seg_own, seg_blk, own_places, offset + jnp.arange(row_tokens))
        running_top, running_sum, weighted = inner_state
        scores = (
            jnp.einsum("rqhe,rkhe->rhqk", query_low, key_blk, preferred_element_type=jnp.float32)
            * score_scale
        )
        scores = jnp.where(key_mask, scores, neg_large)
        new_top = jnp.maximum(running_top, jnp.max(scores, axis=-1))
        weights = jnp.where(key_mask, jnp.exp(scores - new_top[..., None]), 0.0)
        factor = jnp.exp(running_top - new_top)
        running_sum = running_sum * factor + jnp.sum(weights, axis=-1)
        weighted = weighted * factor[..., None] + jnp.einsum(
            "rhqk,rkhe->rhqe",
            weights.astype(jnp.bfloat16),
            value_blk,
            preferred_element_type=jnp.float32,
        )
        return (new_top, running_sum, weighted)

    running_top, running_sum, weighted = lax.fori_loop(0, turn_count, attend_one_turn, attend_init)
    attended = weighted / running_sum[..., None]
    log_total = running_top + jnp.log(running_sum)
    attended_low = to_tokens(attended).reshape(all_tokens, model_width).astype(jnp.bfloat16)
    gate_sig = jax.nn.sigmoid(gate_pre)
    activated = gate_pre * gate_sig * up_pre
    joined = jnp.concatenate([attended_low, activated.astype(jnp.bfloat16)], axis=1)
    columns = joined
    branch_sum = jnp.dot(
        columns,
        lax.all_gather(out_low, ("dp", "seq"), axis=0, tiled=True),
        preferred_element_type=jnp.float32,
    )
    output = (flat_in + branch_sum).astype(jnp.bfloat16).reshape(rows_here, row_tokens, model_width)
    grad_out = cotangent.reshape(all_tokens, model_width)
    d_joined = lax.dot_general(
        grad_out,
        lax.all_gather(out_low, ("dp", "seq"), axis=0, tiled=True),
        (((1,), (1,)), ((), ())),
        preferred_element_type=jnp.float32,
    )
    d_joined = d_joined.astype(jnp.bfloat16)
    columns = joined
    out_grad = lax.psum_scatter(
        lax.dot_general(
            columns, grad_out, (((0,), (0,)), ((), ())), preferred_element_type=jnp.float32
        ),
        ("dp", "seq"),
        scatter_dimension=0,
        tiled=True,
    )
    d_attended = d_joined[:, :model_width].reshape(shape_heads)
    d_act = d_joined[:, model_width:].astype(jnp.float32)
    d_gate = d_act * up_pre * gate_sig * (1.0 + gate_pre * (1.0 - gate_sig))
    d_up = d_act * gate_pre * gate_sig
    out_dot = jnp.einsum("rqhe,rhqe->rhq", d_attended.astype(jnp.float32), attended)
    grad_zero = jnp.zeros((rows_here, head_count, row_tokens, head_size), jnp.float32)
    query_key_piece = lax.all_gather(key_flat, "seq", axis=1, tiled=True)
    query_value_piece = lax.all_gather(value_flat, "seq", axis=1, tiled=True)
    query_seg_piece = lax.all_gather(seg_low, "seq", axis=1, tiled=True)
    turn_count = query_key_piece.shape[1] // row_tokens

    def query_one_turn(turn_index, inner_state):
        offset = turn_index * row_tokens
        key_blk = lax.dynamic_slice_in_dim(query_key_piece, offset, row_tokens, 1).reshape(
            shape_heads
        )
        value_blk = lax.dynamic_slice_in_dim(query_value_piece, offset, row_tokens, 1).reshape(
            shape_heads
        )
        seg_blk = lax.dynamic_slice_in_dim(query_seg_piece, offset, row_tokens, 1).astype(
            jnp.float32
        )
        key_mask = visible(seg_own, seg_blk, own_places, offset + jnp.arange(row_tokens))
        scores = (
            jnp.einsum("rqhe,rkhe->rhqk", query_low, key_blk, preferred_element_type=jnp.float32)
            * score_scale
        )
        weights = jnp.where(key_mask, jnp.exp(scores - log_total[..., None]), 0.0)
        d_prob = jnp.einsum(
            "rqhe,rkhe->rhqk", d_attended, value_blk, preferred_element_type=jnp.float32
        )
        d_score = (weights * (d_prob - out_dot[..., None])).astype(jnp.bfloat16)
        return (
            inner_state
            + jnp.einsum("rhqk,rkhe->rhqe", d_score, key_blk, preferred_element_type=jnp.float32)
            * score_scale
        )

    d_query = lax.fori_loop(0, turn_count, query_one_turn, grad_zero)
    row_stats = jnp.concatenate(
        [jnp.transpose(log_total, (0, 2, 1)), jnp.transpose(out_dot, (0, 2, 1))], axis=2
    )
    stat_high = row_stats.astype(jnp.bfloat16)
    stat_low = (row_stats - stat_high.astype(jnp.float32)).astype(jnp.bfloat16)
    query_flat = query_low.reshape(rows_here, row_tokens, model_width)
    d_att_flat = d_attended.reshape(rows_here, row_tokens, model_width)
    query_piece = lax.all_gather(query_flat, "seq", axis=1, tiled=True)
    dout_piece = lax.all_gather(d_att_flat, "seq", axis=1, tiled=True)
    high_piece = lax.all_gather(stat_high, "seq", axis=1, tiled=True)
    low_piece = lax.all_gather(stat_low, "seq", axis=1, tiled=True)
    key_seg_piece = lax.all_gather(seg_low, "seq", axis=1, tiled=True)
    turn_count = query_piece.shape[1] // row_tokens

    def key_one_turn(turn_index, inner_state):
        offset = turn_index * row_tokens
        query_blk = lax.dynamic_slice_in_dim(query_piece, offset, row_tokens, 1).reshape(
            shape_heads
        )
        dout_blk = lax.dynamic_slice_in_dim(dout_piece, offset, row_tokens, 1).reshape(shape_heads)
        stat_blk = lax.dynamic_slice_in_dim(high_piece, offset, row_tokens, 1).astype(
            jnp.float32
        ) + lax.dynamic_slice_in_dim(low_piece, offset, row_tokens, 1).astype(jnp.float32)
        lse_blk = jnp.transpose(stat_blk[..., :head_count], (0, 2, 1))
        dot_blk = jnp.transpose(stat_blk[..., head_count:], (0, 2, 1))
        seg_blk = lax.dynamic_slice_in_dim(key_seg_piece, offset, row_tokens, 1).astype(jnp.float32)
        key_mask = visible(seg_blk, seg_own, offset + jnp.arange(row_tokens), own_places)
        d_key, d_value = inner_state
        scores = (
            jnp.einsum("rqhe,rkhe->rhqk", query_blk, key_low, preferred_element_type=jnp.float32)
            * score_scale
        )
        weights = jnp.where(key_mask, jnp.exp(scores - lse_blk[..., None]), 0.0)
        d_value = d_value + jnp.einsum(
            "rhqk,rqhe->rhke",
            weights.astype(jnp.bfloat16),
            dout_blk,
            preferred_element_type=jnp.float32,
        )
        d_prob = jnp.einsum(
            "rqhe,rkhe->rhqk", dout_blk, value_low, preferred_element_type=jnp.float32
        )
        d_score = (weights * (d_prob - dot_blk[..., None])).astype(jnp.bfloat16)
        d_key = (
            d_key
            + jnp.einsum("rhqk,rqhe->rhke", d_score, query_blk, preferred_element_type=jnp.float32)
            * score_scale
        )
        return (d_key, d_value)

    d_key, d_value = lax.fori_loop(0, turn_count, key_one_turn, (grad_zero, grad_zero))
    d_query_tok = undo_rope(to_tokens(d_query), cosine_tab, sine_tab, ROT).reshape(
        all_tokens, model_width
    )
    d_key_tok = undo_rope(to_tokens(d_key), cosine_tab, sine_tab, ROT).reshape(
        all_tokens, model_width
    )
    d_value_tok = to_tokens(d_value).reshape(all_tokens, model_width)
    d_proj = jnp.concatenate([d_query_tok, d_key_tok, d_value_tok, d_gate, d_up], axis=1).astype(
        jnp.bfloat16
    )
    d_hidden = lax.dot_general(
        d_proj,
        lax.all_gather(in_low, ("dp", "seq"), axis=0, tiled=True),
        (((1,), (1,)), ((), ())),
        preferred_element_type=jnp.float32,
    )
    columns = h_piece
    in_grad = lax.psum_scatter(
        lax.dot_general(
            columns, d_proj, (((0,), (0,)), ((), ())), preferred_element_type=jnp.float32
        ),
        ("dp", "seq"),
        scatter_dimension=0,
        tiled=True,
    )
    gain_grad = jnp.sum(d_hidden * normed, axis=0)
    shift_grad = jnp.sum(d_hidden, axis=0)
    bias_grad = (
        jnp.sum(d_proj[:, : 3 * model_width].astype(jnp.float32), axis=0).reshape(3, model_width).T
    )
    small_term = jnp.concatenate([gain_grad[:, None], shift_grad[:, None], bias_grad], axis=1)
    small_grad = lax.psum_scatter(small_term, ("dp", "seq"), scatter_dimension=0, tiled=True)
    d_normed = d_hidden * norm_gain
    input_grad = grad_out.astype(jnp.float32) + inv_std * (
        d_normed
        - jnp.mean(d_normed, axis=-1, keepdims=True)
        - normed * jnp.mean(d_normed * normed, axis=-1, keepdims=True)
    )
    input_grad = input_grad.reshape(rows_here, row_tokens, model_width)
    in_new = adam_update(
        in_weight, in_first, in_second, in_average, in_grad, matrix_rate, weight_decay
    )
    out_new = adam_update(
        out_weight, out_first, out_second, out_average, out_grad, matrix_rate, weight_decay
    )
    small_new = adam_update(
        small_params, small_first, small_second, small_average, small_grad, small_rate, 0.0
    )
    return (
        output,
        input_grad,
        in_new[0],
        in_new[1],
        in_new[2],
        out_new[0],
        out_new[1],
        out_new[2],
        small_new[0],
        small_new[1],
        small_new[2],
        small_grad,
        in_grad,
        out_grad,
    )


def heads_fit(n_dp, n_seq, own_rows, model_width, wide_in):
    dp_rows = own_rows * n_seq
    if n_dp != 4 or HEADS % (2 * n_seq) or not dp_rows < model_width < 2 * dp_rows:
        return False
    att_rows = model_width // n_seq
    late_att = model_width - dp_rows
    first_act = dp_rows - late_att
    if first_act % n_seq:
        return False
    lead = att_rows - own_rows
    return (
        wide_in - 3 * model_width == 2 * (n_dp * dp_rows - model_width)
        and lead == own_rows - first_act // n_seq
        and lead * n_seq == late_att
        and lead % 16 == 0
    )


def attention_kernel(
    q_ref, k_ref, v_ref, bq_ref, bk_ref, bv_ref, da_ref, rope_ref, seg_q_ref, seg_k_ref,
    o_ref, dq_ref, dk_ref, dv_ref, *, head_size, half_rot,
):
    def whole(v):
        across, depth = v.shape[:2]
        parts = [v[x, z].reshape(v.shape[-2:]) for z in range(depth) for x in range(across)]
        return jnp.concatenate(parts, axis=0)

    def store(ref, v):
        across, depth, _, some, _ = ref.shape
        for z in range(depth):
            for x in range(across):
                at = (z * across + x) * some
                ref[x, z, 0] = v[at : at + some].astype(ref.dtype)

    cos, sin_low, sin_high = (whole(rope_ref[i]) for i in range(3))
    tokens, lanes = cos.shape
    scale = head_size ** (-0.5)

    def turn(v, way):
        return (
            v * cos
            + way * pltpu.roll(v, lanes - half_rot, 1) * sin_low
            + way * pltpu.roll(v, half_rot, 1) * sin_high
        )

    query = (turn(whole(q_ref[...]) + bq_ref[...], 1.0)).astype(jnp.bfloat16) * scale
    query = query.astype(jnp.bfloat16)
    key = turn(whole(k_ref[...]) + bk_ref[...], 1.0).astype(jnp.bfloat16)
    value = (whole(v_ref[...]) + bv_ref[...]).astype(jnp.bfloat16)
    d_att = whole(da_ref[...])
    place_q = lax.broadcasted_iota(jnp.int32, (tokens, tokens), 0)
    place_k = lax.broadcasted_iota(jnp.int32, (tokens, tokens), 1)
    mask = (seg_q_ref[0] == seg_k_ref[0]) & (place_k <= place_q)
    lane = lax.broadcasted_iota(jnp.int32, (tokens, lanes), 1)
    nt = (((1,), (1,)), ((), ()))
    tn = (((0,), (0,)), ((), ()))
    dot = functools.partial(lax.dot_general, preferred_element_type=jnp.float32)
    att = jnp.zeros((tokens, lanes), jnp.float32)
    d_query = jnp.zeros((tokens, lanes), jnp.float32)
    d_key = jnp.zeros((tokens, lanes), jnp.float32)
    d_value = jnp.zeros((tokens, lanes), jnp.float32)
    for head in range(lanes // head_size):
        mine = (lane >= head * head_size) & (lane < (head + 1) * head_size)
        q_h = jnp.where(mine, query, jnp.zeros_like(query))
        da_h = jnp.where(mine, d_att, jnp.zeros_like(d_att))
        scores = jnp.where(mask, dot(q_h, key, nt), neg_large)
        top = jnp.max(scores, axis=1, keepdims=True)
        weights = jnp.exp(scores - top)
        probs = weights * (1.0 / jnp.sum(weights, axis=1, keepdims=True))
        probs_low = probs.astype(jnp.bfloat16)
        att_h = jnp.where(mine, dot(probs_low, value, (((1,), (0,)), ((), ()))), 0.0)
        out_dot = jnp.sum(att_h * d_att.astype(jnp.float32), axis=1, keepdims=True)
        d_prob = dot(da_h, value, nt)
        d_score = (probs * (d_prob - out_dot)).astype(jnp.bfloat16)
        att = att + att_h
        d_query = d_query + jnp.where(mine, dot(d_score, key, (((1,), (0,)), ((), ()))), 0.0)
        d_key = d_key + dot(d_score, q_h, tn)
        d_value = d_value + dot(probs_low, da_h, tn)
    store(o_ref, att)
    store(dq_ref, turn(d_query * scale, -1.0))
    store(dk_ref, turn(d_key, -1.0))
    store(dv_ref, d_value)


def attention_both(proj, bias, d_joined, rope, seg, n_seq, att_rows, head_size):
    rows, tokens = seg.shape
    lanes = 2 * head_size
    pairs = att_rows // lanes
    order = (2, n_seq // 2, rows, tokens // n_seq)
    wide = lambda v: v.reshape(order + v.shape[-1:])
    shape = (2, n_seq // 2, 1, tokens // n_seq, lanes)
    block = lambda first: pl.BlockSpec(shape, lambda r, h: (0, 0, r, 0, first + h))
    row = lambda first: pl.BlockSpec((1, lanes), lambda r, h: (0, first + h))
    out = jax.ShapeDtypeStruct(order + (att_rows,), jnp.bfloat16)
    proj, d_joined = wide(proj), wide(d_joined)
    results = pl.pallas_call(
        functools.partial(attention_kernel, head_size=head_size, half_rot=ROT // 2),
        grid=(rows, pairs),
        in_specs=[
            block(0), block(pairs), block(2 * pairs),
            row(0), row(pairs), row(2 * pairs),
            block(0),
            pl.BlockSpec((3,) + shape, lambda r, h: (0, 0, 0, r, 0, 0)),
            pl.BlockSpec((1, tokens, 1), lambda r, h: (r, 0, 0)),
            pl.BlockSpec((1, 1, tokens), lambda r, h: (r, 0, 0)),
        ],
        out_specs=[block(0)] * 4,
        out_shape=[out] * 4,
        compiler_params=pltpu.CompilerParams(vmem_limit_bytes=56 * 2**20),
        cost_estimate=pl.CostEstimate(
            flops=rows * pairs * 2 * 12 * tokens * tokens * lanes,
            bytes_accessed=rows * tokens * att_rows * 20,
            transcendentals=rows * pairs * 2 * tokens * tokens,
        ),
        name="attention",
    )(
        proj, proj, proj, bias, bias, bias, d_joined,
        rope.reshape((3,) + order + (lanes,)), seg[:, :, None], seg[:, None, :],
    )
    return [v.reshape(rows * tokens, att_rows) for v in results]

MESH_ID = pl.DeviceIdType.MESH


def remote(src, dst, send_sem, recv_sem, device):
    return pltpu.make_async_remote_copy(
        src_ref=src,
        dst_ref=dst,
        send_sem=send_sem,
        recv_sem=recv_sem,
        device_id=device,
        device_id_type=MESH_ID,
    )


class Place:
    def __init__(self, n_seq):
        self.n_seq = n_seq
        self.depth = n_seq // 2
        self.p, self.s = lax.axis_index("dp"), lax.axis_index("seq")
        self.y, self.c = self.p // 2, lax.rem(self.p, 2)
        self.z, self.x = self.s // 2, lax.rem(self.s, 2)
        self.p_y = (1 - self.y) * 2 + self.c
        self.p_c = self.y * 2 + 1 - self.c
        self.p_d = (1 - self.y) * 2 + 1 - self.c
        self.to_y = (self.p_y, self.s)
        self.to_c = (self.p_c, self.s)
        self.to_x = (self.p, self.z * 2 + 1 - self.x)
        self.to_up = (self.p, self.s + 2)
        self.to_down = (self.p, self.s - 2)

    def seq(self, hop):
        return lax.rem(self.s + hop + self.n_seq, self.n_seq)

    def meet(self):
        barrier = pltpu.get_barrier_semaphore()

        def greet(hop, carry):
            pl.semaphore_signal(
                barrier, inc=1, device_id=(self.p, self.seq(hop)), device_id_type=MESH_ID
            )
            return carry

        lax.fori_loop(1, self.n_seq, greet, 0)
        for device in (self.to_y, self.to_c):
            pl.semaphore_signal(barrier, inc=1, device_id=device, device_id_type=MESH_ID)
        pl.semaphore_wait(barrier, self.n_seq + 1)


class Spread:
    def __init__(self, at, own, full, sems):
        self.at, self.own, self.full, self.sems = at, own, full, sems

    def along(self, src, up, ref=None):
        sems, at = self.sems, self.at
        here = self.full.at[at.x, src]
        return remote(
            here if ref is None else ref,
            here,
            sems.at[0 if up else 1, src],
            sems.at[3, src],
            at.to_up if up else at.to_down,
        )

    def across(self, src, ref=None):
        sems, at = self.sems, self.at
        here = self.full.at[at.x, src]
        return remote(here if ref is None else ref, here, sems.at[2, src], sems.at[4, src], at.to_x)

    def local(self):
        return pltpu.make_async_copy(
            self.own, self.full.at[self.at.x, self.at.z], self.sems.at[5, 0]
        )

    def begin(self):
        at = self.at

        @pl.when(at.z < at.depth - 1)
        def _():
            self.along(at.z, True, self.own).start()

        @pl.when(at.z > 0)
        def _():
            self.along(at.z, False, self.own).start()

        self.across(at.z, self.own).start()
        self.local().start()

    def step(self, hop):
        at = self.at

        @pl.when(at.z - hop >= 0)
        def _():
            src = at.z - hop
            self.along(src, True).wait_recv()

            @pl.when(at.z < at.depth - 1)
            def _():
                self.along(src, True).start()

            self.across(src).start()

        @pl.when(at.z + hop < at.depth)
        def _():
            src = at.z + hop
            self.along(src, False).wait_recv()

            @pl.when(at.z > 0)
            def _():
                self.along(src, False).start()

            self.across(src).start()

    def arrive(self):
        at = self.at
        for src in range(at.depth):
            here = self.full.at[1 - at.x, src]
            remote(here, here, self.sems.at[2, src], self.sems.at[4, src], at.to_x).wait_recv()
        self.local().wait()

    def sent(self):
        at = self.at
        for src in range(at.depth):
            self.across(src).wait_send()

            @pl.when((at.z < at.depth - 1) & (src <= at.z))
            def _():
                self.along(src, True).wait_send()

            @pl.when((at.z > 0) & (src >= at.z))
            def _():
                self.along(src, False).wait_send()


class Fan:
    def __init__(self, at, pick, sems):
        self.at, self.pick, self.sems = at, pick, sems

    def y(self, k, ref=None):
        at = self.at
        here = self.pick(at.p, k)
        return remote(here if ref is None else ref, here, self.sems.at[0, k], self.sems.at[1, k], at.to_y)

    def core(self, k, ref=None):
        at = self.at
        here = self.pick(at.p, k)
        return remote(here if ref is None else ref, here, self.sems.at[2, k], self.sems.at[3, k], at.to_c)

    def pass_on(self, k):
        at = self.at
        here = self.pick(at.p_y, k)
        return remote(here, here, self.sems.at[4, k], self.sems.at[5, k], at.to_c)

    def from_y(self, k):
        here = self.pick(self.at.p_y, k)
        return remote(here, here, self.sems.at[0, k], self.sems.at[1, k], self.at.to_y)

    def from_core(self, k):
        here = self.pick(self.at.p_c, k)
        return remote(here, here, self.sems.at[2, k], self.sems.at[3, k], self.at.to_c)

    def from_diagonal(self, k):
        here = self.pick(self.at.p_d, k)
        return remote(here, here, self.sems.at[4, k], self.sems.at[5, k], self.at.to_c)


def loop(low, high, body):
    def step(k, carry):
        body(k)
        return carry

    lax.fori_loop(low, high, step, 0)


def gather_kernel(
    x_ref, g_ref, w_ref, o_ref, tile_ref,
    x_full, g_full, w_full, o_full, tiles,
    x_sems, g_sems, w_sems, w_fan_sems, o_sems, o_fan_sems, t_sems, t_fan_sems, local_sems,
    *, n_seq, late,
):
    at = Place(n_seq)
    own = o_ref.shape[0]
    body, extra = pl.ds(0, own), pl.ds(own, late)
    x_go = Spread(at, x_ref, x_full, x_sems)
    g_go = Spread(at, g_ref, g_full, g_sems)
    w_fan = Fan(at, lambda p, k: w_full.at[p, k], w_fan_sems)
    o_fan = Fan(at, lambda p, k: o_full.at[p, body if k == 0 else extra], o_fan_sems)
    t_fan = Fan(at, lambda p, k: tiles.at[p], t_fan_sems)

    def w_send(hop):
        to = at.seq(hop)
        return remote(w_ref.at[to], w_full.at[at.p, at.s], w_sems.at[0, to], w_sems.at[1, at.s], (at.p, to))

    def w_recv(hop):
        src = at.seq(-hop)
        here = w_full.at[at.p, src]
        return remote(here, here, w_sems.at[0, src], w_sems.at[1, src], (at.p, src))

    def t_send(hop):
        to = at.seq(hop)
        return remote(tile_ref, tiles.at[at.p, at.s], t_sems.at[0, to], t_sems.at[1, at.s], (at.p, to))

    def t_recv(hop):
        src = at.seq(-hop)
        here = tiles.at[at.p, src]
        return remote(here, here, t_sems.at[0, src], t_sems.at[1, src], (at.p, src))

    w_local = pltpu.make_async_copy(w_ref.at[at.s], w_full.at[at.p, at.s], local_sems.at[0])
    o_local = pltpu.make_async_copy(o_ref, o_full.at[at.p, body], local_sems.at[1])
    t_local = pltpu.make_async_copy(tile_ref, tiles.at[at.p, at.s], local_sems.at[2])
    head = o_ref.at[pl.ds(0, late)]
    o_send = remote(
        head, o_full.at[at.p, extra], o_sems.at[0], o_sems.at[1], (at.p, at.seq(-1))
    )

    at.meet()
    x_go.begin()
    loop(1, n_seq, lambda hop: t_send(hop).start())
    t_local.start()
    w_fan.y(at.s, w_ref.at[at.s]).start()
    loop(1, n_seq, lambda hop: w_send(hop).start())
    w_fan.core(at.s, w_ref.at[at.s]).start()
    w_local.start()
    o_fan.core(0, o_ref).start()
    o_local.start()
    for hop in range(1, at.depth):
        x_go.step(hop)
    g_go.begin()
    t_local.wait()
    loop(1, n_seq, lambda hop: t_recv(hop).wait_recv())
    t_fan.y(0).start()
    t_fan.core(0).start()

    @pl.when(at.y == 0)
    def _():
        o_send.start()

    def w_step(hop):
        src = at.seq(-hop)
        w_recv(hop).wait_recv()
        w_fan.y(src).start()
        w_fan.core(src).start()

    loop(1, n_seq, w_step)
    t_fan.from_y(0).wait_recv()
    t_fan.pass_on(0).start()
    o_fan.y(0, o_ref).start()
    for hop in range(1, at.depth):
        g_go.step(hop)

    @pl.when(at.y == 0)
    def _():
        o_send.wait_recv()
        o_fan.y(1).start()
        o_fan.core(1).start()

    def w_pass(hop):
        src = at.seq(-hop)
        w_fan.from_y(src).wait_recv()
        w_fan.pass_on(src).start()

    loop(0, n_seq, w_pass)
    o_fan.from_y(0).wait_recv()
    o_fan.pass_on(0).start()

    @pl.when(at.y == 1)
    def _():
        o_fan.from_y(1).wait_recv()
        o_fan.pass_on(1).start()

    x_go.arrive()
    g_go.arrive()
    w_local.wait()
    o_local.wait()
    t_fan.from_core(0).wait_recv()
    t_fan.from_diagonal(0).wait_recv()
    o_fan.from_core(0).wait_recv()
    o_fan.from_diagonal(0).wait_recv()

    @pl.when(at.y == 0)
    def _():
        o_fan.from_core(1).wait_recv()

    @pl.when(at.y == 1)
    def _():
        o_fan.from_diagonal(1).wait_recv()

    def w_last(k):
        w_fan.from_core(k).wait_recv()
        w_fan.from_diagonal(k).wait_recv()
        w_fan.y(k).wait_send()
        w_fan.core(k).wait_send()
        w_fan.pass_on(k).wait_send()

    loop(0, n_seq, w_last)

    x_go.sent()
    g_go.sent()

    def seq_sent(hop):
        w_send(hop).wait_send()
        t_send(hop).wait_send()

    loop(1, n_seq, seq_sent)
    for fan in (t_fan, o_fan):
        fan.y(0).wait_send()
        fan.core(0).wait_send()
        fan.pass_on(0).wait_send()

    @pl.when(at.y == 0)
    def _():
        o_send.wait_send()
        o_fan.y(1).wait_send()
        o_fan.core(1).wait_send()

    @pl.when(at.y == 1)
    def _():
        o_fan.pass_on(1).wait_send()


def gather_all(n_dp, n_seq, late, x, g, w, o, tile):
    depth = n_seq // 2
    own, width = o.shape
    rest = pl.BlockSpec(memory_space=pl.ANY)
    dma = pltpu.SemaphoreType.DMA
    like = lambda lead, ref: jax.ShapeDtypeStruct(lead + ref.shape, ref.dtype)
    return pl.pallas_call(
        functools.partial(gather_kernel, n_seq=n_seq, late=late),
        in_specs=[rest] * 5,
        out_specs=[rest] * 5,
        out_shape=[
            like((2, depth), x),
            like((2, depth), g),
            jax.ShapeDtypeStruct((n_dp,) + w.shape, w.dtype),
            jax.ShapeDtypeStruct((n_dp, own + late, width), o.dtype),
            like((n_dp, n_seq), tile),
        ],
        scratch_shapes=[
            dma((6, depth)), dma((6, depth)), dma((2, n_seq)), dma((6, n_seq)),
            dma((2,)), dma((6, 2)), dma((2, n_seq)), dma((6, 1)), dma((3,)),
        ],
        compiler_params=pltpu.CompilerParams(collective_id=0, has_side_effects=True),
        name="gather_all",
    )(x, g, w, o, tile)

def add_rows(out, terms, rows=32):
    count = out.shape[0]

    def some(k):
        at = pl.ds(pl.multiple_of(k * rows, rows), rows)
        total = terms[0][at].astype(jnp.float32)
        for term in terms[1:]:
            total = total + term[at].astype(jnp.float32)
        out[at] = total.astype(out.dtype)

    loop(0, count // rows, some)


def reduce_kernel(
    d_ref, b_ref, in_ref, out_ref, normed_ref, small_ref,
    sums, in_sum, out_sum, out_prev, small_sum,
    own_parts, x_got, z_got, in_own, in_core, in_y, out_own, out_core, out_y,
    small_own, small_core, small_y, small_seq,
    load_sems, x_sems, z_sems, in_core_sems, in_y_sems, in_sems, out_sems, small_sems, local_sem,
    *, n_seq, late, starts, keep,
):
    at = Place(n_seq)
    depth = at.depth
    parts = (d_ref, b_ref)
    main = out_own.shape[1] - late
    body, extra = pl.ds(0, main), pl.ds(main, late)
    y, c, z, x, s = at.y, at.c, at.z, at.x, at.s

    def out_start(y_to, c_to):
        one = jnp.where(y_to == 0, starts[1], starts[3])
        zero = jnp.where(y_to == 0, starts[0], starts[2])
        return pl.multiple_of(jnp.where(c_to == 0, zero, one), 16)

    loads = [
        pltpu.make_async_copy(parts[kind].at[x], own_parts.at[kind], load_sems.at[kind])
        for kind in range(2)
    ]
    for y_to in range(2):
        p_to = 2 * y_to + c
        loads.append(pltpu.make_async_copy(in_ref.at[p_to], in_own.at[y_to], load_sems.at[2 + y_to]))
        loads.append(
            pltpu.make_async_copy(
                out_ref.at[pl.ds(out_start(y_to, c), main)],
                out_own.at[y_to, body],
                load_sems.at[4 + y_to],
            )
        )
    loads.append(
        pltpu.make_async_copy(
            out_ref.at[pl.ds(keep, late)], out_own.at[0, extra], load_sems.at[6]
        )
    )

    def in_to_core(y_to, k):
        return remote(
            in_ref.at[2 * y_to + 1 - c, k], in_core.at[y_to, k],
            in_core_sems.at[0, y_to, k], in_core_sems.at[1, y_to, k], at.to_c,
        )

    def out_to_core(y_to):
        return remote(
            out_ref.at[pl.ds(out_start(y_to, 1 - c), main)], out_core.at[y_to, body],
            out_sems.at[0, y_to], out_sems.at[1, y_to], at.to_c,
        )

    extra_to_core = remote(
        out_ref.at[pl.ds(keep, late)], out_core.at[0, extra],
        out_sems.at[0, 2], out_sems.at[1, 2], at.to_c,
    )

    def to_across(kind, k):
        return remote(
            parts[kind].at[1 - x, k], x_got.at[kind, k],
            x_sems.at[0, kind, k], x_sems.at[1, kind, k], at.to_x,
        )

    def to_depth(kind, k):
        return remote(
            x_got.at[kind, k], z_got.at[kind, z],
            z_sems.at[0, kind, k], z_sems.at[1, kind, z], (at.p, 2 * k + x),
        )

    def from_depth(kind, k):
        here = z_got.at[kind, k]
        return remote(here, here, z_sems.at[0, kind, k], z_sems.at[1, kind, k], (at.p, 2 * k + x))

    def in_to_y(k):
        return remote(
            in_core.at[1 - y, k], in_y.at[k], in_y_sems.at[0, k], in_y_sems.at[1, k], at.to_y
        )

    def in_to_owner(k):
        return remote(
            in_core.at[y, k], in_sum.at[s], in_sems.at[0, k], in_sems.at[1, s], (at.p, k)
        )

    def in_from(k):
        here = in_sum.at[k]
        return remote(here, here, in_sems.at[0, k], in_sems.at[1, k], (at.p, k))

    in_keep = pltpu.make_async_copy(in_core.at[y, s], in_sum.at[s], local_sem.at[0])
    out_to_y = remote(
        out_core.at[1 - y, body], out_y.at[body], out_sems.at[0, 3], out_sems.at[1, 3], at.to_y
    )
    extra_to_y = remote(
        out_core.at[0, extra], out_y.at[extra], out_sems.at[0, 4], out_sems.at[1, 4], at.to_y
    )

    def out_shift(start):
        return remote(
            out_sum.at[pl.ds(start, late)], out_prev,
            out_sems.at[0, 5], out_sems.at[1, 5], (at.p, at.seq(1)),
        )

    small_to_core = remote(small_own, small_core, small_sems.at[0, 0], small_sems.at[1, 0], at.to_c)
    small_to_y = remote(small_core, small_y, small_sems.at[0, 1], small_sems.at[1, 1], at.to_y)

    def small_to(hop):
        to = at.seq(hop)
        return remote(
            small_y, small_seq.at[s], small_sems.at[0, 2 + to], small_sems.at[1, 2 + s], (at.p, to)
        )

    def small_from(hop):
        src = at.seq(-hop)
        here = small_seq.at[src]
        return remote(
            here, here, small_sems.at[0, 2 + src], small_sems.at[1, 2 + src], (at.p, src)
        )

    def around_z(hop):
        return lax.rem(z + hop, depth)

    at.meet()
    for hop in range(1, depth + 1):
        to_across(0, around_z(hop)).start()
    loop(0, n_seq, lambda hop: in_to_core(1 - y, at.seq(hop)).start())
    for load in loads:
        load.start()
    loop(0, n_seq, lambda hop: in_to_core(y, at.seq(hop)).start())
    out_to_core(1 - y).start()
    out_to_core(y).start()
    extra_to_core.start()
    for hop in range(1, depth + 1):
        to_across(1, around_z(hop)).start()
    for load in loads:
        load.wait()

    def to_y_step(hop):
        k = at.seq(hop)
        in_to_core(1 - y, k).wait_recv()
        add_rows(in_core.at[1 - y, k], [in_core.at[1 - y, k], in_own.at[1 - y, k]])
        in_to_y(k).start()

    loop(0, n_seq, to_y_step)
    out_to_core(1 - y).wait_recv()
    extra_to_core.wait_recv()
    add_rows(out_core.at[1 - y, body], [out_core.at[1 - y, body], out_own.at[1 - y, body]])
    out_to_y.start()

    @pl.when(y == 1)
    def _():
        add_rows(out_core.at[0, extra], [out_core.at[0, extra], out_own.at[0, extra]])
        extra_to_y.start()

    def depth_step(kind, hop):
        k = around_z(hop)
        to_across(kind, k).wait_recv()
        add_rows(x_got.at[kind, k], [x_got.at[kind, k], own_parts.at[kind, k]])
        if hop < depth:
            to_depth(kind, k).start()

    def owner_step(hop):
        k = at.seq(hop)
        in_to_core(y, k).wait_recv()
        in_to_y(k).wait_recv()
        add_rows(in_core.at[y, k], [in_core.at[y, k], in_own.at[y, k], in_y.at[k]])

        @pl.when(k != s)
        def _():
            in_to_owner(k).start()

        @pl.when(k == s)
        def _():
            in_keep.start()

    for hop in range(1, depth + 1):
        depth_step(0, hop)
        for one in range(n_seq // depth):
            owner_step((hop - 1) * (n_seq // depth) + one + 1)

    def finish(kind):
        others = [around_z(hop) for hop in range(1, depth)]
        for k in others:
            from_depth(kind, k).wait_recv()
        add_rows(
            sums.at[kind], [x_got.at[kind, z]] + [z_got.at[kind, k] for k in others], rows=16
        )

    depth_step(1, 1)
    finish(0)

    small_own[...] = small_ref[...]
    d_hidden = sums[0]
    small_own[0:1, :] = jnp.sum(d_hidden * normed_ref[...], axis=0, keepdims=True)
    small_own[1:2, :] = jnp.sum(d_hidden, axis=0, keepdims=True)
    small_to_core.start()
    depth_step(1, 2)
    small_to_core.wait_recv()
    small_core[...] = small_core[...] + small_own[...]
    small_to_y.start()
    out_to_core(y).wait_recv()
    out_to_y.wait_recv()
    add_rows(out_sum.at[body], [out_core.at[y, body], out_own.at[y, body], out_y.at[body]])

    @pl.when(y == 0)
    def _():
        extra_to_y.wait_recv()
        add_rows(out_sum.at[extra], [out_core.at[0, extra], out_own.at[0, extra], out_y.at[extra]])

        @pl.when(c == 0)
        def _():
            out_shift(keep).start()

        @pl.when((c == 1) & (s == n_seq - 1))
        def _():
            out_shift(main).start()

        @pl.when((c == 1) & (s < n_seq - 1))
        def _():
            out_shift(starts[2] - starts[1] - late).start()

    depth_step(1, 3)
    small_to_y.wait()
    small_y[...] = small_core[...] + small_y[...]
    loop(1, n_seq, lambda hop: small_to(hop).start())
    for hop in range(4, depth + 1):
        depth_step(1, hop)
    small_sum[...] = small_y[...]

    def small_add(hop):
        small_from(hop).wait_recv()
        small_sum[...] = small_sum[...] + small_seq[at.seq(-hop)]

    loop(1, n_seq, small_add)
    finish(1)

    @pl.when(y == 0)
    def _():
        out_shift(0).wait()

    def in_last(hop):
        k = at.seq(hop)
        in_from(k).wait_recv()
        in_to_owner(k).wait_send()

    loop(1, n_seq, in_last)
    in_keep.wait()

    def seq_sent(k):
        for y_to in range(2):
            in_to_core(y_to, k).wait_send()
        in_to_y(k).wait_send()

    loop(0, n_seq, seq_sent)
    loop(1, n_seq, lambda hop: small_to(hop).wait_send())
    small_to_core.wait_send()
    for y_to in range(2):
        out_to_core(y_to).wait_send()
    extra_to_core.wait_send()
    out_to_y.wait_send()

    @pl.when(y == 1)
    def _():
        extra_to_y.wait_send()

    for kind in range(2):
        for k in range(depth):
            to_across(kind, k).wait_send()
        for hop in range(1, depth):
            to_depth(kind, around_z(hop)).wait_send()


def reduce_all(n_dp, n_seq, late, starts, keep, d_part, b_part, in_part, out_part, normed, small):
    depth = n_seq // 2
    block = d_part.shape[2:]
    in_block = in_part.shape[2:]
    width = block[1]
    main = starts[1] - starts[0]
    slot = main + late
    bf16, f32 = jnp.bfloat16, jnp.float32
    rest, near = pl.BlockSpec(memory_space=pl.ANY), pl.BlockSpec(memory_space=pltpu.VMEM)
    dma = pltpu.SemaphoreType.DMA
    return pl.pallas_call(
        functools.partial(reduce_kernel, n_seq=n_seq, late=late, starts=starts, keep=keep),
        in_specs=[rest, rest, rest, rest, near, near],
        out_specs=[near, rest, near, rest, near],
        out_shape=[
            jax.ShapeDtypeStruct((2,) + block, f32),
            jax.ShapeDtypeStruct((n_seq,) + in_block, bf16),
            jax.ShapeDtypeStruct((slot, width), bf16),
            jax.ShapeDtypeStruct((late, width), bf16),
            jax.ShapeDtypeStruct(small.shape, f32),
        ],
        scratch_shapes=[
            pltpu.VMEM((2, depth) + block, bf16),
            pltpu.VMEM((2, depth) + block, bf16),
            pltpu.VMEM((2, depth) + block, bf16),
            pltpu.VMEM((2, n_seq) + in_block, bf16),
            pltpu.VMEM((2, n_seq) + in_block, bf16),
            pltpu.VMEM((n_seq,) + in_block, bf16),
            pltpu.VMEM((2, slot, width), bf16),
            pltpu.VMEM((2, slot, width), bf16),
            pltpu.VMEM((slot, width), bf16),
            pltpu.VMEM(small.shape, f32),
            pltpu.VMEM(small.shape, f32),
            pltpu.VMEM(small.shape, f32),
            pltpu.VMEM((n_seq,) + small.shape, f32),
            dma((7,)), dma((2, 2, depth)), dma((2, 2, depth)), dma((2, 2, n_seq)), dma((2, n_seq)),
            dma((2, n_seq)), dma((2, 6)), dma((2, 2 + n_seq)), dma((1,)),
        ],
        compiler_params=pltpu.CompilerParams(
            collective_id=1, has_side_effects=True, vmem_limit_bytes=56 * 2**20
        ),
        name="reduce_all",
    )(d_part, b_part, in_part, out_part, normed, small)

def split_heads(
    n_dp, n_seq, tokens, cotangent, segment_ids, doc_positions,
    in_weight, in_first, in_second, in_average,
    out_weight, out_first, out_second, out_average,
    small_params, small_first, small_second, small_average,
):
    bf16, f32 = jnp.bfloat16, jnp.float32
    rows, own_tokens, width = tokens.shape
    row_tokens = own_tokens * n_seq
    all_tokens = rows * row_tokens
    head_size = width // HEADS
    ffn = (in_weight.shape[1] - 3 * width) // 2
    in_rows, own = in_weight.shape[0], out_weight.shape[0]
    dp_rows = own * n_seq
    att = width // n_seq
    late = width - dp_rows
    act = [(dp_rows - late) // n_seq, own, own]
    act_all = sum(act)
    cuts = [0, act[0] * n_seq, (act[0] + own) * n_seq, ffn]
    lead = att - own
    p, s = lax.axis_index("dp"), lax.axis_index("seq")

    def share(v):
        parts = [v[:, i * width : (i + 1) * width].reshape(-1, n_seq, att) for i in range(3)]
        for half in range(2):
            base = 3 * width + half * ffn
            for i in range(3):
                parts.append(v[:, base + cuts[i] : base + cuts[i + 1]].reshape(-1, n_seq, act[i]))
        return jnp.transpose(jnp.concatenate(parts, axis=2), (1, 0, 2))

    def unshare(v):
        v = jnp.transpose(v, (1, 0, 2))
        sizes = [att] * 3 + act * 2
        parts, at = [], 0
        for size in sizes:
            parts.append(v[:, :, at : at + size].reshape(v.shape[0], n_seq * size))
            at += size
        return jnp.concatenate(parts, axis=1)

    out_low = out_weight.astype(bf16)
    small_low = small_params.astype(bf16).astype(f32).T
    widen = lambda v, n: jnp.pad(v, ((0, n - v.shape[0]), (0, 128 - v.shape[1])))
    tile = jnp.concatenate(
        [
            widen(small_low, 8),
            widen(jnp.concatenate([segment_ids, doc_positions], axis=0).astype(f32), 8),
        ],
        axis=0,
    )
    x_full, g_full, in_low, slots, tiles = gather_all(
        n_dp, n_seq, late, tokens, cotangent, share(in_weight.astype(bf16)), out_low, tile
    )
    x_full, g_full = x_full.reshape(all_tokens, width), g_full.reshape(all_tokens, width)
    in_low = in_low.reshape(n_dp * n_seq * in_rows, 3 * att + 2 * act_all)

    small_low = jnp.transpose(tiles[:, :, :5, :in_rows], (2, 0, 1, 3)).reshape(5, width)
    gain, shift = small_low[0], small_low[1]
    bias = lax.dynamic_slice_in_dim(small_low[2:5], s * att, att, 1).reshape(1, 3 * att)
    docs = lax.dynamic_index_in_dim(tiles, p, 0, keepdims=False)[:, 8:, :own_tokens]
    seg_full = jnp.transpose(docs[:, :rows], (1, 0, 2)).reshape(rows, row_tokens)
    pos_full = docs[:, rows : 2 * rows].reshape(n_seq // 2, 2, rows, own_tokens)
    pos_full = jnp.transpose(pos_full, (1, 0, 2, 3))

    late_at = late - lead * s
    first = lax.dynamic_slice_in_dim(slots[0], lead * s, att, 0)
    second = lax.dynamic_slice_in_dim(slots[1], late_at, act[0], 0)
    last = s == n_seq - 1
    keep = att - late
    spare = -(att + act_all) % 128
    out_mine = jnp.concatenate(
        [
            first[:keep],
            jnp.where(last, slots[1, own:], first[keep:]),
            second,
            slots[2, :own],
            slots[3, :own],
            jnp.zeros((spare, width), bf16),
        ],
        axis=0,
    )

    def normalise(v):
        v = v.astype(f32)
        centered = v - jnp.mean(v, axis=-1, keepdims=True)
        inv_std = lax.rsqrt(jnp.mean(centered * centered, axis=-1, keepdims=True) + norm_eps)
        return centered * inv_std, inv_std

    hidden = (normalise(x_full)[0] * gain + shift).astype(bf16)
    proj = jnp.dot(hidden, in_low, preferred_element_type=f32)
    d_joined = lax.dot_general(
        g_full, out_mine, (((1,), (1,)), ((), ())), preferred_element_type=f32
    ).astype(bf16)

    half_rot = ROT // 2
    inv_freq = rope_base ** (-2.0 * jnp.arange(half_rot, dtype=f32) / ROT)
    angles = pos_full.reshape(all_tokens, 1).astype(f32) * inv_freq
    cos, sin = jnp.cos(angles), jnp.sin(angles)
    rest = head_size - ROT
    one, zero = jnp.ones((all_tokens, rest), f32), jnp.zeros((all_tokens, rest), f32)
    none = jnp.zeros_like(sin)
    rope = jnp.stack(
        [
            jnp.concatenate([cos, cos, one] * 2, axis=1),
            jnp.concatenate([-sin, none, zero] * 2, axis=1),
            jnp.concatenate([none, sin, zero] * 2, axis=1),
        ]
    )
    att_low, d_query, d_key, d_value = attention_both(
        proj, bias, d_joined, rope, seg_full, n_seq, att, head_size
    )

    gate = proj[:, 3 * att : 3 * att + act_all]
    up = proj[:, 3 * att + act_all :]
    sig = jax.nn.sigmoid(gate)
    silu = gate * sig
    joined = jnp.concatenate(
        [att_low, (silu * up).astype(bf16), jnp.zeros((all_tokens, spare), bf16)], axis=1
    )
    d_act = d_joined[:, att : att + act_all].astype(f32)
    d_gate = d_act * up * sig * (1.0 + gate * (1.0 - sig))
    d_up = d_act * silu
    d_proj = jnp.concatenate(
        [d_query, d_key, d_value, d_gate.astype(bf16), d_up.astype(bf16)], axis=1
    )

    blocks = lambda v: v.reshape(2, n_seq // 2, rows * own_tokens, width)
    branch = jnp.dot(joined, out_mine, preferred_element_type=f32).astype(bf16)
    d_hidden = lax.dot_general(
        d_proj, in_low, (((1,), (1,)), ((), ())), preferred_element_type=f32
    ).astype(bf16)
    out_part = lax.dot_general(
        joined, g_full, (((0,), (0,)), ((), ())), preferred_element_type=f32
    ).astype(bf16)
    in_part = lax.dot_general(
        hidden, d_proj, (((0,), (0,)), ((), ())), preferred_element_type=f32
    ).astype(bf16)
    normed, inv_std = normalise(tokens.reshape(rows * own_tokens, width))
    bias_part = jnp.sum(d_proj[:, : 3 * att].astype(f32), axis=0).reshape(3, att)
    small_part = lax.dynamic_update_slice(jnp.zeros((8, width), f32), bias_part, (2, s * att))
    starts = (0, att, att + act[0], att + act[0] + own)
    sums, in_sum, out_sum, from_prev, small_sum = reduce_all(
        n_dp, n_seq, late, starts, keep,
        blocks(d_hidden), blocks(branch),
        in_part.reshape(n_dp, n_seq, in_rows, -1), out_part, normed, small_part,
    )
    d_hidden, branch = sums[0], sums[1]

    output = (tokens.astype(f32) + branch.reshape(tokens.shape)).astype(bf16)
    d_normed = d_hidden * gain
    input_grad = cotangent.astype(f32) + (
        inv_std
        * (
            d_normed
            - jnp.mean(d_normed, axis=-1, keepdims=True)
            - normed * jnp.mean(d_normed * normed, axis=-1, keepdims=True)
        )
    ).reshape(tokens.shape)
    small_grad = lax.dynamic_slice(small_sum, (0, (p * n_seq + s) * in_rows), (8, in_rows))[:5].T

    count = jnp.where(p == 0, lead * s, jnp.where(p == 1, late - lead * s, 0))
    out_grad = lax.dynamic_slice_in_dim(
        jnp.concatenate([from_prev, out_sum[:own]], axis=0), late - count, own, 0
    ).astype(f32)
    in_grad = unshare(in_sum).astype(f32)

    in_new = adam_update(
        in_weight, in_first, in_second, in_average, in_grad, matrix_rate, weight_decay
    )
    out_new = adam_update(
        out_weight, out_first, out_second, out_average, out_grad, matrix_rate, weight_decay
    )
    small_new = adam_update(
        small_params, small_first, small_second, small_average, small_grad, small_rate, 0.0
    )
    return (output, input_grad, *in_new, *out_new, *small_new, small_grad, in_grad, out_grad)


def solution(mesh):
    n_dp, n_seq = mesh.shape["dp"], mesh.shape["seq"]

    def choose(*operands):
        own_rows = operands[8].shape[0]
        model_width = operands[0].shape[2]
        if heads_fit(n_dp, n_seq, own_rows, model_width, operands[4].shape[1]):
            return split_heads(n_dp, n_seq, *operands)
        return per_device(*operands)

    return jax.shard_map(
        choose,
        mesh=mesh,
        in_specs=(
            P("dp", "seq", None),
            P("dp", "seq", None),
            P("dp", "seq"),
            P("dp", "seq"),
            P(("dp", "seq"), None),
            P(("dp", "seq"), None),
            P(("dp", "seq"), None),
            P(("dp", "seq"), None),
            P(("dp", "seq"), None),
            P(("dp", "seq"), None),
            P(("dp", "seq"), None),
            P(("dp", "seq"), None),
            P(("dp", "seq"), None),
            P(("dp", "seq"), None),
            P(("dp", "seq"), None),
            P(("dp", "seq"), None),
        ),
        out_specs=(
            P("dp", "seq", None),
            P("dp", "seq", None),
            P(("dp", "seq"), None),
            P(("dp", "seq"), None),
            P(("dp", "seq"), None),
            P(("dp", "seq"), None),
            P(("dp", "seq"), None),
            P(("dp", "seq"), None),
            P(("dp", "seq"), None),
            P(("dp", "seq"), None),
            P(("dp", "seq"), None),
            P(("dp", "seq"), None),
            P(("dp", "seq"), None),
            P(("dp", "seq"), None),
        ),
        check_vma=False,
    )
```

```python
import functools

import jax
import jax.numpy as jnp
from jax import lax
from jax.experimental import pallas as pl
from jax.experimental.pallas import tpu as pltpu
from jax.sharding import PartitionSpec as P

HEADS = 32
ROT = 16
STEP = 2


beta_one = 0.9
adam_eps = 1e-08
matrix_rate = 0.001
small_rate = 0.01
weight_decay = 0.1
norm_eps = 1e-05
rope_base = 10000.0
neg_large = -1e30


def rope_tables(positions, rot_dims):
    half_rot = rot_dims // 2
    inv_freq = rope_base ** (-2.0 * jnp.arange(half_rot, dtype=jnp.float32) / rot_dims)
    angles = positions.astype(jnp.float32)[..., None] * inv_freq
    return (jnp.cos(angles)[..., None, :], jnp.sin(angles)[..., None, :])


def apply_rope(field_in, cosine_tab, sine_tab, rot_dims):
    half_rot = rot_dims // 2
    low_half = field_in[..., :half_rot]
    high_half = field_in[..., half_rot:rot_dims]
    return jnp.concatenate(
        [
            low_half * cosine_tab - high_half * sine_tab,
            high_half * cosine_tab + low_half * sine_tab,
            field_in[..., rot_dims:],
        ],
        axis=-1,
    )


def undo_rope(grad_in, cosine_tab, sine_tab, rot_dims):
    half_rot = rot_dims // 2
    low_half = grad_in[..., :half_rot]
    high_half = grad_in[..., half_rot:rot_dims]
    return jnp.concatenate(
        [
            low_half * cosine_tab + high_half * sine_tab,
            high_half * cosine_tab - low_half * sine_tab,
            grad_in[..., rot_dims:],
        ],
        axis=-1,
    )


def visible(query_seg, key_seg, query_pos, key_pos):
    same_doc = query_seg[:, :, None] == key_seg[:, None, :]
    causal = key_pos[None, :] <= query_pos[:, None]
    return (same_doc & causal[None])[:, None]


def to_tokens(head_major):
    return jnp.transpose(head_major, (0, 2, 1, 3))


def adam_update(weight, first, second, average, gradient, rate, decay_rate):
    beta_two = 1.0 - STEP ** (-0.8)
    average_keep = min(0.999, (1.0 + STEP) / (10.0 + STEP))
    first_new = beta_one * first + (1.0 - beta_one) * gradient
    second_new = beta_two * second + (1.0 - beta_two) * gradient * gradient
    moment_hat = beta_one * first_new / (1.0 - beta_one ** (STEP + 1)) + (
        1.0 - beta_one
    ) * gradient / (1.0 - beta_one**STEP)
    weight_new = weight - rate * (
        moment_hat / (jnp.sqrt(second_new) + adam_eps) + decay_rate * weight
    )
    average_new = average_keep * average + (1.0 - average_keep) * weight_new
    return (weight_new, second_new, average_new)


def per_device(
    tokens,
    cotangent,
    segment_ids,
    doc_positions,
    in_weight,
    in_first,
    in_second,
    in_average,
    out_weight,
    out_first,
    out_second,
    out_average,
    small_params,
    small_first,
    small_second,
    small_average,
):
    rows_here, row_tokens, model_width = tokens.shape
    head_count = HEADS
    head_size = model_width // head_count
    score_scale = head_size ** (-0.5)
    all_tokens = rows_here * row_tokens
    wide_in = in_weight.shape[1]
    ffn_width = (wide_in - 3 * model_width) // 2
    shape_heads = (rows_here, row_tokens, head_count, head_size)
    own_places = lax.axis_index("seq") * row_tokens + jnp.arange(row_tokens)
    flat_in = tokens.astype(jnp.float32).reshape(all_tokens, model_width)
    centered = flat_in - jnp.mean(flat_in, axis=-1, keepdims=True)
    inv_std = lax.rsqrt(jnp.mean(centered * centered, axis=-1, keepdims=True) + norm_eps)
    normed = centered * inv_std
    in_low = in_weight.astype(jnp.bfloat16)
    out_low = out_weight.astype(jnp.bfloat16)
    small_low = small_params.astype(jnp.bfloat16)
    w_piece = lax.all_gather(in_low, ("dp", "seq"), axis=0, tiled=True)
    s_piece = lax.all_gather(small_low, ("dp", "seq"), axis=0, tiled=True)
    columns = normed
    s_float = s_piece.astype(jnp.float32)
    h_piece = (columns * s_float[:, 0] + s_float[:, 1]).astype(jnp.bfloat16)
    proj_acc = jnp.dot(h_piece, w_piece, preferred_element_type=jnp.float32)
    norm_gain = s_float[:, 0]
    qkv_bias = s_float[:, 2:5].T.reshape(3 * model_width)
    qkv_full = proj_acc[:, : 3 * model_width] + qkv_bias
    gate_pre = proj_acc[:, 3 * model_width : 3 * model_width + ffn_width]
    up_pre = proj_acc[:, 3 * model_width + ffn_width :]
    cosine_tab, sine_tab = rope_tables(doc_positions, ROT)
    query_low = apply_rope(
        qkv_full[:, :model_width].reshape(shape_heads), cosine_tab, sine_tab, ROT
    ).astype(jnp.bfloat16)
    key_low = apply_rope(
        qkv_full[:, model_width : 2 * model_width].reshape(shape_heads), cosine_tab, sine_tab, ROT
    ).astype(jnp.bfloat16)
    value_low = qkv_full[:, 2 * model_width :].reshape(shape_heads).astype(jnp.bfloat16)
    seg_low = segment_ids.astype(jnp.bfloat16)
    seg_own = segment_ids.astype(jnp.float32)
    key_flat = key_low.reshape(rows_here, row_tokens, model_width)
    value_flat = value_low.reshape(rows_here, row_tokens, model_width)
    attend_init = (
        jnp.full((rows_here, head_count, row_tokens), neg_large, jnp.float32),
        jnp.zeros((rows_here, head_count, row_tokens), jnp.float32),
        jnp.zeros((rows_here, head_count, row_tokens, head_size), jnp.float32),
    )
    key_piece = lax.all_gather(key_flat, "seq", axis=1, tiled=True)
    value_piece = lax.all_gather(value_flat, "seq", axis=1, tiled=True)
    seg_piece = lax.all_gather(seg_low, "seq", axis=1, tiled=True)
    turn_count = key_piece.shape[1] // row_tokens

    def attend_one_turn(turn_index, inner_state):
        offset = turn_index * row_tokens
        key_blk = lax.dynamic_slice_in_dim(key_piece, offset, row_tokens, 1).reshape(shape_heads)
        value_blk = lax.dynamic_slice_in_dim(value_piece, offset, row_tokens, 1).reshape(
            shape_heads
        )
        seg_blk = lax.dynamic_slice_in_dim(seg_piece, offset, row_tokens, 1).astype(jnp.float32)
        key_mask = visible(seg_own, seg_blk, own_places, offset + jnp.arange(row_tokens))
        running_top, running_sum, weighted = inner_state
        scores = (
            jnp.einsum("rqhe,rkhe->rhqk", query_low, key_blk, preferred_element_type=jnp.float32)
            * score_scale
        )
        scores = jnp.where(key_mask, scores, neg_large)
        new_top = jnp.maximum(running_top, jnp.max(scores, axis=-1))
        weights = jnp.where(key_mask, jnp.exp(scores - new_top[..., None]), 0.0)
        factor = jnp.exp(running_top - new_top)
        running_sum = running_sum * factor + jnp.sum(weights, axis=-1)
        weighted = weighted * factor[..., None] + jnp.einsum(
            "rhqk,rkhe->rhqe",
            weights.astype(jnp.bfloat16),
            value_blk,
            preferred_element_type=jnp.float32,
        )
        return (new_top, running_sum, weighted)

    running_top, running_sum, weighted = lax.fori_loop(0, turn_count, attend_one_turn, attend_init)
    attended = weighted / running_sum[..., None]
    log_total = running_top + jnp.log(running_sum)
    attended_low = to_tokens(attended).reshape(all_tokens, model_width).astype(jnp.bfloat16)
    gate_sig = jax.nn.sigmoid(gate_pre)
    activated = gate_pre * gate_sig * up_pre
    joined = jnp.concatenate([attended_low, activated.astype(jnp.bfloat16)], axis=1)
    columns = joined
    branch_sum = jnp.dot(
        columns,
        lax.all_gather(out_low, ("dp", "seq"), axis=0, tiled=True),
        preferred_element_type=jnp.float32,
    )
    output = (flat_in + branch_sum).astype(jnp.bfloat16).reshape(rows_here, row_tokens, model_width)
    grad_out = cotangent.reshape(all_tokens, model_width)
    d_joined = lax.dot_general(
        grad_out,
        lax.all_gather(out_low, ("dp", "seq"), axis=0, tiled=True),
        (((1,), (1,)), ((), ())),
        preferred_element_type=jnp.float32,
    )
    d_joined = d_joined.astype(jnp.bfloat16)
    columns = joined
    out_grad = lax.psum_scatter(
        lax.dot_general(
            columns, grad_out, (((0,), (0,)), ((), ())), preferred_element_type=jnp.float32
        ),
        ("dp", "seq"),
        scatter_dimension=0,
        tiled=True,
    )
    d_attended = d_joined[:, :model_width].reshape(shape_heads)
    d_act = d_joined[:, model_width:].astype(jnp.float32)
    d_gate = d_act * up_pre * gate_sig * (1.0 + gate_pre * (1.0 - gate_sig))
    d_up = d_act * gate_pre * gate_sig
    out_dot = jnp.einsum("rqhe,rhqe->rhq", d_attended.astype(jnp.float32), attended)
    grad_zero = jnp.zeros((rows_here, head_count, row_tokens, head_size), jnp.float32)
    query_key_piece = lax.all_gather(key_flat, "seq", axis=1, tiled=True)
    query_value_piece = lax.all_gather(value_flat, "seq", axis=1, tiled=True)
    query_seg_piece = lax.all_gather(seg_low, "seq", axis=1, tiled=True)
    turn_count = query_key_piece.shape[1] // row_tokens

    def query_one_turn(turn_index, inner_state):
        offset = turn_index * row_tokens
        key_blk = lax.dynamic_slice_in_dim(query_key_piece, offset, row_tokens, 1).reshape(
            shape_heads
        )
        value_blk = lax.dynamic_slice_in_dim(query_value_piece, offset, row_tokens, 1).reshape(
            shape_heads
        )
        seg_blk = lax.dynamic_slice_in_dim(query_seg_piece, offset, row_tokens, 1).astype(
            jnp.float32
        )
        key_mask = visible(seg_own, seg_blk, own_places, offset + jnp.arange(row_tokens))
        scores = (
            jnp.einsum("rqhe,rkhe->rhqk", query_low, key_blk, preferred_element_type=jnp.float32)
            * score_scale
        )
        weights = jnp.where(key_mask, jnp.exp(scores - log_total[..., None]), 0.0)
        d_prob = jnp.einsum(
            "rqhe,rkhe->rhqk", d_attended, value_blk, preferred_element_type=jnp.float32
        )
        d_score = (weights * (d_prob - out_dot[..., None])).astype(jnp.bfloat16)
        return (
            inner_state
            + jnp.einsum("rhqk,rkhe->rhqe", d_score, key_blk, preferred_element_type=jnp.float32)
            * score_scale
        )

    d_query = lax.fori_loop(0, turn_count, query_one_turn, grad_zero)
    row_stats = jnp.concatenate(
        [jnp.transpose(log_total, (0, 2, 1)), jnp.transpose(out_dot, (0, 2, 1))], axis=2
    )
    stat_high = row_stats.astype(jnp.bfloat16)
    stat_low = (row_stats - stat_high.astype(jnp.float32)).astype(jnp.bfloat16)
    query_flat = query_low.reshape(rows_here, row_tokens, model_width)
    d_att_flat = d_attended.reshape(rows_here, row_tokens, model_width)
    query_piece = lax.all_gather(query_flat, "seq", axis=1, tiled=True)
    dout_piece = lax.all_gather(d_att_flat, "seq", axis=1, tiled=True)
    high_piece = lax.all_gather(stat_high, "seq", axis=1, tiled=True)
    low_piece = lax.all_gather(stat_low, "seq", axis=1, tiled=True)
    key_seg_piece = lax.all_gather(seg_low, "seq", axis=1, tiled=True)
    turn_count = query_piece.shape[1] // row_tokens

    def key_one_turn(turn_index, inner_state):
        offset = turn_index * row_tokens
        query_blk = lax.dynamic_slice_in_dim(query_piece, offset, row_tokens, 1).reshape(
            shape_heads
        )
        dout_blk = lax.dynamic_slice_in_dim(dout_piece, offset, row_tokens, 1).reshape(shape_heads)
        stat_blk = lax.dynamic_slice_in_dim(high_piece, offset, row_tokens, 1).astype(
            jnp.float32
        ) + lax.dynamic_slice_in_dim(low_piece, offset, row_tokens, 1).astype(jnp.float32)
        lse_blk = jnp.transpose(stat_blk[..., :head_count], (0, 2, 1))
        dot_blk = jnp.transpose(stat_blk[..., head_count:], (0, 2, 1))
        seg_blk = lax.dynamic_slice_in_dim(key_seg_piece, offset, row_tokens, 1).astype(jnp.float32)
        key_mask = visible(seg_blk, seg_own, offset + jnp.arange(row_tokens), own_places)
        d_key, d_value = inner_state
        scores = (
            jnp.einsum("rqhe,rkhe->rhqk", query_blk, key_low, preferred_element_type=jnp.float32)
            * score_scale
        )
        weights = jnp.where(key_mask, jnp.exp(scores - lse_blk[..., None]), 0.0)
        d_value = d_value + jnp.einsum(
            "rhqk,rqhe->rhke",
            weights.astype(jnp.bfloat16),
            dout_blk,
            preferred_element_type=jnp.float32,
        )
        d_prob = jnp.einsum(
            "rqhe,rkhe->rhqk", dout_blk, value_low, preferred_element_type=jnp.float32
        )
        d_score = (weights * (d_prob - dot_blk[..., None])).astype(jnp.bfloat16)
        d_key = (
            d_key
            + jnp.einsum("rhqk,rqhe->rhke", d_score, query_blk, preferred_element_type=jnp.float32)
            * score_scale
        )
        return (d_key, d_value)

    d_key, d_value = lax.fori_loop(0, turn_count, key_one_turn, (grad_zero, grad_zero))
    d_query_tok = undo_rope(to_tokens(d_query), cosine_tab, sine_tab, ROT).reshape(
        all_tokens, model_width
    )
    d_key_tok = undo_rope(to_tokens(d_key), cosine_tab, sine_tab, ROT).reshape(
        all_tokens, model_width
    )
    d_value_tok = to_tokens(d_value).reshape(all_tokens, model_width)
    d_proj = jnp.concatenate([d_query_tok, d_key_tok, d_value_tok, d_gate, d_up], axis=1).astype(
        jnp.bfloat16
    )
    d_hidden = lax.dot_general(
        d_proj,
        lax.all_gather(in_low, ("dp", "seq"), axis=0, tiled=True),
        (((1,), (1,)), ((), ())),
        preferred_element_type=jnp.float32,
    )
    columns = h_piece
    in_grad = lax.psum_scatter(
        lax.dot_general(
            columns, d_proj, (((0,), (0,)), ((), ())), preferred_element_type=jnp.float32
        ),
        ("dp", "seq"),
        scatter_dimension=0,
        tiled=True,
    )
    gain_grad = jnp.sum(d_hidden * normed, axis=0)
    shift_grad = jnp.sum(d_hidden, axis=0)
    bias_grad = (
        jnp.sum(d_proj[:, : 3 * model_width].astype(jnp.float32), axis=0).reshape(3, model_width).T
    )
    small_term = jnp.concatenate([gain_grad[:, None], shift_grad[:, None], bias_grad], axis=1)
    small_grad = lax.psum_scatter(small_term, ("dp", "seq"), scatter_dimension=0, tiled=True)
    d_normed = d_hidden * norm_gain
    input_grad = grad_out.astype(jnp.float32) + inv_std * (
        d_normed
        - jnp.mean(d_normed, axis=-1, keepdims=True)
        - normed * jnp.mean(d_normed * normed, axis=-1, keepdims=True)
    )
    input_grad = input_grad.reshape(rows_here, row_tokens, model_width)
    in_new = adam_update(
        in_weight, in_first, in_second, in_average, in_grad, matrix_rate, weight_decay
    )
    out_new = adam_update(
        out_weight, out_first, out_second, out_average, out_grad, matrix_rate, weight_decay
    )
    small_new = adam_update(
        small_params, small_first, small_second, small_average, small_grad, small_rate, 0.0
    )
    return (
        output,
        input_grad,
        in_new[0],
        in_new[1],
        in_new[2],
        out_new[0],
        out_new[1],
        out_new[2],
        small_new[0],
        small_new[1],
        small_new[2],
        small_grad,
        in_grad,
        out_grad,
    )


def heads_fit(n_dp, n_seq, own_rows, model_width, wide_in):
    dp_rows = own_rows * n_seq
    if n_dp != 4 or HEADS % (2 * n_seq) or not dp_rows < model_width < 2 * dp_rows:
        return False
    att_rows = model_width // n_seq
    late_att = model_width - dp_rows
    first_act = dp_rows - late_att
    if first_act % n_seq:
        return False
    lead = att_rows - own_rows
    return (
        wide_in - 3 * model_width == 2 * (n_dp * dp_rows - model_width)
        and lead == own_rows - first_act // n_seq
        and lead * n_seq == late_att
        and lead % 16 == 0
    )


def middle_kernel(
    q_ref, k_ref, v_ref, bq_ref, bk_ref, bv_ref, da_ref, act_ref, d_act_ref, rope_ref,
    seg_q_ref, seg_k_ref,
    joined_ref, d_proj_ref, bias_ref,
    *, head_size, half_rot, att_rows, act_rows,
):
    row, pair = pl.program_id(0), pl.program_id(1)
    lanes = 2 * head_size
    half = act_ref.shape[3]
    bf16, f32 = jnp.bfloat16, jnp.float32

    def feed_forward(step):
        x, z = lax.rem(step, 2), step // 2
        raw = act_ref[x, z, 0]
        gate = raw[:, 3 * att_rows : 3 * att_rows + act_rows]
        up = raw[:, 3 * att_rows + act_rows :]
        d_act = d_act_ref[x, z, 0][:, att_rows : att_rows + act_rows].astype(f32)
        sig = 1.0 / (1.0 + jnp.exp(-gate))
        silu = gate * sig
        spare = joined_ref.shape[4] - att_rows - act_rows
        rows = pl.ds(pl.multiple_of(pair * half, half), half)
        joined_ref[x, z, row, rows, att_rows:] = jnp.concatenate(
            [silu * up, jnp.zeros((half, spare), f32)], axis=1
        ).astype(bf16)
        d_gate = d_act * up * sig * (1.0 + gate * (1.0 - sig))
        d_proj_ref[x, z, row, rows, 3 * att_rows :] = jnp.concatenate(
            [d_gate, d_act * silu], axis=1
        ).astype(bf16)

    loop(0, act_ref.shape[0] * act_ref.shape[1], feed_forward)

    def whole(v):
        across, depth = v.shape[:2]
        parts = [v[x, z].reshape(v.shape[-2:]) for z in range(depth) for x in range(across)]
        return jnp.concatenate(parts, axis=0)

    def store(ref, first, v):
        across, depth, _, some, _ = ref.shape
        columns = pl.ds(pl.multiple_of(first + pair * lanes, lanes), lanes)
        for z in range(depth):
            for x in range(across):
                at = (z * across + x) * some
                ref[x, z, row, :, columns] = v[at : at + some]

    cos, sin_low, sin_high = (rope_ref[0, i].T for i in range(3))
    tokens = cos.shape[0]
    scale = head_size ** (-0.5)

    def turn(v, way):
        return (
            v * cos
            + way * pltpu.roll(v, lanes - half_rot, 1) * sin_low
            + way * pltpu.roll(v, half_rot, 1) * sin_high
        )

    query = (turn(whole(q_ref[...]) + bq_ref[...], 1.0)).astype(bf16) * scale
    query = query.astype(bf16)
    key = turn(whole(k_ref[...]) + bk_ref[...], 1.0).astype(bf16)
    value = (whole(v_ref[...]) + bv_ref[...]).astype(bf16)
    d_att = whole(da_ref[...])
    place_q = lax.broadcasted_iota(jnp.int32, (tokens, tokens), 0)
    place_k = lax.broadcasted_iota(jnp.int32, (tokens, tokens), 1)
    mask = (seg_q_ref[0] == seg_k_ref[0]) & (place_k <= place_q)
    lane = lax.broadcasted_iota(jnp.int32, (tokens, lanes), 1)
    nt = (((1,), (1,)), ((), ()))
    tn = (((0,), (0,)), ((), ()))
    dot = functools.partial(lax.dot_general, preferred_element_type=f32)
    att = jnp.zeros((tokens, lanes), f32)
    d_query = jnp.zeros((tokens, lanes), f32)
    d_key = jnp.zeros((tokens, lanes), f32)
    d_value = jnp.zeros((tokens, lanes), f32)
    for head in range(lanes // head_size):
        mine = (lane >= head * head_size) & (lane < (head + 1) * head_size)
        q_h = jnp.where(mine, query, jnp.zeros_like(query))
        da_h = jnp.where(mine, d_att, jnp.zeros_like(d_att))
        scores = jnp.where(mask, dot(q_h, key, nt), neg_large)
        top = jnp.max(scores, axis=1, keepdims=True)
        weights = jnp.exp(scores - top)
        probs = weights * (1.0 / jnp.sum(weights, axis=1, keepdims=True))
        probs_low = probs.astype(bf16)
        att_h = jnp.where(mine, dot(probs_low, value, (((1,), (0,)), ((), ()))), 0.0)
        out_dot = jnp.sum(att_h * d_att.astype(f32), axis=1, keepdims=True)
        d_prob = dot(da_h, value, nt)
        d_score = (probs * (d_prob - out_dot)).astype(bf16)
        att = att + att_h
        d_query = d_query + jnp.where(mine, dot(d_score, key, (((1,), (0,)), ((), ()))), 0.0)
        d_key = d_key + dot(d_score, q_h, tn)
        d_value = d_value + dot(probs_low, da_h, tn)
    store(joined_ref, 0, att.astype(bf16))
    grads = (turn(d_query * scale, -1.0), turn(d_key, -1.0), d_value)
    columns = pl.ds(pl.multiple_of(pair * lanes, lanes), lanes)
    for i, grad in enumerate(grads):
        grad = grad.astype(bf16)
        store(d_proj_ref, i * att_rows, grad)
        total = jnp.sum(grad.astype(f32), axis=0, keepdims=True)

        @pl.when(row == 0)
        def _():
            bias_ref[i : i + 1, columns] = total

        @pl.when(row > 0)
        def _():
            bias_ref[i : i + 1, columns] = bias_ref[i : i + 1, columns] + total


def middle(proj, bias, d_joined, rope, seg, n_seq, att_rows, act_rows, head_size):
    rows, tokens = seg.shape
    lanes = 2 * head_size
    pairs = att_rows // lanes
    bf16, f32 = jnp.bfloat16, jnp.float32
    order = (2, n_seq // 2, rows, tokens // n_seq)
    wide = lambda v: v.reshape(order + v.shape[-1:])
    shape = (2, n_seq // 2, 1, tokens // n_seq, lanes)
    block = lambda first: pl.BlockSpec(shape, lambda r, h: (0, 0, r, 0, first + h))
    row = lambda first: pl.BlockSpec((1, lanes), lambda r, h: (0, first + h))
    half = lambda v: pl.BlockSpec(
        (2, n_seq // 2, 1, tokens // n_seq // pairs, v.shape[-1]), lambda r, h: (0, 0, r, h, 0)
    )
    all_of = lambda v: pl.BlockSpec(v.shape, lambda r, h: (0,) * len(v.shape))
    outs = [
        jax.ShapeDtypeStruct(order + (d_joined.shape[-1],), bf16),
        jax.ShapeDtypeStruct(order + (proj.shape[-1],), bf16),
        jax.ShapeDtypeStruct((8, att_rows), f32),
    ]
    proj, d_joined = wide(proj), wide(d_joined)
    joined, d_proj, bias_sums = pl.pallas_call(
        functools.partial(
            middle_kernel,
            head_size=head_size, half_rot=ROT // 2, att_rows=att_rows, act_rows=act_rows,
        ),
        grid=(rows, pairs),
        in_specs=[
            block(0), block(pairs), block(2 * pairs),
            row(0), row(pairs), row(2 * pairs),
            block(0), half(proj), half(d_joined),
            pl.BlockSpec((1, 3, lanes, tokens), lambda r, h: (r, 0, 0, 0)),
            pl.BlockSpec((1, tokens, 1), lambda r, h: (r, 0, 0)),
            pl.BlockSpec((1, 1, tokens), lambda r, h: (r, 0, 0)),
        ],
        out_specs=[all_of(v) for v in outs],
        out_shape=outs,
        compiler_params=pltpu.CompilerParams(vmem_limit_bytes=56 * 2**20),
        name="middle",
    )(
        proj, proj, proj, bias, bias, bias, d_joined, proj, d_joined,
        rope, seg[:, :, None], seg[:, None, :],
    )
    flat = lambda v: v.reshape(rows * tokens, v.shape[-1])
    return flat(joined), flat(d_proj), bias_sums

MESH_ID = pl.DeviceIdType.MESH


def remote(src, dst, send_sem, recv_sem, device):
    return pltpu.make_async_remote_copy(
        src_ref=src,
        dst_ref=dst,
        send_sem=send_sem,
        recv_sem=recv_sem,
        device_id=device,
        device_id_type=MESH_ID,
    )


class Place:
    def __init__(self, n_seq):
        self.n_seq = n_seq
        self.depth = n_seq // 2
        self.p, self.s = lax.axis_index("dp"), lax.axis_index("seq")
        self.y, self.c = self.p // 2, lax.rem(self.p, 2)
        self.z, self.x = self.s // 2, lax.rem(self.s, 2)
        self.p_y = (1 - self.y) * 2 + self.c
        self.p_c = self.y * 2 + 1 - self.c
        self.p_d = (1 - self.y) * 2 + 1 - self.c
        self.to_y = (self.p_y, self.s)
        self.to_c = (self.p_c, self.s)
        self.to_x = (self.p, self.z * 2 + 1 - self.x)
        self.to_up = (self.p, self.s + 2)
        self.to_down = (self.p, self.s - 2)

    def seq(self, hop):
        return lax.rem(self.s + hop + self.n_seq, self.n_seq)

    def meet(self):
        barrier = pltpu.get_barrier_semaphore()

        def greet(hop, carry):
            pl.semaphore_signal(
                barrier, inc=1, device_id=(self.p, self.seq(hop)), device_id_type=MESH_ID
            )
            return carry

        lax.fori_loop(1, self.n_seq, greet, 0)
        for device in (self.to_y, self.to_c):
            pl.semaphore_signal(barrier, inc=1, device_id=device, device_id_type=MESH_ID)
        pl.semaphore_wait(barrier, self.n_seq + 1)


class Spread:
    def __init__(self, at, own, full, sems):
        self.at, self.own, self.full, self.sems = at, own, full, sems

    def along(self, src, up, ref=None):
        sems, at = self.sems, self.at
        here = self.full.at[at.x, src]
        return remote(
            here if ref is None else ref,
            here,
            sems.at[0 if up else 1, src],
            sems.at[3, src],
            at.to_up if up else at.to_down,
        )

    def across(self, src, ref=None):
        sems, at = self.sems, self.at
        here = self.full.at[at.x, src]
        return remote(here if ref is None else ref, here, sems.at[2, src], sems.at[4, src], at.to_x)

    def local(self):
        return pltpu.make_async_copy(
            self.own, self.full.at[self.at.x, self.at.z], self.sems.at[5, 0]
        )

    def begin_across(self):
        self.across(self.at.z, self.own).start()
        self.local().start()

    def begin_along(self):
        at = self.at

        @pl.when(at.z < at.depth - 1)
        def _():
            self.along(at.z, True, self.own).start()

        @pl.when(at.z > 0)
        def _():
            self.along(at.z, False, self.own).start()

    def step(self, hop):
        at = self.at

        @pl.when(at.z - hop >= 0)
        def _():
            src = at.z - hop
            self.along(src, True).wait_recv()

            @pl.when(at.z < at.depth - 1)
            def _():
                self.along(src, True).start()

            self.across(src).start()

        @pl.when(at.z + hop < at.depth)
        def _():
            src = at.z + hop
            self.along(src, False).wait_recv()

            @pl.when(at.z > 0)
            def _():
                self.along(src, False).start()

            self.across(src).start()

    def arrive(self):
        at = self.at
        for src in range(at.depth):
            here = self.full.at[1 - at.x, src]
            remote(here, here, self.sems.at[2, src], self.sems.at[4, src], at.to_x).wait_recv()
        self.local().wait()

    def sent(self):
        at = self.at
        for src in range(at.depth):
            self.across(src).wait_send()

            @pl.when((at.z < at.depth - 1) & (src <= at.z))
            def _():
                self.along(src, True).wait_send()

            @pl.when((at.z > 0) & (src >= at.z))
            def _():
                self.along(src, False).wait_send()


class Fan:
    def __init__(self, at, pick, sems):
        self.at, self.pick, self.sems = at, pick, sems

    def y(self, k, ref=None):
        at = self.at
        here = self.pick(at.p, k)
        return remote(here if ref is None else ref, here, self.sems.at[0, k], self.sems.at[1, k], at.to_y)

    def core(self, k, ref=None):
        at = self.at
        here = self.pick(at.p, k)
        return remote(here if ref is None else ref, here, self.sems.at[2, k], self.sems.at[3, k], at.to_c)

    def pass_on(self, k):
        at = self.at
        here = self.pick(at.p_y, k)
        return remote(here, here, self.sems.at[4, k], self.sems.at[5, k], at.to_c)

    def from_y(self, k):
        here = self.pick(self.at.p_y, k)
        return remote(here, here, self.sems.at[0, k], self.sems.at[1, k], self.at.to_y)

    def from_core(self, k):
        here = self.pick(self.at.p_c, k)
        return remote(here, here, self.sems.at[2, k], self.sems.at[3, k], self.at.to_c)

    def from_diagonal(self, k):
        here = self.pick(self.at.p_d, k)
        return remote(here, here, self.sems.at[4, k], self.sems.at[5, k], self.at.to_c)


def loop(low, high, body):
    def step(k, carry):
        body(k)
        return carry

    lax.fori_loop(low, high, step, 0)


def gather_kernel(
    x_ref, g_ref, w_ref, o_ref, tile_ref,
    x_full, g_full, w_full, o_full, tiles, hidden, out_mine, proj, d_joined,
    x_block, hid, w_near, p_block, g_near, o_near, t_near, small,
    x_sems, g_sems, w_sems, w_fan_sems, o_sems, o_fan_sems, t_sems, t_fan_sems, local_sems,
    x_in_sems, hid_sems, w_in_sems, p_sems, g_in_sems, o_in_sems,
    *, n_seq, late, lead,
):
    at = Place(n_seq)
    depth = at.depth
    bf16, f32 = jnp.bfloat16, jnp.float32
    own, width = o_ref.shape
    att = own + lead
    first_act = own - lead
    body, extra = pl.ds(0, own), pl.ds(own, late)
    x_go = Spread(at, x_ref, x_full, x_sems)
    g_go = Spread(at, g_ref, g_full, g_sems)
    w_fan = Fan(at, lambda p, k: w_full.at[p, k], w_fan_sems)
    o_fan = Fan(at, lambda p, k: o_full.at[p, body if k == 0 else extra], o_fan_sems)
    t_fan = Fan(at, lambda p, k: tiles.at[p], t_fan_sems)

    def w_send(hop):
        to = at.seq(hop)
        return remote(w_ref.at[to], w_full.at[at.p, at.s], w_sems.at[0, to], w_sems.at[1, at.s], (at.p, to))

    def w_recv(hop):
        src = at.seq(-hop)
        here = w_full.at[at.p, src]
        return remote(here, here, w_sems.at[0, src], w_sems.at[1, src], (at.p, src))

    def t_send(hop):
        to = at.seq(hop)
        return remote(tile_ref, tiles.at[at.p, at.s], t_sems.at[0, to], t_sems.at[1, at.s], (at.p, to))

    def t_recv(hop):
        src = at.seq(-hop)
        here = tiles.at[at.p, src]
        return remote(here, here, t_sems.at[0, src], t_sems.at[1, src], (at.p, src))

    w_local = pltpu.make_async_copy(w_ref.at[at.s], w_full.at[at.p, at.s], local_sems.at[0])
    o_local = pltpu.make_async_copy(o_ref, o_full.at[at.p, body], local_sems.at[1])
    t_local = pltpu.make_async_copy(tile_ref, tiles.at[at.p, at.s], local_sems.at[2])
    head = o_ref.at[pl.ds(0, late)]
    o_send = remote(
        head, o_full.at[at.p, extra], o_sems.at[0], o_sems.at[1], (at.p, at.seq(-1))
    )

    def place(i):
        return lax.rem(at.x + i // depth, 2), lax.rem(at.z + i, depth)

    def block_in(i):
        col, deep = place(i)
        return pltpu.make_async_copy(x_full.at[col, deep], x_block, x_in_sems.at[0])

    def hid_out(i):
        col, deep = place(i)
        return pltpu.make_async_copy(hid.at[col, deep], hidden.at[col, deep], hid_sems.at[i])

    def norm_block(i):
        col, deep = place(i)

        @pl.when(i >= depth)
        def _():
            here = x_full.at[1 - at.x, deep]
            remote(here, here, x_sems.at[2, deep], x_sems.at[4, deep], at.to_x).wait_recv()

        block_in(i).start()
        block_in(i).wait()
        some = 32

        def rows(k):
            part = pl.ds(pl.multiple_of(lax.rem(k, 2) * some, some), some)
            v = x_block[k // 2, part, :].astype(f32)
            centered = v - jnp.mean(v, axis=-1, keepdims=True)
            inv_std = lax.rsqrt(jnp.mean(centered * centered, axis=-1, keepdims=True) + norm_eps)
            done = centered * inv_std * small[0:1, :] + small[1:2, :]
            hid[col, deep, pl.ds(pl.multiple_of(k * some, some), some), :] = done.astype(bf16)

        loop(0, hid.shape[2] // some, rows)
        hid_out(i).start()

    def w_in(p, k):
        return pltpu.make_async_copy(w_full.at[p], w_near.at[p], w_in_sems.at[k])

    def g_in():
        return pltpu.make_async_copy(g_full, g_near, g_in_sems.at[0])

    def o_in(k):
        last = at.s == n_seq - 1
        lead_at = pl.multiple_of(lead * at.s, 16)
        late_at = pl.multiple_of(late - lead * at.s, 16)
        src, dst, count = [
            (o_full.at[0, pl.ds(lead_at, att - late)], 0, att - late),
            (o_full.at[0, pl.ds(lead_at + (att - late), late)], att - late, late),
            (o_full.at[1, pl.ds(late_at, first_act)], att, first_act),
            (o_full.at[2, body], att + first_act, own),
            (o_full.at[3, body], att + first_act + own, own),
            (o_full.at[1, extra], att - late, late),
        ][k]
        return pltpu.make_async_copy(src, o_near.at[pl.ds(dst, count)], o_in_sems.at[k])

    step_rows = p_block.shape[1]
    steps = hid.shape[0] * depth * hid.shape[2] // step_rows
    per_block = step_rows // hid.shape[2]

    def p_out(k):
        return pltpu.make_async_copy(
            p_block.at[lax.rem(k, 2)],
            proj.at[pl.ds(pl.multiple_of(k * step_rows, step_rows), step_rows)],
            p_sems.at[lax.rem(k, 2)],
        )

    def project(k):
        @pl.when(k >= 2)
        def _():
            p_out(k - 2).wait()

        rows = per_block * k
        left = hid[rows // depth, pl.ds(lax.rem(rows, depth), per_block)]
        left = left.reshape(step_rows, width)
        columns = p_block.shape[2]
        for n in range(0, columns, 512):
            some = min(512, columns - n)
            right = w_near[:, :, :, n : n + some].reshape(width, some)
            p_block[lax.rem(k, 2), :, n : n + some] = jnp.dot(
                left, right, preferred_element_type=f32
            )
        p_out(k).start()

    def join_back(k):
        rows = per_block * k
        left = g_near[rows // depth, pl.ds(lax.rem(rows, depth), per_block)]
        left = left.reshape(step_rows, width)
        d_joined[pl.ds(pl.multiple_of(k * step_rows, step_rows), step_rows), :] = (
            lax.dot_general(
                left, o_near[...], (((1,), (1,)), ((), ())), preferred_element_type=f32
            ).astype(bf16)
        )

    at.meet()
    x_go.begin_along()
    x_go.begin_across()
    g_go.begin_across()
    loop(1, n_seq, lambda hop: t_send(hop).start())
    t_local.start()
    w_fan.y(at.s, w_ref.at[at.s]).start()
    w_fan.core(at.s, w_ref.at[at.s]).start()
    w_local.start()
    o_fan.y(0, o_ref).start()
    o_fan.core(0, o_ref).start()
    o_local.start()
    w_send(1).start()
    w_send(n_seq - 1).start()
    for hop in range(1, depth):
        x_go.step(hop)
        if hop == 1:
            t_local.wait()
            loop(1, n_seq, lambda k: t_recv(k).wait_recv())
            t_fan.y(0).start()
            t_fan.core(0).start()
        if hop == 2:
            t_fan.from_y(0).wait_recv()
            t_fan.pass_on(0).start()
        w_send(hop + 1).start()
        if hop + 1 < n_seq - hop - 1:
            w_send(n_seq - hop - 1).start()
    g_go.begin_along()

    @pl.when(at.y == 0)
    def _():
        o_send.start()

    t_fan.from_core(0).wait_recv()
    t_fan.from_diagonal(0).wait_recv()
    t_load = pltpu.make_async_copy(tiles, t_near, local_sems.at[3])
    t_load.start()
    t_load.wait()
    for p in range(t_near.shape[0]):
        for pair in range(n_seq // 2):
            two = t_near[p, 2 * pair, 0:8] + t_near[p, 2 * pair + 1, 0:8]
            lanes = two.shape[1]
            first = (p * (n_seq // 2) + pair) * lanes
            small[:, first : first + lanes] = two
    o_near[att + first_act + 2 * own :, :] = jnp.zeros_like(o_near[att + first_act + 2 * own :, :])
    x_go.local().wait()

    def w_step(hop):
        src = at.seq(-hop)
        w_recv(hop).wait_recv()
        w_fan.y(src).start()
        w_fan.core(src).start()
        norm_block(hop - 1)

    loop(1, n_seq, w_step)
    norm_block(n_seq - 1)
    w_local.wait()
    w_in(at.p, 0).start()
    def w_pass(hop):
        src = at.seq(-hop)
        w_fan.from_y(src).wait_recv()
        w_fan.pass_on(src).start()

    for hop in range(1, depth):
        g_go.step(hop)
        loop((hop - 1) * 3, min(hop * 3, n_seq), w_pass)
        if hop == 1:

            @pl.when(at.y == 0)
            def _():
                o_send.wait_recv()
                o_fan.y(1).start()
                o_fan.core(1).start()

    loop((depth - 1) * 3, n_seq, w_pass)
    w_in(at.p_y, 1).start()

    def w_last(k):
        w_fan.from_core(k).wait_recv()
        w_fan.from_diagonal(k).wait_recv()

    loop(0, n_seq, w_last)
    w_in(at.p_c, 2).start()
    w_in(at.p_d, 3).start()
    o_fan.from_y(0).wait_recv()
    o_fan.pass_on(0).start()

    @pl.when(at.y == 1)
    def _():
        o_fan.from_y(1).wait_recv()
        o_fan.pass_on(1).start()

    for k, p in enumerate((at.p, at.p_y, at.p_c, at.p_d)):
        w_in(p, k).wait()
    loop(0, steps, project)

    o_local.wait()
    o_fan.from_core(0).wait_recv()
    o_fan.from_diagonal(0).wait_recv()

    @pl.when(at.y == 0)
    def _():
        o_fan.from_core(1).wait_recv()

    @pl.when(at.y == 1)
    def _():
        o_fan.from_diagonal(1).wait_recv()

    for k in (0, 2, 3, 4):
        o_in(k).start()

    @pl.when(at.s < n_seq - 1)
    def _():
        o_in(1).start()
        o_in(1).wait()

    @pl.when(at.s == n_seq - 1)
    def _():
        o_in(5).start()
        o_in(5).wait()

    for k in (0, 2, 3, 4):
        o_in(k).wait()
    o_out = pltpu.make_async_copy(o_near, out_mine, o_in_sems.at[6])
    o_out.start()
    g_go.arrive()
    g_in().start()
    g_in().wait()
    loop(0, steps, join_back)

    o_out.wait()
    loop(steps - 2, steps, lambda k: p_out(k).wait())
    loop(0, n_seq, lambda i: hid_out(i).wait())
    x_go.sent()
    g_go.sent()

    def w_sent(k):
        w_fan.y(k).wait_send()
        w_fan.core(k).wait_send()
        w_fan.pass_on(k).wait_send()

    loop(0, n_seq, w_sent)

    def seq_sent(hop):
        w_send(hop).wait_send()
        t_send(hop).wait_send()

    loop(1, n_seq, seq_sent)
    for fan in (t_fan, o_fan):
        fan.y(0).wait_send()
        fan.core(0).wait_send()
        fan.pass_on(0).wait_send()

    @pl.when(at.y == 0)
    def _():
        o_send.wait_send()
        o_fan.y(1).wait_send()
        o_fan.core(1).wait_send()

    @pl.when(at.y == 1)
    def _():
        o_fan.pass_on(1).wait_send()


def gather_all(n_dp, n_seq, late, lead, x, g, w, o, tile):
    depth = n_seq // 2
    own, width = o.shape
    block = x.shape[0] * x.shape[1]
    tokens = n_seq * block
    columns = w.shape[2]
    mine = -(-(own * n_dp) // 128) * 128
    bf16, f32 = jnp.bfloat16, jnp.float32
    rest, near = pl.BlockSpec(memory_space=pl.ANY), pl.BlockSpec(memory_space=pltpu.VMEM)
    dma = pltpu.SemaphoreType.DMA
    like = lambda lead, ref: jax.ShapeDtypeStruct(lead + ref.shape, ref.dtype)
    return pl.pallas_call(
        functools.partial(gather_kernel, n_seq=n_seq, late=late, lead=lead),
        in_specs=[rest] * 5,
        out_specs=[rest] * 8 + [near],
        out_shape=[
            like((2, depth), x),
            like((2, depth), g),
            jax.ShapeDtypeStruct((n_dp,) + w.shape, w.dtype),
            jax.ShapeDtypeStruct((n_dp, own + late, width), o.dtype),
            like((n_dp, n_seq), tile),
            jax.ShapeDtypeStruct((2, depth, block, width), bf16),
            jax.ShapeDtypeStruct((mine, width), bf16),
            jax.ShapeDtypeStruct((tokens, columns), f32),
            jax.ShapeDtypeStruct((tokens, mine), bf16),
        ],
        scratch_shapes=[
            pltpu.VMEM(x.shape, bf16),
            pltpu.VMEM((2, depth, block, width), bf16),
            pltpu.VMEM((n_dp,) + w.shape, bf16),
            pltpu.VMEM((2, 2 * block, columns), f32),
            pltpu.VMEM((2, depth) + g.shape, bf16),
            pltpu.VMEM((mine, width), bf16),
            pltpu.VMEM((n_dp, n_seq) + tile.shape, f32),
            pltpu.VMEM((8, width), f32),
            dma((6, depth)), dma((6, depth)), dma((2, n_seq)), dma((6, n_seq)),
            dma((2,)), dma((6, 2)), dma((2, n_seq)), dma((6, 1)), dma((4,)),
            dma((1,)), dma((n_seq,)), dma((4,)), dma((2,)), dma((1,)), dma((7,)),
        ],
        compiler_params=pltpu.CompilerParams(
            collective_id=0, has_side_effects=True, vmem_limit_bytes=56 * 2**20
        ),
        name="gather_all",
    )(x, g, w, o, tile)

def add_rows(out, terms, rows=32):
    count = out.shape[0]

    def some(k):
        at = pl.ds(pl.multiple_of(k * rows, rows), rows)
        total = terms[0][at].astype(jnp.float32)
        for term in terms[1:]:
            total = total + term[at].astype(jnp.float32)
        out[at] = total.astype(out.dtype)

    loop(0, count // rows, some)


def reduce_kernel(
    d_ref, b_ref, in_ref, out_ref, normed_ref, small_ref,
    sums, in_sum, out_sum, out_prev, small_sum,
    own_parts, x_got, z_got, in_own, in_core, in_y, out_own, out_core, out_y,
    small_own, small_core, small_y, small_seq,
    load_sems, x_sems, z_sems, in_core_sems, in_y_sems, in_sems, out_sems, small_sems, local_sem,
    *, n_seq, late, starts, keep,
):
    at = Place(n_seq)
    depth = at.depth
    parts = (d_ref, b_ref)
    main = out_own.shape[1] - late
    body, extra = pl.ds(0, main), pl.ds(main, late)
    y, c, z, x, s = at.y, at.c, at.z, at.x, at.s

    def out_start(y_to, c_to):
        one = jnp.where(y_to == 0, starts[1], starts[3])
        zero = jnp.where(y_to == 0, starts[0], starts[2])
        return pl.multiple_of(jnp.where(c_to == 0, zero, one), 16)

    loads = [
        pltpu.make_async_copy(parts[kind].at[x], own_parts.at[kind], load_sems.at[kind])
        for kind in range(2)
    ]
    for y_to in range(2):
        p_to = 2 * y_to + c
        loads.append(pltpu.make_async_copy(in_ref.at[p_to], in_own.at[y_to], load_sems.at[2 + y_to]))
        loads.append(
            pltpu.make_async_copy(
                out_ref.at[pl.ds(out_start(y_to, c), main)],
                out_own.at[y_to, body],
                load_sems.at[4 + y_to],
            )
        )
    loads.append(
        pltpu.make_async_copy(
            out_ref.at[pl.ds(keep, late)], out_own.at[0, extra], load_sems.at[6]
        )
    )

    def in_to_core(y_to, k):
        return remote(
            in_ref.at[2 * y_to + 1 - c, k], in_core.at[y_to, k],
            in_core_sems.at[0, y_to, k], in_core_sems.at[1, y_to, k], at.to_c,
        )

    def out_to_core(y_to):
        return remote(
            out_ref.at[pl.ds(out_start(y_to, 1 - c), main)], out_core.at[y_to, body],
            out_sems.at[0, y_to], out_sems.at[1, y_to], at.to_c,
        )

    extra_to_core = remote(
        out_ref.at[pl.ds(keep, late)], out_core.at[0, extra],
        out_sems.at[0, 2], out_sems.at[1, 2], at.to_c,
    )

    def to_across(kind, k):
        return remote(
            parts[kind].at[1 - x, k], x_got.at[kind, k],
            x_sems.at[0, kind, k], x_sems.at[1, kind, k], at.to_x,
        )

    def to_depth(kind, k):
        return remote(
            x_got.at[kind, k], z_got.at[kind, z],
            z_sems.at[0, kind, k], z_sems.at[1, kind, z], (at.p, 2 * k + x),
        )

    def from_depth(kind, k):
        here = z_got.at[kind, k]
        return remote(here, here, z_sems.at[0, kind, k], z_sems.at[1, kind, k], (at.p, 2 * k + x))

    def in_to_y(k):
        return remote(
            in_core.at[1 - y, k], in_y.at[k], in_y_sems.at[0, k], in_y_sems.at[1, k], at.to_y
        )

    def in_to_owner(k):
        return remote(
            in_core.at[y, k], in_sum.at[s], in_sems.at[0, k], in_sems.at[1, s], (at.p, k)
        )

    def in_from(k):
        here = in_sum.at[k]
        return remote(here, here, in_sems.at[0, k], in_sems.at[1, k], (at.p, k))

    in_keep = pltpu.make_async_copy(in_core.at[y, s], in_sum.at[s], local_sem.at[0])
    out_to_y = remote(
        out_core.at[1 - y, body], out_y.at[body], out_sems.at[0, 3], out_sems.at[1, 3], at.to_y
    )
    extra_to_y = remote(
        out_core.at[0, extra], out_y.at[extra], out_sems.at[0, 4], out_sems.at[1, 4], at.to_y
    )

    def out_shift(start):
        return remote(
            out_sum.at[pl.ds(start, late)], out_prev,
            out_sems.at[0, 5], out_sems.at[1, 5], (at.p, at.seq(1)),
        )

    small_to_core = remote(small_own, small_core, small_sems.at[0, 0], small_sems.at[1, 0], at.to_c)
    small_to_y = remote(small_core, small_y, small_sems.at[0, 1], small_sems.at[1, 1], at.to_y)

    def small_to(hop):
        to = at.seq(hop)
        return remote(
            small_y, small_seq.at[s], small_sems.at[0, 2 + to], small_sems.at[1, 2 + s], (at.p, to)
        )

    def small_from(hop):
        src = at.seq(-hop)
        here = small_seq.at[src]
        return remote(
            here, here, small_sems.at[0, 2 + src], small_sems.at[1, 2 + src], (at.p, src)
        )

    def around_z(hop):
        return lax.rem(z + hop, depth)

    at.meet()
    for hop in range(1, depth + 1):
        to_across(0, around_z(hop)).start()
    loop(0, n_seq, lambda hop: in_to_core(1 - y, at.seq(hop)).start())
    for load in loads:
        load.start()
    loop(0, n_seq, lambda hop: in_to_core(y, at.seq(hop)).start())
    out_to_core(1 - y).start()
    out_to_core(y).start()
    extra_to_core.start()
    for hop in range(1, depth + 1):
        to_across(1, around_z(hop)).start()
    for load in loads:
        load.wait()

    def to_y_step(hop):
        k = at.seq(hop)
        in_to_core(1 - y, k).wait_recv()
        add_rows(in_core.at[1 - y, k], [in_core.at[1 - y, k], in_own.at[1 - y, k]])
        in_to_y(k).start()

    loop(0, n_seq, to_y_step)
    out_to_core(1 - y).wait_recv()
    extra_to_core.wait_recv()
    add_rows(out_core.at[1 - y, body], [out_core.at[1 - y, body], out_own.at[1 - y, body]])
    out_to_y.start()

    @pl.when(y == 1)
    def _():
        add_rows(out_core.at[0, extra], [out_core.at[0, extra], out_own.at[0, extra]])
        extra_to_y.start()

    def depth_step(kind, hop):
        k = around_z(hop)
        to_across(kind, k).wait_recv()
        add_rows(x_got.at[kind, k], [x_got.at[kind, k], own_parts.at[kind, k]])
        if hop < depth:
            to_depth(kind, k).start()

    def owner_step(hop):
        k = at.seq(hop)
        in_to_core(y, k).wait_recv()
        in_to_y(k).wait_recv()
        add_rows(in_core.at[y, k], [in_core.at[y, k], in_own.at[y, k], in_y.at[k]])

        @pl.when(k != s)
        def _():
            in_to_owner(k).start()

        @pl.when(k == s)
        def _():
            in_keep.start()

    for hop in range(1, depth + 1):
        depth_step(0, hop)
        for one in range(n_seq // depth):
            owner_step((hop - 1) * (n_seq // depth) + one + 1)

    def finish(kind):
        others = [around_z(hop) for hop in range(1, depth)]
        for k in others:
            from_depth(kind, k).wait_recv()
        add_rows(
            sums.at[kind], [x_got.at[kind, z]] + [z_got.at[kind, k] for k in others], rows=16
        )

    depth_step(1, 1)
    finish(0)

    small_own[...] = small_ref[...]
    d_hidden = sums[0]
    small_own[0:1, :] = jnp.sum(d_hidden * normed_ref[...], axis=0, keepdims=True)
    small_own[1:2, :] = jnp.sum(d_hidden, axis=0, keepdims=True)
    small_to_core.start()
    depth_step(1, 2)
    small_to_core.wait_recv()
    small_core[...] = small_core[...] + small_own[...]
    small_to_y.start()
    out_to_core(y).wait_recv()
    out_to_y.wait_recv()
    add_rows(out_sum.at[body], [out_core.at[y, body], out_own.at[y, body], out_y.at[body]])

    @pl.when(y == 0)
    def _():
        extra_to_y.wait_recv()
        add_rows(out_sum.at[extra], [out_core.at[0, extra], out_own.at[0, extra], out_y.at[extra]])

        @pl.when(c == 0)
        def _():
            out_shift(keep).start()

        @pl.when((c == 1) & (s == n_seq - 1))
        def _():
            out_shift(main).start()

        @pl.when((c == 1) & (s < n_seq - 1))
        def _():
            out_shift(starts[2] - starts[1] - late).start()

    depth_step(1, 3)
    small_to_y.wait()
    small_y[...] = small_core[...] + small_y[...]
    loop(1, n_seq, lambda hop: small_to(hop).start())
    for hop in range(4, depth + 1):
        depth_step(1, hop)
    small_sum[...] = small_y[...]

    def small_add(hop):
        small_from(hop).wait_recv()
        small_sum[...] = small_sum[...] + small_seq[at.seq(-hop)]

    loop(1, n_seq, small_add)
    finish(1)

    @pl.when(y == 0)
    def _():
        out_shift(0).wait()

    def in_last(hop):
        k = at.seq(hop)
        in_from(k).wait_recv()
        in_to_owner(k).wait_send()

    loop(1, n_seq, in_last)
    in_keep.wait()

    def seq_sent(k):
        for y_to in range(2):
            in_to_core(y_to, k).wait_send()
        in_to_y(k).wait_send()

    loop(0, n_seq, seq_sent)
    loop(1, n_seq, lambda hop: small_to(hop).wait_send())
    small_to_core.wait_send()
    for y_to in range(2):
        out_to_core(y_to).wait_send()
    extra_to_core.wait_send()
    out_to_y.wait_send()

    @pl.when(y == 1)
    def _():
        extra_to_y.wait_send()

    for kind in range(2):
        for k in range(depth):
            to_across(kind, k).wait_send()
        for hop in range(1, depth):
            to_depth(kind, around_z(hop)).wait_send()


def reduce_all(n_dp, n_seq, late, starts, keep, d_part, b_part, in_part, out_part, normed, small):
    depth = n_seq // 2
    block = d_part.shape[2:]
    in_block = in_part.shape[2:]
    width = block[1]
    main = starts[1] - starts[0]
    slot = main + late
    bf16, f32 = jnp.bfloat16, jnp.float32
    rest, near = pl.BlockSpec(memory_space=pl.ANY), pl.BlockSpec(memory_space=pltpu.VMEM)
    dma = pltpu.SemaphoreType.DMA
    return pl.pallas_call(
        functools.partial(reduce_kernel, n_seq=n_seq, late=late, starts=starts, keep=keep),
        in_specs=[rest, rest, rest, rest, near, near],
        out_specs=[near, rest, near, rest, near],
        out_shape=[
            jax.ShapeDtypeStruct((2,) + block, f32),
            jax.ShapeDtypeStruct((n_seq,) + in_block, bf16),
            jax.ShapeDtypeStruct((slot, width), bf16),
            jax.ShapeDtypeStruct((late, width), bf16),
            jax.ShapeDtypeStruct(small.shape, f32),
        ],
        scratch_shapes=[
            pltpu.VMEM((2, depth) + block, bf16),
            pltpu.VMEM((2, depth) + block, bf16),
            pltpu.VMEM((2, depth) + block, bf16),
            pltpu.VMEM((2, n_seq) + in_block, bf16),
            pltpu.VMEM((2, n_seq) + in_block, bf16),
            pltpu.VMEM((n_seq,) + in_block, bf16),
            pltpu.VMEM((2, slot, width), bf16),
            pltpu.VMEM((2, slot, width), bf16),
            pltpu.VMEM((slot, width), bf16),
            pltpu.VMEM(small.shape, f32),
            pltpu.VMEM(small.shape, f32),
            pltpu.VMEM(small.shape, f32),
            pltpu.VMEM((n_seq,) + small.shape, f32),
            dma((7,)), dma((2, 2, depth)), dma((2, 2, depth)), dma((2, 2, n_seq)), dma((2, n_seq)),
            dma((2, n_seq)), dma((2, 6)), dma((2, 2 + n_seq)), dma((1,)),
        ],
        compiler_params=pltpu.CompilerParams(
            collective_id=1, has_side_effects=True, vmem_limit_bytes=56 * 2**20
        ),
        name="reduce_all",
    )(d_part, b_part, in_part, out_part, normed, small)

def split_heads(
    n_dp, n_seq, tokens, cotangent, segment_ids, doc_positions,
    in_weight, in_first, in_second, in_average,
    out_weight, out_first, out_second, out_average,
    small_params, small_first, small_second, small_average,
):
    bf16, f32 = jnp.bfloat16, jnp.float32
    rows, own_tokens, width = tokens.shape
    row_tokens = own_tokens * n_seq
    all_tokens = rows * row_tokens
    head_size = width // HEADS
    ffn = (in_weight.shape[1] - 3 * width) // 2
    in_rows, own = in_weight.shape[0], out_weight.shape[0]
    dp_rows = own * n_seq
    att = width // n_seq
    late = width - dp_rows
    act = [(dp_rows - late) // n_seq, own, own]
    act_all = sum(act)
    cuts = [0, act[0] * n_seq, (act[0] + own) * n_seq, ffn]
    lead = att - own
    p, s = lax.axis_index("dp"), lax.axis_index("seq")

    def share(v):
        parts = [v[:, i * width : (i + 1) * width].reshape(-1, n_seq, att) for i in range(3)]
        for half in range(2):
            base = 3 * width + half * ffn
            for i in range(3):
                parts.append(v[:, base + cuts[i] : base + cuts[i + 1]].reshape(-1, n_seq, act[i]))
        return jnp.transpose(jnp.concatenate(parts, axis=2), (1, 0, 2))

    def unshare(v):
        v = jnp.transpose(v, (1, 0, 2))
        sizes = [att] * 3 + act * 2
        parts, at = [], 0
        for size in sizes:
            parts.append(v[:, :, at : at + size].reshape(v.shape[0], n_seq * size))
            at += size
        return jnp.concatenate(parts, axis=1)

    out_low = out_weight.astype(bf16)
    small_low = small_params.astype(bf16).astype(f32).T
    widen = lambda v, n: jnp.pad(v, ((0, n - v.shape[0]), (0, 128 - v.shape[1])))
    tile = jnp.concatenate(
        [
            widen(small_low, 8),
            widen(jnp.concatenate([segment_ids, doc_positions], axis=0).astype(f32), 8),
        ],
        axis=0,
    )
    odd = jnp.concatenate([jnp.zeros_like(tile[:8, :in_rows]), tile[:8, :in_rows]], axis=1)
    tile = jnp.concatenate([jnp.where(s % 2 == 1, odd, tile[:8]), tile[8:]], axis=0)
    _, g_full, in_low, _, tiles, hidden, out_mine, proj, d_joined = gather_all(
        n_dp, n_seq, late, lead, tokens, cotangent, share(in_weight.astype(bf16)), out_low, tile
    )
    g_full, hidden = g_full.reshape(all_tokens, width), hidden.reshape(all_tokens, width)
    in_low = in_low.reshape(n_dp * n_seq * in_rows, 3 * att + 2 * act_all)

    pairs = tiles[:, :, :5].reshape(n_dp, n_seq // 2, 2, 5, 2 * in_rows).sum(axis=2)
    small_low = jnp.transpose(pairs, (2, 0, 1, 3)).reshape(5, width)
    gain = small_low[0]
    bias = lax.dynamic_slice_in_dim(small_low[2:5], s * att, att, 1).reshape(1, 3 * att)
    docs = lax.dynamic_index_in_dim(tiles, p, 0, keepdims=False)[:, 8:, :own_tokens]
    seg_full = jnp.transpose(docs[:, :rows], (1, 0, 2)).reshape(rows, row_tokens)
    pos_full = jnp.transpose(docs[:, rows : 2 * rows], (1, 0, 2)).reshape(rows, row_tokens)
    last = s == n_seq - 1
    keep = att - late

    def normalise(v):
        v = v.astype(f32)
        centered = v - jnp.mean(v, axis=-1, keepdims=True)
        inv_std = lax.rsqrt(jnp.mean(centered * centered, axis=-1, keepdims=True) + norm_eps)
        return centered * inv_std, inv_std

    half_rot = ROT // 2
    inv_freq = rope_base ** (-2.0 * jnp.arange(half_rot, dtype=f32) / ROT)
    angles = pos_full[:, None, :] * inv_freq[:, None]
    cos, sin = jnp.cos(angles), jnp.sin(angles)
    one, zero = jnp.ones((rows, head_size - ROT, row_tokens), f32), jnp.zeros_like(cos)
    rest = 0.0 * one
    rope = jnp.stack(
        [
            jnp.concatenate([cos, cos, one] * 2, axis=1),
            jnp.concatenate([-sin, zero, rest] * 2, axis=1),
            jnp.concatenate([zero, sin, rest] * 2, axis=1),
        ],
        axis=1,
    )
    joined, d_proj, bias_part = middle(
        proj, bias, d_joined, rope, seg_full, n_seq, att, act_all, head_size
    )

    blocks = lambda v: v.reshape(2, n_seq // 2, rows * own_tokens, width)
    branch = jnp.dot(joined, out_mine, preferred_element_type=f32).astype(bf16)
    d_hidden = lax.dot_general(
        d_proj, in_low, (((1,), (1,)), ((), ())), preferred_element_type=f32
    ).astype(bf16)
    out_part = lax.dot_general(
        joined, g_full, (((0,), (0,)), ((), ())), preferred_element_type=f32
    ).astype(bf16)
    in_part = lax.dot_general(
        hidden, d_proj, (((0,), (0,)), ((), ())), preferred_element_type=f32
    ).astype(bf16)
    normed, inv_std = normalise(tokens.reshape(rows * own_tokens, width))
    small_part = lax.dynamic_update_slice(jnp.zeros((8, width), f32), bias_part[:3], (2, s * att))
    starts = (0, att, att + act[0], att + act[0] + own)
    sums, in_sum, out_sum, from_prev, small_sum = reduce_all(
        n_dp, n_seq, late, starts, keep,
        blocks(d_hidden), blocks(branch),
        in_part.reshape(n_dp, n_seq, in_rows, -1), out_part, normed, small_part,
    )
    d_hidden, branch = sums[0], sums[1]

    output = (tokens.astype(f32) + branch.reshape(tokens.shape)).astype(bf16)
    d_normed = d_hidden * gain
    input_grad = cotangent.astype(f32) + (
        inv_std
        * (
            d_normed
            - jnp.mean(d_normed, axis=-1, keepdims=True)
            - normed * jnp.mean(d_normed * normed, axis=-1, keepdims=True)
        )
    ).reshape(tokens.shape)
    small_grad = lax.dynamic_slice(small_sum, (0, (p * n_seq + s) * in_rows), (8, in_rows))[:5].T

    count = jnp.where(p == 0, lead * s, jnp.where(p == 1, late - lead * s, 0))
    out_grad = lax.dynamic_slice_in_dim(
        jnp.concatenate([from_prev, out_sum[:own]], axis=0), late - count, own, 0
    ).astype(f32)
    in_grad = unshare(in_sum).astype(f32)

    in_new = adam_update(
        in_weight, in_first, in_second, in_average, in_grad, matrix_rate, weight_decay
    )
    out_new = adam_update(
        out_weight, out_first, out_second, out_average, out_grad, matrix_rate, weight_decay
    )
    small_new = adam_update(
        small_params, small_first, small_second, small_average, small_grad, small_rate, 0.0
    )
    return (output, input_grad, *in_new, *out_new, *small_new, small_grad, in_grad, out_grad)


def solution(mesh):
    n_dp, n_seq = mesh.shape["dp"], mesh.shape["seq"]

    def choose(*operands):
        own_rows = operands[8].shape[0]
        model_width = operands[0].shape[2]
        if heads_fit(n_dp, n_seq, own_rows, model_width, operands[4].shape[1]):
            return split_heads(n_dp, n_seq, *operands)
        return per_device(*operands)

    return jax.shard_map(
        choose,
        mesh=mesh,
        in_specs=(
            P("dp", "seq", None),
            P("dp", "seq", None),
            P("dp", "seq"),
            P("dp", "seq"),
            P(("dp", "seq"), None),
            P(("dp", "seq"), None),
            P(("dp", "seq"), None),
            P(("dp", "seq"), None),
            P(("dp", "seq"), None),
            P(("dp", "seq"), None),
            P(("dp", "seq"), None),
            P(("dp", "seq"), None),
            P(("dp", "seq"), None),
            P(("dp", "seq"), None),
            P(("dp", "seq"), None),
            P(("dp", "seq"), None),
        ),
        out_specs=(
            P("dp", "seq", None),
            P("dp", "seq", None),
            P(("dp", "seq"), None),
            P(("dp", "seq"), None),
            P(("dp", "seq"), None),
            P(("dp", "seq"), None),
            P(("dp", "seq"), None),
            P(("dp", "seq"), None),
            P(("dp", "seq"), None),
            P(("dp", "seq"), None),
            P(("dp", "seq"), None),
            P(("dp", "seq"), None),
            P(("dp", "seq"), None),
            P(("dp", "seq"), None),
        ),
        check_vma=False,
    )
```

```python
import functools

import jax
import jax.numpy as jnp
from jax import lax
from jax.experimental import pallas as pl
from jax.experimental.pallas import tpu as pltpu
from jax.sharding import PartitionSpec as P

HEADS = 32
ROT = 16
STEP = 2


beta_one = 0.9
adam_eps = 1e-08
matrix_rate = 0.001
small_rate = 0.01
weight_decay = 0.1
norm_eps = 1e-05
rope_base = 10000.0
neg_large = -1e30


def rope_tables(positions, rot_dims):
    half_rot = rot_dims // 2
    inv_freq = rope_base ** (-2.0 * jnp.arange(half_rot, dtype=jnp.float32) / rot_dims)
    angles = positions.astype(jnp.float32)[..., None] * inv_freq
    return (jnp.cos(angles)[..., None, :], jnp.sin(angles)[..., None, :])


def apply_rope(field_in, cosine_tab, sine_tab, rot_dims):
    half_rot = rot_dims // 2
    low_half = field_in[..., :half_rot]
    high_half = field_in[..., half_rot:rot_dims]
    return jnp.concatenate(
        [
            low_half * cosine_tab - high_half * sine_tab,
            high_half * cosine_tab + low_half * sine_tab,
            field_in[..., rot_dims:],
        ],
        axis=-1,
    )


def undo_rope(grad_in, cosine_tab, sine_tab, rot_dims):
    half_rot = rot_dims // 2
    low_half = grad_in[..., :half_rot]
    high_half = grad_in[..., half_rot:rot_dims]
    return jnp.concatenate(
        [
            low_half * cosine_tab + high_half * sine_tab,
            high_half * cosine_tab - low_half * sine_tab,
            grad_in[..., rot_dims:],
        ],
        axis=-1,
    )


def visible(query_seg, key_seg, query_pos, key_pos):
    same_doc = query_seg[:, :, None] == key_seg[:, None, :]
    causal = key_pos[None, :] <= query_pos[:, None]
    return (same_doc & causal[None])[:, None]


def to_tokens(head_major):
    return jnp.transpose(head_major, (0, 2, 1, 3))


def adam_update(weight, first, second, average, gradient, rate, decay_rate):
    beta_two = 1.0 - STEP ** (-0.8)
    average_keep = min(0.999, (1.0 + STEP) / (10.0 + STEP))
    first_new = beta_one * first + (1.0 - beta_one) * gradient
    second_new = beta_two * second + (1.0 - beta_two) * gradient * gradient
    moment_hat = beta_one * first_new / (1.0 - beta_one ** (STEP + 1)) + (
        1.0 - beta_one
    ) * gradient / (1.0 - beta_one**STEP)
    weight_new = weight - rate * (
        moment_hat / (jnp.sqrt(second_new) + adam_eps) + decay_rate * weight
    )
    average_new = average_keep * average + (1.0 - average_keep) * weight_new
    return (weight_new, second_new, average_new)


def per_device(
    tokens,
    cotangent,
    segment_ids,
    doc_positions,
    in_weight,
    in_first,
    in_second,
    in_average,
    out_weight,
    out_first,
    out_second,
    out_average,
    small_params,
    small_first,
    small_second,
    small_average,
):
    rows_here, row_tokens, model_width = tokens.shape
    head_count = HEADS
    head_size = model_width // head_count
    score_scale = head_size ** (-0.5)
    all_tokens = rows_here * row_tokens
    wide_in = in_weight.shape[1]
    ffn_width = (wide_in - 3 * model_width) // 2
    shape_heads = (rows_here, row_tokens, head_count, head_size)
    own_places = lax.axis_index("seq") * row_tokens + jnp.arange(row_tokens)
    flat_in = tokens.astype(jnp.float32).reshape(all_tokens, model_width)
    centered = flat_in - jnp.mean(flat_in, axis=-1, keepdims=True)
    inv_std = lax.rsqrt(jnp.mean(centered * centered, axis=-1, keepdims=True) + norm_eps)
    normed = centered * inv_std
    in_low = in_weight.astype(jnp.bfloat16)
    out_low = out_weight.astype(jnp.bfloat16)
    small_low = small_params.astype(jnp.bfloat16)
    w_piece = lax.all_gather(in_low, ("dp", "seq"), axis=0, tiled=True)
    s_piece = lax.all_gather(small_low, ("dp", "seq"), axis=0, tiled=True)
    columns = normed
    s_float = s_piece.astype(jnp.float32)
    h_piece = (columns * s_float[:, 0] + s_float[:, 1]).astype(jnp.bfloat16)
    proj_acc = jnp.dot(h_piece, w_piece, preferred_element_type=jnp.float32)
    norm_gain = s_float[:, 0]
    qkv_bias = s_float[:, 2:5].T.reshape(3 * model_width)
    qkv_full = proj_acc[:, : 3 * model_width] + qkv_bias
    gate_pre = proj_acc[:, 3 * model_width : 3 * model_width + ffn_width]
    up_pre = proj_acc[:, 3 * model_width + ffn_width :]
    cosine_tab, sine_tab = rope_tables(doc_positions, ROT)
    query_low = apply_rope(
        qkv_full[:, :model_width].reshape(shape_heads), cosine_tab, sine_tab, ROT
    ).astype(jnp.bfloat16)
    key_low = apply_rope(
        qkv_full[:, model_width : 2 * model_width].reshape(shape_heads), cosine_tab, sine_tab, ROT
    ).astype(jnp.bfloat16)
    value_low = qkv_full[:, 2 * model_width :].reshape(shape_heads).astype(jnp.bfloat16)
    seg_low = segment_ids.astype(jnp.bfloat16)
    seg_own = segment_ids.astype(jnp.float32)
    key_flat = key_low.reshape(rows_here, row_tokens, model_width)
    value_flat = value_low.reshape(rows_here, row_tokens, model_width)
    attend_init = (
        jnp.full((rows_here, head_count, row_tokens), neg_large, jnp.float32),
        jnp.zeros((rows_here, head_count, row_tokens), jnp.float32),
        jnp.zeros((rows_here, head_count, row_tokens, head_size), jnp.float32),
    )
    key_piece = lax.all_gather(key_flat, "seq", axis=1, tiled=True)
    value_piece = lax.all_gather(value_flat, "seq", axis=1, tiled=True)
    seg_piece = lax.all_gather(seg_low, "seq", axis=1, tiled=True)
    turn_count = key_piece.shape[1] // row_tokens

    def attend_one_turn(turn_index, inner_state):
        offset = turn_index * row_tokens
        key_blk = lax.dynamic_slice_in_dim(key_piece, offset, row_tokens, 1).reshape(shape_heads)
        value_blk = lax.dynamic_slice_in_dim(value_piece, offset, row_tokens, 1).reshape(
            shape_heads
        )
        seg_blk = lax.dynamic_slice_in_dim(seg_piece, offset, row_tokens, 1).astype(jnp.float32)
        key_mask = visible(seg_own, seg_blk, own_places, offset + jnp.arange(row_tokens))
        running_top, running_sum, weighted = inner_state
        scores = (
            jnp.einsum("rqhe,rkhe->rhqk", query_low, key_blk, preferred_element_type=jnp.float32)
            * score_scale
        )
        scores = jnp.where(key_mask, scores, neg_large)
        new_top = jnp.maximum(running_top, jnp.max(scores, axis=-1))
        weights = jnp.where(key_mask, jnp.exp(scores - new_top[..., None]), 0.0)
        factor = jnp.exp(running_top - new_top)
        running_sum = running_sum * factor + jnp.sum(weights, axis=-1)
        weighted = weighted * factor[..., None] + jnp.einsum(
            "rhqk,rkhe->rhqe",
            weights.astype(jnp.bfloat16),
            value_blk,
            preferred_element_type=jnp.float32,
        )
        return (new_top, running_sum, weighted)

    running_top, running_sum, weighted = lax.fori_loop(0, turn_count, attend_one_turn, attend_init)
    attended = weighted / running_sum[..., None]
    log_total = running_top + jnp.log(running_sum)
    attended_low = to_tokens(attended).reshape(all_tokens, model_width).astype(jnp.bfloat16)
    gate_sig = jax.nn.sigmoid(gate_pre)
    activated = gate_pre * gate_sig * up_pre
    joined = jnp.concatenate([attended_low, activated.astype(jnp.bfloat16)], axis=1)
    columns = joined
    branch_sum = jnp.dot(
        columns,
        lax.all_gather(out_low, ("dp", "seq"), axis=0, tiled=True),
        preferred_element_type=jnp.float32,
    )
    output = (flat_in + branch_sum).astype(jnp.bfloat16).reshape(rows_here, row_tokens, model_width)
    grad_out = cotangent.reshape(all_tokens, model_width)
    d_joined = lax.dot_general(
        grad_out,
        lax.all_gather(out_low, ("dp", "seq"), axis=0, tiled=True),
        (((1,), (1,)), ((), ())),
        preferred_element_type=jnp.float32,
    )
    d_joined = d_joined.astype(jnp.bfloat16)
    columns = joined
    out_grad = lax.psum_scatter(
        lax.dot_general(
            columns, grad_out, (((0,), (0,)), ((), ())), preferred_element_type=jnp.float32
        ),
        ("dp", "seq"),
        scatter_dimension=0,
        tiled=True,
    )
    d_attended = d_joined[:, :model_width].reshape(shape_heads)
    d_act = d_joined[:, model_width:].astype(jnp.float32)
    d_gate = d_act * up_pre * gate_sig * (1.0 + gate_pre * (1.0 - gate_sig))
    d_up = d_act * gate_pre * gate_sig
    out_dot = jnp.einsum("rqhe,rhqe->rhq", d_attended.astype(jnp.float32), attended)
    grad_zero = jnp.zeros((rows_here, head_count, row_tokens, head_size), jnp.float32)
    query_key_piece = lax.all_gather(key_flat, "seq", axis=1, tiled=True)
    query_value_piece = lax.all_gather(value_flat, "seq", axis=1, tiled=True)
    query_seg_piece = lax.all_gather(seg_low, "seq", axis=1, tiled=True)
    turn_count = query_key_piece.shape[1] // row_tokens

    def query_one_turn(turn_index, inner_state):
        offset = turn_index * row_tokens
        key_blk = lax.dynamic_slice_in_dim(query_key_piece, offset, row_tokens, 1).reshape(
            shape_heads
        )
        value_blk = lax.dynamic_slice_in_dim(query_value_piece, offset, row_tokens, 1).reshape(
            shape_heads
        )
        seg_blk = lax.dynamic_slice_in_dim(query_seg_piece, offset, row_tokens, 1).astype(
            jnp.float32
        )
        key_mask = visible(seg_own, seg_blk, own_places, offset + jnp.arange(row_tokens))
        scores = (
            jnp.einsum("rqhe,rkhe->rhqk", query_low, key_blk, preferred_element_type=jnp.float32)
            * score_scale
        )
        weights = jnp.where(key_mask, jnp.exp(scores - log_total[..., None]), 0.0)
        d_prob = jnp.einsum(
            "rqhe,rkhe->rhqk", d_attended, value_blk, preferred_element_type=jnp.float32
        )
        d_score = (weights * (d_prob - out_dot[..., None])).astype(jnp.bfloat16)
        return (
            inner_state
            + jnp.einsum("rhqk,rkhe->rhqe", d_score, key_blk, preferred_element_type=jnp.float32)
            * score_scale
        )

    d_query = lax.fori_loop(0, turn_count, query_one_turn, grad_zero)
    row_stats = jnp.concatenate(
        [jnp.transpose(log_total, (0, 2, 1)), jnp.transpose(out_dot, (0, 2, 1))], axis=2
    )
    stat_high = row_stats.astype(jnp.bfloat16)
    stat_low = (row_stats - stat_high.astype(jnp.float32)).astype(jnp.bfloat16)
    query_flat = query_low.reshape(rows_here, row_tokens, model_width)
    d_att_flat = d_attended.reshape(rows_here, row_tokens, model_width)
    query_piece = lax.all_gather(query_flat, "seq", axis=1, tiled=True)
    dout_piece = lax.all_gather(d_att_flat, "seq", axis=1, tiled=True)
    high_piece = lax.all_gather(stat_high, "seq", axis=1, tiled=True)
    low_piece = lax.all_gather(stat_low, "seq", axis=1, tiled=True)
    key_seg_piece = lax.all_gather(seg_low, "seq", axis=1, tiled=True)
    turn_count = query_piece.shape[1] // row_tokens

    def key_one_turn(turn_index, inner_state):
        offset = turn_index * row_tokens
        query_blk = lax.dynamic_slice_in_dim(query_piece, offset, row_tokens, 1).reshape(
            shape_heads
        )
        dout_blk = lax.dynamic_slice_in_dim(dout_piece, offset, row_tokens, 1).reshape(shape_heads)
        stat_blk = lax.dynamic_slice_in_dim(high_piece, offset, row_tokens, 1).astype(
            jnp.float32
        ) + lax.dynamic_slice_in_dim(low_piece, offset, row_tokens, 1).astype(jnp.float32)
        lse_blk = jnp.transpose(stat_blk[..., :head_count], (0, 2, 1))
        dot_blk = jnp.transpose(stat_blk[..., head_count:], (0, 2, 1))
        seg_blk = lax.dynamic_slice_in_dim(key_seg_piece, offset, row_tokens, 1).astype(jnp.float32)
        key_mask = visible(seg_blk, seg_own, offset + jnp.arange(row_tokens), own_places)
        d_key, d_value = inner_state
        scores = (
            jnp.einsum("rqhe,rkhe->rhqk", query_blk, key_low, preferred_element_type=jnp.float32)
            * score_scale
        )
        weights = jnp.where(key_mask, jnp.exp(scores - lse_blk[..., None]), 0.0)
        d_value = d_value + jnp.einsum(
            "rhqk,rqhe->rhke",
            weights.astype(jnp.bfloat16),
            dout_blk,
            preferred_element_type=jnp.float32,
        )
        d_prob = jnp.einsum(
            "rqhe,rkhe->rhqk", dout_blk, value_low, preferred_element_type=jnp.float32
        )
        d_score = (weights * (d_prob - dot_blk[..., None])).astype(jnp.bfloat16)
        d_key = (
            d_key
            + jnp.einsum("rhqk,rqhe->rhke", d_score, query_blk, preferred_element_type=jnp.float32)
            * score_scale
        )
        return (d_key, d_value)

    d_key, d_value = lax.fori_loop(0, turn_count, key_one_turn, (grad_zero, grad_zero))
    d_query_tok = undo_rope(to_tokens(d_query), cosine_tab, sine_tab, ROT).reshape(
        all_tokens, model_width
    )
    d_key_tok = undo_rope(to_tokens(d_key), cosine_tab, sine_tab, ROT).reshape(
        all_tokens, model_width
    )
    d_value_tok = to_tokens(d_value).reshape(all_tokens, model_width)
    d_proj = jnp.concatenate([d_query_tok, d_key_tok, d_value_tok, d_gate, d_up], axis=1).astype(
        jnp.bfloat16
    )
    d_hidden = lax.dot_general(
        d_proj,
        lax.all_gather(in_low, ("dp", "seq"), axis=0, tiled=True),
        (((1,), (1,)), ((), ())),
        preferred_element_type=jnp.float32,
    )
    columns = h_piece
    in_grad = lax.psum_scatter(
        lax.dot_general(
            columns, d_proj, (((0,), (0,)), ((), ())), preferred_element_type=jnp.float32
        ),
        ("dp", "seq"),
        scatter_dimension=0,
        tiled=True,
    )
    gain_grad = jnp.sum(d_hidden * normed, axis=0)
    shift_grad = jnp.sum(d_hidden, axis=0)
    bias_grad = (
        jnp.sum(d_proj[:, : 3 * model_width].astype(jnp.float32), axis=0).reshape(3, model_width).T
    )
    small_term = jnp.concatenate([gain_grad[:, None], shift_grad[:, None], bias_grad], axis=1)
    small_grad = lax.psum_scatter(small_term, ("dp", "seq"), scatter_dimension=0, tiled=True)
    d_normed = d_hidden * norm_gain
    input_grad = grad_out.astype(jnp.float32) + inv_std * (
        d_normed
        - jnp.mean(d_normed, axis=-1, keepdims=True)
        - normed * jnp.mean(d_normed * normed, axis=-1, keepdims=True)
    )
    input_grad = input_grad.reshape(rows_here, row_tokens, model_width)
    in_new = adam_update(
        in_weight, in_first, in_second, in_average, in_grad, matrix_rate, weight_decay
    )
    out_new = adam_update(
        out_weight, out_first, out_second, out_average, out_grad, matrix_rate, weight_decay
    )
    small_new = adam_update(
        small_params, small_first, small_second, small_average, small_grad, small_rate, 0.0
    )
    return (
        output,
        input_grad,
        in_new[0],
        in_new[1],
        in_new[2],
        out_new[0],
        out_new[1],
        out_new[2],
        small_new[0],
        small_new[1],
        small_new[2],
        small_grad,
        in_grad,
        out_grad,
    )


def heads_fit(n_dp, n_seq, own_rows, model_width, wide_in):
    dp_rows = own_rows * n_seq
    if n_dp != 4 or HEADS % (2 * n_seq) or not dp_rows < model_width < 2 * dp_rows:
        return False
    att_rows = model_width // n_seq
    late_att = model_width - dp_rows
    first_act = dp_rows - late_att
    if first_act % n_seq:
        return False
    lead = att_rows - own_rows
    return (
        wide_in - 3 * model_width == 2 * (n_dp * dp_rows - model_width)
        and lead == own_rows - first_act // n_seq
        and lead * n_seq == late_att
        and lead % 16 == 0
    )


def middle_kernel(
    q_ref, k_ref, v_ref, bq_ref, bk_ref, bv_ref, da_ref, act_ref, d_act_ref, rope_ref,
    seg_q_ref, seg_k_ref,
    joined_ref, d_proj_ref, bias_ref,
    *, head_size, half_rot, att_rows, act,
):
    row, pair = pl.program_id(0), pl.program_id(1)
    lanes = 2 * head_size
    half = act_ref.shape[3]
    act_rows = sum(act)
    bf16, f32 = jnp.bfloat16, jnp.float32

    def feed_forward(step):
        x, z = lax.rem(step, 2), step // 2
        raw = act_ref[x, z, 0]
        gate = raw[:, 3 * att_rows : 3 * att_rows + act_rows]
        up = raw[:, 3 * att_rows + act_rows :]
        joint = d_act_ref[x, z, 0]
        d_act = jnp.concatenate(
            [joint[:, (i + 1) * att_rows :][:, :some] for i, some in enumerate(act)], axis=1
        ).astype(f32)
        sig = 1.0 / (1.0 + jnp.exp(-gate))
        silu = gate * sig
        rows = pl.ds(pl.multiple_of(pair * half, half), half)
        active, parts, first = silu * up, [], 0
        for some in act:
            parts.append(active[:, first : first + some])
            parts.append(jnp.zeros((half, att_rows - some), f32))
            first += some
        joined_ref[x, z, row, rows, att_rows:] = jnp.concatenate(parts, axis=1).astype(bf16)
        d_gate = d_act * up * sig * (1.0 + gate * (1.0 - sig))
        d_proj_ref[x, z, row, rows, 3 * att_rows :] = jnp.concatenate(
            [d_gate, d_act * silu], axis=1
        ).astype(bf16)

    loop(0, act_ref.shape[0] * act_ref.shape[1], feed_forward)

    def whole(v):
        across, depth = v.shape[:2]
        parts = [v[x, z].reshape(v.shape[-2:]) for z in range(depth) for x in range(across)]
        return jnp.concatenate(parts, axis=0)

    def store(ref, first, v):
        across, depth, _, some, _ = ref.shape
        columns = pl.ds(pl.multiple_of(first + pair * lanes, lanes), lanes)
        for z in range(depth):
            for x in range(across):
                at = (z * across + x) * some
                ref[x, z, row, :, columns] = v[at : at + some]

    cos, sin_low, sin_high = (rope_ref[0, i].T for i in range(3))
    tokens = cos.shape[0]
    scale = head_size ** (-0.5)

    def turn(v, way):
        return (
            v * cos
            + way * pltpu.roll(v, lanes - half_rot, 1) * sin_low
            + way * pltpu.roll(v, half_rot, 1) * sin_high
        )

    query = (turn(whole(q_ref[...]) + bq_ref[...], 1.0)).astype(bf16) * scale
    query = query.astype(bf16)
    key = turn(whole(k_ref[...]) + bk_ref[...], 1.0).astype(bf16)
    value = (whole(v_ref[...]) + bv_ref[...]).astype(bf16)
    d_att = whole(da_ref[...])
    place_q = lax.broadcasted_iota(jnp.int32, (tokens, tokens), 0)
    place_k = lax.broadcasted_iota(jnp.int32, (tokens, tokens), 1)
    mask = (seg_q_ref[0] == seg_k_ref[0]) & (place_k <= place_q)
    lane = lax.broadcasted_iota(jnp.int32, (tokens, lanes), 1)
    nt = (((1,), (1,)), ((), ()))
    tn = (((0,), (0,)), ((), ()))
    dot = functools.partial(lax.dot_general, preferred_element_type=f32)
    att = jnp.zeros((tokens, lanes), f32)
    d_query = jnp.zeros((tokens, lanes), f32)
    d_key = jnp.zeros((tokens, lanes), f32)
    d_value = jnp.zeros((tokens, lanes), f32)
    for head in range(lanes // head_size):
        mine = (lane >= head * head_size) & (lane < (head + 1) * head_size)
        q_h = jnp.where(mine, query, jnp.zeros_like(query))
        da_h = jnp.where(mine, d_att, jnp.zeros_like(d_att))
        scores = jnp.where(mask, dot(q_h, key, nt), neg_large)
        top = jnp.max(scores, axis=1, keepdims=True)
        weights = jnp.exp(scores - top)
        probs = weights * (1.0 / jnp.sum(weights, axis=1, keepdims=True))
        probs_low = probs.astype(bf16)
        att_h = jnp.where(mine, dot(probs_low, value, (((1,), (0,)), ((), ()))), 0.0)
        out_dot = jnp.sum(att_h * d_att.astype(f32), axis=1, keepdims=True)
        d_prob = dot(da_h, value, nt)
        d_score = (probs * (d_prob - out_dot)).astype(bf16)
        att = att + att_h
        d_query = d_query + jnp.where(mine, dot(d_score, key, (((1,), (0,)), ((), ()))), 0.0)
        d_key = d_key + dot(d_score, q_h, tn)
        d_value = d_value + dot(probs_low, da_h, tn)
    store(joined_ref, 0, att.astype(bf16))
    grads = (turn(d_query * scale, -1.0), turn(d_key, -1.0), d_value)
    columns = pl.ds(pl.multiple_of(pair * lanes, lanes), lanes)
    for i, grad in enumerate(grads):
        grad = grad.astype(bf16)
        store(d_proj_ref, i * att_rows, grad)
        total = jnp.sum(grad.astype(f32), axis=0, keepdims=True)

        @pl.when(row == 0)
        def _():
            bias_ref[i : i + 1, columns] = total

        @pl.when(row > 0)
        def _():
            bias_ref[i : i + 1, columns] = bias_ref[i : i + 1, columns] + total


def middle(proj, bias, d_joined, rope, seg, n_seq, att_rows, act, head_size):
    rows, tokens = seg.shape
    lanes = 2 * head_size
    pairs = att_rows // lanes
    bf16, f32 = jnp.bfloat16, jnp.float32
    order = (2, n_seq // 2, rows, tokens // n_seq)
    wide = lambda v: v.reshape(order + v.shape[-1:])
    shape = (2, n_seq // 2, 1, tokens // n_seq, lanes)
    block = lambda first: pl.BlockSpec(shape, lambda r, h: (0, 0, r, 0, first + h))
    row = lambda first: pl.BlockSpec((1, lanes), lambda r, h: (0, first + h))
    half = lambda v: pl.BlockSpec(
        (2, n_seq // 2, 1, tokens // n_seq // pairs, v.shape[-1]), lambda r, h: (0, 0, r, h, 0)
    )
    all_of = lambda v: pl.BlockSpec(v.shape, lambda r, h: (0,) * len(v.shape))
    outs = [
        jax.ShapeDtypeStruct(order + (d_joined.shape[-1],), bf16),
        jax.ShapeDtypeStruct(order + (proj.shape[-1],), bf16),
        jax.ShapeDtypeStruct((8, att_rows), f32),
    ]
    proj, d_joined = wide(proj), wide(d_joined)
    joined, d_proj, bias_sums = pl.pallas_call(
        functools.partial(
            middle_kernel,
            head_size=head_size, half_rot=ROT // 2, att_rows=att_rows, act=act,
        ),
        grid=(rows, pairs),
        in_specs=[
            block(0), block(pairs), block(2 * pairs),
            row(0), row(pairs), row(2 * pairs),
            block(0), half(proj), half(d_joined),
            pl.BlockSpec((1, 3, lanes, tokens), lambda r, h: (r, 0, 0, 0)),
            pl.BlockSpec((1, tokens, 1), lambda r, h: (r, 0, 0)),
            pl.BlockSpec((1, 1, tokens), lambda r, h: (r, 0, 0)),
        ],
        out_specs=[all_of(v) for v in outs],
        out_shape=outs,
        compiler_params=pltpu.CompilerParams(vmem_limit_bytes=56 * 2**20),
        name="middle",
    )(
        proj, proj, proj, bias, bias, bias, d_joined, proj, d_joined,
        rope, seg[:, :, None], seg[:, None, :],
    )
    flat = lambda v: v.reshape(rows * tokens, v.shape[-1])
    return flat(joined), flat(d_proj), bias_sums

MESH_ID = pl.DeviceIdType.MESH


def remote(src, dst, send_sem, recv_sem, device):
    return pltpu.make_async_remote_copy(
        src_ref=src,
        dst_ref=dst,
        send_sem=send_sem,
        recv_sem=recv_sem,
        device_id=device,
        device_id_type=MESH_ID,
    )


class Place:
    def __init__(self, n_seq):
        self.n_seq = n_seq
        self.depth = n_seq // 2
        self.p, self.s = lax.axis_index("dp"), lax.axis_index("seq")
        self.y, self.c = self.p // 2, lax.rem(self.p, 2)
        self.z, self.x = self.s // 2, lax.rem(self.s, 2)
        self.p_y = (1 - self.y) * 2 + self.c
        self.p_c = self.y * 2 + 1 - self.c
        self.p_d = (1 - self.y) * 2 + 1 - self.c
        self.to_y = (self.p_y, self.s)
        self.to_c = (self.p_c, self.s)
        self.to_x = (self.p, self.z * 2 + 1 - self.x)
        self.to_up = (self.p, self.s + 2)
        self.to_down = (self.p, self.s - 2)

    def seq(self, hop):
        return lax.rem(self.s + hop + self.n_seq, self.n_seq)

    def meet(self):
        barrier = pltpu.get_barrier_semaphore()

        def greet(hop, carry):
            pl.semaphore_signal(
                barrier, inc=1, device_id=(self.p, self.seq(hop)), device_id_type=MESH_ID
            )
            return carry

        lax.fori_loop(1, self.n_seq, greet, 0)
        for device in (self.to_y, self.to_c):
            pl.semaphore_signal(barrier, inc=1, device_id=device, device_id_type=MESH_ID)
        pl.semaphore_wait(barrier, self.n_seq + 1)


class Spread:
    def __init__(self, at, own, full, sems):
        self.at, self.own, self.full, self.sems = at, own, full, sems

    def along(self, src, up, ref=None):
        sems, at = self.sems, self.at
        here = self.full.at[at.x, src]
        return remote(
            here if ref is None else ref,
            here,
            sems.at[0 if up else 1, src],
            sems.at[3, src],
            at.to_up if up else at.to_down,
        )

    def across(self, src, ref=None):
        sems, at = self.sems, self.at
        here = self.full.at[at.x, src]
        return remote(here if ref is None else ref, here, sems.at[2, src], sems.at[4, src], at.to_x)

    def local(self):
        return pltpu.make_async_copy(
            self.own, self.full.at[self.at.x, self.at.z], self.sems.at[5, 0]
        )

    def begin_across(self):
        self.across(self.at.z, self.own).start()
        self.local().start()

    def begin_along(self):
        at = self.at

        @pl.when(at.z < at.depth - 1)
        def _():
            self.along(at.z, True, self.own).start()

        @pl.when(at.z > 0)
        def _():
            self.along(at.z, False, self.own).start()

    def step(self, hop):
        at = self.at

        @pl.when(at.z - hop >= 0)
        def _():
            src = at.z - hop
            self.along(src, True).wait_recv()

            @pl.when(at.z < at.depth - 1)
            def _():
                self.along(src, True).start()

            self.across(src).start()

        @pl.when(at.z + hop < at.depth)
        def _():
            src = at.z + hop
            self.along(src, False).wait_recv()

            @pl.when(at.z > 0)
            def _():
                self.along(src, False).start()

            self.across(src).start()

    def arrive(self):
        at = self.at
        for src in range(at.depth):
            here = self.full.at[1 - at.x, src]
            remote(here, here, self.sems.at[2, src], self.sems.at[4, src], at.to_x).wait_recv()
        self.local().wait()

    def sent(self):
        at = self.at
        for src in range(at.depth):
            self.across(src).wait_send()

            @pl.when((at.z < at.depth - 1) & (src <= at.z))
            def _():
                self.along(src, True).wait_send()

            @pl.when((at.z > 0) & (src >= at.z))
            def _():
                self.along(src, False).wait_send()


class Fan:
    def __init__(self, at, pick, sems):
        self.at, self.pick, self.sems = at, pick, sems

    def y(self, k, ref=None):
        at = self.at
        here = self.pick(at.p, k)
        return remote(here if ref is None else ref, here, self.sems.at[0, k], self.sems.at[1, k], at.to_y)

    def core(self, k, ref=None):
        at = self.at
        here = self.pick(at.p, k)
        return remote(here if ref is None else ref, here, self.sems.at[2, k], self.sems.at[3, k], at.to_c)

    def pass_on(self, k):
        at = self.at
        here = self.pick(at.p_y, k)
        return remote(here, here, self.sems.at[4, k], self.sems.at[5, k], at.to_c)

    def from_y(self, k):
        here = self.pick(self.at.p_y, k)
        return remote(here, here, self.sems.at[0, k], self.sems.at[1, k], self.at.to_y)

    def from_core(self, k):
        here = self.pick(self.at.p_c, k)
        return remote(here, here, self.sems.at[2, k], self.sems.at[3, k], self.at.to_c)

    def from_diagonal(self, k):
        here = self.pick(self.at.p_d, k)
        return remote(here, here, self.sems.at[4, k], self.sems.at[5, k], self.at.to_c)


def loop(low, high, body):
    def step(k, carry):
        body(k)
        return carry

    lax.fori_loop(low, high, step, 0)


def gather_kernel(
    x_ref, g_ref, w_ref, o_ref, tile_ref,
    x_full, g_full, w_full, o_full, tiles, hidden, out_mine, proj, d_joined,
    x_block, hid, w_near, p_block, g_near, o_near, t_near, small,
    x_sems, g_sems, w_sems, w_fan_sems, o_sems, o_fan_sems, t_sems, t_fan_sems, local_sems,
    x_in_sems, hid_sems, w_in_sems, p_sems, g_in_sems, o_in_sems,
    *, n_seq, late, lead,
):
    at = Place(n_seq)
    depth = at.depth
    bf16, f32 = jnp.bfloat16, jnp.float32
    own, width = o_ref.shape
    att = own + lead
    first_act = own - lead
    body, extra = pl.ds(0, own), pl.ds(own, late)
    x_go = Spread(at, x_ref, x_full, x_sems)
    g_go = Spread(at, g_ref, g_full, g_sems)
    w_fan = Fan(at, lambda p, k: w_full.at[p, k], w_fan_sems)
    o_fan = Fan(at, lambda p, k: o_full.at[p, body if k == 0 else extra], o_fan_sems)
    t_fan = Fan(at, lambda p, k: tiles.at[p], t_fan_sems)

    def w_send(hop):
        to = at.seq(hop)
        return remote(w_ref.at[to], w_full.at[at.p, at.s], w_sems.at[0, to], w_sems.at[1, at.s], (at.p, to))

    def w_recv(hop):
        src = at.seq(-hop)
        here = w_full.at[at.p, src]
        return remote(here, here, w_sems.at[0, src], w_sems.at[1, src], (at.p, src))

    def t_send(hop):
        to = at.seq(hop)
        return remote(tile_ref, tiles.at[at.p, at.s], t_sems.at[0, to], t_sems.at[1, at.s], (at.p, to))

    def t_recv(hop):
        src = at.seq(-hop)
        here = tiles.at[at.p, src]
        return remote(here, here, t_sems.at[0, src], t_sems.at[1, src], (at.p, src))

    w_local = pltpu.make_async_copy(w_ref.at[at.s], w_full.at[at.p, at.s], local_sems.at[0])
    o_local = pltpu.make_async_copy(o_ref, o_full.at[at.p, body], local_sems.at[1])
    t_local = pltpu.make_async_copy(tile_ref, tiles.at[at.p, at.s], local_sems.at[2])
    head = o_ref.at[pl.ds(0, late)]
    o_send = remote(
        head, o_full.at[at.p, extra], o_sems.at[0], o_sems.at[1], (at.p, at.seq(-1))
    )

    def place(i):
        return lax.rem(at.x + i // depth, 2), lax.rem(at.z + i, depth)

    def block_in(i):
        col, deep = place(i)
        return pltpu.make_async_copy(x_full.at[col, deep], x_block, x_in_sems.at[0])

    def hid_out(i):
        col, deep = place(i)
        return pltpu.make_async_copy(hid.at[col, deep], hidden.at[col, deep], hid_sems.at[i])

    def norm_block(i):
        col, deep = place(i)

        @pl.when(i >= depth)
        def _():
            here = x_full.at[1 - at.x, deep]
            remote(here, here, x_sems.at[2, deep], x_sems.at[4, deep], at.to_x).wait_recv()

        block_in(i).start()
        block_in(i).wait()
        some = 32

        def rows(k):
            part = pl.ds(pl.multiple_of(lax.rem(k, 2) * some, some), some)
            v = x_block[k // 2, part, :].astype(f32)
            centered = v - jnp.mean(v, axis=-1, keepdims=True)
            inv_std = lax.rsqrt(jnp.mean(centered * centered, axis=-1, keepdims=True) + norm_eps)
            done = centered * inv_std * small[0:1, :] + small[1:2, :]
            hid[col, deep, pl.ds(pl.multiple_of(k * some, some), some), :] = done.astype(bf16)

        loop(0, hid.shape[2] // some, rows)
        hid_out(i).start()

    def w_in(p, k):
        return pltpu.make_async_copy(w_full.at[p], w_near.at[p], w_in_sems.at[k])

    def g_in():
        return pltpu.make_async_copy(g_full, g_near, g_in_sems.at[0])

    def o_in(k):
        last = at.s == n_seq - 1
        lead_at = pl.multiple_of(lead * at.s, 16)
        late_at = pl.multiple_of(late - lead * at.s, 16)
        src, dst, count = [
            (o_full.at[0, pl.ds(lead_at, att - late)], 0, att - late),
            (o_full.at[0, pl.ds(lead_at + (att - late), late)], att - late, late),
            (o_full.at[1, pl.ds(late_at, first_act)], att, first_act),
            (o_full.at[2, body], 2 * att, own),
            (o_full.at[3, body], 3 * att, own),
            (o_full.at[1, extra], att - late, late),
        ][k]
        return pltpu.make_async_copy(src, o_near.at[pl.ds(dst, count)], o_in_sems.at[k])

    step_rows = p_block.shape[1]
    steps = hid.shape[0] * depth * hid.shape[2] // step_rows
    per_block = step_rows // hid.shape[2]

    def p_out(k):
        return pltpu.make_async_copy(
            p_block.at[lax.rem(k, 2)],
            proj.at[pl.ds(pl.multiple_of(k * step_rows, step_rows), step_rows)],
            p_sems.at[lax.rem(k, 2)],
        )

    def project(k):
        @pl.when(k >= 2)
        def _():
            p_out(k - 2).wait()

        rows = per_block * k
        left = hid[rows // depth, pl.ds(lax.rem(rows, depth), per_block)]
        left = left.reshape(step_rows, width)
        columns = p_block.shape[2]
        for n in range(0, columns, 512):
            some = min(512, columns - n)
            right = w_near[:, :, :, n : n + some].reshape(width, some)
            p_block[lax.rem(k, 2), :, n : n + some] = jnp.dot(
                left, right, preferred_element_type=f32
            )
        p_out(k).start()

    def join_back(k):
        rows = per_block * k
        left = g_near[rows // depth, pl.ds(lax.rem(rows, depth), per_block)]
        left = left.reshape(step_rows, width)
        d_joined[pl.ds(pl.multiple_of(k * step_rows, step_rows), step_rows), :] = (
            lax.dot_general(
                left, o_near[...], (((1,), (1,)), ((), ())), preferred_element_type=f32
            ).astype(bf16)
        )

    at.meet()
    x_go.begin_along()
    x_go.begin_across()
    g_go.begin_across()
    loop(1, n_seq, lambda hop: t_send(hop).start())
    t_local.start()
    w_fan.y(at.s, w_ref.at[at.s]).start()
    w_fan.core(at.s, w_ref.at[at.s]).start()
    w_local.start()
    o_fan.y(0, o_ref).start()
    o_fan.core(0, o_ref).start()
    o_local.start()
    w_send(1).start()
    w_send(n_seq - 1).start()
    for hop in range(1, depth):
        x_go.step(hop)
        if hop == 1:
            t_local.wait()
            loop(1, n_seq, lambda k: t_recv(k).wait_recv())
            t_fan.y(0).start()
            t_fan.core(0).start()
        if hop == 2:
            t_fan.from_y(0).wait_recv()
            t_fan.pass_on(0).start()
        w_send(hop + 1).start()
        if hop + 1 < n_seq - hop - 1:
            w_send(n_seq - hop - 1).start()
    g_go.begin_along()

    @pl.when(at.y == 0)
    def _():
        o_send.start()

    t_fan.from_core(0).wait_recv()
    t_fan.from_diagonal(0).wait_recv()
    t_load = pltpu.make_async_copy(tiles, t_near, local_sems.at[3])
    t_load.start()
    t_load.wait()
    for p in range(t_near.shape[0]):
        for pair in range(n_seq // 2):
            two = t_near[p, 2 * pair, 0:8] + t_near[p, 2 * pair + 1, 0:8]
            lanes = two.shape[1]
            first = (p * (n_seq // 2) + pair) * lanes
            small[:, first : first + lanes] = two
    for k, some in enumerate((first_act, own, own)):
        o_near[(k + 1) * att + some : (k + 2) * att, :] = jnp.zeros((att - some, width), bf16)
    x_go.local().wait()

    def w_step(hop):
        src = at.seq(-hop)
        w_recv(hop).wait_recv()
        w_fan.y(src).start()
        w_fan.core(src).start()
        norm_block(hop - 1)

    loop(1, n_seq, w_step)
    norm_block(n_seq - 1)
    w_local.wait()
    w_in(at.p, 0).start()
    def w_pass(hop):
        src = at.seq(-hop)
        w_fan.from_y(src).wait_recv()
        w_fan.pass_on(src).start()

    for hop in range(1, depth):
        g_go.step(hop)
        loop((hop - 1) * 3, min(hop * 3, n_seq), w_pass)
        if hop == 1:

            @pl.when(at.y == 0)
            def _():
                o_send.wait_recv()
                o_fan.y(1).start()
                o_fan.core(1).start()

    loop((depth - 1) * 3, n_seq, w_pass)
    w_in(at.p_y, 1).start()

    def w_last(k):
        w_fan.from_core(k).wait_recv()
        w_fan.from_diagonal(k).wait_recv()

    loop(0, n_seq, w_last)
    w_in(at.p_c, 2).start()
    w_in(at.p_d, 3).start()
    o_fan.from_y(0).wait_recv()
    o_fan.pass_on(0).start()

    @pl.when(at.y == 1)
    def _():
        o_fan.from_y(1).wait_recv()
        o_fan.pass_on(1).start()

    for k, p in enumerate((at.p, at.p_y, at.p_c, at.p_d)):
        w_in(p, k).wait()
    loop(0, steps, project)

    o_local.wait()
    o_fan.from_core(0).wait_recv()
    o_fan.from_diagonal(0).wait_recv()

    @pl.when(at.y == 0)
    def _():
        o_fan.from_core(1).wait_recv()

    @pl.when(at.y == 1)
    def _():
        o_fan.from_diagonal(1).wait_recv()

    for k in (0, 2, 3, 4):
        o_in(k).start()

    @pl.when(at.s < n_seq - 1)
    def _():
        o_in(1).start()
        o_in(1).wait()

    @pl.when(at.s == n_seq - 1)
    def _():
        o_in(5).start()
        o_in(5).wait()

    for k in (0, 2, 3, 4):
        o_in(k).wait()
    o_out = pltpu.make_async_copy(o_near, out_mine, o_in_sems.at[6])
    o_out.start()
    g_go.arrive()
    g_in().start()
    g_in().wait()
    loop(0, steps, join_back)

    o_out.wait()
    loop(steps - 2, steps, lambda k: p_out(k).wait())
    loop(0, n_seq, lambda i: hid_out(i).wait())
    x_go.sent()
    g_go.sent()

    def w_sent(k):
        w_fan.y(k).wait_send()
        w_fan.core(k).wait_send()
        w_fan.pass_on(k).wait_send()

    loop(0, n_seq, w_sent)

    def seq_sent(hop):
        w_send(hop).wait_send()
        t_send(hop).wait_send()

    loop(1, n_seq, seq_sent)
    for fan in (t_fan, o_fan):
        fan.y(0).wait_send()
        fan.core(0).wait_send()
        fan.pass_on(0).wait_send()

    @pl.when(at.y == 0)
    def _():
        o_send.wait_send()
        o_fan.y(1).wait_send()
        o_fan.core(1).wait_send()

    @pl.when(at.y == 1)
    def _():
        o_fan.pass_on(1).wait_send()


def gather_all(n_dp, n_seq, late, lead, x, g, w, o, tile):
    depth = n_seq // 2
    own, width = o.shape
    block = x.shape[0] * x.shape[1]
    tokens = n_seq * block
    columns = w.shape[2]
    mine = n_dp * (own + lead)
    bf16, f32 = jnp.bfloat16, jnp.float32
    rest, near = pl.BlockSpec(memory_space=pl.ANY), pl.BlockSpec(memory_space=pltpu.VMEM)
    dma = pltpu.SemaphoreType.DMA
    like = lambda lead, ref: jax.ShapeDtypeStruct(lead + ref.shape, ref.dtype)
    return pl.pallas_call(
        functools.partial(gather_kernel, n_seq=n_seq, late=late, lead=lead),
        in_specs=[rest] * 5,
        out_specs=[rest] * 8 + [near],
        out_shape=[
            like((2, depth), x),
            like((2, depth), g),
            jax.ShapeDtypeStruct((n_dp,) + w.shape, w.dtype),
            jax.ShapeDtypeStruct((n_dp, own + late, width), o.dtype),
            like((n_dp, n_seq), tile),
            jax.ShapeDtypeStruct((2, depth, block, width), bf16),
            jax.ShapeDtypeStruct((mine, width), bf16),
            jax.ShapeDtypeStruct((tokens, columns), f32),
            jax.ShapeDtypeStruct((tokens, mine), bf16),
        ],
        scratch_shapes=[
            pltpu.VMEM(x.shape, bf16),
            pltpu.VMEM((2, depth, block, width), bf16),
            pltpu.VMEM((n_dp,) + w.shape, bf16),
            pltpu.VMEM((2, 2 * block, columns), f32),
            pltpu.VMEM((2, depth) + g.shape, bf16),
            pltpu.VMEM((mine, width), bf16),
            pltpu.VMEM((n_dp, n_seq) + tile.shape, f32),
            pltpu.VMEM((8, width), f32),
            dma((6, depth)), dma((6, depth)), dma((2, n_seq)), dma((6, n_seq)),
            dma((2,)), dma((6, 2)), dma((2, n_seq)), dma((6, 1)), dma((4,)),
            dma((1,)), dma((n_seq,)), dma((4,)), dma((2,)), dma((1,)), dma((7,)),
        ],
        compiler_params=pltpu.CompilerParams(
            collective_id=0, has_side_effects=True, vmem_limit_bytes=56 * 2**20
        ),
        name="gather_all",
    )(x, g, w, o, tile)

def add_rows(out, terms, rows=32):
    count = out.shape[0]

    def some(k):
        at = pl.ds(pl.multiple_of(k * rows, rows), rows)
        total = terms[0][at].astype(jnp.float32)
        for term in terms[1:]:
            total = total + term[at].astype(jnp.float32)
        out[at] = total.astype(out.dtype)

    loop(0, count // rows, some)


def reduce_kernel(
    d_ref, b_ref, in_ref, out_ref, d_proj_ref, joined_ref, hidden_ref, g_ref, w_ref, o_ref,
    normed_ref, small_ref,
    sums, in_sum, out_sum, out_prev, small_sum,
    own_parts, x_got, z_got, in_own, in_core, in_y, out_own, out_core, out_y,
    small_own, small_core, small_y, small_seq,
    d_near, j_near, h_near, g_near, w_near, o_near,
    load_sems, x_sems, z_sems, in_core_sems, in_y_sems, in_sems, out_sems, small_sems, local_sem,
    w_sems, o_sems,
    *, n_seq, late, first_act, keep, plan,
):
    at = Place(n_seq)
    depth = at.depth
    parts = (d_ref, b_ref)
    main = out_own.shape[1] - late
    body, extra = pl.ds(0, main), pl.ds(main, late)
    y, c, z, x, s = at.y, at.c, at.z, at.x, at.s

    loads = [
        pltpu.make_async_copy(d_proj_ref, d_near, load_sems.at[0]),
        pltpu.make_async_copy(joined_ref, j_near, load_sems.at[1]),
        pltpu.make_async_copy(g_ref, g_near, load_sems.at[2]),
    ]
    feats = h_near.shape[4]
    for y_to in range(2):
        first = pl.multiple_of((2 * y_to + c) * feats, feats)
        loads.append(
            pltpu.make_async_copy(
                hidden_ref.at[:, :, :, pl.ds(first, feats)], h_near.at[y_to], load_sems.at[3 + y_to]
            )
        )
    dot = functools.partial(lax.dot_general, preferred_element_type=jnp.float32)
    low = jnp.bfloat16
    block_rows, width = own_parts.shape[2:]
    flat = lambda v: v.reshape(-1, v.shape[-1])

    def w_load(i):
        some = w_near.shape[1]
        return pltpu.make_async_copy(
            w_ref.at[pl.ds(pl.multiple_of(i * some, some), some)],
            w_near.at[lax.rem(i, 2)], w_sems.at[lax.rem(i, 2)],
        )

    def o_load(i):
        some = o_near.shape[2]
        return pltpu.make_async_copy(
            o_ref.at[:, pl.ds(pl.multiple_of(i * some, some), some)],
            o_near.at[lax.rem(i, 2)], o_sems.at[lax.rem(i, 2)],
        )

    def streamed(kind, load, count, some, product):
        load(0).start()

        def one(i):
            @pl.when(i + 1 < count)
            def _():
                load(i + 1).start()

            load(i).wait()
            done = product(lax.rem(i, 2)).astype(low)
            columns = pl.ds(pl.multiple_of(i * some, some), some)
            own_parts[kind, :, :, columns] = done.reshape(depth, block_rows, some)

        loop(0, count, one)

    def work(i):
        if i == 0:
            some = w_near.shape[1]
            left = flat(d_near[x])
            streamed(
                0, w_load, width // some, some,
                lambda k: dot(left, w_near[k], (((1,), (1,)), ((), ()))),
            )
        elif i == 1:
            some = o_near.shape[2]
            left = flat(j_near[x])
            streamed(
                1, o_load, width // some, some,
                lambda k: dot(left, o_near[k], (((1,), (0,)), ((), ()))),
            )
        elif i < 4:
            y_to = 1 - y if i == 2 else y
            left = flat(h_near[y_to])
            right = flat(d_near[...])
            total = right.shape[1]
            for first in range(0, total, 512):
                some = min(512, total - first)
                done = dot(left, right[:, first : first + some], (((0,), (0,)), ((), ())))
                in_own[y_to, :, :, first : first + some] = done.astype(low).reshape(
                    n_seq, -1, some
                )
        else:
            right = flat(g_near[...])
            for y_to in range(2):
                columns = pl.ds(pl.multiple_of((2 * y_to + c) * main, main), main)
                out_own[y_to, body] = dot(
                    flat(j_near[:, :, :, columns]), right, (((0,), (0,)), ((), ()))
                ).astype(low)
            out_own[0, extra] = dot(
                flat(j_near[:, :, :, keep : keep + late]), right, (((0,), (0,)), ((), ()))
            ).astype(low)

    def in_to_core(y_to, k):
        return remote(
            in_ref.at[y_to, k], in_core.at[y_to, k],
            in_core_sems.at[0, y_to, k], in_core_sems.at[1, y_to, k], at.to_c,
        )

    def out_to_core(y_to):
        return remote(
            out_ref.at[pl.ds(pl.multiple_of(y_to * main, main), main)], out_core.at[y_to, body],
            out_sems.at[0, y_to], out_sems.at[1, y_to], at.to_c,
        )

    extra_to_core = remote(
        out_ref.at[pl.ds(2 * main, late)], out_core.at[0, extra],
        out_sems.at[0, 2], out_sems.at[1, 2], at.to_c,
    )

    def to_across(kind, k):
        return remote(
            parts[kind].at[k], x_got.at[kind, k],
            x_sems.at[0, kind, k], x_sems.at[1, kind, k], at.to_x,
        )

    def to_up(kind, k):
        return remote(
            x_got.at[kind, k], z_got.at[kind, k],
            z_sems.at[0, kind, k], z_sems.at[1, kind, k], at.to_up,
        )

    def to_down(kind, k):
        slot = jnp.where(k == z - 1, depth, k)
        return remote(
            x_got.at[kind, k], z_got.at[kind, slot],
            z_sems.at[0, kind, k], z_sems.at[1, kind, slot], at.to_down,
        )

    def from_depth(kind, slot):
        here = z_got.at[kind, slot]
        return remote(here, here, z_sems.at[0, kind, slot], z_sems.at[1, kind, slot], at.to_up)

    def in_to_y(k):
        return remote(
            in_core.at[1 - y, k], in_y.at[k], in_y_sems.at[0, k], in_y_sems.at[1, k], at.to_y
        )

    def in_to_owner(k):
        return remote(
            in_core.at[y, k], in_sum.at[s], in_sems.at[0, k], in_sems.at[1, s], (at.p, k)
        )

    def in_from(k):
        here = in_sum.at[k]
        return remote(here, here, in_sems.at[0, k], in_sems.at[1, k], (at.p, k))

    in_keep = pltpu.make_async_copy(in_core.at[y, s], in_sum.at[s], local_sem.at[0])
    out_to_y = remote(
        out_core.at[1 - y, body], out_y.at[body], out_sems.at[0, 3], out_sems.at[1, 3], at.to_y
    )
    extra_to_y = remote(
        out_core.at[0, extra], out_y.at[extra], out_sems.at[0, 4], out_sems.at[1, 4], at.to_y
    )

    def out_shift(start):
        return remote(
            out_sum.at[pl.ds(start, late)], out_prev,
            out_sems.at[0, 5], out_sems.at[1, 5], (at.p, at.seq(1)),
        )

    small_to_core = remote(small_own, small_core, small_sems.at[0, 0], small_sems.at[1, 0], at.to_c)
    small_to_y = remote(small_core, small_y, small_sems.at[0, 1], small_sems.at[1, 1], at.to_y)

    def small_to(hop):
        to = at.seq(hop)
        first = (at.p * n_seq + to) // 2 * lanes
        return remote(
            small_y.at[:, pl.ds(pl.multiple_of(first, lanes), lanes)], small_seq.at[s],
            small_sems.at[0, 2 + to], small_sems.at[1, 2 + s], (at.p, to),
        )

    def small_from(hop):
        src = at.seq(-hop)
        here = small_seq.at[src]
        return remote(
            here, here, small_sems.at[0, 2 + src], small_sems.at[1, 2 + src], (at.p, src)
        )

    chained, steps = plan
    lanes = small_sum.shape[1]

    def around_z(hop):
        return lax.rem(z + hop, depth)

    def to_depth(kind, k):
        return remote(
            x_got.at[kind, k], z_got.at[kind, z],
            z_sems.at[0, kind, k], z_sems.at[1, kind, z], (at.p, 2 * k + x),
        )

    def turn(i):
        return jnp.where(lax.rem(i, 2) == 0, depth - 1 - i // 2, i // 2)

    def order(kind, i):
        return turn(i) if chained[kind] else around_z(i + 1)

    def across(j):
        to_across(j // depth, order(j // depth, j % depth)).start()

    def straight(kind, i):
        k = around_z(i + 1)
        to_across(kind, k).wait_recv()
        add_rows(x_got.at[kind, k], [x_got.at[kind, k], own_parts.at[kind, k]])
        if i + 1 < depth:
            to_depth(kind, k).start()

    def chain(kind, i):
        k = turn(i)
        to_across(kind, k).wait_recv()
        got, mine = x_got.at[kind, k], own_parts.at[kind, k]
        begins = ((z == 0) & (k > 0)) | ((z == depth - 1) & (k < depth - 1)) | (z == k)

        @pl.when(begins)
        def _():
            add_rows(got, [got, mine])

        @pl.when(jnp.logical_not(begins))
        def _():
            from_depth(kind, k).wait_recv()
            add_rows(got, [got, mine, z_got.at[kind, k]])

        @pl.when(z < k)
        def _():
            to_up(kind, k).start()

        @pl.when(z > k)
        def _():
            to_down(kind, k).start()

    def finish(kind):
        if not chained[kind]:
            others = [around_z(hop) for hop in range(1, depth)]
            for k in others:
                from_depth(kind, k).wait_recv()
            add_rows(
                sums.at[kind], [x_got.at[kind, z]] + [z_got.at[kind, k] for k in others], rows=16
            )
            return
        add_rows(sums.at[kind], [x_got.at[kind, z]], rows=16)

        @pl.when(z > 0)
        def _():
            from_depth(kind, z).wait_recv()
            add_rows(sums.at[kind], [sums.at[kind], z_got.at[kind, z]], rows=16)

        @pl.when(z < depth - 1)
        def _():
            from_depth(kind, depth).wait_recv()
            add_rows(sums.at[kind], [sums.at[kind], z_got.at[kind, depth]], rows=16)

    def to_y_step(hop):
        k = at.seq(hop)
        in_to_core(1 - y, k).wait_recv()
        add_rows(in_core.at[1 - y, k], [in_core.at[1 - y, k], in_own.at[1 - y, k]])
        in_to_y(k).start()

    def owner_step(hop):
        k = at.seq(hop)
        in_to_core(y, k).wait_recv()
        in_to_y(k).wait_recv()
        add_rows(in_core.at[y, k], [in_core.at[y, k], in_own.at[y, k], in_y.at[k]])

        @pl.when(k != s)
        def _():
            in_to_owner(k).start()

        @pl.when(k == s)
        def _():
            in_keep.start()

    def out_y_step():
        out_to_core(1 - y).wait_recv()
        extra_to_core.wait_recv()
        add_rows(out_core.at[1 - y, body], [out_core.at[1 - y, body], out_own.at[1 - y, body]])
        out_to_y.start()

        @pl.when(y == 1)
        def _():
            add_rows(out_core.at[0, extra], [out_core.at[0, extra], out_own.at[0, extra]])
            extra_to_y.start()

    def out_end():
        out_to_core(y).wait_recv()
        out_to_y.wait_recv()
        add_rows(out_sum.at[body], [out_core.at[y, body], out_own.at[y, body], out_y.at[body]])

        @pl.when(y == 0)
        def _():
            extra_to_y.wait_recv()
            add_rows(
                out_sum.at[extra], [out_core.at[0, extra], out_own.at[0, extra], out_y.at[extra]]
            )

            @pl.when(c == 0)
            def _():
                out_shift(keep).start()

            @pl.when((c == 1) & (s == n_seq - 1))
            def _():
                out_shift(main).start()

            @pl.when((c == 1) & (s < n_seq - 1))
            def _():
                out_shift(first_act - late).start()

    def small_step(i):
        if i == 0:
            finish(0)
            small_own[...] = small_ref[...]
            d_hidden = sums[0]
            small_own[0:1, :] = jnp.sum(d_hidden * normed_ref[...], axis=0, keepdims=True)
            small_own[1:2, :] = jnp.sum(d_hidden, axis=0, keepdims=True)
            small_to_core.start()
        elif i == 1:
            small_to_core.wait_recv()
            small_core[...] = small_core[...] + small_own[...]
            small_to_y.start()
        elif i == 2:
            small_to_y.wait()
            small_y[...] = small_core[...] + small_y[...]
            loop(1, n_seq, lambda hop: small_to(hop).start())
        else:
            first = (at.p * n_seq + s) // 2 * lanes
            small_sum[...] = small_y[:, pl.ds(pl.multiple_of(first, lanes), lanes)]

            def small_add(hop):
                small_from(hop).wait_recv()
                small_sum[...] = small_sum[...] + small_seq[at.seq(-hop)]

            loop(1, n_seq, small_add)

    def core_step(i):
        if i == 0:
            loop(0, n_seq, lambda hop: in_to_core(1 - y, at.seq(hop)).start())
            for load in loads:
                load.start()
        elif i == 1:
            loop(0, n_seq, lambda hop: in_to_core(y, at.seq(hop)).start())
        elif i == 2:
            out_to_core(1 - y).start()
            out_to_core(y).start()
            extra_to_core.start()
        else:
            for load in loads:
                load.wait()

    at.meet()
    for what, i in steps:
        if what == 0:
            across(i)
        elif what == 1:
            core_step(i)
        elif what == 2:
            to_y_step(i)
        elif what == 3:
            owner_step(i)
        elif what == 4:
            kind = i // depth
            (chain if chained[kind] else straight)(kind, i % depth)
        elif what == 5:
            small_step(i)
        elif what == 7:
            work(i)
        elif i == 0:
            out_y_step()
        else:
            out_end()
    finish(1)

    @pl.when(y == 0)
    def _():
        out_shift(0).wait()

    def in_last(hop):
        k = at.seq(hop)
        in_from(k).wait_recv()
        in_to_owner(k).wait_send()

    loop(1, n_seq, in_last)
    in_keep.wait()

    def seq_sent(k):
        for y_to in range(2):
            in_to_core(y_to, k).wait_send()
        in_to_y(k).wait_send()

    loop(0, n_seq, seq_sent)
    loop(1, n_seq, lambda hop: small_to(hop).wait_send())
    small_to_core.wait_send()
    for y_to in range(2):
        out_to_core(y_to).wait_send()
    extra_to_core.wait_send()
    out_to_y.wait_send()

    @pl.when(y == 1)
    def _():
        extra_to_y.wait_send()

    for kind in range(2):
        for k in range(depth):
            to_across(kind, k).wait_send()

            @pl.when(z < k)
            def _():
                (to_up if chained[kind] else to_depth)(kind, k).wait_send()

            @pl.when(z > k)
            def _():
                (to_down if chained[kind] else to_depth)(kind, k).wait_send()


def reduce_all(
    plan, n_dp, n_seq, late, first_act, keep, sent, d_proj, joined, hidden, g, w, o, normed, small
):
    depth = n_seq // 2
    d_sent, _, in_sent, out_sent = sent
    block = d_sent.shape[1:]
    in_block = in_sent.shape[2:]
    width = block[1]
    main = joined.shape[-1] // n_dp
    slot = main + late
    bf16, f32 = jnp.bfloat16, jnp.float32
    rest, near = pl.BlockSpec(memory_space=pl.ANY), pl.BlockSpec(memory_space=pltpu.VMEM)
    dma = pltpu.SemaphoreType.DMA
    return pl.pallas_call(
        functools.partial(
            reduce_kernel, n_seq=n_seq, late=late, first_act=first_act, keep=keep, plan=plan
        ),
        in_specs=[rest] * 10 + [near, near],
        out_specs=[near, rest, near, rest, near],
        out_shape=[
            jax.ShapeDtypeStruct((2,) + block, f32),
            jax.ShapeDtypeStruct((n_seq,) + in_block, bf16),
            jax.ShapeDtypeStruct((slot, width), bf16),
            jax.ShapeDtypeStruct((late, width), bf16),
            jax.ShapeDtypeStruct((small.shape[0], 128), f32),
        ],
        scratch_shapes=[
            pltpu.VMEM((2, depth) + block, bf16),
            pltpu.VMEM((2, depth) + block, bf16),
            pltpu.VMEM((2, depth + 1) + block, bf16),
            pltpu.VMEM((2, n_seq) + in_block, bf16),
            pltpu.VMEM((2, n_seq) + in_block, bf16),
            pltpu.VMEM((n_seq,) + in_block, bf16),
            pltpu.VMEM((2, slot, width), bf16),
            pltpu.VMEM((2, slot, width), bf16),
            pltpu.VMEM((slot, width), bf16),
            pltpu.VMEM(small.shape, f32),
            pltpu.VMEM(small.shape, f32),
            pltpu.VMEM(small.shape, f32),
            pltpu.VMEM((n_seq, small.shape[0], 128), f32),
            pltpu.VMEM(d_proj.shape, bf16),
            pltpu.VMEM(joined.shape, bf16),
            pltpu.VMEM((2,) + hidden.shape[:3] + (width // n_dp,), bf16),
            pltpu.VMEM(g.shape, bf16),
            pltpu.VMEM((2, 256, w.shape[1]), bf16),
            pltpu.VMEM((2, o.shape[0], 512), bf16),
            dma((7,)), dma((2, 2, depth)), dma((2, 2, depth + 1)), dma((2, 2, n_seq)), dma((2, n_seq)),
            dma((2, n_seq)), dma((2, 6)), dma((2, 2 + n_seq)), dma((1,)), dma((2,)), dma((2,)),
        ],
        compiler_params=pltpu.CompilerParams(
            collective_id=1, has_side_effects=True, vmem_limit_bytes=60 * 2**20
        ),
        name="reduce_all",
    )(*sent, d_proj, joined, hidden, g, w, o, normed, small)

def shares(n_seq, width, ffn, att, act):
    stretches, at = [], 0
    for i in range(3):
        stretches.append((i * width, at, att))
        at += att
    for half in range(2):
        first = 3 * width + half * ffn
        for some in act:
            stretches.append((first, at, some))
            at += some
            first += some * n_seq
    return stretches


def share_kernel(w_ref, out_ref, *, stretches):
    for s in range(out_ref.shape[0]):
        parts = [w_ref[:, first + s * some : first + (s + 1) * some] for first, _, some in stretches]
        out_ref[s] = jnp.concatenate(parts, axis=1).astype(out_ref.dtype)


def share_out(weight, n_seq, stretches):
    rows, columns = weight.shape
    step = 16
    return pl.pallas_call(
        functools.partial(share_kernel, stretches=stretches),
        grid=(rows // step,),
        in_specs=[pl.BlockSpec((step, columns), lambda i: (i, 0))],
        out_specs=pl.BlockSpec((n_seq, step, columns // n_seq), lambda i: (0, i, 0)),
        out_shape=jax.ShapeDtypeStruct((n_seq, rows, columns // n_seq), jnp.bfloat16),
        compiler_params=pltpu.CompilerParams(vmem_limit_bytes=56 * 2**20),
        name="share_out",
    )(weight)


def update_kernel(
    sum_ref, w_ref, m_ref, v_ref, a_ref, w_out, v_out, a_out, g_out, *, stretches, rate, decay
):
    n_seq = sum_ref.shape[0]
    for first, at, some in stretches:
        columns = slice(first, first + n_seq * some)
        parts = [sum_ref[s, :, at : at + some].astype(jnp.float32) for s in range(n_seq)]
        gradient = jnp.concatenate(parts, axis=1)
        g_out[:, columns] = gradient
        w_out[:, columns], v_out[:, columns], a_out[:, columns] = adam_update(
            w_ref[:, columns], m_ref[:, columns], v_ref[:, columns], a_ref[:, columns],
            gradient, rate, decay,
        )


def update_in(sums, weight, first, second, average, stretches):
    n_seq, rows, share = sums.shape
    step = 16
    wide = pl.BlockSpec((step, weight.shape[1]), lambda i: (i, 0))
    out = jax.ShapeDtypeStruct(weight.shape, jnp.float32)
    return pl.pallas_call(
        functools.partial(
            update_kernel, stretches=stretches, rate=matrix_rate, decay=weight_decay
        ),
        grid=(rows // step,),
        in_specs=[pl.BlockSpec((n_seq, step, share), lambda i: (0, i, 0))] + [wide] * 4,
        out_specs=[wide] * 4,
        out_shape=[out] * 4,
        compiler_params=pltpu.CompilerParams(vmem_limit_bytes=56 * 2**20),
        name="update_in",
    )(sums, weight, first, second, average)

def split_heads(
    n_dp, n_seq, tokens, cotangent, segment_ids, doc_positions,
    in_weight, in_first, in_second, in_average,
    out_weight, out_first, out_second, out_average,
    small_params, small_first, small_second, small_average,
):
    bf16, f32 = jnp.bfloat16, jnp.float32
    rows, own_tokens, width = tokens.shape
    row_tokens = own_tokens * n_seq
    all_tokens = rows * row_tokens
    head_size = width // HEADS
    ffn = (in_weight.shape[1] - 3 * width) // 2
    in_rows, own = in_weight.shape[0], out_weight.shape[0]
    dp_rows = own * n_seq
    att = width // n_seq
    late = width - dp_rows
    act = [(dp_rows - late) // n_seq, own, own]
    act_all = sum(act)
    lead = att - own
    p, s = lax.axis_index("dp"), lax.axis_index("seq")

    stretches = shares(n_seq, width, ffn, att, act)
    out_low = out_weight.astype(bf16)
    small_low = small_params.astype(bf16).astype(f32).T
    widen = lambda v, n: jnp.pad(v, ((0, n - v.shape[0]), (0, 128 - v.shape[1])))
    tile = jnp.concatenate(
        [
            widen(small_low, 8),
            widen(jnp.concatenate([segment_ids, doc_positions], axis=0).astype(f32), 8),
        ],
        axis=0,
    )
    odd = jnp.concatenate([jnp.zeros_like(tile[:8, :in_rows]), tile[:8, :in_rows]], axis=1)
    tile = jnp.concatenate([jnp.where(s % 2 == 1, odd, tile[:8]), tile[8:]], axis=0)
    _, g_full, in_low, _, tiles, hidden, out_mine, proj, d_joined = gather_all(
        n_dp, n_seq, late, lead, tokens, cotangent, share_out(in_weight, n_seq, stretches), out_low, tile
    )
    g_full, hidden = g_full.reshape(all_tokens, width), hidden.reshape(all_tokens, width)
    in_low = in_low.reshape(n_dp * n_seq * in_rows, 3 * att + 2 * act_all)

    pairs = tiles[:, :, :5].reshape(n_dp, n_seq // 2, 2, 5, 2 * in_rows).sum(axis=2)
    small_low = jnp.transpose(pairs, (2, 0, 1, 3)).reshape(5, width)
    gain = small_low[0]
    bias = lax.dynamic_slice_in_dim(small_low[2:5], s * att, att, 1).reshape(1, 3 * att)
    docs = lax.dynamic_index_in_dim(tiles, p, 0, keepdims=False)[:, 8:, :own_tokens]
    seg_full = jnp.transpose(docs[:, :rows], (1, 0, 2)).reshape(rows, row_tokens)
    pos_full = jnp.transpose(docs[:, rows : 2 * rows], (1, 0, 2)).reshape(rows, row_tokens)
    last = s == n_seq - 1
    keep = att - late

    def normalise(v):
        v = v.astype(f32)
        centered = v - jnp.mean(v, axis=-1, keepdims=True)
        inv_std = lax.rsqrt(jnp.mean(centered * centered, axis=-1, keepdims=True) + norm_eps)
        return centered * inv_std, inv_std

    half_rot = ROT // 2
    inv_freq = rope_base ** (-2.0 * jnp.arange(half_rot, dtype=f32) / ROT)
    angles = pos_full[:, None, :] * inv_freq[:, None]
    cos, sin = jnp.cos(angles), jnp.sin(angles)
    one, zero = jnp.ones((rows, head_size - ROT, row_tokens), f32), jnp.zeros_like(cos)
    rest = 0.0 * one
    rope = jnp.stack(
        [
            jnp.concatenate([cos, cos, one] * 2, axis=1),
            jnp.concatenate([-sin, zero, rest] * 2, axis=1),
            jnp.concatenate([zero, sin, rest] * 2, axis=1),
        ],
        axis=1,
    )
    joined, d_proj, bias_part = middle(
        proj, bias, d_joined, rope, seg_full, n_seq, att, act, head_size
    )

    blocks = lambda v: v.reshape(2, n_seq // 2, rows * own_tokens, v.shape[-1])
    x, c = s % 2, p % 2
    across = lambda v: lax.dynamic_index_in_dim(blocks(v), 1 - x, 0, keepdims=False)
    d_sent = jnp.einsum("ztk,fk->ztf", across(d_proj), in_low, preferred_element_type=f32)
    b_sent = jnp.einsum("ztk,kf->ztf", across(joined), out_mine, preferred_element_type=f32)

    def to_core(v):
        some = v.shape[1] // n_dp
        firsts = [(2 * y_to + 1 - c) * some for y_to in range(2)]
        return [lax.dynamic_slice_in_dim(v, first, some, 1) for first in firsts]

    over_tokens = lambda a, b: lax.dot_general(
        a, b, (((0,), (0,)), ((), ())), preferred_element_type=f32
    ).astype(bf16)
    in_sent = over_tokens(jnp.concatenate(to_core(hidden), axis=1), d_proj).reshape(2, n_seq, in_rows, -1)
    left = jnp.concatenate([*to_core(joined), joined[:, keep:att]], axis=1)
    out_sent = over_tokens(left, g_full)
    normed, inv_std = normalise(tokens.reshape(rows * own_tokens, width))
    small_part = lax.dynamic_update_slice(jnp.zeros((8, width), f32), bias_part[:3], (2, s * att))
    plan = ((1, 1), ((0, 0), (0, 1), (1, 0), (1, 1), (1, 2), (0, 2), (0, 3), (1, 3), (7, 2), (0, 4), (0, 5), (0, 6), (0, 7), (7, 0), (2, 0), (2, 1), (2, 2), (2, 3), (2, 4), (2, 5), (2, 6), (2, 7), (7, 4), (6, 0), (7, 3), (4, 0), (3, 0), (3, 1), (4, 1), (3, 2), (3, 3), (7, 1), (4, 2), (3, 4), (4, 3), (3, 5), (5, 0), (4, 4), (5, 1), (4, 5), (5, 2), (4, 6), (6, 1), (4, 7), (3, 6), (3, 7), (5, 3)))
    sums, in_sum, out_sum, from_prev, small_sum = reduce_all(
        plan, n_dp, n_seq, late, act[0], keep,
        (d_sent.astype(bf16), b_sent.astype(bf16), in_sent, out_sent),
        blocks(d_proj), blocks(joined), blocks(hidden), blocks(g_full), in_low, out_mine,
        normed, small_part,
    )
    d_hidden, branch = sums[0], sums[1]

    output = (tokens.astype(f32) + branch.reshape(tokens.shape)).astype(bf16)
    d_normed = d_hidden * gain
    input_grad = cotangent.astype(f32) + (
        inv_std
        * (
            d_normed
            - jnp.mean(d_normed, axis=-1, keepdims=True)
            - normed * jnp.mean(d_normed * normed, axis=-1, keepdims=True)
        )
    ).reshape(tokens.shape)
    small_grad = lax.dynamic_slice(small_sum, (0, s % 2 * in_rows), (8, in_rows))[:5].T

    count = jnp.where(p == 0, lead * s, jnp.where(p == 1, late - lead * s, 0))
    out_grad = lax.dynamic_slice_in_dim(
        jnp.concatenate([from_prev, out_sum[:own]], axis=0), late - count, own, 0
    ).astype(f32)

    *in_new, in_grad = update_in(
        in_sum, in_weight, in_first, in_second, in_average, stretches
    )
    out_new = adam_update(
        out_weight, out_first, out_second, out_average, out_grad, matrix_rate, weight_decay
    )
    small_new = adam_update(
        small_params, small_first, small_second, small_average, small_grad, small_rate, 0.0
    )
    return (output, input_grad, *in_new, *out_new, *small_new, small_grad, in_grad, out_grad)


def solution(mesh):
    n_dp, n_seq = mesh.shape["dp"], mesh.shape["seq"]

    def choose(*operands):
        own_rows = operands[8].shape[0]
        model_width = operands[0].shape[2]
        if heads_fit(n_dp, n_seq, own_rows, model_width, operands[4].shape[1]):
            return split_heads(n_dp, n_seq, *operands)
        return per_device(*operands)

    return jax.shard_map(
        choose,
        mesh=mesh,
        in_specs=(
            P("dp", "seq", None),
            P("dp", "seq", None),
            P("dp", "seq"),
            P("dp", "seq"),
            P(("dp", "seq"), None),
            P(("dp", "seq"), None),
            P(("dp", "seq"), None),
            P(("dp", "seq"), None),
            P(("dp", "seq"), None),
            P(("dp", "seq"), None),
            P(("dp", "seq"), None),
            P(("dp", "seq"), None),
            P(("dp", "seq"), None),
            P(("dp", "seq"), None),
            P(("dp", "seq"), None),
            P(("dp", "seq"), None),
        ),
        out_specs=(
            P("dp", "seq", None),
            P("dp", "seq", None),
            P(("dp", "seq"), None),
            P(("dp", "seq"), None),
            P(("dp", "seq"), None),
            P(("dp", "seq"), None),
            P(("dp", "seq"), None),
            P(("dp", "seq"), None),
            P(("dp", "seq"), None),
            P(("dp", "seq"), None),
            P(("dp", "seq"), None),
            P(("dp", "seq"), None),
            P(("dp", "seq"), None),
            P(("dp", "seq"), None),
        ),
        check_vma=False,
    )
```

```python
import functools

import jax
import jax.numpy as jnp
from jax import lax
from jax.experimental import pallas as pl
from jax.experimental.pallas import tpu as pltpu
from jax.sharding import PartitionSpec as P

HEADS = 32
ROT = 16
STEP = 2


beta_one = 0.9
adam_eps = 1e-08
matrix_rate = 0.001
small_rate = 0.01
weight_decay = 0.1
norm_eps = 1e-05
rope_base = 10000.0
neg_large = -1e30


def rope_tables(positions, rot_dims):
    half_rot = rot_dims // 2
    inv_freq = rope_base ** (-2.0 * jnp.arange(half_rot, dtype=jnp.float32) / rot_dims)
    angles = positions.astype(jnp.float32)[..., None] * inv_freq
    return (jnp.cos(angles)[..., None, :], jnp.sin(angles)[..., None, :])


def apply_rope(field_in, cosine_tab, sine_tab, rot_dims):
    half_rot = rot_dims // 2
    low_half = field_in[..., :half_rot]
    high_half = field_in[..., half_rot:rot_dims]
    return jnp.concatenate(
        [
            low_half * cosine_tab - high_half * sine_tab,
            high_half * cosine_tab + low_half * sine_tab,
            field_in[..., rot_dims:],
        ],
        axis=-1,
    )


def undo_rope(grad_in, cosine_tab, sine_tab, rot_dims):
    half_rot = rot_dims // 2
    low_half = grad_in[..., :half_rot]
    high_half = grad_in[..., half_rot:rot_dims]
    return jnp.concatenate(
        [
            low_half * cosine_tab + high_half * sine_tab,
            high_half * cosine_tab - low_half * sine_tab,
            grad_in[..., rot_dims:],
        ],
        axis=-1,
    )


def visible(query_seg, key_seg, query_pos, key_pos):
    same_doc = query_seg[:, :, None] == key_seg[:, None, :]
    causal = key_pos[None, :] <= query_pos[:, None]
    return (same_doc & causal[None])[:, None]


def to_tokens(head_major):
    return jnp.transpose(head_major, (0, 2, 1, 3))


def adam_update(weight, first, second, average, gradient, rate, decay_rate):
    beta_two = 1.0 - STEP ** (-0.8)
    average_keep = min(0.999, (1.0 + STEP) / (10.0 + STEP))
    first_new = beta_one * first + (1.0 - beta_one) * gradient
    second_new = beta_two * second + (1.0 - beta_two) * gradient * gradient
    moment_hat = beta_one * first_new / (1.0 - beta_one ** (STEP + 1)) + (
        1.0 - beta_one
    ) * gradient / (1.0 - beta_one**STEP)
    weight_new = weight - rate * (
        moment_hat / (jnp.sqrt(second_new) + adam_eps) + decay_rate * weight
    )
    average_new = average_keep * average + (1.0 - average_keep) * weight_new
    return (weight_new, second_new, average_new)


def per_device(
    tokens,
    cotangent,
    segment_ids,
    doc_positions,
    in_weight,
    in_first,
    in_second,
    in_average,
    out_weight,
    out_first,
    out_second,
    out_average,
    small_params,
    small_first,
    small_second,
    small_average,
):
    rows_here, row_tokens, model_width = tokens.shape
    head_count = HEADS
    head_size = model_width // head_count
    score_scale = head_size ** (-0.5)
    all_tokens = rows_here * row_tokens
    wide_in = in_weight.shape[1]
    ffn_width = (wide_in - 3 * model_width) // 2
    shape_heads = (rows_here, row_tokens, head_count, head_size)
    own_places = lax.axis_index("seq") * row_tokens + jnp.arange(row_tokens)
    flat_in = tokens.astype(jnp.float32).reshape(all_tokens, model_width)
    centered = flat_in - jnp.mean(flat_in, axis=-1, keepdims=True)
    inv_std = lax.rsqrt(jnp.mean(centered * centered, axis=-1, keepdims=True) + norm_eps)
    normed = centered * inv_std
    in_low = in_weight.astype(jnp.bfloat16)
    out_low = out_weight.astype(jnp.bfloat16)
    small_low = small_params.astype(jnp.bfloat16)
    w_piece = lax.all_gather(in_low, ("dp", "seq"), axis=0, tiled=True)
    s_piece = lax.all_gather(small_low, ("dp", "seq"), axis=0, tiled=True)
    columns = normed
    s_float = s_piece.astype(jnp.float32)
    h_piece = (columns * s_float[:, 0] + s_float[:, 1]).astype(jnp.bfloat16)
    proj_acc = jnp.dot(h_piece, w_piece, preferred_element_type=jnp.float32)
    norm_gain = s_float[:, 0]
    qkv_bias = s_float[:, 2:5].T.reshape(3 * model_width)
    qkv_full = proj_acc[:, : 3 * model_width] + qkv_bias
    gate_pre = proj_acc[:, 3 * model_width : 3 * model_width + ffn_width]
    up_pre = proj_acc[:, 3 * model_width + ffn_width :]
    cosine_tab, sine_tab = rope_tables(doc_positions, ROT)
    query_low = apply_rope(
        qkv_full[:, :model_width].reshape(shape_heads), cosine_tab, sine_tab, ROT
    ).astype(jnp.bfloat16)
    key_low = apply_rope(
        qkv_full[:, model_width : 2 * model_width].reshape(shape_heads), cosine_tab, sine_tab, ROT
    ).astype(jnp.bfloat16)
    value_low = qkv_full[:, 2 * model_width :].reshape(shape_heads).astype(jnp.bfloat16)
    seg_low = segment_ids.astype(jnp.bfloat16)
    seg_own = segment_ids.astype(jnp.float32)
    key_flat = key_low.reshape(rows_here, row_tokens, model_width)
    value_flat = value_low.reshape(rows_here, row_tokens, model_width)
    attend_init = (
        jnp.full((rows_here, head_count, row_tokens), neg_large, jnp.float32),
        jnp.zeros((rows_here, head_count, row_tokens), jnp.float32),
        jnp.zeros((rows_here, head_count, row_tokens, head_size), jnp.float32),
    )
    key_piece = lax.all_gather(key_flat, "seq", axis=1, tiled=True)
    value_piece = lax.all_gather(value_flat, "seq", axis=1, tiled=True)
    seg_piece = lax.all_gather(seg_low, "seq", axis=1, tiled=True)
    turn_count = key_piece.shape[1] // row_tokens

    def attend_one_turn(turn_index, inner_state):
        offset = turn_index * row_tokens
        key_blk = lax.dynamic_slice_in_dim(key_piece, offset, row_tokens, 1).reshape(shape_heads)
        value_blk = lax.dynamic_slice_in_dim(value_piece, offset, row_tokens, 1).reshape(
            shape_heads
        )
        seg_blk = lax.dynamic_slice_in_dim(seg_piece, offset, row_tokens, 1).astype(jnp.float32)
        key_mask = visible(seg_own, seg_blk, own_places, offset + jnp.arange(row_tokens))
        running_top, running_sum, weighted = inner_state
        scores = (
            jnp.einsum("rqhe,rkhe->rhqk", query_low, key_blk, preferred_element_type=jnp.float32)
            * score_scale
        )
        scores = jnp.where(key_mask, scores, neg_large)
        new_top = jnp.maximum(running_top, jnp.max(scores, axis=-1))
        weights = jnp.where(key_mask, jnp.exp(scores - new_top[..., None]), 0.0)
        factor = jnp.exp(running_top - new_top)
        running_sum = running_sum * factor + jnp.sum(weights, axis=-1)
        weighted = weighted * factor[..., None] + jnp.einsum(
            "rhqk,rkhe->rhqe",
            weights.astype(jnp.bfloat16),
            value_blk,
            preferred_element_type=jnp.float32,
        )
        return (new_top, running_sum, weighted)

    running_top, running_sum, weighted = lax.fori_loop(0, turn_count, attend_one_turn, attend_init)
    attended = weighted / running_sum[..., None]
    log_total = running_top + jnp.log(running_sum)
    attended_low = to_tokens(attended).reshape(all_tokens, model_width).astype(jnp.bfloat16)
    gate_sig = jax.nn.sigmoid(gate_pre)
    activated = gate_pre * gate_sig * up_pre
    joined = jnp.concatenate([attended_low, activated.astype(jnp.bfloat16)], axis=1)
    columns = joined
    branch_sum = jnp.dot(
        columns,
        lax.all_gather(out_low, ("dp", "seq"), axis=0, tiled=True),
        preferred_element_type=jnp.float32,
    )
    output = (flat_in + branch_sum).astype(jnp.bfloat16).reshape(rows_here, row_tokens, model_width)
    grad_out = cotangent.reshape(all_tokens, model_width)
    d_joined = lax.dot_general(
        grad_out,
        lax.all_gather(out_low, ("dp", "seq"), axis=0, tiled=True),
        (((1,), (1,)), ((), ())),
        preferred_element_type=jnp.float32,
    )
    d_joined = d_joined.astype(jnp.bfloat16)
    columns = joined
    out_grad = lax.psum_scatter(
        lax.dot_general(
            columns, grad_out, (((0,), (0,)), ((), ())), preferred_element_type=jnp.float32
        ),
        ("dp", "seq"),
        scatter_dimension=0,
        tiled=True,
    )
    d_attended = d_joined[:, :model_width].reshape(shape_heads)
    d_act = d_joined[:, model_width:].astype(jnp.float32)
    d_gate = d_act * up_pre * gate_sig * (1.0 + gate_pre * (1.0 - gate_sig))
    d_up = d_act * gate_pre * gate_sig
    out_dot = jnp.einsum("rqhe,rhqe->rhq", d_attended.astype(jnp.float32), attended)
    grad_zero = jnp.zeros((rows_here, head_count, row_tokens, head_size), jnp.float32)
    query_key_piece = lax.all_gather(key_flat, "seq", axis=1, tiled=True)
    query_value_piece = lax.all_gather(value_flat, "seq", axis=1, tiled=True)
    query_seg_piece = lax.all_gather(seg_low, "seq", axis=1, tiled=True)
    turn_count = query_key_piece.shape[1] // row_tokens

    def query_one_turn(turn_index, inner_state):
        offset = turn_index * row_tokens
        key_blk = lax.dynamic_slice_in_dim(query_key_piece, offset, row_tokens, 1).reshape(
            shape_heads
        )
        value_blk = lax.dynamic_slice_in_dim(query_value_piece, offset, row_tokens, 1).reshape(
            shape_heads
        )
        seg_blk = lax.dynamic_slice_in_dim(query_seg_piece, offset, row_tokens, 1).astype(
            jnp.float32
        )
        key_mask = visible(seg_own, seg_blk, own_places, offset + jnp.arange(row_tokens))
        scores = (
            jnp.einsum("rqhe,rkhe->rhqk", query_low, key_blk, preferred_element_type=jnp.float32)
            * score_scale
        )
        weights = jnp.where(key_mask, jnp.exp(scores - log_total[..., None]), 0.0)
        d_prob = jnp.einsum(
            "rqhe,rkhe->rhqk", d_attended, value_blk, preferred_element_type=jnp.float32
        )
        d_score = (weights * (d_prob - out_dot[..., None])).astype(jnp.bfloat16)
        return (
            inner_state
            + jnp.einsum("rhqk,rkhe->rhqe", d_score, key_blk, preferred_element_type=jnp.float32)
            * score_scale
        )

    d_query = lax.fori_loop(0, turn_count, query_one_turn, grad_zero)
    row_stats = jnp.concatenate(
        [jnp.transpose(log_total, (0, 2, 1)), jnp.transpose(out_dot, (0, 2, 1))], axis=2
    )
    stat_high = row_stats.astype(jnp.bfloat16)
    stat_low = (row_stats - stat_high.astype(jnp.float32)).astype(jnp.bfloat16)
    query_flat = query_low.reshape(rows_here, row_tokens, model_width)
    d_att_flat = d_attended.reshape(rows_here, row_tokens, model_width)
    query_piece = lax.all_gather(query_flat, "seq", axis=1, tiled=True)
    dout_piece = lax.all_gather(d_att_flat, "seq", axis=1, tiled=True)
    high_piece = lax.all_gather(stat_high, "seq", axis=1, tiled=True)
    low_piece = lax.all_gather(stat_low, "seq", axis=1, tiled=True)
    key_seg_piece = lax.all_gather(seg_low, "seq", axis=1, tiled=True)
    turn_count = query_piece.shape[1] // row_tokens

    def key_one_turn(turn_index, inner_state):
        offset = turn_index * row_tokens
        query_blk = lax.dynamic_slice_in_dim(query_piece, offset, row_tokens, 1).reshape(
            shape_heads
        )
        dout_blk = lax.dynamic_slice_in_dim(dout_piece, offset, row_tokens, 1).reshape(shape_heads)
        stat_blk = lax.dynamic_slice_in_dim(high_piece, offset, row_tokens, 1).astype(
            jnp.float32
        ) + lax.dynamic_slice_in_dim(low_piece, offset, row_tokens, 1).astype(jnp.float32)
        lse_blk = jnp.transpose(stat_blk[..., :head_count], (0, 2, 1))
        dot_blk = jnp.transpose(stat_blk[..., head_count:], (0, 2, 1))
        seg_blk = lax.dynamic_slice_in_dim(key_seg_piece, offset, row_tokens, 1).astype(jnp.float32)
        key_mask = visible(seg_blk, seg_own, offset + jnp.arange(row_tokens), own_places)
        d_key, d_value = inner_state
        scores = (
            jnp.einsum("rqhe,rkhe->rhqk", query_blk, key_low, preferred_element_type=jnp.float32)
            * score_scale
        )
        weights = jnp.where(key_mask, jnp.exp(scores - lse_blk[..., None]), 0.0)
        d_value = d_value + jnp.einsum(
            "rhqk,rqhe->rhke",
            weights.astype(jnp.bfloat16),
            dout_blk,
            preferred_element_type=jnp.float32,
        )
        d_prob = jnp.einsum(
            "rqhe,rkhe->rhqk", dout_blk, value_low, preferred_element_type=jnp.float32
        )
        d_score = (weights * (d_prob - dot_blk[..., None])).astype(jnp.bfloat16)
        d_key = (
            d_key
            + jnp.einsum("rhqk,rqhe->rhke", d_score, query_blk, preferred_element_type=jnp.float32)
            * score_scale
        )
        return (d_key, d_value)

    d_key, d_value = lax.fori_loop(0, turn_count, key_one_turn, (grad_zero, grad_zero))
    d_query_tok = undo_rope(to_tokens(d_query), cosine_tab, sine_tab, ROT).reshape(
        all_tokens, model_width
    )
    d_key_tok = undo_rope(to_tokens(d_key), cosine_tab, sine_tab, ROT).reshape(
        all_tokens, model_width
    )
    d_value_tok = to_tokens(d_value).reshape(all_tokens, model_width)
    d_proj = jnp.concatenate([d_query_tok, d_key_tok, d_value_tok, d_gate, d_up], axis=1).astype(
        jnp.bfloat16
    )
    d_hidden = lax.dot_general(
        d_proj,
        lax.all_gather(in_low, ("dp", "seq"), axis=0, tiled=True),
        (((1,), (1,)), ((), ())),
        preferred_element_type=jnp.float32,
    )
    columns = h_piece
    in_grad = lax.psum_scatter(
        lax.dot_general(
            columns, d_proj, (((0,), (0,)), ((), ())), preferred_element_type=jnp.float32
        ),
        ("dp", "seq"),
        scatter_dimension=0,
        tiled=True,
    )
    gain_grad = jnp.sum(d_hidden * normed, axis=0)
    shift_grad = jnp.sum(d_hidden, axis=0)
    bias_grad = (
        jnp.sum(d_proj[:, : 3 * model_width].astype(jnp.float32), axis=0).reshape(3, model_width).T
    )
    small_term = jnp.concatenate([gain_grad[:, None], shift_grad[:, None], bias_grad], axis=1)
    small_grad = lax.psum_scatter(small_term, ("dp", "seq"), scatter_dimension=0, tiled=True)
    d_normed = d_hidden * norm_gain
    input_grad = grad_out.astype(jnp.float32) + inv_std * (
        d_normed
        - jnp.mean(d_normed, axis=-1, keepdims=True)
        - normed * jnp.mean(d_normed * normed, axis=-1, keepdims=True)
    )
    input_grad = input_grad.reshape(rows_here, row_tokens, model_width)
    in_new = adam_update(
        in_weight, in_first, in_second, in_average, in_grad, matrix_rate, weight_decay
    )
    out_new = adam_update(
        out_weight, out_first, out_second, out_average, out_grad, matrix_rate, weight_decay
    )
    small_new = adam_update(
        small_params, small_first, small_second, small_average, small_grad, small_rate, 0.0
    )
    return (
        output,
        input_grad,
        in_new[0],
        in_new[1],
        in_new[2],
        out_new[0],
        out_new[1],
        out_new[2],
        small_new[0],
        small_new[1],
        small_new[2],
        small_grad,
        in_grad,
        out_grad,
    )


def heads_fit(n_dp, n_seq, own_rows, model_width, wide_in):
    dp_rows = own_rows * n_seq
    if n_dp != 4 or HEADS % (2 * n_seq) or not dp_rows < model_width < 2 * dp_rows:
        return False
    att_rows = model_width // n_seq
    late_att = model_width - dp_rows
    first_act = dp_rows - late_att
    if first_act % n_seq:
        return False
    lead = att_rows - own_rows
    return (
        wide_in - 3 * model_width == 2 * (n_dp * dp_rows - model_width)
        and lead == own_rows - first_act // n_seq
        and lead * n_seq == late_att
        and lead % 16 == 0
    )


def middle_kernel(
    q_ref, k_ref, v_ref, bq_ref, bk_ref, bv_ref, da_ref, act_ref, d_act_ref, rope_ref,
    seg_q_ref, seg_k_ref,
    joined_ref, d_proj_ref, bias_ref,
    *, head_size, half_rot, att_rows, act,
):
    row, pair = pl.program_id(0), pl.program_id(1)
    lanes = 2 * head_size
    half = act_ref.shape[3]
    act_rows = sum(act)
    bf16, f32 = jnp.bfloat16, jnp.float32

    def feed_forward(step):
        x, z = lax.rem(step, 2), step // 2
        raw = act_ref[x, z, 0]
        gate = raw[:, 3 * att_rows : 3 * att_rows + act_rows]
        up = raw[:, 3 * att_rows + act_rows :]
        joint = d_act_ref[x, z, 0]
        d_act = jnp.concatenate(
            [joint[:, (i + 1) * att_rows :][:, :some] for i, some in enumerate(act)], axis=1
        ).astype(f32)
        sig = 1.0 / (1.0 + jnp.exp(-gate))
        silu = gate * sig
        rows = pl.ds(pl.multiple_of(pair * half, half), half)
        active, parts, first = silu * up, [], 0
        for some in act:
            parts.append(active[:, first : first + some])
            parts.append(jnp.zeros((half, att_rows - some), f32))
            first += some
        joined_ref[x, z, row, rows, att_rows:] = jnp.concatenate(parts, axis=1).astype(bf16)
        d_gate = d_act * up * sig * (1.0 + gate * (1.0 - sig))
        d_proj_ref[x, z, row, rows, 3 * att_rows :] = jnp.concatenate(
            [d_gate, d_act * silu], axis=1
        ).astype(bf16)

    loop(0, act_ref.shape[0] * act_ref.shape[1], feed_forward)

    def whole(v):
        across, depth = v.shape[:2]
        parts = [v[x, z].reshape(v.shape[-2:]) for z in range(depth) for x in range(across)]
        return jnp.concatenate(parts, axis=0)

    def store(ref, first, v):
        across, depth, _, some, _ = ref.shape
        columns = pl.ds(pl.multiple_of(first + pair * lanes, lanes), lanes)
        for z in range(depth):
            for x in range(across):
                at = (z * across + x) * some
                ref[x, z, row, :, columns] = v[at : at + some]

    cos, sin_low, sin_high = (rope_ref[0, i].T for i in range(3))
    tokens = cos.shape[0]
    scale = head_size ** (-0.5)

    def turn(v, way):
        return (
            v * cos
            + way * pltpu.roll(v, lanes - half_rot, 1) * sin_low
            + way * pltpu.roll(v, half_rot, 1) * sin_high
        )

    query = (turn(whole(q_ref[...]) + bq_ref[...], 1.0)).astype(bf16) * scale
    query = query.astype(bf16)
    key = turn(whole(k_ref[...]) + bk_ref[...], 1.0).astype(bf16)
    value = (whole(v_ref[...]) + bv_ref[...]).astype(bf16)
    d_att = whole(da_ref[...])
    place_q = lax.broadcasted_iota(jnp.int32, (tokens, tokens), 0)
    place_k = lax.broadcasted_iota(jnp.int32, (tokens, tokens), 1)
    mask = (seg_q_ref[0] == seg_k_ref[0]) & (place_k <= place_q)
    lane = lax.broadcasted_iota(jnp.int32, (tokens, lanes), 1)
    nt = (((1,), (1,)), ((), ()))
    tn = (((0,), (0,)), ((), ()))
    dot = functools.partial(lax.dot_general, preferred_element_type=f32)
    att = jnp.zeros((tokens, lanes), f32)
    d_query = jnp.zeros((tokens, lanes), f32)
    d_key = jnp.zeros((tokens, lanes), f32)
    d_value = jnp.zeros((tokens, lanes), f32)
    for head in range(lanes // head_size):
        mine = (lane >= head * head_size) & (lane < (head + 1) * head_size)
        q_h = jnp.where(mine, query, jnp.zeros_like(query))
        da_h = jnp.where(mine, d_att, jnp.zeros_like(d_att))
        scores = jnp.where(mask, dot(q_h, key, nt), neg_large)
        top = jnp.max(scores, axis=1, keepdims=True)
        weights = jnp.exp(scores - top)
        probs = weights * (1.0 / jnp.sum(weights, axis=1, keepdims=True))
        probs_low = probs.astype(bf16)
        att_h = jnp.where(mine, dot(probs_low, value, (((1,), (0,)), ((), ()))), 0.0)
        out_dot = jnp.sum(att_h * d_att.astype(f32), axis=1, keepdims=True)
        d_prob = dot(da_h, value, nt)
        d_score = (probs * (d_prob - out_dot)).astype(bf16)
        att = att + att_h
        d_query = d_query + jnp.where(mine, dot(d_score, key, (((1,), (0,)), ((), ()))), 0.0)
        d_key = d_key + dot(d_score, q_h, tn)
        d_value = d_value + dot(probs_low, da_h, tn)
    store(joined_ref, 0, att.astype(bf16))
    grads = (turn(d_query * scale, -1.0), turn(d_key, -1.0), d_value)
    columns = pl.ds(pl.multiple_of(pair * lanes, lanes), lanes)
    for i, grad in enumerate(grads):
        grad = grad.astype(bf16)
        store(d_proj_ref, i * att_rows, grad)
        total = jnp.sum(grad.astype(f32), axis=0, keepdims=True)

        @pl.when(row == 0)
        def _():
            bias_ref[i : i + 1, columns] = total

        @pl.when(row > 0)
        def _():
            bias_ref[i : i + 1, columns] = bias_ref[i : i + 1, columns] + total


def middle(proj, bias, d_joined, rope, seg, n_seq, att_rows, act, head_size):
    rows, tokens = seg.shape
    lanes = 2 * head_size
    pairs = att_rows // lanes
    bf16, f32 = jnp.bfloat16, jnp.float32
    order = (2, n_seq // 2, rows, tokens // n_seq)
    wide = lambda v: v.reshape(order + v.shape[-1:])
    shape = (2, n_seq // 2, 1, tokens // n_seq, lanes)
    block = lambda first: pl.BlockSpec(shape, lambda r, h: (0, 0, r, 0, first + h))
    row = lambda first: pl.BlockSpec((1, lanes), lambda r, h: (0, first + h))
    half = lambda v: pl.BlockSpec(
        (2, n_seq // 2, 1, tokens // n_seq // pairs, v.shape[-1]), lambda r, h: (0, 0, r, h, 0)
    )
    all_of = lambda v: pl.BlockSpec(v.shape, lambda r, h: (0,) * len(v.shape))
    outs = [
        jax.ShapeDtypeStruct(order + (d_joined.shape[-1],), bf16),
        jax.ShapeDtypeStruct(order + (proj.shape[-1],), bf16),
        jax.ShapeDtypeStruct((8, att_rows), f32),
    ]
    proj, d_joined = wide(proj), wide(d_joined)
    joined, d_proj, bias_sums = pl.pallas_call(
        functools.partial(
            middle_kernel,
            head_size=head_size, half_rot=ROT // 2, att_rows=att_rows, act=act,
        ),
        grid=(rows, pairs),
        in_specs=[
            block(0), block(pairs), block(2 * pairs),
            row(0), row(pairs), row(2 * pairs),
            block(0), half(proj), half(d_joined),
            pl.BlockSpec((1, 3, lanes, tokens), lambda r, h: (r, 0, 0, 0)),
            pl.BlockSpec((1, tokens, 1), lambda r, h: (r, 0, 0)),
            pl.BlockSpec((1, 1, tokens), lambda r, h: (r, 0, 0)),
        ],
        out_specs=[all_of(v) for v in outs],
        out_shape=outs,
        compiler_params=pltpu.CompilerParams(vmem_limit_bytes=56 * 2**20),
        name="middle",
    )(
        proj, proj, proj, bias, bias, bias, d_joined, proj, d_joined,
        rope, seg[:, :, None], seg[:, None, :],
    )
    flat = lambda v: v.reshape(rows * tokens, v.shape[-1])
    return flat(joined), flat(d_proj), bias_sums

MESH_ID = pl.DeviceIdType.MESH


def remote(src, dst, send_sem, recv_sem, device):
    return pltpu.make_async_remote_copy(
        src_ref=src,
        dst_ref=dst,
        send_sem=send_sem,
        recv_sem=recv_sem,
        device_id=device,
        device_id_type=MESH_ID,
    )


class Place:
    def __init__(self, n_seq):
        self.n_seq = n_seq
        self.depth = n_seq // 2
        self.p, self.s = lax.axis_index("dp"), lax.axis_index("seq")
        self.y, self.c = self.p // 2, lax.rem(self.p, 2)
        self.z, self.x = self.s // 2, lax.rem(self.s, 2)
        self.p_y = (1 - self.y) * 2 + self.c
        self.p_c = self.y * 2 + 1 - self.c
        self.p_d = (1 - self.y) * 2 + 1 - self.c
        self.to_y = (self.p_y, self.s)
        self.to_c = (self.p_c, self.s)
        self.to_x = (self.p, self.z * 2 + 1 - self.x)
        self.to_up = (self.p, self.s + 2)
        self.to_down = (self.p, self.s - 2)

    def seq(self, hop):
        return lax.rem(self.s + hop + self.n_seq, self.n_seq)

    def meet(self):
        barrier = pltpu.get_barrier_semaphore()

        def greet(hop, carry):
            pl.semaphore_signal(
                barrier, inc=1, device_id=(self.p, self.seq(hop)), device_id_type=MESH_ID
            )
            return carry

        lax.fori_loop(1, self.n_seq, greet, 0)
        for device in (self.to_y, self.to_c):
            pl.semaphore_signal(barrier, inc=1, device_id=device, device_id_type=MESH_ID)
        pl.semaphore_wait(barrier, self.n_seq + 1)


class Spread:
    def __init__(self, at, own, full, sems):
        self.at, self.own, self.full, self.sems = at, own, full, sems

    def along(self, src, up, ref=None):
        sems, at = self.sems, self.at
        here = self.full.at[at.x, src]
        return remote(
            here if ref is None else ref,
            here,
            sems.at[0 if up else 1, src],
            sems.at[3, src],
            at.to_up if up else at.to_down,
        )

    def across(self, src, ref=None):
        sems, at = self.sems, self.at
        here = self.full.at[at.x, src]
        return remote(here if ref is None else ref, here, sems.at[2, src], sems.at[4, src], at.to_x)

    def local(self):
        return pltpu.make_async_copy(
            self.own, self.full.at[self.at.x, self.at.z], self.sems.at[5, 0]
        )

    def begin_across(self):
        self.across(self.at.z, self.own).start()
        self.local().start()

    def begin_along(self):
        at = self.at

        @pl.when(at.z < at.depth - 1)
        def _():
            self.along(at.z, True, self.own).start()

        @pl.when(at.z > 0)
        def _():
            self.along(at.z, False, self.own).start()

    def step(self, hop):
        at = self.at

        @pl.when(at.z - hop >= 0)
        def _():
            src = at.z - hop
            self.along(src, True).wait_recv()

            @pl.when(at.z < at.depth - 1)
            def _():
                self.along(src, True).start()

            self.across(src).start()

        @pl.when(at.z + hop < at.depth)
        def _():
            src = at.z + hop
            self.along(src, False).wait_recv()

            @pl.when(at.z > 0)
            def _():
                self.along(src, False).start()

            self.across(src).start()

    def arrive(self):
        at = self.at
        for src in range(at.depth):
            here = self.full.at[1 - at.x, src]
            remote(here, here, self.sems.at[2, src], self.sems.at[4, src], at.to_x).wait_recv()
        self.local().wait()

    def sent(self):
        at = self.at
        for src in range(at.depth):
            self.across(src).wait_send()

            @pl.when((at.z < at.depth - 1) & (src <= at.z))
            def _():
                self.along(src, True).wait_send()

            @pl.when((at.z > 0) & (src >= at.z))
            def _():
                self.along(src, False).wait_send()


class Fan:
    def __init__(self, at, pick, sems):
        self.at, self.pick, self.sems = at, pick, sems

    def y(self, k, ref=None):
        at = self.at
        here = self.pick(at.p, k)
        return remote(here if ref is None else ref, here, self.sems.at[0, k], self.sems.at[1, k], at.to_y)

    def core(self, k, ref=None):
        at = self.at
        here = self.pick(at.p, k)
        return remote(here if ref is None else ref, here, self.sems.at[2, k], self.sems.at[3, k], at.to_c)

    def pass_on(self, k):
        at = self.at
        here = self.pick(at.p_y, k)
        return remote(here, here, self.sems.at[4, k], self.sems.at[5, k], at.to_c)

    def from_y(self, k):
        here = self.pick(self.at.p_y, k)
        return remote(here, here, self.sems.at[0, k], self.sems.at[1, k], self.at.to_y)

    def from_core(self, k):
        here = self.pick(self.at.p_c, k)
        return remote(here, here, self.sems.at[2, k], self.sems.at[3, k], self.at.to_c)

    def from_diagonal(self, k):
        here = self.pick(self.at.p_d, k)
        return remote(here, here, self.sems.at[4, k], self.sems.at[5, k], self.at.to_c)


def loop(low, high, body):
    def step(k, carry):
        body(k)
        return carry

    lax.fori_loop(low, high, step, 0)


def gather_kernel(
    x_ref, g_ref, w_ref, o_ref, tile_ref,
    x_full, g_full, w_full, o_full, tiles, hidden, out_mine, proj, d_joined,
    x_block, hid, w_near, p_block, g_near, o_near, t_near, small,
    x_sems, g_sems, w_sems, w_fan_sems, o_sems, o_fan_sems, t_sems, t_fan_sems, local_sems,
    x_in_sems, hid_sems, w_in_sems, p_sems, g_in_sems, o_in_sems,
    *, n_seq, late, lead,
):
    at = Place(n_seq)
    depth = at.depth
    bf16, f32 = jnp.bfloat16, jnp.float32
    own, width = o_ref.shape
    att = own + lead
    first_act = own - lead
    body, extra = pl.ds(0, own), pl.ds(own, late)
    x_go = Spread(at, x_ref, x_full, x_sems)
    g_go = Spread(at, g_ref, g_full, g_sems)
    w_fan = Fan(at, lambda p, k: w_full.at[p, k], w_fan_sems)
    o_fan = Fan(at, lambda p, k: o_full.at[p, body if k == 0 else extra], o_fan_sems)
    t_fan = Fan(at, lambda p, k: tiles.at[p], t_fan_sems)

    def w_send(hop):
        to = at.seq(hop)
        return remote(w_ref.at[to], w_full.at[at.p, at.s], w_sems.at[0, to], w_sems.at[1, at.s], (at.p, to))

    def w_recv(hop):
        src = at.seq(-hop)
        here = w_full.at[at.p, src]
        return remote(here, here, w_sems.at[0, src], w_sems.at[1, src], (at.p, src))

    def t_send(hop):
        to = at.seq(hop)
        return remote(tile_ref, tiles.at[at.p, at.s], t_sems.at[0, to], t_sems.at[1, at.s], (at.p, to))

    def t_recv(hop):
        src = at.seq(-hop)
        here = tiles.at[at.p, src]
        return remote(here, here, t_sems.at[0, src], t_sems.at[1, src], (at.p, src))

    w_local = pltpu.make_async_copy(w_ref.at[at.s], w_full.at[at.p, at.s], local_sems.at[0])
    o_local = pltpu.make_async_copy(o_ref, o_full.at[at.p, body], local_sems.at[1])
    t_local = pltpu.make_async_copy(tile_ref, tiles.at[at.p, at.s], local_sems.at[2])
    head = o_ref.at[pl.ds(0, late)]
    o_send = remote(
        head, o_full.at[at.p, extra], o_sems.at[0], o_sems.at[1], (at.p, at.seq(-1))
    )

    def place(i):
        return lax.rem(at.x + i // depth, 2), lax.rem(at.z + i, depth)

    def block_in(i):
        col, deep = place(i)
        return pltpu.make_async_copy(x_full.at[col, deep], x_block, x_in_sems.at[0])

    def hid_out(i):
        col, deep = place(i)
        return pltpu.make_async_copy(hid.at[col, deep], hidden.at[col, deep], hid_sems.at[i])

    def norm_block(i):
        col, deep = place(i)

        @pl.when(i >= depth)
        def _():
            here = x_full.at[1 - at.x, deep]
            remote(here, here, x_sems.at[2, deep], x_sems.at[4, deep], at.to_x).wait_recv()

        block_in(i).start()
        block_in(i).wait()
        some = 32

        def rows(k):
            part = pl.ds(pl.multiple_of(lax.rem(k, 2) * some, some), some)
            v = x_block[k // 2, part, :].astype(f32)
            centered = v - jnp.mean(v, axis=-1, keepdims=True)
            inv_std = lax.rsqrt(jnp.mean(centered * centered, axis=-1, keepdims=True) + norm_eps)
            done = centered * inv_std * small[0:1, :] + small[1:2, :]
            hid[col, deep, pl.ds(pl.multiple_of(k * some, some), some), :] = done.astype(bf16)

        loop(0, hid.shape[2] // some, rows)
        hid_out(i).start()

    def w_in(p, k):
        return pltpu.make_async_copy(w_full.at[p], w_near.at[p], w_in_sems.at[k])

    def g_in():
        return pltpu.make_async_copy(g_full, g_near, g_in_sems.at[0])

    def o_in(k):
        last = at.s == n_seq - 1
        lead_at = pl.multiple_of(lead * at.s, 16)
        late_at = pl.multiple_of(late - lead * at.s, 16)
        src, dst, count = [
            (o_full.at[0, pl.ds(lead_at, att - late)], 0, att - late),
            (o_full.at[0, pl.ds(lead_at + (att - late), late)], att - late, late),
            (o_full.at[1, pl.ds(late_at, first_act)], att, first_act),
            (o_full.at[2, body], 2 * att, own),
            (o_full.at[3, body], 3 * att, own),
            (o_full.at[1, extra], att - late, late),
        ][k]
        return pltpu.make_async_copy(src, o_near.at[pl.ds(dst, count)], o_in_sems.at[k])

    step_rows = p_block.shape[1]
    steps = hid.shape[0] * depth * hid.shape[2] // step_rows
    per_block = step_rows // hid.shape[2]

    def p_out(k):
        return pltpu.make_async_copy(
            p_block.at[lax.rem(k, 2)],
            proj.at[pl.ds(pl.multiple_of(k * step_rows, step_rows), step_rows)],
            p_sems.at[lax.rem(k, 2)],
        )

    def project(k):
        @pl.when(k >= 2)
        def _():
            p_out(k - 2).wait()

        rows = per_block * k
        left = hid[rows // depth, pl.ds(lax.rem(rows, depth), per_block)]
        left = left.reshape(step_rows, width)
        columns = p_block.shape[2]
        for n in range(0, columns, 512):
            some = min(512, columns - n)
            right = w_near[:, :, :, n : n + some].reshape(width, some)
            p_block[lax.rem(k, 2), :, n : n + some] = jnp.dot(
                left, right, preferred_element_type=f32
            )
        p_out(k).start()

    def join_back(k):
        rows = per_block * k
        left = g_near[rows // depth, pl.ds(lax.rem(rows, depth), per_block)]
        left = left.reshape(step_rows, width)
        d_joined[pl.ds(pl.multiple_of(k * step_rows, step_rows), step_rows), :] = (
            lax.dot_general(
                left, o_near[...], (((1,), (1,)), ((), ())), preferred_element_type=f32
            ).astype(bf16)
        )

    at.meet()
    x_go.begin_along()
    x_go.begin_across()
    g_go.begin_across()
    loop(1, n_seq, lambda hop: t_send(hop).start())
    t_local.start()
    w_fan.y(at.s, w_ref.at[at.s]).start()
    w_fan.core(at.s, w_ref.at[at.s]).start()
    w_local.start()
    o_fan.y(0, o_ref).start()
    o_fan.core(0, o_ref).start()
    o_local.start()
    w_send(1).start()
    w_send(n_seq - 1).start()
    for hop in range(1, depth):
        x_go.step(hop)
        if hop == 1:
            t_local.wait()
            loop(1, n_seq, lambda k: t_recv(k).wait_recv())
            t_fan.y(0).start()
            t_fan.core(0).start()
        if hop == 2:
            t_fan.from_y(0).wait_recv()
            t_fan.pass_on(0).start()
        w_send(hop + 1).start()
        if hop + 1 < n_seq - hop - 1:
            w_send(n_seq - hop - 1).start()
    g_go.begin_along()

    @pl.when(at.y == 0)
    def _():
        o_send.start()

    t_fan.from_core(0).wait_recv()
    t_fan.from_diagonal(0).wait_recv()
    t_load = pltpu.make_async_copy(tiles, t_near, local_sems.at[3])
    t_load.start()
    t_load.wait()
    for p in range(t_near.shape[0]):
        for pair in range(n_seq // 2):
            two = t_near[p, 2 * pair, 0:8] + t_near[p, 2 * pair + 1, 0:8]
            lanes = two.shape[1]
            first = (p * (n_seq // 2) + pair) * lanes
            small[:, first : first + lanes] = two
    for k, some in enumerate((first_act, own, own)):
        o_near[(k + 1) * att + some : (k + 2) * att, :] = jnp.zeros((att - some, width), bf16)
    x_go.local().wait()

    def w_step(hop):
        src = at.seq(-hop)
        w_recv(hop).wait_recv()
        w_fan.y(src).start()
        w_fan.core(src).start()
        norm_block(hop - 1)

    loop(1, n_seq, w_step)
    norm_block(n_seq - 1)
    w_local.wait()
    w_in(at.p, 0).start()
    def w_pass(hop):
        src = at.seq(-hop)
        w_fan.from_y(src).wait_recv()
        w_fan.pass_on(src).start()

    for hop in range(1, depth):
        g_go.step(hop)
        loop((hop - 1) * 3, min(hop * 3, n_seq), w_pass)
        if hop == 1:

            @pl.when(at.y == 0)
            def _():
                o_send.wait_recv()
                o_fan.y(1).start()
                o_fan.core(1).start()

    loop((depth - 1) * 3, n_seq, w_pass)
    w_in(at.p_y, 1).start()

    def w_last(k):
        w_fan.from_core(k).wait_recv()
        w_fan.from_diagonal(k).wait_recv()

    loop(0, n_seq, w_last)
    w_in(at.p_c, 2).start()
    w_in(at.p_d, 3).start()
    o_fan.from_y(0).wait_recv()
    o_fan.pass_on(0).start()

    @pl.when(at.y == 1)
    def _():
        o_fan.from_y(1).wait_recv()
        o_fan.pass_on(1).start()

    for k, p in enumerate((at.p, at.p_y, at.p_c, at.p_d)):
        w_in(p, k).wait()
    loop(0, steps, project)

    o_local.wait()
    o_fan.from_core(0).wait_recv()
    o_fan.from_diagonal(0).wait_recv()

    @pl.when(at.y == 0)
    def _():
        o_fan.from_core(1).wait_recv()

    @pl.when(at.y == 1)
    def _():
        o_fan.from_diagonal(1).wait_recv()

    for k in (0, 2, 3, 4):
        o_in(k).start()

    @pl.when(at.s < n_seq - 1)
    def _():
        o_in(1).start()
        o_in(1).wait()

    @pl.when(at.s == n_seq - 1)
    def _():
        o_in(5).start()
        o_in(5).wait()

    for k in (0, 2, 3, 4):
        o_in(k).wait()
    o_out = pltpu.make_async_copy(o_near, out_mine, o_in_sems.at[6])
    o_out.start()
    g_go.arrive()
    g_in().start()
    g_in().wait()
    loop(0, steps, join_back)

    o_out.wait()
    loop(steps - 2, steps, lambda k: p_out(k).wait())
    loop(0, n_seq, lambda i: hid_out(i).wait())
    x_go.sent()
    g_go.sent()

    def w_sent(k):
        w_fan.y(k).wait_send()
        w_fan.core(k).wait_send()
        w_fan.pass_on(k).wait_send()

    loop(0, n_seq, w_sent)

    def seq_sent(hop):
        w_send(hop).wait_send()
        t_send(hop).wait_send()

    loop(1, n_seq, seq_sent)
    for fan in (t_fan, o_fan):
        fan.y(0).wait_send()
        fan.core(0).wait_send()
        fan.pass_on(0).wait_send()

    @pl.when(at.y == 0)
    def _():
        o_send.wait_send()
        o_fan.y(1).wait_send()
        o_fan.core(1).wait_send()

    @pl.when(at.y == 1)
    def _():
        o_fan.pass_on(1).wait_send()


def gather_all(n_dp, n_seq, late, lead, x, g, w, o, tile):
    depth = n_seq // 2
    own, width = o.shape
    block = x.shape[0] * x.shape[1]
    tokens = n_seq * block
    columns = w.shape[2]
    mine = n_dp * (own + lead)
    bf16, f32 = jnp.bfloat16, jnp.float32
    rest, near = pl.BlockSpec(memory_space=pl.ANY), pl.BlockSpec(memory_space=pltpu.VMEM)
    dma = pltpu.SemaphoreType.DMA
    like = lambda lead, ref: jax.ShapeDtypeStruct(lead + ref.shape, ref.dtype)
    return pl.pallas_call(
        functools.partial(gather_kernel, n_seq=n_seq, late=late, lead=lead),
        in_specs=[rest] * 5,
        out_specs=[rest] * 8 + [near],
        out_shape=[
            like((2, depth), x),
            like((2, depth), g),
            jax.ShapeDtypeStruct((n_dp,) + w.shape, w.dtype),
            jax.ShapeDtypeStruct((n_dp, own + late, width), o.dtype),
            like((n_dp, n_seq), tile),
            jax.ShapeDtypeStruct((2, depth, block, width), bf16),
            jax.ShapeDtypeStruct((mine, width), bf16),
            jax.ShapeDtypeStruct((tokens, columns), f32),
            jax.ShapeDtypeStruct((tokens, mine), bf16),
        ],
        scratch_shapes=[
            pltpu.VMEM(x.shape, bf16),
            pltpu.VMEM((2, depth, block, width), bf16),
            pltpu.VMEM((n_dp,) + w.shape, bf16),
            pltpu.VMEM((2, 2 * block, columns), f32),
            pltpu.VMEM((2, depth) + g.shape, bf16),
            pltpu.VMEM((mine, width), bf16),
            pltpu.VMEM((n_dp, n_seq) + tile.shape, f32),
            pltpu.VMEM((8, width), f32),
            dma((6, depth)), dma((6, depth)), dma((2, n_seq)), dma((6, n_seq)),
            dma((2,)), dma((6, 2)), dma((2, n_seq)), dma((6, 1)), dma((4,)),
            dma((1,)), dma((n_seq,)), dma((4,)), dma((2,)), dma((1,)), dma((7,)),
        ],
        compiler_params=pltpu.CompilerParams(
            collective_id=0, has_side_effects=True, vmem_limit_bytes=56 * 2**20
        ),
        name="gather_all",
    )(x, g, w, o, tile)

def add_rows(out, terms, rows=32):
    count = out.shape[0]

    def some(k):
        at = pl.ds(pl.multiple_of(k * rows, rows), rows)
        total = terms[0][at].astype(jnp.float32)
        for term in terms[1:]:
            total = total + term[at].astype(jnp.float32)
        out[at] = total.astype(out.dtype)

    loop(0, count // rows, some)


def reduce_kernel(
    d_ref, in_ref, d_proj_ref, joined_ref, hidden_ref, g_ref, w_ref, o_ref,
    normed_ref, small_ref,
    sums, in_sum, out_sum, out_prev, small_sum,
    own_parts, x_got, z_got, in_own, in_core, in_y, out_own, out_core, out_y,
    small_own, small_core, small_y, small_seq,
    d_near, j_near, h_near, g_near, w_near, o_near, b_ref, out_ref,
    load_sems, x_sems, z_sems, in_core_sems, in_y_sems, in_sems, out_sems, small_sems, local_sem,
    w_sems, o_sems,
    *, n_seq, late, first_act, keep, plan,
):
    at = Place(n_seq)
    depth = at.depth
    parts = (d_ref, b_ref)
    main = out_own.shape[1] - late
    body, extra = pl.ds(0, main), pl.ds(main, late)
    y, c, z, x, s = at.y, at.c, at.z, at.x, at.s

    loads = [
        pltpu.make_async_copy(d_proj_ref, d_near, load_sems.at[0]),
        pltpu.make_async_copy(joined_ref, j_near, load_sems.at[1]),
        pltpu.make_async_copy(g_ref, g_near, load_sems.at[2]),
    ]
    feats = h_near.shape[4]
    for y_to in range(2):
        first = pl.multiple_of((2 * y_to + c) * feats, feats)
        loads.append(
            pltpu.make_async_copy(
                hidden_ref.at[:, :, :, pl.ds(first, feats)], h_near.at[y_to], load_sems.at[3 + y_to]
            )
        )
    dot = functools.partial(lax.dot_general, preferred_element_type=jnp.float32)
    low = jnp.bfloat16
    block_rows, width = own_parts.shape[2:]
    flat = lambda v: v.reshape(-1, v.shape[-1])

    def w_load(i):
        some = w_near.shape[1]
        return pltpu.make_async_copy(
            w_ref.at[pl.ds(pl.multiple_of(i * some, some), some)],
            w_near.at[lax.rem(i, 2)], w_sems.at[lax.rem(i, 2)],
        )

    def o_load(i):
        some = o_near.shape[2]
        return pltpu.make_async_copy(
            o_ref.at[:, pl.ds(pl.multiple_of(i * some, some), some)],
            o_near.at[lax.rem(i, 2)], o_sems.at[lax.rem(i, 2)],
        )

    def streamed(out, load, count, some, product):
        load(0).start()

        def one(i):
            @pl.when(i + 1 < count)
            def _():
                load(i + 1).start()

            load(i).wait()
            done = product(lax.rem(i, 2)).astype(low)
            columns = pl.ds(pl.multiple_of(i * some, some), some)
            out[:, :, columns] = done.reshape(depth, block_rows, some)

        loop(0, count, one)

    def work(i):
        if i == 0:
            some = w_near.shape[1]
            left = flat(d_near[x])
            streamed(
                own_parts.at[0], w_load, width // some, some,
                lambda k: dot(left, w_near[k], (((1,), (1,)), ((), ()))),
            )
        elif i in (1, 5):
            some = o_near.shape[2]
            left = flat(j_near[x if i == 1 else 1 - x])
            streamed(
                own_parts.at[1] if i == 1 else b_ref, o_load, width // some, some,
                lambda k: dot(left, o_near[k], (((1,), (0,)), ((), ()))),
            )
        elif i < 4:
            y_to = 1 - y if i == 2 else y
            left = flat(h_near[y_to])
            right = flat(d_near[...])
            total = right.shape[1]
            for first in range(0, total, 256):
                some = min(256, total - first)
                done = dot(left, right[:, first : first + some], (((0,), (0,)), ((), ())))
                in_own[y_to, :, :, first : first + some] = done.astype(low).reshape(
                    n_seq, -1, some
                )
        else:
            core = c if i == 4 else 1 - c
            for first in range(0, width, width // 4):
                at_n = slice(first, first + width // 4)
                right = flat(g_near[:, :, :, at_n])
                for y_to in range(2):
                    columns = pl.ds(pl.multiple_of((2 * y_to + core) * main, main), main)
                    done = dot(flat(j_near[:, :, :, columns]), right, (((0,), (0,)), ((), ())))
                    if i == 4:
                        out_own[y_to, body, at_n] = done.astype(low)
                    else:
                        out_ref[y_to * main : (y_to + 1) * main, at_n] = done.astype(low)
                if i == 4:
                    out_own[0, extra, at_n] = dot(
                        flat(j_near[:, :, :, keep : keep + late]), right, (((0,), (0,)), ((), ()))
                    ).astype(low)
            if i == 6:
                out_ref[2 * main :] = out_own[0, extra]

    def in_to_core(y_to, k):
        return remote(
            in_ref.at[y_to, k], in_core.at[y_to, k],
            in_core_sems.at[0, y_to, k], in_core_sems.at[1, y_to, k], at.to_c,
        )

    def out_to_core(y_to):
        return remote(
            out_ref.at[pl.ds(pl.multiple_of(y_to * main, main), main)], out_core.at[y_to, body],
            out_sems.at[0, y_to], out_sems.at[1, y_to], at.to_c,
        )

    extra_to_core = remote(
        out_ref.at[pl.ds(2 * main, late)], out_core.at[0, extra],
        out_sems.at[0, 2], out_sems.at[1, 2], at.to_c,
    )

    def to_across(kind, k):
        return remote(
            parts[kind].at[k], x_got.at[kind, k],
            x_sems.at[0, kind, k], x_sems.at[1, kind, k], at.to_x,
        )

    def to_up(kind, k):
        return remote(
            x_got.at[kind, k], z_got.at[kind, k],
            z_sems.at[0, kind, k], z_sems.at[1, kind, k], at.to_up,
        )

    def to_down(kind, k):
        slot = jnp.where(k == z - 1, depth, k)
        return remote(
            x_got.at[kind, k], z_got.at[kind, slot],
            z_sems.at[0, kind, k], z_sems.at[1, kind, slot], at.to_down,
        )

    def from_depth(kind, slot):
        here = z_got.at[kind, slot]
        return remote(here, here, z_sems.at[0, kind, slot], z_sems.at[1, kind, slot], at.to_up)

    def in_to_y(k):
        return remote(
            in_core.at[1 - y, k], in_y.at[k], in_y_sems.at[0, k], in_y_sems.at[1, k], at.to_y
        )

    def in_to_owner(k):
        return remote(
            in_core.at[y, k], in_sum.at[s], in_sems.at[0, k], in_sems.at[1, s], (at.p, k)
        )

    def in_from(k):
        here = in_sum.at[k]
        return remote(here, here, in_sems.at[0, k], in_sems.at[1, k], (at.p, k))

    in_keep = pltpu.make_async_copy(in_core.at[y, s], in_sum.at[s], local_sem.at[0])
    out_to_y = remote(
        out_core.at[1 - y, body], out_y.at[body], out_sems.at[0, 3], out_sems.at[1, 3], at.to_y
    )
    extra_to_y = remote(
        out_core.at[0, extra], out_y.at[extra], out_sems.at[0, 4], out_sems.at[1, 4], at.to_y
    )

    def out_shift(start):
        return remote(
            out_sum.at[pl.ds(start, late)], out_prev,
            out_sems.at[0, 5], out_sems.at[1, 5], (at.p, at.seq(1)),
        )

    small_to_core = remote(small_own, small_core, small_sems.at[0, 0], small_sems.at[1, 0], at.to_c)
    small_to_y = remote(small_core, small_y, small_sems.at[0, 1], small_sems.at[1, 1], at.to_y)

    def small_to(hop):
        to = at.seq(hop)
        first = (at.p * n_seq + to) // 2 * lanes
        return remote(
            small_y.at[:, pl.ds(pl.multiple_of(first, lanes), lanes)], small_seq.at[s],
            small_sems.at[0, 2 + to], small_sems.at[1, 2 + s], (at.p, to),
        )

    def small_from(hop):
        src = at.seq(-hop)
        here = small_seq.at[src]
        return remote(
            here, here, small_sems.at[0, 2 + src], small_sems.at[1, 2 + src], (at.p, src)
        )

    chained, steps = plan
    lanes = small_sum.shape[1]

    def around_z(hop):
        return lax.rem(z + hop, depth)

    def to_depth(kind, k):
        return remote(
            x_got.at[kind, k], z_got.at[kind, z],
            z_sems.at[0, kind, k], z_sems.at[1, kind, z], (at.p, 2 * k + x),
        )

    def turn(i):
        return jnp.where(lax.rem(i, 2) == 0, depth - 1 - i // 2, i // 2)

    def order(kind, i):
        return turn(i) if chained[kind] else around_z(i + 1)

    def across(j):
        to_across(j // depth, order(j // depth, j % depth)).start()

    def straight(kind, i):
        k = around_z(i + 1)
        to_across(kind, k).wait_recv()
        add_rows(x_got.at[kind, k], [x_got.at[kind, k], own_parts.at[kind, k]])
        if i + 1 < depth:
            to_depth(kind, k).start()

    def chain(kind, i):
        k = turn(i)
        to_across(kind, k).wait_recv()
        got, mine = x_got.at[kind, k], own_parts.at[kind, k]
        begins = ((z == 0) & (k > 0)) | ((z == depth - 1) & (k < depth - 1)) | (z == k)

        @pl.when(begins)
        def _():
            add_rows(got, [got, mine])

        @pl.when(jnp.logical_not(begins))
        def _():
            from_depth(kind, k).wait_recv()
            add_rows(got, [got, mine, z_got.at[kind, k]])

        @pl.when(z < k)
        def _():
            to_up(kind, k).start()

        @pl.when(z > k)
        def _():
            to_down(kind, k).start()

    def finish(kind):
        if not chained[kind]:
            others = [around_z(hop) for hop in range(1, depth)]
            for k in others:
                from_depth(kind, k).wait_recv()
            add_rows(
                sums.at[kind], [x_got.at[kind, z]] + [z_got.at[kind, k] for k in others], rows=16
            )
            return
        add_rows(sums.at[kind], [x_got.at[kind, z]], rows=16)

        @pl.when(z > 0)
        def _():
            from_depth(kind, z).wait_recv()
            add_rows(sums.at[kind], [sums.at[kind], z_got.at[kind, z]], rows=16)

        @pl.when(z < depth - 1)
        def _():
            from_depth(kind, depth).wait_recv()
            add_rows(sums.at[kind], [sums.at[kind], z_got.at[kind, depth]], rows=16)

    def to_y_step(hop):
        k = at.seq(hop)
        in_to_core(1 - y, k).wait_recv()
        add_rows(in_core.at[1 - y, k], [in_core.at[1 - y, k], in_own.at[1 - y, k]])
        in_to_y(k).start()

    def owner_step(hop):
        k = at.seq(hop)
        in_to_core(y, k).wait_recv()
        in_to_y(k).wait_recv()
        add_rows(in_core.at[y, k], [in_core.at[y, k], in_own.at[y, k], in_y.at[k]])

        @pl.when(k != s)
        def _():
            in_to_owner(k).start()

        @pl.when(k == s)
        def _():
            in_keep.start()

    def out_y_step():
        out_to_core(1 - y).wait_recv()
        extra_to_core.wait_recv()
        add_rows(out_core.at[1 - y, body], [out_core.at[1 - y, body], out_own.at[1 - y, body]])
        out_to_y.start()

        @pl.when(y == 1)
        def _():
            add_rows(out_core.at[0, extra], [out_core.at[0, extra], out_own.at[0, extra]])
            extra_to_y.start()

    def out_end():
        out_to_core(y).wait_recv()
        out_to_y.wait_recv()
        add_rows(out_sum.at[body], [out_core.at[y, body], out_own.at[y, body], out_y.at[body]])

        @pl.when(y == 0)
        def _():
            extra_to_y.wait_recv()
            add_rows(
                out_sum.at[extra], [out_core.at[0, extra], out_own.at[0, extra], out_y.at[extra]]
            )

            @pl.when(c == 0)
            def _():
                out_shift(keep).start()

            @pl.when((c == 1) & (s == n_seq - 1))
            def _():
                out_shift(main).start()

            @pl.when((c == 1) & (s < n_seq - 1))
            def _():
                out_shift(first_act - late).start()

    def small_step(i):
        if i == 0:
            finish(0)
            small_own[...] = small_ref[...]
            d_hidden = sums[0]
            small_own[0:1, :] = jnp.sum(d_hidden * normed_ref[...], axis=0, keepdims=True)
            small_own[1:2, :] = jnp.sum(d_hidden, axis=0, keepdims=True)
            small_to_core.start()
        elif i == 1:
            small_to_core.wait_recv()
            small_core[...] = small_core[...] + small_own[...]
            small_to_y.start()
        elif i == 2:
            small_to_y.wait()
            small_y[...] = small_core[...] + small_y[...]
            loop(1, n_seq, lambda hop: small_to(hop).start())
        else:
            first = (at.p * n_seq + s) // 2 * lanes
            small_sum[...] = small_y[:, pl.ds(pl.multiple_of(first, lanes), lanes)]

            def small_add(hop):
                small_from(hop).wait_recv()
                small_sum[...] = small_sum[...] + small_seq[at.seq(-hop)]

            loop(1, n_seq, small_add)

    def core_step(i):
        if i == 0:
            loop(0, n_seq, lambda hop: in_to_core(1 - y, at.seq(hop)).start())
            for load in loads:
                load.start()
        elif i == 1:
            loop(0, n_seq, lambda hop: in_to_core(y, at.seq(hop)).start())
        elif i == 2:
            out_to_core(1 - y).start()
            out_to_core(y).start()
            extra_to_core.start()
        else:
            for load in loads:
                load.wait()

    at.meet()
    for what, i in steps:
        if what == 0:
            across(i)
        elif what == 1:
            core_step(i)
        elif what == 2:
            to_y_step(i)
        elif what == 3:
            owner_step(i)
        elif what == 4:
            kind = i // depth
            (chain if chained[kind] else straight)(kind, i % depth)
        elif what == 5:
            small_step(i)
        elif what == 7:
            work(i)
        elif i == 0:
            out_y_step()
        else:
            out_end()
    finish(1)

    @pl.when(y == 0)
    def _():
        out_shift(0).wait()

    def in_last(hop):
        k = at.seq(hop)
        in_from(k).wait_recv()
        in_to_owner(k).wait_send()

    loop(1, n_seq, in_last)
    in_keep.wait()

    def seq_sent(k):
        for y_to in range(2):
            in_to_core(y_to, k).wait_send()
        in_to_y(k).wait_send()

    loop(0, n_seq, seq_sent)
    loop(1, n_seq, lambda hop: small_to(hop).wait_send())
    small_to_core.wait_send()
    for y_to in range(2):
        out_to_core(y_to).wait_send()
    extra_to_core.wait_send()
    out_to_y.wait_send()

    @pl.when(y == 1)
    def _():
        extra_to_y.wait_send()

    for kind in range(2):
        for k in range(depth):
            to_across(kind, k).wait_send()

            @pl.when(z < k)
            def _():
                (to_up if chained[kind] else to_depth)(kind, k).wait_send()

            @pl.when(z > k)
            def _():
                (to_down if chained[kind] else to_depth)(kind, k).wait_send()


def reduce_all(
    plan, n_dp, n_seq, late, first_act, keep, sent, d_proj, joined, hidden, g, w, o, normed, small
):
    depth = n_seq // 2
    d_sent, in_sent = sent
    block = d_sent.shape[1:]
    in_block = in_sent.shape[2:]
    width = block[1]
    main = joined.shape[-1] // n_dp
    slot = main + late
    bf16, f32 = jnp.bfloat16, jnp.float32
    rest, near = pl.BlockSpec(memory_space=pl.ANY), pl.BlockSpec(memory_space=pltpu.VMEM)
    dma = pltpu.SemaphoreType.DMA
    return pl.pallas_call(
        functools.partial(
            reduce_kernel, n_seq=n_seq, late=late, first_act=first_act, keep=keep, plan=plan
        ),
        in_specs=[rest] * 8 + [near, near],
        out_specs=[near, rest, near, rest, near],
        out_shape=[
            jax.ShapeDtypeStruct((2,) + block, f32),
            jax.ShapeDtypeStruct((n_seq,) + in_block, bf16),
            jax.ShapeDtypeStruct((slot, width), bf16),
            jax.ShapeDtypeStruct((late, width), bf16),
            jax.ShapeDtypeStruct((small.shape[0], 128), f32),
        ],
        scratch_shapes=[
            pltpu.VMEM((2, depth) + block, bf16),
            pltpu.VMEM((2, depth) + block, bf16),
            pltpu.VMEM((2, depth + 1) + block, bf16),
            pltpu.VMEM((2, n_seq) + in_block, bf16),
            pltpu.VMEM((2, n_seq) + in_block, bf16),
            pltpu.VMEM((n_seq,) + in_block, bf16),
            pltpu.VMEM((2, slot, width), bf16),
            pltpu.VMEM((2, slot, width), bf16),
            pltpu.VMEM((slot, width), bf16),
            pltpu.VMEM(small.shape, f32),
            pltpu.VMEM(small.shape, f32),
            pltpu.VMEM(small.shape, f32),
            pltpu.VMEM((n_seq, small.shape[0], 128), f32),
            pltpu.VMEM(d_proj.shape, bf16),
            pltpu.VMEM(joined.shape, bf16),
            pltpu.VMEM((2,) + hidden.shape[:3] + (width // n_dp,), bf16),
            pltpu.VMEM(g.shape, bf16),
            pltpu.VMEM((2, 256, w.shape[1]), bf16),
            pltpu.VMEM((2, o.shape[0], 256), bf16),
            pltpu.VMEM((depth,) + block, bf16),
            pltpu.VMEM((2 * main + late, width), bf16),
            dma((7,)), dma((2, 2, depth)), dma((2, 2, depth + 1)), dma((2, 2, n_seq)), dma((2, n_seq)),
            dma((2, n_seq)), dma((2, 6)), dma((2, 2 + n_seq)), dma((1,)), dma((2,)), dma((2,)),
        ],
        compiler_params=pltpu.CompilerParams(
            collective_id=1, has_side_effects=True, vmem_limit_bytes=60 * 2**20
        ),
        name="reduce_all",
    )(*sent, d_proj, joined, hidden, g, w, o, normed, small)

def shares(n_seq, width, ffn, att, act):
    stretches, at = [], 0
    for i in range(3):
        stretches.append((i * width, at, att))
        at += att
    for half in range(2):
        first = 3 * width + half * ffn
        for some in act:
            stretches.append((first, at, some))
            at += some
            first += some * n_seq
    return stretches


def share_kernel(w_ref, out_ref, *, stretches):
    for s in range(out_ref.shape[0]):
        parts = [w_ref[:, first + s * some : first + (s + 1) * some] for first, _, some in stretches]
        out_ref[s] = jnp.concatenate(parts, axis=1).astype(out_ref.dtype)


def share_out(weight, n_seq, stretches):
    rows, columns = weight.shape
    step = 16
    return pl.pallas_call(
        functools.partial(share_kernel, stretches=stretches),
        grid=(rows // step,),
        in_specs=[pl.BlockSpec((step, columns), lambda i: (i, 0))],
        out_specs=pl.BlockSpec((n_seq, step, columns // n_seq), lambda i: (0, i, 0)),
        out_shape=jax.ShapeDtypeStruct((n_seq, rows, columns // n_seq), jnp.bfloat16),
        compiler_params=pltpu.CompilerParams(vmem_limit_bytes=56 * 2**20),
        name="share_out",
    )(weight)


def update_kernel(
    sum_ref, w_ref, m_ref, v_ref, a_ref, w_out, v_out, a_out, g_out, *, stretches, rate, decay
):
    n_seq = sum_ref.shape[0]
    for first, at, some in stretches:
        columns = slice(first, first + n_seq * some)
        parts = [sum_ref[s, :, at : at + some].astype(jnp.float32) for s in range(n_seq)]
        gradient = jnp.concatenate(parts, axis=1)
        g_out[:, columns] = gradient
        w_out[:, columns], v_out[:, columns], a_out[:, columns] = adam_update(
            w_ref[:, columns], m_ref[:, columns], v_ref[:, columns], a_ref[:, columns],
            gradient, rate, decay,
        )


def update_in(sums, weight, first, second, average, stretches):
    n_seq, rows, share = sums.shape
    step = 16
    wide = pl.BlockSpec((step, weight.shape[1]), lambda i: (i, 0))
    out = jax.ShapeDtypeStruct(weight.shape, jnp.float32)
    return pl.pallas_call(
        functools.partial(
            update_kernel, stretches=stretches, rate=matrix_rate, decay=weight_decay
        ),
        grid=(rows // step,),
        in_specs=[pl.BlockSpec((n_seq, step, share), lambda i: (0, i, 0))] + [wide] * 4,
        out_specs=[wide] * 4,
        out_shape=[out] * 4,
        compiler_params=pltpu.CompilerParams(vmem_limit_bytes=56 * 2**20),
        name="update_in",
    )(sums, weight, first, second, average)

def split_heads(
    n_dp, n_seq, tokens, cotangent, segment_ids, doc_positions,
    in_weight, in_first, in_second, in_average,
    out_weight, out_first, out_second, out_average,
    small_params, small_first, small_second, small_average,
):
    bf16, f32 = jnp.bfloat16, jnp.float32
    rows, own_tokens, width = tokens.shape
    row_tokens = own_tokens * n_seq
    all_tokens = rows * row_tokens
    head_size = width // HEADS
    ffn = (in_weight.shape[1] - 3 * width) // 2
    in_rows, own = in_weight.shape[0], out_weight.shape[0]
    dp_rows = own * n_seq
    att = width // n_seq
    late = width - dp_rows
    act = [(dp_rows - late) // n_seq, own, own]
    act_all = sum(act)
    lead = att - own
    p, s = lax.axis_index("dp"), lax.axis_index("seq")

    stretches = shares(n_seq, width, ffn, att, act)
    out_low = out_weight.astype(bf16)
    small_low = small_params.astype(bf16).astype(f32).T
    widen = lambda v, n: jnp.pad(v, ((0, n - v.shape[0]), (0, 128 - v.shape[1])))
    tile = jnp.concatenate(
        [
            widen(small_low, 8),
            widen(jnp.concatenate([segment_ids, doc_positions], axis=0).astype(f32), 8),
        ],
        axis=0,
    )
    odd = jnp.concatenate([jnp.zeros_like(tile[:8, :in_rows]), tile[:8, :in_rows]], axis=1)
    tile = jnp.concatenate([jnp.where(s % 2 == 1, odd, tile[:8]), tile[8:]], axis=0)
    _, g_full, in_low, _, tiles, hidden, out_mine, proj, d_joined = gather_all(
        n_dp, n_seq, late, lead, tokens, cotangent, share_out(in_weight, n_seq, stretches), out_low, tile
    )
    g_full, hidden = g_full.reshape(all_tokens, width), hidden.reshape(all_tokens, width)
    in_low = in_low.reshape(n_dp * n_seq * in_rows, 3 * att + 2 * act_all)

    pairs = tiles[:, :, :5].reshape(n_dp, n_seq // 2, 2, 5, 2 * in_rows).sum(axis=2)
    small_low = jnp.transpose(pairs, (2, 0, 1, 3)).reshape(5, width)
    gain = small_low[0]
    bias = lax.dynamic_slice_in_dim(small_low[2:5], s * att, att, 1).reshape(1, 3 * att)
    docs = lax.dynamic_index_in_dim(tiles, p, 0, keepdims=False)[:, 8:, :own_tokens]
    seg_full = jnp.transpose(docs[:, :rows], (1, 0, 2)).reshape(rows, row_tokens)
    pos_full = jnp.transpose(docs[:, rows : 2 * rows], (1, 0, 2)).reshape(rows, row_tokens)
    last = s == n_seq - 1
    keep = att - late

    def normalise(v):
        v = v.astype(f32)
        centered = v - jnp.mean(v, axis=-1, keepdims=True)
        inv_std = lax.rsqrt(jnp.mean(centered * centered, axis=-1, keepdims=True) + norm_eps)
        return centered * inv_std, inv_std

    half_rot = ROT // 2
    inv_freq = rope_base ** (-2.0 * jnp.arange(half_rot, dtype=f32) / ROT)
    angles = pos_full[:, None, :] * inv_freq[:, None]
    cos, sin = jnp.cos(angles), jnp.sin(angles)
    one, zero = jnp.ones((rows, head_size - ROT, row_tokens), f32), jnp.zeros_like(cos)
    rest = 0.0 * one
    rope = jnp.stack(
        [
            jnp.concatenate([cos, cos, one] * 2, axis=1),
            jnp.concatenate([-sin, zero, rest] * 2, axis=1),
            jnp.concatenate([zero, sin, rest] * 2, axis=1),
        ],
        axis=1,
    )
    joined, d_proj, bias_part = middle(
        proj, bias, d_joined, rope, seg_full, n_seq, att, act, head_size
    )

    blocks = lambda v: v.reshape(2, n_seq // 2, rows * own_tokens, v.shape[-1])
    x, c = s % 2, p % 2
    across = lambda v: lax.dynamic_index_in_dim(blocks(v), 1 - x, 0, keepdims=False)
    d_sent = jnp.einsum("ztk,fk->ztf", across(d_proj), in_low, preferred_element_type=f32)

    def to_core(v):
        some = v.shape[1] // n_dp
        firsts = [(2 * y_to + 1 - c) * some for y_to in range(2)]
        return [lax.dynamic_slice_in_dim(v, first, some, 1) for first in firsts]

    over_tokens = lambda a, b: lax.dot_general(
        a, b, (((0,), (0,)), ((), ())), preferred_element_type=f32
    ).astype(bf16)
    in_sent = over_tokens(jnp.concatenate(to_core(hidden), axis=1), d_proj).reshape(2, n_seq, in_rows, -1)
    normed, inv_std = normalise(tokens.reshape(rows * own_tokens, width))
    small_part = lax.dynamic_update_slice(jnp.zeros((8, width), f32), bias_part[:3], (2, s * att))
    plan = ((1, 1), ((0, 0), (0, 1), (0, 2), (0, 3), (1, 0), (1, 1), (1, 3), (7, 2), (2, 0), (2, 1), (2, 2), (2, 3), (2, 4), (2, 5), (2, 6), (2, 7), (7, 4), (7, 6), (1, 2), (7, 0), (4, 0), (7, 3), (3, 0), (3, 1), (6, 0), (4, 1), (7, 5), (0, 4), (0, 5), (0, 6), (0, 7), (3, 2), (3, 3), (4, 2), (3, 4), (3, 5), (7, 1), (4, 3), (3, 6), (3, 7), (5, 0), (4, 4), (5, 1), (4, 5), (5, 2), (6, 1), (4, 6), (4, 7), (5, 3)))
    sums, in_sum, out_sum, from_prev, small_sum = reduce_all(
        plan, n_dp, n_seq, late, act[0], keep,
        (d_sent.astype(bf16), in_sent),
        blocks(d_proj), blocks(joined), blocks(hidden), blocks(g_full), in_low, out_mine,
        normed, small_part,
    )
    d_hidden, branch = sums[0], sums[1]

    output = (tokens.astype(f32) + branch.reshape(tokens.shape)).astype(bf16)
    d_normed = d_hidden * gain
    input_grad = cotangent.astype(f32) + (
        inv_std
        * (
            d_normed
            - jnp.mean(d_normed, axis=-1, keepdims=True)
            - normed * jnp.mean(d_normed * normed, axis=-1, keepdims=True)
        )
    ).reshape(tokens.shape)
    small_grad = lax.dynamic_slice(small_sum, (0, s % 2 * in_rows), (8, in_rows))[:5].T

    count = jnp.where(p == 0, lead * s, jnp.where(p == 1, late - lead * s, 0))
    out_grad = lax.dynamic_slice_in_dim(
        jnp.concatenate([from_prev, out_sum[:own]], axis=0), late - count, own, 0
    ).astype(f32)

    *in_new, in_grad = update_in(
        in_sum, in_weight, in_first, in_second, in_average, stretches
    )
    out_new = adam_update(
        out_weight, out_first, out_second, out_average, out_grad, matrix_rate, weight_decay
    )
    small_new = adam_update(
        small_params, small_first, small_second, small_average, small_grad, small_rate, 0.0
    )
    return (output, input_grad, *in_new, *out_new, *small_new, small_grad, in_grad, out_grad)


def solution(mesh):
    n_dp, n_seq = mesh.shape["dp"], mesh.shape["seq"]

    def choose(*operands):
        own_rows = operands[8].shape[0]
        model_width = operands[0].shape[2]
        if heads_fit(n_dp, n_seq, own_rows, model_width, operands[4].shape[1]):
            return split_heads(n_dp, n_seq, *operands)
        return per_device(*operands)

    return jax.shard_map(
        choose,
        mesh=mesh,
        in_specs=(
            P("dp", "seq", None),
            P("dp", "seq", None),
            P("dp", "seq"),
            P("dp", "seq"),
            P(("dp", "seq"), None),
            P(("dp", "seq"), None),
            P(("dp", "seq"), None),
            P(("dp", "seq"), None),
            P(("dp", "seq"), None),
            P(("dp", "seq"), None),
            P(("dp", "seq"), None),
            P(("dp", "seq"), None),
            P(("dp", "seq"), None),
            P(("dp", "seq"), None),
            P(("dp", "seq"), None),
            P(("dp", "seq"), None),
        ),
        out_specs=(
            P("dp", "seq", None),
            P("dp", "seq", None),
            P(("dp", "seq"), None),
            P(("dp", "seq"), None),
            P(("dp", "seq"), None),
            P(("dp", "seq"), None),
            P(("dp", "seq"), None),
            P(("dp", "seq"), None),
            P(("dp", "seq"), None),
            P(("dp", "seq"), None),
            P(("dp", "seq"), None),
            P(("dp", "seq"), None),
            P(("dp", "seq"), None),
            P(("dp", "seq"), None),
        ),
        check_vma=False,
    )
```

```python
import functools

import jax
import jax.numpy as jnp
from jax import lax
from jax.experimental import pallas as pl
from jax.experimental.pallas import tpu as pltpu
from jax.sharding import PartitionSpec as P

HEADS = 32
ROT = 16
STEP = 2


beta_one = 0.9
adam_eps = 1e-08
matrix_rate = 0.001
small_rate = 0.01
weight_decay = 0.1
norm_eps = 1e-05
rope_base = 10000.0
neg_large = -1e30


def rope_tables(positions, rot_dims):
    half_rot = rot_dims // 2
    inv_freq = rope_base ** (-2.0 * jnp.arange(half_rot, dtype=jnp.float32) / rot_dims)
    angles = positions.astype(jnp.float32)[..., None] * inv_freq
    return (jnp.cos(angles)[..., None, :], jnp.sin(angles)[..., None, :])


def apply_rope(field_in, cosine_tab, sine_tab, rot_dims):
    half_rot = rot_dims // 2
    low_half = field_in[..., :half_rot]
    high_half = field_in[..., half_rot:rot_dims]
    return jnp.concatenate(
        [
            low_half * cosine_tab - high_half * sine_tab,
            high_half * cosine_tab + low_half * sine_tab,
            field_in[..., rot_dims:],
        ],
        axis=-1,
    )


def undo_rope(grad_in, cosine_tab, sine_tab, rot_dims):
    half_rot = rot_dims // 2
    low_half = grad_in[..., :half_rot]
    high_half = grad_in[..., half_rot:rot_dims]
    return jnp.concatenate(
        [
            low_half * cosine_tab + high_half * sine_tab,
            high_half * cosine_tab - low_half * sine_tab,
            grad_in[..., rot_dims:],
        ],
        axis=-1,
    )


def visible(query_seg, key_seg, query_pos, key_pos):
    same_doc = query_seg[:, :, None] == key_seg[:, None, :]
    causal = key_pos[None, :] <= query_pos[:, None]
    return (same_doc & causal[None])[:, None]


def to_tokens(head_major):
    return jnp.transpose(head_major, (0, 2, 1, 3))


def adam_update(weight, first, second, average, gradient, rate, decay_rate):
    beta_two = 1.0 - STEP ** (-0.8)
    average_keep = min(0.999, (1.0 + STEP) / (10.0 + STEP))
    first_new = beta_one * first + (1.0 - beta_one) * gradient
    second_new = beta_two * second + (1.0 - beta_two) * gradient * gradient
    moment_hat = beta_one * first_new / (1.0 - beta_one ** (STEP + 1)) + (
        1.0 - beta_one
    ) * gradient / (1.0 - beta_one**STEP)
    weight_new = weight - rate * (
        moment_hat / (jnp.sqrt(second_new) + adam_eps) + decay_rate * weight
    )
    average_new = average_keep * average + (1.0 - average_keep) * weight_new
    return (weight_new, second_new, average_new)


def per_device(
    tokens,
    cotangent,
    segment_ids,
    doc_positions,
    in_weight,
    in_first,
    in_second,
    in_average,
    out_weight,
    out_first,
    out_second,
    out_average,
    small_params,
    small_first,
    small_second,
    small_average,
):
    rows_here, row_tokens, model_width = tokens.shape
    head_count = HEADS
    head_size = model_width // head_count
    score_scale = head_size ** (-0.5)
    all_tokens = rows_here * row_tokens
    wide_in = in_weight.shape[1]
    ffn_width = (wide_in - 3 * model_width) // 2
    shape_heads = (rows_here, row_tokens, head_count, head_size)
    own_places = lax.axis_index("seq") * row_tokens + jnp.arange(row_tokens)
    flat_in = tokens.astype(jnp.float32).reshape(all_tokens, model_width)
    centered = flat_in - jnp.mean(flat_in, axis=-1, keepdims=True)
    inv_std = lax.rsqrt(jnp.mean(centered * centered, axis=-1, keepdims=True) + norm_eps)
    normed = centered * inv_std
    in_low = in_weight.astype(jnp.bfloat16)
    out_low = out_weight.astype(jnp.bfloat16)
    small_low = small_params.astype(jnp.bfloat16)
    w_piece = lax.all_gather(in_low, ("dp", "seq"), axis=0, tiled=True)
    s_piece = lax.all_gather(small_low, ("dp", "seq"), axis=0, tiled=True)
    columns = normed
    s_float = s_piece.astype(jnp.float32)
    h_piece = (columns * s_float[:, 0] + s_float[:, 1]).astype(jnp.bfloat16)
    proj_acc = jnp.dot(h_piece, w_piece, preferred_element_type=jnp.float32)
    norm_gain = s_float[:, 0]
    qkv_bias = s_float[:, 2:5].T.reshape(3 * model_width)
    qkv_full = proj_acc[:, : 3 * model_width] + qkv_bias
    gate_pre = proj_acc[:, 3 * model_width : 3 * model_width + ffn_width]
    up_pre = proj_acc[:, 3 * model_width + ffn_width :]
    cosine_tab, sine_tab = rope_tables(doc_positions, ROT)
    query_low = apply_rope(
        qkv_full[:, :model_width].reshape(shape_heads), cosine_tab, sine_tab, ROT
    ).astype(jnp.bfloat16)
    key_low = apply_rope(
        qkv_full[:, model_width : 2 * model_width].reshape(shape_heads), cosine_tab, sine_tab, ROT
    ).astype(jnp.bfloat16)
    value_low = qkv_full[:, 2 * model_width :].reshape(shape_heads).astype(jnp.bfloat16)
    seg_low = segment_ids.astype(jnp.bfloat16)
    seg_own = segment_ids.astype(jnp.float32)
    key_flat = key_low.reshape(rows_here, row_tokens, model_width)
    value_flat = value_low.reshape(rows_here, row_tokens, model_width)
    attend_init = (
        jnp.full((rows_here, head_count, row_tokens), neg_large, jnp.float32),
        jnp.zeros((rows_here, head_count, row_tokens), jnp.float32),
        jnp.zeros((rows_here, head_count, row_tokens, head_size), jnp.float32),
    )
    key_piece = lax.all_gather(key_flat, "seq", axis=1, tiled=True)
    value_piece = lax.all_gather(value_flat, "seq", axis=1, tiled=True)
    seg_piece = lax.all_gather(seg_low, "seq", axis=1, tiled=True)
    turn_count = key_piece.shape[1] // row_tokens

    def attend_one_turn(turn_index, inner_state):
        offset = turn_index * row_tokens
        key_blk = lax.dynamic_slice_in_dim(key_piece, offset, row_tokens, 1).reshape(shape_heads)
        value_blk = lax.dynamic_slice_in_dim(value_piece, offset, row_tokens, 1).reshape(
            shape_heads
        )
        seg_blk = lax.dynamic_slice_in_dim(seg_piece, offset, row_tokens, 1).astype(jnp.float32)
        key_mask = visible(seg_own, seg_blk, own_places, offset + jnp.arange(row_tokens))
        running_top, running_sum, weighted = inner_state
        scores = (
            jnp.einsum("rqhe,rkhe->rhqk", query_low, key_blk, preferred_element_type=jnp.float32)
            * score_scale
        )
        scores = jnp.where(key_mask, scores, neg_large)
        new_top = jnp.maximum(running_top, jnp.max(scores, axis=-1))
        weights = jnp.where(key_mask, jnp.exp(scores - new_top[..., None]), 0.0)
        factor = jnp.exp(running_top - new_top)
        running_sum = running_sum * factor + jnp.sum(weights, axis=-1)
        weighted = weighted * factor[..., None] + jnp.einsum(
            "rhqk,rkhe->rhqe",
            weights.astype(jnp.bfloat16),
            value_blk,
            preferred_element_type=jnp.float32,
        )
        return (new_top, running_sum, weighted)

    running_top, running_sum, weighted = lax.fori_loop(0, turn_count, attend_one_turn, attend_init)
    attended = weighted / running_sum[..., None]
    log_total = running_top + jnp.log(running_sum)
    attended_low = to_tokens(attended).reshape(all_tokens, model_width).astype(jnp.bfloat16)
    gate_sig = jax.nn.sigmoid(gate_pre)
    activated = gate_pre * gate_sig * up_pre
    joined = jnp.concatenate([attended_low, activated.astype(jnp.bfloat16)], axis=1)
    columns = joined
    branch_sum = jnp.dot(
        columns,
        lax.all_gather(out_low, ("dp", "seq"), axis=0, tiled=True),
        preferred_element_type=jnp.float32,
    )
    output = (flat_in + branch_sum).astype(jnp.bfloat16).reshape(rows_here, row_tokens, model_width)
    grad_out = cotangent.reshape(all_tokens, model_width)
    d_joined = lax.dot_general(
        grad_out,
        lax.all_gather(out_low, ("dp", "seq"), axis=0, tiled=True),
        (((1,), (1,)), ((), ())),
        preferred_element_type=jnp.float32,
    )
    d_joined = d_joined.astype(jnp.bfloat16)
    columns = joined
    out_grad = lax.psum_scatter(
        lax.dot_general(
            columns, grad_out, (((0,), (0,)), ((), ())), preferred_element_type=jnp.float32
        ),
        ("dp", "seq"),
        scatter_dimension=0,
        tiled=True,
    )
    d_attended = d_joined[:, :model_width].reshape(shape_heads)
    d_act = d_joined[:, model_width:].astype(jnp.float32)
    d_gate = d_act * up_pre * gate_sig * (1.0 + gate_pre * (1.0 - gate_sig))
    d_up = d_act * gate_pre * gate_sig
    out_dot = jnp.einsum("rqhe,rhqe->rhq", d_attended.astype(jnp.float32), attended)
    grad_zero = jnp.zeros((rows_here, head_count, row_tokens, head_size), jnp.float32)
    query_key_piece = lax.all_gather(key_flat, "seq", axis=1, tiled=True)
    query_value_piece = lax.all_gather(value_flat, "seq", axis=1, tiled=True)
    query_seg_piece = lax.all_gather(seg_low, "seq", axis=1, tiled=True)
    turn_count = query_key_piece.shape[1] // row_tokens

    def query_one_turn(turn_index, inner_state):
        offset = turn_index * row_tokens
        key_blk = lax.dynamic_slice_in_dim(query_key_piece, offset, row_tokens, 1).reshape(
            shape_heads
        )
        value_blk = lax.dynamic_slice_in_dim(query_value_piece, offset, row_tokens, 1).reshape(
            shape_heads
        )
        seg_blk = lax.dynamic_slice_in_dim(query_seg_piece, offset, row_tokens, 1).astype(
            jnp.float32
        )
        key_mask = visible(seg_own, seg_blk, own_places, offset + jnp.arange(row_tokens))
        scores = (
            jnp.einsum("rqhe,rkhe->rhqk", query_low, key_blk, preferred_element_type=jnp.float32)
            * score_scale
        )
        weights = jnp.where(key_mask, jnp.exp(scores - log_total[..., None]), 0.0)
        d_prob = jnp.einsum(
            "rqhe,rkhe->rhqk", d_attended, value_blk, preferred_element_type=jnp.float32
        )
        d_score = (weights * (d_prob - out_dot[..., None])).astype(jnp.bfloat16)
        return (
            inner_state
            + jnp.einsum("rhqk,rkhe->rhqe", d_score, key_blk, preferred_element_type=jnp.float32)
            * score_scale
        )

    d_query = lax.fori_loop(0, turn_count, query_one_turn, grad_zero)
    row_stats = jnp.concatenate(
        [jnp.transpose(log_total, (0, 2, 1)), jnp.transpose(out_dot, (0, 2, 1))], axis=2
    )
    stat_high = row_stats.astype(jnp.bfloat16)
    stat_low = (row_stats - stat_high.astype(jnp.float32)).astype(jnp.bfloat16)
    query_flat = query_low.reshape(rows_here, row_tokens, model_width)
    d_att_flat = d_attended.reshape(rows_here, row_tokens, model_width)
    query_piece = lax.all_gather(query_flat, "seq", axis=1, tiled=True)
    dout_piece = lax.all_gather(d_att_flat, "seq", axis=1, tiled=True)
    high_piece = lax.all_gather(stat_high, "seq", axis=1, tiled=True)
    low_piece = lax.all_gather(stat_low, "seq", axis=1, tiled=True)
    key_seg_piece = lax.all_gather(seg_low, "seq", axis=1, tiled=True)
    turn_count = query_piece.shape[1] // row_tokens

    def key_one_turn(turn_index, inner_state):
        offset = turn_index * row_tokens
        query_blk = lax.dynamic_slice_in_dim(query_piece, offset, row_tokens, 1).reshape(
            shape_heads
        )
        dout_blk = lax.dynamic_slice_in_dim(dout_piece, offset, row_tokens, 1).reshape(shape_heads)
        stat_blk = lax.dynamic_slice_in_dim(high_piece, offset, row_tokens, 1).astype(
            jnp.float32
        ) + lax.dynamic_slice_in_dim(low_piece, offset, row_tokens, 1).astype(jnp.float32)
        lse_blk = jnp.transpose(stat_blk[..., :head_count], (0, 2, 1))
        dot_blk = jnp.transpose(stat_blk[..., head_count:], (0, 2, 1))
        seg_blk = lax.dynamic_slice_in_dim(key_seg_piece, offset, row_tokens, 1).astype(jnp.float32)
        key_mask = visible(seg_blk, seg_own, offset + jnp.arange(row_tokens), own_places)
        d_key, d_value = inner_state
        scores = (
            jnp.einsum("rqhe,rkhe->rhqk", query_blk, key_low, preferred_element_type=jnp.float32)
            * score_scale
        )
        weights = jnp.where(key_mask, jnp.exp(scores - lse_blk[..., None]), 0.0)
        d_value = d_value + jnp.einsum(
            "rhqk,rqhe->rhke",
            weights.astype(jnp.bfloat16),
            dout_blk,
            preferred_element_type=jnp.float32,
        )
        d_prob = jnp.einsum(
            "rqhe,rkhe->rhqk", dout_blk, value_low, preferred_element_type=jnp.float32
        )
        d_score = (weights * (d_prob - dot_blk[..., None])).astype(jnp.bfloat16)
        d_key = (
            d_key
            + jnp.einsum("rhqk,rqhe->rhke", d_score, query_blk, preferred_element_type=jnp.float32)
            * score_scale
        )
        return (d_key, d_value)

    d_key, d_value = lax.fori_loop(0, turn_count, key_one_turn, (grad_zero, grad_zero))
    d_query_tok = undo_rope(to_tokens(d_query), cosine_tab, sine_tab, ROT).reshape(
        all_tokens, model_width
    )
    d_key_tok = undo_rope(to_tokens(d_key), cosine_tab, sine_tab, ROT).reshape(
        all_tokens, model_width
    )
    d_value_tok = to_tokens(d_value).reshape(all_tokens, model_width)
    d_proj = jnp.concatenate([d_query_tok, d_key_tok, d_value_tok, d_gate, d_up], axis=1).astype(
        jnp.bfloat16
    )
    d_hidden = lax.dot_general(
        d_proj,
        lax.all_gather(in_low, ("dp", "seq"), axis=0, tiled=True),
        (((1,), (1,)), ((), ())),
        preferred_element_type=jnp.float32,
    )
    columns = h_piece
    in_grad = lax.psum_scatter(
        lax.dot_general(
            columns, d_proj, (((0,), (0,)), ((), ())), preferred_element_type=jnp.float32
        ),
        ("dp", "seq"),
        scatter_dimension=0,
        tiled=True,
    )
    gain_grad = jnp.sum(d_hidden * normed, axis=0)
    shift_grad = jnp.sum(d_hidden, axis=0)
    bias_grad = (
        jnp.sum(d_proj[:, : 3 * model_width].astype(jnp.float32), axis=0).reshape(3, model_width).T
    )
    small_term = jnp.concatenate([gain_grad[:, None], shift_grad[:, None], bias_grad], axis=1)
    small_grad = lax.psum_scatter(small_term, ("dp", "seq"), scatter_dimension=0, tiled=True)
    d_normed = d_hidden * norm_gain
    input_grad = grad_out.astype(jnp.float32) + inv_std * (
        d_normed
        - jnp.mean(d_normed, axis=-1, keepdims=True)
        - normed * jnp.mean(d_normed * normed, axis=-1, keepdims=True)
    )
    input_grad = input_grad.reshape(rows_here, row_tokens, model_width)
    in_new = adam_update(
        in_weight, in_first, in_second, in_average, in_grad, matrix_rate, weight_decay
    )
    out_new = adam_update(
        out_weight, out_first, out_second, out_average, out_grad, matrix_rate, weight_decay
    )
    small_new = adam_update(
        small_params, small_first, small_second, small_average, small_grad, small_rate, 0.0
    )
    return (
        output,
        input_grad,
        in_new[0],
        in_new[1],
        in_new[2],
        out_new[0],
        out_new[1],
        out_new[2],
        small_new[0],
        small_new[1],
        small_new[2],
        small_grad,
        in_grad,
        out_grad,
    )


def heads_fit(n_dp, n_seq, own_rows, model_width, wide_in):
    dp_rows = own_rows * n_seq
    if n_dp != 4 or HEADS % (2 * n_seq) or not dp_rows < model_width < 2 * dp_rows:
        return False
    att_rows = model_width // n_seq
    late_att = model_width - dp_rows
    first_act = dp_rows - late_att
    if first_act % n_seq:
        return False
    lead = att_rows - own_rows
    return (
        wide_in - 3 * model_width == 2 * (n_dp * dp_rows - model_width)
        and lead == own_rows - first_act // n_seq
        and lead * n_seq == late_att
        and lead % 16 == 0
    )


def middle_kernel(
    q_ref, k_ref, v_ref, bq_ref, bk_ref, bv_ref, da_ref, act_ref, d_act_ref, rope_ref,
    seg_q_ref, seg_k_ref,
    joined_ref, d_proj_ref, bias_ref,
    *, head_size, half_rot, att_rows, act,
):
    row, pair = pl.program_id(0), pl.program_id(1)
    lanes = 2 * head_size
    half = act_ref.shape[3]
    act_rows = sum(act)
    bf16, f32 = jnp.bfloat16, jnp.float32

    def feed_forward(step):
        x, z = lax.rem(step, 2), step // 2
        raw = act_ref[x, z, 0]
        gate = raw[:, 3 * att_rows : 3 * att_rows + act_rows]
        up = raw[:, 3 * att_rows + act_rows :]
        joint = d_act_ref[x, z, 0]
        d_act = jnp.concatenate(
            [joint[:, (i + 1) * att_rows :][:, :some] for i, some in enumerate(act)], axis=1
        ).astype(f32)
        sig = 1.0 / (1.0 + jnp.exp(-gate))
        silu = gate * sig
        rows = pl.ds(pl.multiple_of(pair * half, half), half)
        active, parts, first = silu * up, [], 0
        for some in act:
            parts.append(active[:, first : first + some])
            parts.append(jnp.zeros((half, att_rows - some), f32))
            first += some
        joined_ref[x, z, row, rows, att_rows:] = jnp.concatenate(parts, axis=1).astype(bf16)
        d_gate = d_act * up * sig * (1.0 + gate * (1.0 - sig))
        d_proj_ref[x, z, row, rows, 3 * att_rows :] = jnp.concatenate(
            [d_gate, d_act * silu], axis=1
        ).astype(bf16)

    loop(0, act_ref.shape[0] * act_ref.shape[1], feed_forward)

    def whole(v):
        across, depth = v.shape[:2]
        parts = [v[x, z].reshape(v.shape[-2:]) for z in range(depth) for x in range(across)]
        return jnp.concatenate(parts, axis=0)

    def store(ref, first, v):
        across, depth, _, some, _ = ref.shape
        columns = pl.ds(pl.multiple_of(first + pair * lanes, lanes), lanes)
        for z in range(depth):
            for x in range(across):
                at = (z * across + x) * some
                ref[x, z, row, :, columns] = v[at : at + some]

    cos, sin_low, sin_high = (rope_ref[0, i].T for i in range(3))
    tokens = cos.shape[0]
    scale = head_size ** (-0.5)

    def turn(v, way):
        return (
            v * cos
            + way * pltpu.roll(v, lanes - half_rot, 1) * sin_low
            + way * pltpu.roll(v, half_rot, 1) * sin_high
        )

    query = (turn(whole(q_ref[...]) + bq_ref[...], 1.0)).astype(bf16) * scale
    query = query.astype(bf16)
    key = turn(whole(k_ref[...]) + bk_ref[...], 1.0).astype(bf16)
    value = (whole(v_ref[...]) + bv_ref[...]).astype(bf16)
    d_att = whole(da_ref[...])
    place_q = lax.broadcasted_iota(jnp.int32, (tokens, tokens), 0)
    place_k = lax.broadcasted_iota(jnp.int32, (tokens, tokens), 1)
    mask = (seg_q_ref[0] == seg_k_ref[0]) & (place_k <= place_q)
    lane = lax.broadcasted_iota(jnp.int32, (tokens, lanes), 1)
    nt = (((1,), (1,)), ((), ()))
    tn = (((0,), (0,)), ((), ()))
    dot = functools.partial(lax.dot_general, preferred_element_type=f32)
    att = jnp.zeros((tokens, lanes), f32)
    d_query = jnp.zeros((tokens, lanes), f32)
    d_key = jnp.zeros((tokens, lanes), f32)
    d_value = jnp.zeros((tokens, lanes), f32)
    for head in range(lanes // head_size):
        mine = (lane >= head * head_size) & (lane < (head + 1) * head_size)
        q_h = jnp.where(mine, query, jnp.zeros_like(query))
        da_h = jnp.where(mine, d_att, jnp.zeros_like(d_att))
        scores = jnp.where(mask, dot(q_h, key, nt), neg_large)
        top = jnp.max(scores, axis=1, keepdims=True)
        weights = jnp.exp(scores - top)
        probs = weights * (1.0 / jnp.sum(weights, axis=1, keepdims=True))
        probs_low = probs.astype(bf16)
        att_h = jnp.where(mine, dot(probs_low, value, (((1,), (0,)), ((), ()))), 0.0)
        out_dot = jnp.sum(att_h * d_att.astype(f32), axis=1, keepdims=True)
        d_prob = dot(da_h, value, nt)
        d_score = (probs * (d_prob - out_dot)).astype(bf16)
        att = att + att_h
        d_query = d_query + jnp.where(mine, dot(d_score, key, (((1,), (0,)), ((), ()))), 0.0)
        d_key = d_key + dot(d_score, q_h, tn)
        d_value = d_value + dot(probs_low, da_h, tn)
    store(joined_ref, 0, att.astype(bf16))
    grads = (turn(d_query * scale, -1.0), turn(d_key, -1.0), d_value)
    columns = pl.ds(pl.multiple_of(pair * lanes, lanes), lanes)
    for i, grad in enumerate(grads):
        grad = grad.astype(bf16)
        store(d_proj_ref, i * att_rows, grad)
        total = jnp.sum(grad.astype(f32), axis=0, keepdims=True)

        @pl.when(row == 0)
        def _():
            bias_ref[i : i + 1, columns] = total

        @pl.when(row > 0)
        def _():
            bias_ref[i : i + 1, columns] = bias_ref[i : i + 1, columns] + total


def middle(proj, bias, d_joined, rope, seg, n_seq, att_rows, act, head_size):
    rows, tokens = seg.shape
    lanes = 2 * head_size
    pairs = att_rows // lanes
    bf16, f32 = jnp.bfloat16, jnp.float32
    order = (2, n_seq // 2, rows, tokens // n_seq)
    wide = lambda v: v.reshape(order + v.shape[-1:])
    shape = (2, n_seq // 2, 1, tokens // n_seq, lanes)
    block = lambda first: pl.BlockSpec(shape, lambda r, h: (0, 0, r, 0, first + h))
    row = lambda first: pl.BlockSpec((1, lanes), lambda r, h: (0, first + h))
    half = lambda v: pl.BlockSpec(
        (2, n_seq // 2, 1, tokens // n_seq // pairs, v.shape[-1]), lambda r, h: (0, 0, r, h, 0)
    )
    all_of = lambda v: pl.BlockSpec(v.shape, lambda r, h: (0,) * len(v.shape))
    outs = [
        jax.ShapeDtypeStruct(order + (d_joined.shape[-1],), bf16),
        jax.ShapeDtypeStruct(order + (proj.shape[-1],), bf16),
        jax.ShapeDtypeStruct((8, att_rows), f32),
    ]
    proj, d_joined = wide(proj), wide(d_joined)
    joined, d_proj, bias_sums = pl.pallas_call(
        functools.partial(
            middle_kernel,
            head_size=head_size, half_rot=ROT // 2, att_rows=att_rows, act=act,
        ),
        grid=(rows, pairs),
        in_specs=[
            block(0), block(pairs), block(2 * pairs),
            row(0), row(pairs), row(2 * pairs),
            block(0), half(proj), half(d_joined),
            pl.BlockSpec((1, 3, lanes, tokens), lambda r, h: (r, 0, 0, 0)),
            pl.BlockSpec((1, tokens, 1), lambda r, h: (r, 0, 0)),
            pl.BlockSpec((1, 1, tokens), lambda r, h: (r, 0, 0)),
        ],
        out_specs=[all_of(v) for v in outs],
        out_shape=outs,
        compiler_params=pltpu.CompilerParams(vmem_limit_bytes=56 * 2**20),
        name="middle",
    )(
        proj, proj, proj, bias, bias, bias, d_joined, proj, d_joined,
        rope, seg[:, :, None], seg[:, None, :],
    )
    flat = lambda v: v.reshape(rows * tokens, v.shape[-1])
    return flat(joined), flat(d_proj), bias_sums

MESH_ID = pl.DeviceIdType.MESH


def remote(src, dst, send_sem, recv_sem, device):
    return pltpu.make_async_remote_copy(
        src_ref=src,
        dst_ref=dst,
        send_sem=send_sem,
        recv_sem=recv_sem,
        device_id=device,
        device_id_type=MESH_ID,
    )


class Place:
    def __init__(self, n_seq):
        self.n_seq = n_seq
        self.depth = n_seq // 2
        self.p, self.s = lax.axis_index("dp"), lax.axis_index("seq")
        self.y, self.c = self.p // 2, lax.rem(self.p, 2)
        self.z, self.x = self.s // 2, lax.rem(self.s, 2)
        self.p_y = (1 - self.y) * 2 + self.c
        self.p_c = self.y * 2 + 1 - self.c
        self.p_d = (1 - self.y) * 2 + 1 - self.c
        self.to_y = (self.p_y, self.s)
        self.to_c = (self.p_c, self.s)
        self.to_x = (self.p, self.z * 2 + 1 - self.x)
        self.to_up = (self.p, self.s + 2)
        self.to_down = (self.p, self.s - 2)

    def seq(self, hop):
        return lax.rem(self.s + hop + self.n_seq, self.n_seq)

    def meet(self):
        barrier = pltpu.get_barrier_semaphore()

        def greet(hop, carry):
            pl.semaphore_signal(
                barrier, inc=1, device_id=(self.p, self.seq(hop)), device_id_type=MESH_ID
            )
            return carry

        lax.fori_loop(1, self.n_seq, greet, 0)
        for device in (self.to_y, self.to_c):
            pl.semaphore_signal(barrier, inc=1, device_id=device, device_id_type=MESH_ID)
        pl.semaphore_wait(barrier, self.n_seq + 1)


class Spread:
    def __init__(self, at, own, full, sems):
        self.at, self.own, self.full, self.sems = at, own, full, sems

    def along(self, src, up, ref=None):
        sems, at = self.sems, self.at
        here = self.full.at[at.x, src]
        return remote(
            here if ref is None else ref,
            here,
            sems.at[0 if up else 1, src],
            sems.at[3, src],
            at.to_up if up else at.to_down,
        )

    def across(self, src, ref=None):
        sems, at = self.sems, self.at
        here = self.full.at[at.x, src]
        return remote(here if ref is None else ref, here, sems.at[2, src], sems.at[4, src], at.to_x)

    def local(self):
        return pltpu.make_async_copy(
            self.own, self.full.at[self.at.x, self.at.z], self.sems.at[5, 0]
        )

    def begin_across(self):
        self.across(self.at.z, self.own).start()
        self.local().start()

    def begin_along(self):
        at = self.at

        @pl.when(at.z < at.depth - 1)
        def _():
            self.along(at.z, True, self.own).start()

        @pl.when(at.z > 0)
        def _():
            self.along(at.z, False, self.own).start()

    def step(self, hop):
        at = self.at

        @pl.when(at.z - hop >= 0)
        def _():
            src = at.z - hop
            self.along(src, True).wait_recv()

            @pl.when(at.z < at.depth - 1)
            def _():
                self.along(src, True).start()

            self.across(src).start()

        @pl.when(at.z + hop < at.depth)
        def _():
            src = at.z + hop
            self.along(src, False).wait_recv()

            @pl.when(at.z > 0)
            def _():
                self.along(src, False).start()

            self.across(src).start()

    def arrive(self):
        at = self.at
        for src in range(at.depth):
            here = self.full.at[1 - at.x, src]
            remote(here, here, self.sems.at[2, src], self.sems.at[4, src], at.to_x).wait_recv()

    def sent(self):
        at = self.at
        for src in range(at.depth):
            self.across(src).wait_send()

            @pl.when((at.z < at.depth - 1) & (src <= at.z))
            def _():
                self.along(src, True).wait_send()

            @pl.when((at.z > 0) & (src >= at.z))
            def _():
                self.along(src, False).wait_send()


class Fan:
    def __init__(self, at, pick, sems):
        self.at, self.pick, self.sems = at, pick, sems

    def y(self, k, ref=None):
        at = self.at
        here = self.pick(at.p, k)
        return remote(here if ref is None else ref, here, self.sems.at[0, k], self.sems.at[1, k], at.to_y)

    def core(self, k, ref=None):
        at = self.at
        here = self.pick(at.p, k)
        return remote(here if ref is None else ref, here, self.sems.at[2, k], self.sems.at[3, k], at.to_c)

    def pass_on(self, k):
        at = self.at
        here = self.pick(at.p_y, k)
        return remote(here, here, self.sems.at[4, k], self.sems.at[5, k], at.to_c)

    def from_y(self, k):
        here = self.pick(self.at.p_y, k)
        return remote(here, here, self.sems.at[0, k], self.sems.at[1, k], self.at.to_y)

    def from_core(self, k):
        here = self.pick(self.at.p_c, k)
        return remote(here, here, self.sems.at[2, k], self.sems.at[3, k], self.at.to_c)

    def from_diagonal(self, k):
        here = self.pick(self.at.p_d, k)
        return remote(here, here, self.sems.at[4, k], self.sems.at[5, k], self.at.to_c)


def loop(low, high, body):
    def step(k, carry):
        body(k)
        return carry

    lax.fori_loop(low, high, step, 0)


def gather_kernel(
    x_ref, g_ref, w_ref, o_ref, tile_ref,
    x_full, g_full, w_full, o_full, tiles, hidden, out_mine, proj, d_joined,
    x_block, hid, w_near, p_all, g_near, o_near, t_near, small,
    x_sems, g_sems, w_sems, w_fan_sems, o_sems, o_fan_sems, t_sems, t_fan_sems, local_sems,
    x_in_sems, hid_sems, w_in_sems, p_sems, g_in_sems, o_in_sems,
    *, n_seq, late, lead,
):
    at = Place(n_seq)
    depth = at.depth
    bf16, f32 = jnp.bfloat16, jnp.float32
    own, width = o_ref.shape
    att = own + lead
    first_act = own - lead
    body, extra = pl.ds(0, own), pl.ds(own, late)
    x_go = Spread(at, x_ref, x_full, x_sems)
    g_go = Spread(at, g_ref, g_full, g_sems)
    w_fan = Fan(at, lambda p, k: w_full.at[p, k], w_fan_sems)
    o_fan = Fan(at, lambda p, k: o_full.at[p, body if k == 0 else extra], o_fan_sems)
    t_fan = Fan(at, lambda p, k: tiles.at[p], t_fan_sems)

    def w_send(hop):
        to = at.seq(hop)
        return remote(w_ref.at[to], w_full.at[at.p, at.s], w_sems.at[0, to], w_sems.at[1, at.s], (at.p, to))

    def w_recv(hop):
        src = at.seq(-hop)
        here = w_full.at[at.p, src]
        return remote(here, here, w_sems.at[0, src], w_sems.at[1, src], (at.p, src))

    def t_send(hop):
        to = at.seq(hop)
        return remote(tile_ref, tiles.at[at.p, at.s], t_sems.at[0, to], t_sems.at[1, at.s], (at.p, to))

    def t_recv(hop):
        src = at.seq(-hop)
        here = tiles.at[at.p, src]
        return remote(here, here, t_sems.at[0, src], t_sems.at[1, src], (at.p, src))

    w_local = pltpu.make_async_copy(w_ref.at[at.s], w_full.at[at.p, at.s], local_sems.at[0])
    o_local = pltpu.make_async_copy(o_ref, o_full.at[at.p, body], local_sems.at[1])
    t_local = pltpu.make_async_copy(tile_ref, tiles.at[at.p, at.s], local_sems.at[2])
    head = o_ref.at[pl.ds(0, late)]
    o_send = remote(
        head, o_full.at[at.p, extra], o_sems.at[0], o_sems.at[1], (at.p, at.seq(-1))
    )

    def place(i):
        return lax.rem(at.x + i // depth, 2), lax.rem(at.z + i, depth)

    def block_in(i):
        col, deep = place(i)
        return pltpu.make_async_copy(x_full.at[col, deep], x_block, x_in_sems.at[0])

    def hid_out(i):
        col, deep = place(i)
        return pltpu.make_async_copy(hid.at[col, deep], hidden.at[col, deep], hid_sems.at[i])

    def norm_block(i):
        col, deep = place(i)

        @pl.when(i >= depth)
        def _():
            here = x_full.at[1 - at.x, deep]
            remote(here, here, x_sems.at[2, deep], x_sems.at[4, deep], at.to_x).wait_recv()

        block_in(i).start()
        block_in(i).wait()
        some = 32

        def rows(k):
            part = pl.ds(pl.multiple_of(lax.rem(k, 2) * some, some), some)
            v = x_block[k // 2, part, :].astype(f32)
            centered = v - jnp.mean(v, axis=-1, keepdims=True)
            inv_std = lax.rsqrt(jnp.mean(centered * centered, axis=-1, keepdims=True) + norm_eps)
            done = centered * inv_std * small[0:1, :] + small[1:2, :]
            hid[col, deep, pl.ds(pl.multiple_of(k * some, some), some), :] = done.astype(bf16)

        loop(0, hid.shape[2] // some, rows)
        hid_out(i).start()

    def w_in(p, k):
        return pltpu.make_async_copy(w_full.at[p], w_near.at[p], w_in_sems.at[k])

    def g_in(col):
        return pltpu.make_async_copy(g_full.at[col], g_near.at[col], g_in_sems.at[col])

    def o_in(k):
        last = at.s == n_seq - 1
        lead_at = pl.multiple_of(lead * at.s, 16)
        late_at = pl.multiple_of(late - lead * at.s, 16)
        src, dst, count = [
            (o_full.at[0, pl.ds(lead_at, att - late)], 0, att - late),
            (o_full.at[0, pl.ds(lead_at + (att - late), late)], att - late, late),
            (o_full.at[1, pl.ds(late_at, first_act)], att, first_act),
            (o_full.at[2, body], 2 * att, own),
            (o_full.at[3, body], 3 * att, own),
            (o_full.at[1, extra], att - late, late),
        ][k]
        return pltpu.make_async_copy(src, o_near.at[pl.ds(dst, count)], o_in_sems.at[k])

    step_rows = 2 * hid.shape[2]
    steps = hid.shape[0] * depth * hid.shape[2] // step_rows
    per_block = step_rows // hid.shape[2]

    def p_out(k):
        rows = pl.ds(pl.multiple_of(k * step_rows, step_rows), step_rows)
        return pltpu.make_async_copy(p_all.at[rows], proj.at[rows], p_sems.at[k])

    feats = width // w_near.shape[0]

    def project(k, p_one, p_two, last):
        rows = per_block * k
        at_rows = pl.ds(pl.multiple_of(k * step_rows, step_rows), step_rows)
        left = [
            hid[
                rows // depth, pl.ds(lax.rem(rows, depth), per_block), :,
                pl.ds(pl.multiple_of(p * feats, feats), feats),
            ].reshape(step_rows, feats)
            for p in (p_one, p_two)
        ]
        columns = p_all.shape[1]
        for n in range(0, columns, 512):
            some = min(512, columns - n)
            total = sum(
                jnp.dot(
                    part, w_near[p, :, :, n : n + some].reshape(feats, some),
                    preferred_element_type=f32,
                )
                for part, p in zip(left, (p_one, p_two))
            )
            if last:
                total = total + p_all[at_rows, n : n + some]
            p_all[at_rows, n : n + some] = total
        if last:
            p_out(k).start()

    def join_back(k):
        rows = per_block * k
        left = g_near[rows // depth, pl.ds(lax.rem(rows, depth), per_block)]
        left = left.reshape(step_rows, width)
        d_joined[pl.ds(pl.multiple_of(k * step_rows, step_rows), step_rows), :] = (
            lax.dot_general(
                left, o_near[...], (((1,), (1,)), ((), ())), preferred_element_type=f32
            ).astype(bf16)
        )

    at.meet()
    x_go.begin_along()
    x_go.begin_across()
    g_go.begin_across()
    loop(1, n_seq, lambda hop: t_send(hop).start())
    t_local.start()
    w_fan.y(at.s, w_ref.at[at.s]).start()
    w_fan.core(at.s, w_ref.at[at.s]).start()
    w_local.start()
    o_fan.y(0, o_ref).start()
    o_fan.core(0, o_ref).start()
    o_local.start()
    w_send(1).start()
    w_send(n_seq - 1).start()
    for hop in range(1, depth):
        x_go.step(hop)
        if hop == 1:
            t_local.wait()
            loop(1, n_seq, lambda k: t_recv(k).wait_recv())
            t_fan.y(0).start()
            t_fan.core(0).start()
        if hop == 2:
            t_fan.from_y(0).wait_recv()
            t_fan.pass_on(0).start()
        w_send(hop + 1).start()
        if hop + 1 < n_seq - hop - 1:
            w_send(n_seq - hop - 1).start()
    g_go.begin_along()

    @pl.when(at.y == 0)
    def _():
        o_send.start()

    t_fan.from_core(0).wait_recv()
    t_fan.from_diagonal(0).wait_recv()
    t_load = pltpu.make_async_copy(tiles, t_near, local_sems.at[3])
    t_load.start()
    t_load.wait()
    for p in range(t_near.shape[0]):
        for pair in range(n_seq // 2):
            two = t_near[p, 2 * pair, 0:8] + t_near[p, 2 * pair + 1, 0:8]
            lanes = two.shape[1]
            first = (p * (n_seq // 2) + pair) * lanes
            small[:, first : first + lanes] = two
    for k, some in enumerate((first_act, own, own)):
        o_near[(k + 1) * att + some : (k + 2) * att, :] = jnp.zeros((att - some, width), bf16)
    x_go.local().wait()

    def w_step(hop):
        src = at.seq(-hop)
        w_recv(hop).wait_recv()
        w_fan.y(src).start()
        w_fan.core(src).start()
        norm_block(hop - 1)

    loop(1, n_seq, w_step)
    norm_block(n_seq - 1)
    w_local.wait()
    w_in(at.p, 0).start()
    loop(0, n_seq, lambda k: w_fan.from_core(k).wait_recv())
    w_in(at.p_c, 2).start()
    def w_pass(hop):
        src = at.seq(-hop)
        w_fan.from_y(src).wait_recv()
        w_fan.pass_on(src).start()

    for hop in range(1, depth):
        g_go.step(hop)
        loop((hop - 1) * 3, min(hop * 3, n_seq), w_pass)
        if hop == 1:

            @pl.when(at.y == 0)
            def _():
                o_send.wait_recv()
                o_fan.y(1).start()
                o_fan.core(1).start()

            w_in(at.p, 0).wait()
            w_in(at.p_c, 2).wait()
        if hop == 2:
            loop(0, steps, lambda k: project(k, at.p, at.p_c, False))

    loop((depth - 1) * 3, n_seq, w_pass)
    w_in(at.p_y, 1).start()

    loop(0, n_seq, lambda k: w_fan.from_diagonal(k).wait_recv())
    w_in(at.p_d, 3).start()
    o_fan.from_y(0).wait_recv()
    o_fan.pass_on(0).start()

    @pl.when(at.y == 1)
    def _():
        o_fan.from_y(1).wait_recv()
        o_fan.pass_on(1).start()

    w_in(at.p_y, 1).wait()
    w_in(at.p_d, 3).wait()
    loop(0, steps, lambda k: project(k, at.p_y, at.p_d, True))

    o_local.wait()
    o_fan.from_core(0).wait_recv()
    o_fan.from_diagonal(0).wait_recv()

    @pl.when(at.y == 0)
    def _():
        o_fan.from_core(1).wait_recv()

    @pl.when(at.y == 1)
    def _():
        o_fan.from_diagonal(1).wait_recv()

    for k in (0, 2, 3, 4):
        o_in(k).start()

    @pl.when(at.s < n_seq - 1)
    def _():
        o_in(1).start()
        o_in(1).wait()

    @pl.when(at.s == n_seq - 1)
    def _():
        o_in(5).start()
        o_in(5).wait()

    for k in (0, 2, 3, 4):
        o_in(k).wait()
    o_out = pltpu.make_async_copy(o_near, out_mine, o_in_sems.at[6])
    o_out.start()
    g_go.local().wait()
    half = steps // 2
    for col in (at.x, 1 - at.x):
        if col is not at.x:
            g_go.arrive()
        g_in(col).start()
        g_in(col).wait()
        loop(0, half, lambda k: join_back(col * half + k))

    o_out.wait()
    loop(0, steps, lambda k: p_out(k).wait())
    loop(0, n_seq, lambda i: hid_out(i).wait())
    x_go.sent()
    g_go.sent()

    def w_sent(k):
        w_fan.y(k).wait_send()
        w_fan.core(k).wait_send()
        w_fan.pass_on(k).wait_send()

    loop(0, n_seq, w_sent)

    def seq_sent(hop):
        w_send(hop).wait_send()
        t_send(hop).wait_send()

    loop(1, n_seq, seq_sent)
    for fan in (t_fan, o_fan):
        fan.y(0).wait_send()
        fan.core(0).wait_send()
        fan.pass_on(0).wait_send()

    @pl.when(at.y == 0)
    def _():
        o_send.wait_send()
        o_fan.y(1).wait_send()
        o_fan.core(1).wait_send()

    @pl.when(at.y == 1)
    def _():
        o_fan.pass_on(1).wait_send()


def gather_all(n_dp, n_seq, late, lead, x, g, w, o, tile):
    depth = n_seq // 2
    own, width = o.shape
    block = x.shape[0] * x.shape[1]
    tokens = n_seq * block
    columns = w.shape[2]
    mine = n_dp * (own + lead)
    bf16, f32 = jnp.bfloat16, jnp.float32
    rest, near = pl.BlockSpec(memory_space=pl.ANY), pl.BlockSpec(memory_space=pltpu.VMEM)
    dma = pltpu.SemaphoreType.DMA
    like = lambda lead, ref: jax.ShapeDtypeStruct(lead + ref.shape, ref.dtype)
    return pl.pallas_call(
        functools.partial(gather_kernel, n_seq=n_seq, late=late, lead=lead),
        in_specs=[rest] * 5,
        out_specs=[rest] * 8 + [near],
        out_shape=[
            like((2, depth), x),
            like((2, depth), g),
            jax.ShapeDtypeStruct((n_dp,) + w.shape, w.dtype),
            jax.ShapeDtypeStruct((n_dp, own + late, width), o.dtype),
            like((n_dp, n_seq), tile),
            jax.ShapeDtypeStruct((2, depth, block, width), bf16),
            jax.ShapeDtypeStruct((mine, width), bf16),
            jax.ShapeDtypeStruct((tokens, columns), f32),
            jax.ShapeDtypeStruct((tokens, mine), bf16),
        ],
        scratch_shapes=[
            pltpu.VMEM(x.shape, bf16),
            pltpu.VMEM((2, depth, block, width), bf16),
            pltpu.VMEM((n_dp,) + w.shape, bf16),
            pltpu.VMEM((tokens, columns), f32),
            pltpu.VMEM((2, depth) + g.shape, bf16),
            pltpu.VMEM((mine, width), bf16),
            pltpu.VMEM((n_dp, n_seq) + tile.shape, f32),
            pltpu.VMEM((8, width), f32),
            dma((6, depth)), dma((6, depth)), dma((2, n_seq)), dma((6, n_seq)),
            dma((2,)), dma((6, 2)), dma((2, n_seq)), dma((6, 1)), dma((4,)),
            dma((1,)), dma((n_seq,)), dma((4,)), dma((tokens // (2 * block),)), dma((2,)), dma((7,)),
        ],
        compiler_params=pltpu.CompilerParams(
            collective_id=0, has_side_effects=True, vmem_limit_bytes=56 * 2**20
        ),
        name="gather_all",
    )(x, g, w, o, tile)

def add_rows(out, terms, rows=32):
    count = out.shape[0]

    def some(k):
        at = pl.ds(pl.multiple_of(k * rows, rows), rows)
        total = terms[0][at].astype(jnp.float32)
        for term in terms[1:]:
            total = total + term[at].astype(jnp.float32)
        out[at] = total.astype(out.dtype)

    loop(0, count // rows, some)


def reduce_kernel(
    in_ref, d_proj_ref, joined_ref, hidden_ref, g_ref, w_ref, o_ref,
    normed_ref, small_ref,
    sums, in_sum, out_sum, out_prev, small_sum,
    own_parts, x_got, z_got, in_own, in_core, in_y, out_own, out_core, out_y,
    small_own, small_core, small_y, small_seq,
    d_near, j_near, h_near, g_near, w_near, o_near, b_ref, out_ref,
    load_sems, x_sems, z_sems, in_core_sems, in_y_sems, in_sems, out_sems, small_sems, local_sem,
    w_sems, o_sems,
    *, n_seq, late, first_act, keep, plan,
):
    at = Place(n_seq)
    depth = at.depth
    main = out_own.shape[1] - late
    body, extra = pl.ds(0, main), pl.ds(main, late)
    y, c, z, x, s = at.y, at.c, at.z, at.x, at.s

    loads = [
        pltpu.make_async_copy(d_proj_ref, d_near, load_sems.at[0]),
        pltpu.make_async_copy(joined_ref, j_near, load_sems.at[1]),
        pltpu.make_async_copy(g_ref, g_near, load_sems.at[2]),
    ]
    feats = h_near.shape[4]
    for y_to in range(2):
        first = pl.multiple_of((2 * y_to + c) * feats, feats)
        loads.append(
            pltpu.make_async_copy(
                hidden_ref.at[:, :, :, pl.ds(first, feats)], h_near.at[y_to], load_sems.at[3 + y_to]
            )
        )
    dot = functools.partial(lax.dot_general, preferred_element_type=jnp.float32)
    low = jnp.bfloat16
    block_rows, width = own_parts.shape[2:]
    flat = lambda v: v.reshape(-1, v.shape[-1])

    def w_load(i):
        some = w_near.shape[1]
        return pltpu.make_async_copy(
            w_ref.at[pl.ds(pl.multiple_of(i * some, some), some)],
            w_near.at[lax.rem(i, 2)], w_sems.at[lax.rem(i, 2)],
        )

    def o_load(i):
        some = o_near.shape[2]
        return pltpu.make_async_copy(
            o_ref.at[:, pl.ds(pl.multiple_of(i * some, some), some)],
            o_near.at[lax.rem(i, 2)], o_sems.at[lax.rem(i, 2)],
        )

    def streamed(out, load, count, some, product):
        load(0).start()

        def one(i):
            @pl.when(i + 1 < count)
            def _():
                load(i + 1).start()

            load(i).wait()
            done = product(lax.rem(i, 2)).astype(low)
            columns = pl.ds(pl.multiple_of(i * some, some), some)
            out[:, :, columns] = done.reshape(depth, block_rows, some)

        loop(0, count, one)

    def work(i):
        if i == 5:
            for k in range(depth):
                to_across(0, k).wait_send()
        if i in (0, 7):
            some = w_near.shape[1]
            left = flat(d_near[x if i == 0 else 1 - x])
            streamed(
                own_parts.at[0] if i == 0 else b_ref, w_load, width // some, some,
                lambda k: dot(left, w_near[k], (((1,), (1,)), ((), ()))),
            )
        elif i in (1, 5):
            some = o_near.shape[2]
            left = flat(j_near[x if i == 1 else 1 - x])
            streamed(
                own_parts.at[1] if i == 1 else b_ref, o_load, width // some, some,
                lambda k: dot(left, o_near[k], (((1,), (0,)), ((), ()))),
            )
        elif i < 4:
            y_to = 1 - y if i == 2 else y
            left = flat(h_near[y_to])
            right = flat(d_near[...])
            total = right.shape[1]
            for first in range(0, total, 256):
                some = min(256, total - first)
                done = dot(left, right[:, first : first + some], (((0,), (0,)), ((), ())))
                in_own[y_to, :, :, first : first + some] = done.astype(low).reshape(
                    n_seq, -1, some
                )
        else:
            core = c if i == 4 else 1 - c
            for first in range(0, width, width // 4):
                at_n = slice(first, first + width // 4)
                right = flat(g_near[:, :, :, at_n])
                for y_to in range(2):
                    columns = pl.ds(pl.multiple_of((2 * y_to + core) * main, main), main)
                    done = dot(flat(j_near[:, :, :, columns]), right, (((0,), (0,)), ((), ())))
                    if i == 4:
                        out_own[y_to, body, at_n] = done.astype(low)
                    else:
                        out_ref[y_to * main : (y_to + 1) * main, at_n] = done.astype(low)
                if i == 4:
                    out_own[0, extra, at_n] = dot(
                        flat(j_near[:, :, :, keep : keep + late]), right, (((0,), (0,)), ((), ()))
                    ).astype(low)
            if i == 6:
                out_ref[2 * main :] = out_own[0, extra]

    def in_to_core(y_to, k):
        return remote(
            in_ref.at[y_to, k], in_core.at[y_to, k],
            in_core_sems.at[0, y_to, k], in_core_sems.at[1, y_to, k], at.to_c,
        )

    def out_to_core(y_to):
        return remote(
            out_ref.at[pl.ds(pl.multiple_of(y_to * main, main), main)], out_core.at[y_to, body],
            out_sems.at[0, y_to], out_sems.at[1, y_to], at.to_c,
        )

    extra_to_core = remote(
        out_ref.at[pl.ds(2 * main, late)], out_core.at[0, extra],
        out_sems.at[0, 2], out_sems.at[1, 2], at.to_c,
    )

    def to_across(kind, k):
        return remote(
            b_ref.at[k], x_got.at[kind, k],
            x_sems.at[0, kind, k], x_sems.at[1, kind, k], at.to_x,
        )

    def to_up(kind, k):
        return remote(
            x_got.at[kind, k], z_got.at[kind, k],
            z_sems.at[0, kind, k], z_sems.at[1, kind, k], at.to_up,
        )

    def to_down(kind, k):
        slot = jnp.where(k == z - 1, depth, k)
        return remote(
            x_got.at[kind, k], z_got.at[kind, slot],
            z_sems.at[0, kind, k], z_sems.at[1, kind, slot], at.to_down,
        )

    def from_depth(kind, slot):
        here = z_got.at[kind, slot]
        return remote(here, here, z_sems.at[0, kind, slot], z_sems.at[1, kind, slot], at.to_up)

    def in_to_y(k):
        return remote(
            in_core.at[1 - y, k], in_y.at[k], in_y_sems.at[0, k], in_y_sems.at[1, k], at.to_y
        )

    def in_to_owner(k):
        return remote(
            in_core.at[y, k], in_sum.at[s], in_sems.at[0, k], in_sems.at[1, s], (at.p, k)
        )

    def in_from(k):
        here = in_sum.at[k]
        return remote(here, here, in_sems.at[0, k], in_sems.at[1, k], (at.p, k))

    in_keep = pltpu.make_async_copy(in_core.at[y, s], in_sum.at[s], local_sem.at[0])
    out_to_y = remote(
        out_core.at[1 - y, body], out_y.at[body], out_sems.at[0, 3], out_sems.at[1, 3], at.to_y
    )
    extra_to_y = remote(
        out_core.at[0, extra], out_y.at[extra], out_sems.at[0, 4], out_sems.at[1, 4], at.to_y
    )

    def out_shift(start):
        return remote(
            out_sum.at[pl.ds(start, late)], out_prev,
            out_sems.at[0, 5], out_sems.at[1, 5], (at.p, at.seq(1)),
        )

    small_to_core = remote(small_own, small_core, small_sems.at[0, 0], small_sems.at[1, 0], at.to_c)
    small_to_y = remote(small_core, small_y, small_sems.at[0, 1], small_sems.at[1, 1], at.to_y)

    def small_to(hop):
        to = at.seq(hop)
        first = (at.p * n_seq + to) // 2 * lanes
        return remote(
            small_y.at[:, pl.ds(pl.multiple_of(first, lanes), lanes)], small_seq.at[s],
            small_sems.at[0, 2 + to], small_sems.at[1, 2 + s], (at.p, to),
        )

    def small_from(hop):
        src = at.seq(-hop)
        here = small_seq.at[src]
        return remote(
            here, here, small_sems.at[0, 2 + src], small_sems.at[1, 2 + src], (at.p, src)
        )

    chained, steps = plan
    lanes = small_sum.shape[1]

    def around_z(hop):
        return lax.rem(z + hop, depth)

    def to_depth(kind, k):
        return remote(
            x_got.at[kind, k], z_got.at[kind, z],
            z_sems.at[0, kind, k], z_sems.at[1, kind, z], (at.p, 2 * k + x),
        )

    def turn(i):
        return jnp.where(lax.rem(i, 2) == 0, depth - 1 - i // 2, i // 2)

    def order(kind, i):
        return turn(i) if chained[kind] else around_z(i + 1)

    def across(j):
        to_across(j // depth, order(j // depth, j % depth)).start()

    def straight(kind, i):
        k = around_z(i + 1)
        to_across(kind, k).wait_recv()
        add_rows(x_got.at[kind, k], [x_got.at[kind, k], own_parts.at[kind, k]])
        if i + 1 < depth:
            to_depth(kind, k).start()

    def chain(kind, i):
        k = turn(i)
        to_across(kind, k).wait_recv()
        got, mine = x_got.at[kind, k], own_parts.at[kind, k]
        begins = ((z == 0) & (k > 0)) | ((z == depth - 1) & (k < depth - 1)) | (z == k)

        @pl.when(begins)
        def _():
            add_rows(got, [got, mine])

        @pl.when(jnp.logical_not(begins))
        def _():
            from_depth(kind, k).wait_recv()
            add_rows(got, [got, mine, z_got.at[kind, k]])

        @pl.when(z < k)
        def _():
            to_up(kind, k).start()

        @pl.when(z > k)
        def _():
            to_down(kind, k).start()

    def finish(kind):
        if not chained[kind]:
            others = [around_z(hop) for hop in range(1, depth)]
            for k in others:
                from_depth(kind, k).wait_recv()
            add_rows(
                sums.at[kind], [x_got.at[kind, z]] + [z_got.at[kind, k] for k in others], rows=16
            )
            return
        add_rows(sums.at[kind], [x_got.at[kind, z]], rows=16)

        @pl.when(z > 0)
        def _():
            from_depth(kind, z).wait_recv()
            add_rows(sums.at[kind], [sums.at[kind], z_got.at[kind, z]], rows=16)

        @pl.when(z < depth - 1)
        def _():
            from_depth(kind, depth).wait_recv()
            add_rows(sums.at[kind], [sums.at[kind], z_got.at[kind, depth]], rows=16)

    def to_y_step(hop):
        k = at.seq(hop)
        in_to_core(1 - y, k).wait_recv()
        add_rows(in_core.at[1 - y, k], [in_core.at[1 - y, k], in_own.at[1 - y, k]])
        in_to_y(k).start()

    def owner_step(hop):
        k = at.seq(hop)
        in_to_core(y, k).wait_recv()
        in_to_y(k).wait_recv()
        add_rows(in_core.at[y, k], [in_core.at[y, k], in_own.at[y, k], in_y.at[k]])

        @pl.when(k != s)
        def _():
            in_to_owner(k).start()

        @pl.when(k == s)
        def _():
            in_keep.start()

    def out_y_step():
        out_to_core(1 - y).wait_recv()
        extra_to_core.wait_recv()
        add_rows(out_core.at[1 - y, body], [out_core.at[1 - y, body], out_own.at[1 - y, body]])
        out_to_y.start()

        @pl.when(y == 1)
        def _():
            add_rows(out_core.at[0, extra], [out_core.at[0, extra], out_own.at[0, extra]])
            extra_to_y.start()

    def out_end():
        out_to_core(y).wait_recv()
        out_to_y.wait_recv()
        add_rows(out_sum.at[body], [out_core.at[y, body], out_own.at[y, body], out_y.at[body]])

        @pl.when(y == 0)
        def _():
            extra_to_y.wait_recv()
            add_rows(
                out_sum.at[extra], [out_core.at[0, extra], out_own.at[0, extra], out_y.at[extra]]
            )

            @pl.when(c == 0)
            def _():
                out_shift(keep).start()

            @pl.when((c == 1) & (s == n_seq - 1))
            def _():
                out_shift(main).start()

            @pl.when((c == 1) & (s < n_seq - 1))
            def _():
                out_shift(first_act - late).start()

    def small_step(i):
        if i == 0:
            finish(0)
            small_own[...] = small_ref[...]
            d_hidden = sums[0]
            small_own[0:1, :] = jnp.sum(d_hidden * normed_ref[...], axis=0, keepdims=True)
            small_own[1:2, :] = jnp.sum(d_hidden, axis=0, keepdims=True)
            small_to_core.start()
        elif i == 1:
            small_to_core.wait_recv()
            small_core[...] = small_core[...] + small_own[...]
            small_to_y.start()
        elif i == 2:
            small_to_y.wait()
            small_y[...] = small_core[...] + small_y[...]
            loop(1, n_seq, lambda hop: small_to(hop).start())
        else:
            first = (at.p * n_seq + s) // 2 * lanes
            small_sum[...] = small_y[:, pl.ds(pl.multiple_of(first, lanes), lanes)]

            def small_add(hop):
                small_from(hop).wait_recv()
                small_sum[...] = small_sum[...] + small_seq[at.seq(-hop)]

            loop(1, n_seq, small_add)

    def core_step(i):
        if i == 0:
            loads[0].start()
            loop(0, n_seq, lambda hop: in_to_core(1 - y, at.seq(hop)).start())
            for load in loads[1:]:
                load.start()
        elif i == 1:
            loop(0, n_seq, lambda hop: in_to_core(y, at.seq(hop)).start())
        elif i == 2:
            out_to_core(1 - y).start()
            out_to_core(y).start()
            extra_to_core.start()
        elif i == 3:
            for load in loads[1:]:
                load.wait()
        else:
            loads[0].wait()

    at.meet()
    for what, i in steps:
        if what == 0:
            across(i)
        elif what == 1:
            core_step(i)
        elif what == 2:
            to_y_step(i)
        elif what == 3:
            owner_step(i)
        elif what == 4:
            kind = i // depth
            (chain if chained[kind] else straight)(kind, i % depth)
        elif what == 5:
            small_step(i)
        elif what == 7:
            work(i)
        elif i == 0:
            out_y_step()
        else:
            out_end()
    finish(1)

    @pl.when(y == 0)
    def _():
        out_shift(0).wait()

    def in_last(hop):
        k = at.seq(hop)
        in_from(k).wait_recv()
        in_to_owner(k).wait_send()

    loop(1, n_seq, in_last)
    in_keep.wait()

    def seq_sent(k):
        for y_to in range(2):
            in_to_core(y_to, k).wait_send()
        in_to_y(k).wait_send()

    loop(0, n_seq, seq_sent)
    loop(1, n_seq, lambda hop: small_to(hop).wait_send())
    small_to_core.wait_send()
    for y_to in range(2):
        out_to_core(y_to).wait_send()
    extra_to_core.wait_send()
    out_to_y.wait_send()

    @pl.when(y == 1)
    def _():
        extra_to_y.wait_send()

    for kind in range(2):
        for k in range(depth):
            if kind == 1:
                to_across(kind, k).wait_send()

            @pl.when(z < k)
            def _():
                (to_up if chained[kind] else to_depth)(kind, k).wait_send()

            @pl.when(z > k)
            def _():
                (to_down if chained[kind] else to_depth)(kind, k).wait_send()


def reduce_all(
    plan, n_dp, n_seq, late, first_act, keep, in_sent, d_proj, joined, hidden, g, w, o, normed, small
):
    depth = n_seq // 2
    block = (g.shape[2], g.shape[3])
    in_block = in_sent.shape[2:]
    width = block[1]
    main = joined.shape[-1] // n_dp
    slot = main + late
    bf16, f32 = jnp.bfloat16, jnp.float32
    rest, near = pl.BlockSpec(memory_space=pl.ANY), pl.BlockSpec(memory_space=pltpu.VMEM)
    dma = pltpu.SemaphoreType.DMA
    return pl.pallas_call(
        functools.partial(
            reduce_kernel, n_seq=n_seq, late=late, first_act=first_act, keep=keep, plan=plan
        ),
        in_specs=[rest] * 7 + [near, near],
        out_specs=[near, rest, near, rest, near],
        out_shape=[
            jax.ShapeDtypeStruct((2,) + block, f32),
            jax.ShapeDtypeStruct((n_seq,) + in_block, bf16),
            jax.ShapeDtypeStruct((slot, width), bf16),
            jax.ShapeDtypeStruct((late, width), bf16),
            jax.ShapeDtypeStruct((small.shape[0], 128), f32),
        ],
        scratch_shapes=[
            pltpu.VMEM((2, depth) + block, bf16),
            pltpu.VMEM((2, depth) + block, bf16),
            pltpu.VMEM((2, depth + 1) + block, bf16),
            pltpu.VMEM((2, n_seq) + in_block, bf16),
            pltpu.VMEM((2, n_seq) + in_block, bf16),
            pltpu.VMEM((n_seq,) + in_block, bf16),
            pltpu.VMEM((2, slot, width), bf16),
            pltpu.VMEM((2, slot, width), bf16),
            pltpu.VMEM((slot, width), bf16),
            pltpu.VMEM(small.shape, f32),
            pltpu.VMEM(small.shape, f32),
            pltpu.VMEM(small.shape, f32),
            pltpu.VMEM((n_seq, small.shape[0], 128), f32),
            pltpu.VMEM(d_proj.shape, bf16),
            pltpu.VMEM(joined.shape, bf16),
            pltpu.VMEM((2,) + hidden.shape[:3] + (width // n_dp,), bf16),
            pltpu.VMEM(g.shape, bf16),
            pltpu.VMEM((2, 256, w.shape[1]), bf16),
            pltpu.VMEM((2, o.shape[0], 256), bf16),
            pltpu.VMEM((depth,) + block, bf16),
            pltpu.VMEM((2 * main + late, width), bf16),
            dma((7,)), dma((2, 2, depth)), dma((2, 2, depth + 1)), dma((2, 2, n_seq)), dma((2, n_seq)),
            dma((2, n_seq)), dma((2, 6)), dma((2, 2 + n_seq)), dma((1,)), dma((2,)), dma((2,)),
        ],
        compiler_params=pltpu.CompilerParams(
            collective_id=1, has_side_effects=True, vmem_limit_bytes=60 * 2**20
        ),
        name="reduce_all",
    )(in_sent, d_proj, joined, hidden, g, w, o, normed, small)

def shares(n_seq, width, ffn, att, act):
    stretches, at = [], 0
    for i in range(3):
        stretches.append((i * width, at, att))
        at += att
    for half in range(2):
        first = 3 * width + half * ffn
        for some in act:
            stretches.append((first, at, some))
            at += some
            first += some * n_seq
    return stretches


def share_kernel(w_ref, out_ref, *, stretches):
    for s in range(out_ref.shape[0]):
        parts = [w_ref[:, first + s * some : first + (s + 1) * some] for first, _, some in stretches]
        out_ref[s] = jnp.concatenate(parts, axis=1).astype(out_ref.dtype)


def share_out(weight, n_seq, stretches):
    rows, columns = weight.shape
    step = 16
    return pl.pallas_call(
        functools.partial(share_kernel, stretches=stretches),
        grid=(rows // step,),
        in_specs=[pl.BlockSpec((step, columns), lambda i: (i, 0))],
        out_specs=pl.BlockSpec((n_seq, step, columns // n_seq), lambda i: (0, i, 0)),
        out_shape=jax.ShapeDtypeStruct((n_seq, rows, columns // n_seq), jnp.bfloat16),
        compiler_params=pltpu.CompilerParams(vmem_limit_bytes=56 * 2**20),
        name="share_out",
    )(weight)


def update_kernel(
    sum_ref, w_ref, m_ref, v_ref, a_ref, w_out, v_out, a_out, g_out, *, stretches, rate, decay
):
    n_seq = sum_ref.shape[0]
    for first, at, some in stretches:
        columns = slice(first, first + n_seq * some)
        parts = [sum_ref[s, :, at : at + some].astype(jnp.float32) for s in range(n_seq)]
        gradient = jnp.concatenate(parts, axis=1)
        g_out[:, columns] = gradient
        w_out[:, columns], v_out[:, columns], a_out[:, columns] = adam_update(
            w_ref[:, columns], m_ref[:, columns], v_ref[:, columns], a_ref[:, columns],
            gradient, rate, decay,
        )


def update_in(sums, weight, first, second, average, stretches):
    n_seq, rows, share = sums.shape
    step = 16
    wide = pl.BlockSpec((step, weight.shape[1]), lambda i: (i, 0))
    out = jax.ShapeDtypeStruct(weight.shape, jnp.float32)
    return pl.pallas_call(
        functools.partial(
            update_kernel, stretches=stretches, rate=matrix_rate, decay=weight_decay
        ),
        grid=(rows // step,),
        in_specs=[pl.BlockSpec((n_seq, step, share), lambda i: (0, i, 0))] + [wide] * 4,
        out_specs=[wide] * 4,
        out_shape=[out] * 4,
        compiler_params=pltpu.CompilerParams(vmem_limit_bytes=56 * 2**20),
        name="update_in",
    )(sums, weight, first, second, average)

def split_heads(
    n_dp, n_seq, tokens, cotangent, segment_ids, doc_positions,
    in_weight, in_first, in_second, in_average,
    out_weight, out_first, out_second, out_average,
    small_params, small_first, small_second, small_average,
):
    bf16, f32 = jnp.bfloat16, jnp.float32
    rows, own_tokens, width = tokens.shape
    row_tokens = own_tokens * n_seq
    all_tokens = rows * row_tokens
    head_size = width // HEADS
    ffn = (in_weight.shape[1] - 3 * width) // 2
    in_rows, own = in_weight.shape[0], out_weight.shape[0]
    dp_rows = own * n_seq
    att = width // n_seq
    late = width - dp_rows
    act = [(dp_rows - late) // n_seq, own, own]
    act_all = sum(act)
    lead = att - own
    p, s = lax.axis_index("dp"), lax.axis_index("seq")

    stretches = shares(n_seq, width, ffn, att, act)
    out_low = out_weight.astype(bf16)
    small_low = small_params.astype(bf16).astype(f32).T
    widen = lambda v, n: jnp.pad(v, ((0, n - v.shape[0]), (0, 128 - v.shape[1])))
    tile = jnp.concatenate(
        [
            widen(small_low, 8),
            widen(jnp.concatenate([segment_ids, doc_positions], axis=0).astype(f32), 8),
        ],
        axis=0,
    )
    odd = jnp.concatenate([jnp.zeros_like(tile[:8, :in_rows]), tile[:8, :in_rows]], axis=1)
    tile = jnp.concatenate([jnp.where(s % 2 == 1, odd, tile[:8]), tile[8:]], axis=0)
    _, g_full, in_low, _, tiles, hidden, out_mine, proj, d_joined = gather_all(
        n_dp, n_seq, late, lead, tokens, cotangent, share_out(in_weight, n_seq, stretches), out_low, tile
    )
    g_full, hidden = g_full.reshape(all_tokens, width), hidden.reshape(all_tokens, width)
    in_low = in_low.reshape(n_dp * n_seq * in_rows, 3 * att + 2 * act_all)

    pairs = tiles[:, :, :5].reshape(n_dp, n_seq // 2, 2, 5, 2 * in_rows).sum(axis=2)
    small_low = jnp.transpose(pairs, (2, 0, 1, 3)).reshape(5, width)
    gain = small_low[0]
    bias = lax.dynamic_slice_in_dim(small_low[2:5], s * att, att, 1).reshape(1, 3 * att)
    docs = lax.dynamic_index_in_dim(tiles, p, 0, keepdims=False)[:, 8:, :own_tokens]
    seg_full = jnp.transpose(docs[:, :rows], (1, 0, 2)).reshape(rows, row_tokens)
    pos_full = jnp.transpose(docs[:, rows : 2 * rows], (1, 0, 2)).reshape(rows, row_tokens)
    last = s == n_seq - 1
    keep = att - late

    def normalise(v):
        v = v.astype(f32)
        centered = v - jnp.mean(v, axis=-1, keepdims=True)
        inv_std = lax.rsqrt(jnp.mean(centered * centered, axis=-1, keepdims=True) + norm_eps)
        return centered * inv_std, inv_std

    half_rot = ROT // 2
    inv_freq = rope_base ** (-2.0 * jnp.arange(half_rot, dtype=f32) / ROT)
    angles = pos_full[:, None, :] * inv_freq[:, None]
    cos, sin = jnp.cos(angles), jnp.sin(angles)
    one, zero = jnp.ones((rows, head_size - ROT, row_tokens), f32), jnp.zeros_like(cos)
    rest = 0.0 * one
    rope = jnp.stack(
        [
            jnp.concatenate([cos, cos, one] * 2, axis=1),
            jnp.concatenate([-sin, zero, rest] * 2, axis=1),
            jnp.concatenate([zero, sin, rest] * 2, axis=1),
        ],
        axis=1,
    )
    joined, d_proj, bias_part = middle(
        proj, bias, d_joined, rope, seg_full, n_seq, att, act, head_size
    )

    blocks = lambda v: v.reshape(2, n_seq // 2, rows * own_tokens, v.shape[-1])
    c = p % 2
    def to_core(v):
        some = v.shape[1] // n_dp
        firsts = [(2 * y_to + 1 - c) * some for y_to in range(2)]
        return [lax.dynamic_slice_in_dim(v, first, some, 1) for first in firsts]

    over_tokens = lambda a, b: lax.dot_general(
        a, b, (((0,), (0,)), ((), ())), preferred_element_type=f32
    ).astype(bf16)
    in_sent = over_tokens(jnp.concatenate(to_core(hidden), axis=1), d_proj).reshape(2, n_seq, in_rows, -1)
    normed, inv_std = normalise(tokens.reshape(rows * own_tokens, width))
    small_part = lax.dynamic_update_slice(jnp.zeros((8, width), f32), bias_part[:3], (2, s * att))
    plan = ((1, 1), ((1, 0), (1, 4), (7, 7), (0, 0), (0, 1), (0, 2), (0, 3), (1, 1), (1, 3), (7, 2), (2, 0), (2, 1), (2, 2), (2, 3), (2, 4), (2, 5), (2, 6), (2, 7), (7, 4), (7, 6), (1, 2), (7, 0), (4, 0), (7, 3), (3, 0), (3, 1), (6, 0), (4, 1), (3, 2), (3, 3), (4, 2), (7, 5), (0, 4), (0, 5), (0, 6), (0, 7), (3, 4), (3, 5), (7, 1), (4, 3), (3, 6), (3, 7), (5, 0), (4, 4), (5, 1), (4, 5), (5, 2), (6, 1), (4, 6), (4, 7), (5, 3)))
    sums, in_sum, out_sum, from_prev, small_sum = reduce_all(
        plan, n_dp, n_seq, late, act[0], keep,
        in_sent,
        blocks(d_proj), blocks(joined), blocks(hidden), blocks(g_full), in_low, out_mine,
        normed, small_part,
    )
    d_hidden, branch = sums[0], sums[1]

    output = (tokens.astype(f32) + branch.reshape(tokens.shape)).astype(bf16)
    d_normed = d_hidden * gain
    input_grad = cotangent.astype(f32) + (
        inv_std
        * (
            d_normed
            - jnp.mean(d_normed, axis=-1, keepdims=True)
            - normed * jnp.mean(d_normed * normed, axis=-1, keepdims=True)
        )
    ).reshape(tokens.shape)
    small_grad = lax.dynamic_slice(small_sum, (0, s % 2 * in_rows), (8, in_rows))[:5].T

    count = jnp.where(p == 0, lead * s, jnp.where(p == 1, late - lead * s, 0))
    out_grad = lax.dynamic_slice_in_dim(
        jnp.concatenate([from_prev, out_sum[:own]], axis=0), late - count, own, 0
    ).astype(f32)

    *in_new, in_grad = update_in(
        in_sum, in_weight, in_first, in_second, in_average, stretches
    )
    out_new = adam_update(
        out_weight, out_first, out_second, out_average, out_grad, matrix_rate, weight_decay
    )
    small_new = adam_update(
        small_params, small_first, small_second, small_average, small_grad, small_rate, 0.0
    )
    return (output, input_grad, *in_new, *out_new, *small_new, small_grad, in_grad, out_grad)


def solution(mesh):
    n_dp, n_seq = mesh.shape["dp"], mesh.shape["seq"]

    def choose(*operands):
        own_rows = operands[8].shape[0]
        model_width = operands[0].shape[2]
        if heads_fit(n_dp, n_seq, own_rows, model_width, operands[4].shape[1]):
            return split_heads(n_dp, n_seq, *operands)
        return per_device(*operands)

    return jax.shard_map(
        choose,
        mesh=mesh,
        in_specs=(
            P("dp", "seq", None),
            P("dp", "seq", None),
            P("dp", "seq"),
            P("dp", "seq"),
            P(("dp", "seq"), None),
            P(("dp", "seq"), None),
            P(("dp", "seq"), None),
            P(("dp", "seq"), None),
            P(("dp", "seq"), None),
            P(("dp", "seq"), None),
            P(("dp", "seq"), None),
            P(("dp", "seq"), None),
            P(("dp", "seq"), None),
            P(("dp", "seq"), None),
            P(("dp", "seq"), None),
            P(("dp", "seq"), None),
        ),
        out_specs=(
            P("dp", "seq", None),
            P("dp", "seq", None),
            P(("dp", "seq"), None),
            P(("dp", "seq"), None),
            P(("dp", "seq"), None),
            P(("dp", "seq"), None),
            P(("dp", "seq"), None),
            P(("dp", "seq"), None),
            P(("dp", "seq"), None),
            P(("dp", "seq"), None),
            P(("dp", "seq"), None),
            P(("dp", "seq"), None),
            P(("dp", "seq"), None),
            P(("dp", "seq"), None),
        ),
        check_vma=False,
    )
```

```python
import functools

import jax
import jax.numpy as jnp
from jax import lax
from jax.experimental import pallas as pl
from jax.experimental.pallas import tpu as pltpu
from jax.sharding import PartitionSpec as P

HEADS = 32
ROT = 16
STEP = 2


beta_one = 0.9
adam_eps = 1e-08
matrix_rate = 0.001
small_rate = 0.01
weight_decay = 0.1
norm_eps = 1e-05
rope_base = 10000.0
neg_large = -1e30


def rope_tables(positions, rot_dims):
    half_rot = rot_dims // 2
    inv_freq = rope_base ** (-2.0 * jnp.arange(half_rot, dtype=jnp.float32) / rot_dims)
    angles = positions.astype(jnp.float32)[..., None] * inv_freq
    return (jnp.cos(angles)[..., None, :], jnp.sin(angles)[..., None, :])


def apply_rope(field_in, cosine_tab, sine_tab, rot_dims):
    half_rot = rot_dims // 2
    low_half = field_in[..., :half_rot]
    high_half = field_in[..., half_rot:rot_dims]
    return jnp.concatenate(
        [
            low_half * cosine_tab - high_half * sine_tab,
            high_half * cosine_tab + low_half * sine_tab,
            field_in[..., rot_dims:],
        ],
        axis=-1,
    )


def undo_rope(grad_in, cosine_tab, sine_tab, rot_dims):
    half_rot = rot_dims // 2
    low_half = grad_in[..., :half_rot]
    high_half = grad_in[..., half_rot:rot_dims]
    return jnp.concatenate(
        [
            low_half * cosine_tab + high_half * sine_tab,
            high_half * cosine_tab - low_half * sine_tab,
            grad_in[..., rot_dims:],
        ],
        axis=-1,
    )


def visible(query_seg, key_seg, query_pos, key_pos):
    same_doc = query_seg[:, :, None] == key_seg[:, None, :]
    causal = key_pos[None, :] <= query_pos[:, None]
    return (same_doc & causal[None])[:, None]


def to_tokens(head_major):
    return jnp.transpose(head_major, (0, 2, 1, 3))


def adam_update(weight, first, second, average, gradient, rate, decay_rate):
    beta_two = 1.0 - STEP ** (-0.8)
    average_keep = min(0.999, (1.0 + STEP) / (10.0 + STEP))
    first_new = beta_one * first + (1.0 - beta_one) * gradient
    second_new = beta_two * second + (1.0 - beta_two) * gradient * gradient
    moment_hat = beta_one * first_new / (1.0 - beta_one ** (STEP + 1)) + (
        1.0 - beta_one
    ) * gradient / (1.0 - beta_one**STEP)
    weight_new = weight - rate * (
        moment_hat / (jnp.sqrt(second_new) + adam_eps) + decay_rate * weight
    )
    average_new = average_keep * average + (1.0 - average_keep) * weight_new
    return (weight_new, second_new, average_new)


def per_device(
    tokens,
    cotangent,
    segment_ids,
    doc_positions,
    in_weight,
    in_first,
    in_second,
    in_average,
    out_weight,
    out_first,
    out_second,
    out_average,
    small_params,
    small_first,
    small_second,
    small_average,
):
    rows_here, row_tokens, model_width = tokens.shape
    head_count = HEADS
    head_size = model_width // head_count
    score_scale = head_size ** (-0.5)
    all_tokens = rows_here * row_tokens
    wide_in = in_weight.shape[1]
    ffn_width = (wide_in - 3 * model_width) // 2
    shape_heads = (rows_here, row_tokens, head_count, head_size)
    own_places = lax.axis_index("seq") * row_tokens + jnp.arange(row_tokens)
    flat_in = tokens.astype(jnp.float32).reshape(all_tokens, model_width)
    centered = flat_in - jnp.mean(flat_in, axis=-1, keepdims=True)
    inv_std = lax.rsqrt(jnp.mean(centered * centered, axis=-1, keepdims=True) + norm_eps)
    normed = centered * inv_std
    in_low = in_weight.astype(jnp.bfloat16)
    out_low = out_weight.astype(jnp.bfloat16)
    small_low = small_params.astype(jnp.bfloat16)
    w_piece = lax.all_gather(in_low, ("dp", "seq"), axis=0, tiled=True)
    s_piece = lax.all_gather(small_low, ("dp", "seq"), axis=0, tiled=True)
    columns = normed
    s_float = s_piece.astype(jnp.float32)
    h_piece = (columns * s_float[:, 0] + s_float[:, 1]).astype(jnp.bfloat16)
    proj_acc = jnp.dot(h_piece, w_piece, preferred_element_type=jnp.float32)
    norm_gain = s_float[:, 0]
    qkv_bias = s_float[:, 2:5].T.reshape(3 * model_width)
    qkv_full = proj_acc[:, : 3 * model_width] + qkv_bias
    gate_pre = proj_acc[:, 3 * model_width : 3 * model_width + ffn_width]
    up_pre = proj_acc[:, 3 * model_width + ffn_width :]
    cosine_tab, sine_tab = rope_tables(doc_positions, ROT)
    query_low = apply_rope(
        qkv_full[:, :model_width].reshape(shape_heads), cosine_tab, sine_tab, ROT
    ).astype(jnp.bfloat16)
    key_low = apply_rope(
        qkv_full[:, model_width : 2 * model_width].reshape(shape_heads), cosine_tab, sine_tab, ROT
    ).astype(jnp.bfloat16)
    value_low = qkv_full[:, 2 * model_width :].reshape(shape_heads).astype(jnp.bfloat16)
    seg_low = segment_ids.astype(jnp.bfloat16)
    seg_own = segment_ids.astype(jnp.float32)
    key_flat = key_low.reshape(rows_here, row_tokens, model_width)
    value_flat = value_low.reshape(rows_here, row_tokens, model_width)
    attend_init = (
        jnp.full((rows_here, head_count, row_tokens), neg_large, jnp.float32),
        jnp.zeros((rows_here, head_count, row_tokens), jnp.float32),
        jnp.zeros((rows_here, head_count, row_tokens, head_size), jnp.float32),
    )
    key_piece = lax.all_gather(key_flat, "seq", axis=1, tiled=True)
    value_piece = lax.all_gather(value_flat, "seq", axis=1, tiled=True)
    seg_piece = lax.all_gather(seg_low, "seq", axis=1, tiled=True)
    turn_count = key_piece.shape[1] // row_tokens

    def attend_one_turn(turn_index, inner_state):
        offset = turn_index * row_tokens
        key_blk = lax.dynamic_slice_in_dim(key_piece, offset, row_tokens, 1).reshape(shape_heads)
        value_blk = lax.dynamic_slice_in_dim(value_piece, offset, row_tokens, 1).reshape(
            shape_heads
        )
        seg_blk = lax.dynamic_slice_in_dim(seg_piece, offset, row_tokens, 1).astype(jnp.float32)
        key_mask = visible(seg_own, seg_blk, own_places, offset + jnp.arange(row_tokens))
        running_top, running_sum, weighted = inner_state
        scores = (
            jnp.einsum("rqhe,rkhe->rhqk", query_low, key_blk, preferred_element_type=jnp.float32)
            * score_scale
        )
        scores = jnp.where(key_mask, scores, neg_large)
        new_top = jnp.maximum(running_top, jnp.max(scores, axis=-1))
        weights = jnp.where(key_mask, jnp.exp(scores - new_top[..., None]), 0.0)
        factor = jnp.exp(running_top - new_top)
        running_sum = running_sum * factor + jnp.sum(weights, axis=-1)
        weighted = weighted * factor[..., None] + jnp.einsum(
            "rhqk,rkhe->rhqe",
            weights.astype(jnp.bfloat16),
            value_blk,
            preferred_element_type=jnp.float32,
        )
        return (new_top, running_sum, weighted)

    running_top, running_sum, weighted = lax.fori_loop(0, turn_count, attend_one_turn, attend_init)
    attended = weighted / running_sum[..., None]
    log_total = running_top + jnp.log(running_sum)
    attended_low = to_tokens(attended).reshape(all_tokens, model_width).astype(jnp.bfloat16)
    gate_sig = jax.nn.sigmoid(gate_pre)
    activated = gate_pre * gate_sig * up_pre
    joined = jnp.concatenate([attended_low, activated.astype(jnp.bfloat16)], axis=1)
    columns = joined
    branch_sum = jnp.dot(
        columns,
        lax.all_gather(out_low, ("dp", "seq"), axis=0, tiled=True),
        preferred_element_type=jnp.float32,
    )
    output = (flat_in + branch_sum).astype(jnp.bfloat16).reshape(rows_here, row_tokens, model_width)
    grad_out = cotangent.reshape(all_tokens, model_width)
    d_joined = lax.dot_general(
        grad_out,
        lax.all_gather(out_low, ("dp", "seq"), axis=0, tiled=True),
        (((1,), (1,)), ((), ())),
        preferred_element_type=jnp.float32,
    )
    d_joined = d_joined.astype(jnp.bfloat16)
    columns = joined
    out_grad = lax.psum_scatter(
        lax.dot_general(
            columns, grad_out, (((0,), (0,)), ((), ())), preferred_element_type=jnp.float32
        ),
        ("dp", "seq"),
        scatter_dimension=0,
        tiled=True,
    )
    d_attended = d_joined[:, :model_width].reshape(shape_heads)
    d_act = d_joined[:, model_width:].astype(jnp.float32)
    d_gate = d_act * up_pre * gate_sig * (1.0 + gate_pre * (1.0 - gate_sig))
    d_up = d_act * gate_pre * gate_sig
    out_dot = jnp.einsum("rqhe,rhqe->rhq", d_attended.astype(jnp.float32), attended)
    grad_zero = jnp.zeros((rows_here, head_count, row_tokens, head_size), jnp.float32)
    query_key_piece = lax.all_gather(key_flat, "seq", axis=1, tiled=True)
    query_value_piece = lax.all_gather(value_flat, "seq", axis=1, tiled=True)
    query_seg_piece = lax.all_gather(seg_low, "seq", axis=1, tiled=True)
    turn_count = query_key_piece.shape[1] // row_tokens

    def query_one_turn(turn_index, inner_state):
        offset = turn_index * row_tokens
        key_blk = lax.dynamic_slice_in_dim(query_key_piece, offset, row_tokens, 1).reshape(
            shape_heads
        )
        value_blk = lax.dynamic_slice_in_dim(query_value_piece, offset, row_tokens, 1).reshape(
            shape_heads
        )
        seg_blk = lax.dynamic_slice_in_dim(query_seg_piece, offset, row_tokens, 1).astype(
            jnp.float32
        )
        key_mask = visible(seg_own, seg_blk, own_places, offset + jnp.arange(row_tokens))
        scores = (
            jnp.einsum("rqhe,rkhe->rhqk", query_low, key_blk, preferred_element_type=jnp.float32)
            * score_scale
        )
        weights = jnp.where(key_mask, jnp.exp(scores - log_total[..., None]), 0.0)
        d_prob = jnp.einsum(
            "rqhe,rkhe->rhqk", d_attended, value_blk, preferred_element_type=jnp.float32
        )
        d_score = (weights * (d_prob - out_dot[..., None])).astype(jnp.bfloat16)
        return (
            inner_state
            + jnp.einsum("rhqk,rkhe->rhqe", d_score, key_blk, preferred_element_type=jnp.float32)
            * score_scale
        )

    d_query = lax.fori_loop(0, turn_count, query_one_turn, grad_zero)
    row_stats = jnp.concatenate(
        [jnp.transpose(log_total, (0, 2, 1)), jnp.transpose(out_dot, (0, 2, 1))], axis=2
    )
    stat_high = row_stats.astype(jnp.bfloat16)
    stat_low = (row_stats - stat_high.astype(jnp.float32)).astype(jnp.bfloat16)
    query_flat = query_low.reshape(rows_here, row_tokens, model_width)
    d_att_flat = d_attended.reshape(rows_here, row_tokens, model_width)
    query_piece = lax.all_gather(query_flat, "seq", axis=1, tiled=True)
    dout_piece = lax.all_gather(d_att_flat, "seq", axis=1, tiled=True)
    high_piece = lax.all_gather(stat_high, "seq", axis=1, tiled=True)
    low_piece = lax.all_gather(stat_low, "seq", axis=1, tiled=True)
    key_seg_piece = lax.all_gather(seg_low, "seq", axis=1, tiled=True)
    turn_count = query_piece.shape[1] // row_tokens

    def key_one_turn(turn_index, inner_state):
        offset = turn_index * row_tokens
        query_blk = lax.dynamic_slice_in_dim(query_piece, offset, row_tokens, 1).reshape(
            shape_heads
        )
        dout_blk = lax.dynamic_slice_in_dim(dout_piece, offset, row_tokens, 1).reshape(shape_heads)
        stat_blk = lax.dynamic_slice_in_dim(high_piece, offset, row_tokens, 1).astype(
            jnp.float32
        ) + lax.dynamic_slice_in_dim(low_piece, offset, row_tokens, 1).astype(jnp.float32)
        lse_blk = jnp.transpose(stat_blk[..., :head_count], (0, 2, 1))
        dot_blk = jnp.transpose(stat_blk[..., head_count:], (0, 2, 1))
        seg_blk = lax.dynamic_slice_in_dim(key_seg_piece, offset, row_tokens, 1).astype(jnp.float32)
        key_mask = visible(seg_blk, seg_own, offset + jnp.arange(row_tokens), own_places)
        d_key, d_value = inner_state
        scores = (
            jnp.einsum("rqhe,rkhe->rhqk", query_blk, key_low, preferred_element_type=jnp.float32)
            * score_scale
        )
        weights = jnp.where(key_mask, jnp.exp(scores - lse_blk[..., None]), 0.0)
        d_value = d_value + jnp.einsum(
            "rhqk,rqhe->rhke",
            weights.astype(jnp.bfloat16),
            dout_blk,
            preferred_element_type=jnp.float32,
        )
        d_prob = jnp.einsum(
            "rqhe,rkhe->rhqk", dout_blk, value_low, preferred_element_type=jnp.float32
        )
        d_score = (weights * (d_prob - dot_blk[..., None])).astype(jnp.bfloat16)
        d_key = (
            d_key
            + jnp.einsum("rhqk,rqhe->rhke", d_score, query_blk, preferred_element_type=jnp.float32)
            * score_scale
        )
        return (d_key, d_value)

    d_key, d_value = lax.fori_loop(0, turn_count, key_one_turn, (grad_zero, grad_zero))
    d_query_tok = undo_rope(to_tokens(d_query), cosine_tab, sine_tab, ROT).reshape(
        all_tokens, model_width
    )
    d_key_tok = undo_rope(to_tokens(d_key), cosine_tab, sine_tab, ROT).reshape(
        all_tokens, model_width
    )
    d_value_tok = to_tokens(d_value).reshape(all_tokens, model_width)
    d_proj = jnp.concatenate([d_query_tok, d_key_tok, d_value_tok, d_gate, d_up], axis=1).astype(
        jnp.bfloat16
    )
    d_hidden = lax.dot_general(
        d_proj,
        lax.all_gather(in_low, ("dp", "seq"), axis=0, tiled=True),
        (((1,), (1,)), ((), ())),
        preferred_element_type=jnp.float32,
    )
    columns = h_piece
    in_grad = lax.psum_scatter(
        lax.dot_general(
            columns, d_proj, (((0,), (0,)), ((), ())), preferred_element_type=jnp.float32
        ),
        ("dp", "seq"),
        scatter_dimension=0,
        tiled=True,
    )
    gain_grad = jnp.sum(d_hidden * normed, axis=0)
    shift_grad = jnp.sum(d_hidden, axis=0)
    bias_grad = (
        jnp.sum(d_proj[:, : 3 * model_width].astype(jnp.float32), axis=0).reshape(3, model_width).T
    )
    small_term = jnp.concatenate([gain_grad[:, None], shift_grad[:, None], bias_grad], axis=1)
    small_grad = lax.psum_scatter(small_term, ("dp", "seq"), scatter_dimension=0, tiled=True)
    d_normed = d_hidden * norm_gain
    input_grad = grad_out.astype(jnp.float32) + inv_std * (
        d_normed
        - jnp.mean(d_normed, axis=-1, keepdims=True)
        - normed * jnp.mean(d_normed * normed, axis=-1, keepdims=True)
    )
    input_grad = input_grad.reshape(rows_here, row_tokens, model_width)
    in_new = adam_update(
        in_weight, in_first, in_second, in_average, in_grad, matrix_rate, weight_decay
    )
    out_new = adam_update(
        out_weight, out_first, out_second, out_average, out_grad, matrix_rate, weight_decay
    )
    small_new = adam_update(
        small_params, small_first, small_second, small_average, small_grad, small_rate, 0.0
    )
    return (
        output,
        input_grad,
        in_new[0],
        in_new[1],
        in_new[2],
        out_new[0],
        out_new[1],
        out_new[2],
        small_new[0],
        small_new[1],
        small_new[2],
        small_grad,
        in_grad,
        out_grad,
    )


def heads_fit(n_dp, n_seq, own_rows, model_width, wide_in):
    dp_rows = own_rows * n_seq
    if n_dp != 4 or HEADS % (2 * n_seq) or not dp_rows < model_width < 2 * dp_rows:
        return False
    att_rows = model_width // n_seq
    late_att = model_width - dp_rows
    first_act = dp_rows - late_att
    if first_act % n_seq:
        return False
    lead = att_rows - own_rows
    return (
        wide_in - 3 * model_width == 2 * (n_dp * dp_rows - model_width)
        and lead == own_rows - first_act // n_seq
        and lead * n_seq == late_att
        and lead % 16 == 0
    )


def middle_kernel(
    q_ref, k_ref, v_ref, bq_ref, bk_ref, bv_ref, da_ref, act_ref, d_act_ref, rope_ref,
    seg_q_ref, seg_k_ref,
    joined_ref, d_proj_ref, bias_ref,
    *, head_size, half_rot, att_rows, act,
):
    row, pair = pl.program_id(0), pl.program_id(1)
    lanes = 2 * head_size
    half = act_ref.shape[3]
    act_rows = sum(act)
    bf16, f32 = jnp.bfloat16, jnp.float32

    def feed_forward(step):
        x, z = lax.rem(step, 2), step // 2
        raw = act_ref[x, z, 0]
        gate = raw[:, 3 * att_rows : 3 * att_rows + act_rows]
        up = raw[:, 3 * att_rows + act_rows :]
        joint = d_act_ref[x, z, 0]
        d_act = jnp.concatenate(
            [joint[:, (i + 1) * att_rows :][:, :some] for i, some in enumerate(act)], axis=1
        ).astype(f32)
        sig = 1.0 / (1.0 + jnp.exp(-gate))
        silu = gate * sig
        rows = pl.ds(pl.multiple_of(pair * half, half), half)
        active, parts, first = silu * up, [], 0
        for some in act:
            parts.append(active[:, first : first + some])
            parts.append(jnp.zeros((half, att_rows - some), f32))
            first += some
        joined_ref[x, z, row, rows, att_rows:] = jnp.concatenate(parts, axis=1).astype(bf16)
        d_gate = d_act * up * sig * (1.0 + gate * (1.0 - sig))
        d_proj_ref[x, z, row, rows, 3 * att_rows :] = jnp.concatenate(
            [d_gate, d_act * silu], axis=1
        ).astype(bf16)

    loop(0, act_ref.shape[0] * act_ref.shape[1], feed_forward)

    def whole(v):
        across, depth = v.shape[:2]
        parts = [v[x, z].reshape(v.shape[-2:]) for z in range(depth) for x in range(across)]
        return jnp.concatenate(parts, axis=0)

    def store(ref, first, v):
        across, depth, _, some, _ = ref.shape
        columns = pl.ds(pl.multiple_of(first + pair * lanes, lanes), lanes)
        for z in range(depth):
            for x in range(across):
                at = (z * across + x) * some
                ref[x, z, row, :, columns] = v[at : at + some]

    cos, sin_low, sin_high = (rope_ref[0, i].T for i in range(3))
    tokens = cos.shape[0]
    scale = head_size ** (-0.5)

    def turn(v, way):
        return (
            v * cos
            + way * pltpu.roll(v, lanes - half_rot, 1) * sin_low
            + way * pltpu.roll(v, half_rot, 1) * sin_high
        )

    query = (turn(whole(q_ref[...]) + bq_ref[...], 1.0)).astype(bf16) * scale
    query = query.astype(bf16)
    key = turn(whole(k_ref[...]) + bk_ref[...], 1.0).astype(bf16)
    value = (whole(v_ref[...]) + bv_ref[...]).astype(bf16)
    d_att = whole(da_ref[...])
    place_q = lax.broadcasted_iota(jnp.int32, (tokens, tokens), 0)
    place_k = lax.broadcasted_iota(jnp.int32, (tokens, tokens), 1)
    mask = (seg_q_ref[0] == seg_k_ref[0]) & (place_k <= place_q)
    lane = lax.broadcasted_iota(jnp.int32, (tokens, lanes), 1)
    nt = (((1,), (1,)), ((), ()))
    tn = (((0,), (0,)), ((), ()))
    dot = functools.partial(lax.dot_general, preferred_element_type=f32)
    att = jnp.zeros((tokens, lanes), f32)
    d_query = jnp.zeros((tokens, lanes), f32)
    d_key = jnp.zeros((tokens, lanes), f32)
    d_value = jnp.zeros((tokens, lanes), f32)
    for head in range(lanes // head_size):
        mine = (lane >= head * head_size) & (lane < (head + 1) * head_size)
        q_h = jnp.where(mine, query, jnp.zeros_like(query))
        da_h = jnp.where(mine, d_att, jnp.zeros_like(d_att))
        scores = jnp.where(mask, dot(q_h, key, nt), neg_large)
        top = jnp.max(scores, axis=1, keepdims=True)
        weights = jnp.exp(scores - top)
        probs = weights * (1.0 / jnp.sum(weights, axis=1, keepdims=True))
        probs_low = probs.astype(bf16)
        att_h = jnp.where(mine, dot(probs_low, value, (((1,), (0,)), ((), ()))), 0.0)
        out_dot = jnp.sum(att_h * d_att.astype(f32), axis=1, keepdims=True)
        d_prob = dot(da_h, value, nt)
        d_score = (probs * (d_prob - out_dot)).astype(bf16)
        att = att + att_h
        d_query = d_query + jnp.where(mine, dot(d_score, key, (((1,), (0,)), ((), ()))), 0.0)
        d_key = d_key + dot(d_score, q_h, tn)
        d_value = d_value + dot(probs_low, da_h, tn)
    store(joined_ref, 0, att.astype(bf16))
    grads = (turn(d_query * scale, -1.0), turn(d_key, -1.0), d_value)
    columns = pl.ds(pl.multiple_of(pair * lanes, lanes), lanes)
    for i, grad in enumerate(grads):
        grad = grad.astype(bf16)
        store(d_proj_ref, i * att_rows, grad)
        total = jnp.sum(grad.astype(f32), axis=0, keepdims=True)

        @pl.when(row == 0)
        def _():
            bias_ref[i : i + 1, columns] = total

        @pl.when(row > 0)
        def _():
            bias_ref[i : i + 1, columns] = bias_ref[i : i + 1, columns] + total


def middle(proj, bias, d_joined, rope, seg, n_seq, att_rows, act, head_size):
    rows, tokens = seg.shape
    lanes = 2 * head_size
    pairs = att_rows // lanes
    bf16, f32 = jnp.bfloat16, jnp.float32
    order = (2, n_seq // 2, rows, tokens // n_seq)
    wide = lambda v: v.reshape(order + v.shape[-1:])
    shape = (2, n_seq // 2, 1, tokens // n_seq, lanes)
    block = lambda first: pl.BlockSpec(shape, lambda r, h: (0, 0, r, 0, first + h))
    row = lambda first: pl.BlockSpec((1, lanes), lambda r, h: (0, first + h))
    half = lambda v: pl.BlockSpec(
        (2, n_seq // 2, 1, tokens // n_seq // pairs, v.shape[-1]), lambda r, h: (0, 0, r, h, 0)
    )
    all_of = lambda v: pl.BlockSpec(v.shape, lambda r, h: (0,) * len(v.shape))
    outs = [
        jax.ShapeDtypeStruct(order + (d_joined.shape[-1],), bf16),
        jax.ShapeDtypeStruct(order + (proj.shape[-1],), bf16),
        jax.ShapeDtypeStruct((8, att_rows), f32),
    ]
    proj, d_joined = wide(proj), wide(d_joined)
    joined, d_proj, bias_sums = pl.pallas_call(
        functools.partial(
            middle_kernel,
            head_size=head_size, half_rot=ROT // 2, att_rows=att_rows, act=act,
        ),
        grid=(rows, pairs),
        in_specs=[
            block(0), block(pairs), block(2 * pairs),
            row(0), row(pairs), row(2 * pairs),
            block(0), half(proj), half(d_joined),
            pl.BlockSpec((1, 3, lanes, tokens), lambda r, h: (r, 0, 0, 0)),
            pl.BlockSpec((1, tokens, 1), lambda r, h: (r, 0, 0)),
            pl.BlockSpec((1, 1, tokens), lambda r, h: (r, 0, 0)),
        ],
        out_specs=[all_of(v) for v in outs],
        out_shape=outs,
        compiler_params=pltpu.CompilerParams(vmem_limit_bytes=56 * 2**20),
        name="middle",
    )(
        proj, proj, proj, bias, bias, bias, d_joined, proj, d_joined,
        rope, seg[:, :, None], seg[:, None, :],
    )
    flat = lambda v: v.reshape(rows * tokens, v.shape[-1])
    return flat(joined), flat(d_proj), bias_sums

MESH_ID = pl.DeviceIdType.MESH


def remote(src, dst, send_sem, recv_sem, device):
    return pltpu.make_async_remote_copy(
        src_ref=src,
        dst_ref=dst,
        send_sem=send_sem,
        recv_sem=recv_sem,
        device_id=device,
        device_id_type=MESH_ID,
    )


class Place:
    def __init__(self, n_seq):
        self.n_seq = n_seq
        self.depth = n_seq // 2
        self.p, self.s = lax.axis_index("dp"), lax.axis_index("seq")
        self.y, self.c = self.p // 2, lax.rem(self.p, 2)
        self.z, self.x = self.s // 2, lax.rem(self.s, 2)
        self.p_y = (1 - self.y) * 2 + self.c
        self.p_c = self.y * 2 + 1 - self.c
        self.p_d = (1 - self.y) * 2 + 1 - self.c
        self.to_y = (self.p_y, self.s)
        self.to_c = (self.p_c, self.s)
        self.to_x = (self.p, self.z * 2 + 1 - self.x)
        self.to_up = (self.p, self.s + 2)
        self.to_down = (self.p, self.s - 2)

    def seq(self, hop):
        return lax.rem(self.s + hop + self.n_seq, self.n_seq)

    def meet(self):
        barrier = pltpu.get_barrier_semaphore()

        def greet(hop, carry):
            pl.semaphore_signal(
                barrier, inc=1, device_id=(self.p, self.seq(hop)), device_id_type=MESH_ID
            )
            return carry

        lax.fori_loop(1, self.n_seq, greet, 0)
        for device in (self.to_y, self.to_c):
            pl.semaphore_signal(barrier, inc=1, device_id=device, device_id_type=MESH_ID)
        pl.semaphore_wait(barrier, self.n_seq + 1)


class Spread:
    def __init__(self, at, own, full, sems):
        self.at, self.own, self.full, self.sems = at, own, full, sems

    def along(self, src, up, ref=None):
        sems, at = self.sems, self.at
        here = self.full.at[at.x, src]
        return remote(
            here if ref is None else ref,
            here,
            sems.at[0 if up else 1, src],
            sems.at[3, src],
            at.to_up if up else at.to_down,
        )

    def across(self, src, ref=None):
        sems, at = self.sems, self.at
        here = self.full.at[at.x, src]
        return remote(here if ref is None else ref, here, sems.at[2, src], sems.at[4, src], at.to_x)

    def local(self):
        return pltpu.make_async_copy(
            self.own, self.full.at[self.at.x, self.at.z], self.sems.at[5, 0]
        )

    def begin_across(self):
        self.across(self.at.z, self.own).start()
        self.local().start()

    def begin_along(self):
        at = self.at

        @pl.when(at.z < at.depth - 1)
        def _():
            self.along(at.z, True, self.own).start()

        @pl.when(at.z > 0)
        def _():
            self.along(at.z, False, self.own).start()

    def step(self, hop):
        at = self.at

        @pl.when(at.z - hop >= 0)
        def _():
            src = at.z - hop
            self.along(src, True).wait_recv()

            @pl.when(at.z < at.depth - 1)
            def _():
                self.along(src, True).start()

            self.across(src).start()

        @pl.when(at.z + hop < at.depth)
        def _():
            src = at.z + hop
            self.along(src, False).wait_recv()

            @pl.when(at.z > 0)
            def _():
                self.along(src, False).start()

            self.across(src).start()

    def arrive(self):
        at = self.at
        for src in range(at.depth):
            here = self.full.at[1 - at.x, src]
            remote(here, here, self.sems.at[2, src], self.sems.at[4, src], at.to_x).wait_recv()

    def sent(self):
        at = self.at
        for src in range(at.depth):
            self.across(src).wait_send()

            @pl.when((at.z < at.depth - 1) & (src <= at.z))
            def _():
                self.along(src, True).wait_send()

            @pl.when((at.z > 0) & (src >= at.z))
            def _():
                self.along(src, False).wait_send()


class Fan:
    def __init__(self, at, pick, sems):
        self.at, self.pick, self.sems = at, pick, sems

    def y(self, k, ref=None):
        at = self.at
        here = self.pick(at.p, k)
        return remote(here if ref is None else ref, here, self.sems.at[0, k], self.sems.at[1, k], at.to_y)

    def core(self, k, ref=None):
        at = self.at
        here = self.pick(at.p, k)
        return remote(here if ref is None else ref, here, self.sems.at[2, k], self.sems.at[3, k], at.to_c)

    def pass_on(self, k):
        at = self.at
        here = self.pick(at.p_y, k)
        return remote(here, here, self.sems.at[4, k], self.sems.at[5, k], at.to_c)

    def from_y(self, k):
        here = self.pick(self.at.p_y, k)
        return remote(here, here, self.sems.at[0, k], self.sems.at[1, k], self.at.to_y)

    def from_core(self, k):
        here = self.pick(self.at.p_c, k)
        return remote(here, here, self.sems.at[2, k], self.sems.at[3, k], self.at.to_c)

    def from_diagonal(self, k):
        here = self.pick(self.at.p_d, k)
        return remote(here, here, self.sems.at[4, k], self.sems.at[5, k], self.at.to_c)


def loop(low, high, body):
    def step(k, carry):
        body(k)
        return carry

    lax.fori_loop(low, high, step, 0)


def gather_kernel(
    x_ref, g_ref, w_ref, o_ref, tile_ref,
    x_full, g_full, w_full, o_full, tiles, hidden, out_mine, proj, d_joined,
    x_block, hid, w_near, p_all, g_near, o_near, t_near, small,
    x_sems, g_sems, w_sems, w_fan_sems, o_sems, o_fan_sems, t_sems, t_fan_sems, local_sems,
    x_in_sems, hid_sems, w_in_sems, p_sems, g_in_sems, o_in_sems,
    *, n_seq, late, lead,
):
    at = Place(n_seq)
    depth = at.depth
    bf16, f32 = jnp.bfloat16, jnp.float32
    own, width = o_ref.shape
    att = own + lead
    first_act = own - lead
    body, extra = pl.ds(0, own), pl.ds(own, late)
    x_go = Spread(at, x_ref, x_full, x_sems)
    g_go = Spread(at, g_ref, g_full, g_sems)
    w_fan = Fan(at, lambda p, k: w_full.at[p, k], w_fan_sems)
    o_fan = Fan(at, lambda p, k: o_full.at[p, body if k == 0 else extra], o_fan_sems)
    t_fan = Fan(at, lambda p, k: tiles.at[p], t_fan_sems)

    def w_send(hop):
        to = at.seq(hop)
        return remote(w_ref.at[to], w_full.at[at.p, at.s], w_sems.at[0, to], w_sems.at[1, at.s], (at.p, to))

    def w_recv(hop):
        src = at.seq(-hop)
        here = w_full.at[at.p, src]
        return remote(here, here, w_sems.at[0, src], w_sems.at[1, src], (at.p, src))

    def t_send(hop):
        to = at.seq(hop)
        return remote(tile_ref, tiles.at[at.p, at.s], t_sems.at[0, to], t_sems.at[1, at.s], (at.p, to))

    def t_recv(hop):
        src = at.seq(-hop)
        here = tiles.at[at.p, src]
        return remote(here, here, t_sems.at[0, src], t_sems.at[1, src], (at.p, src))

    w_local = pltpu.make_async_copy(w_ref.at[at.s], w_full.at[at.p, at.s], local_sems.at[0])
    o_local = pltpu.make_async_copy(o_ref, o_full.at[at.p, body], local_sems.at[1])
    t_local = pltpu.make_async_copy(tile_ref, tiles.at[at.p, at.s], local_sems.at[2])
    head = o_ref.at[pl.ds(0, late)]
    o_send = remote(
        head, o_full.at[at.p, extra], o_sems.at[0], o_sems.at[1], (at.p, at.seq(-1))
    )

    def place(i):
        return lax.rem(at.x + i // depth, 2), lax.rem(at.z + i, depth)

    def block_in(i):
        col, deep = place(i)
        return pltpu.make_async_copy(x_full.at[col, deep], x_block, x_in_sems.at[0])

    def hid_out(i):
        col, deep = place(i)
        return pltpu.make_async_copy(hid.at[col, deep], hidden.at[col, deep], hid_sems.at[i])

    def norm_block(i):
        col, deep = place(i)

        @pl.when(i >= depth)
        def _():
            here = x_full.at[1 - at.x, deep]
            remote(here, here, x_sems.at[2, deep], x_sems.at[4, deep], at.to_x).wait_recv()

        block_in(i).start()
        block_in(i).wait()
        some = 32

        def rows(k):
            part = pl.ds(pl.multiple_of(lax.rem(k, 2) * some, some), some)
            v = x_block[k // 2, part, :].astype(f32)
            centered = v - jnp.mean(v, axis=-1, keepdims=True)
            inv_std = lax.rsqrt(jnp.mean(centered * centered, axis=-1, keepdims=True) + norm_eps)
            done = centered * inv_std * small[0:1, :] + small[1:2, :]
            hid[col, deep, pl.ds(pl.multiple_of(k * some, some), some), :] = done.astype(bf16)

        loop(0, hid.shape[2] // some, rows)
        hid_out(i).start()

    def w_in(p, k):
        return pltpu.make_async_copy(w_full.at[p], w_near.at[p], w_in_sems.at[k])

    def g_in(col):
        return pltpu.make_async_copy(g_full.at[col], g_near.at[col], g_in_sems.at[col])

    def o_in(k):
        last = at.s == n_seq - 1
        lead_at = pl.multiple_of(lead * at.s, 16)
        late_at = pl.multiple_of(late - lead * at.s, 16)
        src, dst, count = [
            (o_full.at[0, pl.ds(lead_at, att - late)], 0, att - late),
            (o_full.at[0, pl.ds(lead_at + (att - late), late)], att - late, late),
            (o_full.at[1, pl.ds(late_at, first_act)], att, first_act),
            (o_full.at[2, body], 2 * att, own),
            (o_full.at[3, body], 3 * att, own),
            (o_full.at[1, extra], att - late, late),
        ][k]
        return pltpu.make_async_copy(src, o_near.at[pl.ds(dst, count)], o_in_sems.at[k])

    step_rows = 2 * hid.shape[2]
    steps = hid.shape[0] * depth * hid.shape[2] // step_rows
    per_block = step_rows // hid.shape[2]

    def p_out(k):
        rows = pl.ds(pl.multiple_of(k * step_rows, step_rows), step_rows)
        return pltpu.make_async_copy(p_all.at[rows], proj.at[rows], p_sems.at[k])

    feats = width // w_near.shape[0]

    def project(k, p_one, p_two, last):
        rows = per_block * k
        at_rows = pl.ds(pl.multiple_of(k * step_rows, step_rows), step_rows)
        left = [
            hid[
                rows // depth, pl.ds(lax.rem(rows, depth), per_block), :,
                pl.ds(pl.multiple_of(p * feats, feats), feats),
            ].reshape(step_rows, feats)
            for p in (p_one, p_two)
        ]
        columns = p_all.shape[1]
        for n in range(0, columns, 512):
            some = min(512, columns - n)
            total = sum(
                jnp.dot(
                    part, w_near[p, :, :, n : n + some].reshape(feats, some),
                    preferred_element_type=f32,
                )
                for part, p in zip(left, (p_one, p_two))
            )
            if last:
                total = total + p_all[at_rows, n : n + some]
            p_all[at_rows, n : n + some] = total
        if last:
            p_out(k).start()

    def join_back(k):
        rows = per_block * k
        left = g_near[rows // depth, pl.ds(lax.rem(rows, depth), per_block)]
        left = left.reshape(step_rows, width)
        d_joined[pl.ds(pl.multiple_of(k * step_rows, step_rows), step_rows), :] = (
            lax.dot_general(
                left, o_near[...], (((1,), (1,)), ((), ())), preferred_element_type=f32
            ).astype(bf16)
        )

    at.meet()
    x_go.begin_along()
    x_go.begin_across()
    g_go.begin_across()
    loop(1, n_seq, lambda hop: t_send(hop).start())
    t_local.start()
    w_fan.y(at.s, w_ref.at[at.s]).start()
    w_fan.core(at.s, w_ref.at[at.s]).start()
    w_local.start()
    o_fan.y(0, o_ref).start()
    o_fan.core(0, o_ref).start()
    o_local.start()
    w_send(1).start()
    w_send(n_seq - 1).start()
    for hop in range(1, depth):
        x_go.step(hop)
        if hop == 1:
            t_local.wait()
            loop(1, n_seq, lambda k: t_recv(k).wait_recv())
            t_fan.y(0).start()
            t_fan.core(0).start()
        if hop == 2:
            t_fan.from_y(0).wait_recv()
            t_fan.pass_on(0).start()
        w_send(hop + 1).start()
        if hop + 1 < n_seq - hop - 1:
            w_send(n_seq - hop - 1).start()
    g_go.begin_along()

    @pl.when(at.y == 0)
    def _():
        o_send.start()

    t_fan.from_core(0).wait_recv()
    t_fan.from_diagonal(0).wait_recv()
    t_load = pltpu.make_async_copy(tiles, t_near, local_sems.at[3])
    t_load.start()
    t_load.wait()
    for p in range(t_near.shape[0]):
        for pair in range(n_seq // 2):
            two = t_near[p, 2 * pair, 0:8] + t_near[p, 2 * pair + 1, 0:8]
            lanes = two.shape[1]
            first = (p * (n_seq // 2) + pair) * lanes
            small[:, first : first + lanes] = two
    for k, some in enumerate((first_act, own, own)):
        o_near[(k + 1) * att + some : (k + 2) * att, :] = jnp.zeros((att - some, width), bf16)
    x_go.local().wait()

    def w_step(hop):
        src = at.seq(-hop)
        w_recv(hop).wait_recv()
        w_fan.y(src).start()
        w_fan.core(src).start()
        norm_block(hop - 1)

    loop(1, n_seq, w_step)
    norm_block(n_seq - 1)
    w_local.wait()
    w_in(at.p, 0).start()
    loop(0, n_seq, lambda k: w_fan.from_core(k).wait_recv())
    w_in(at.p_c, 2).start()
    def w_pass(hop):
        src = at.seq(-hop)
        w_fan.from_y(src).wait_recv()
        w_fan.pass_on(src).start()

    for hop in range(1, depth):
        g_go.step(hop)
        loop((hop - 1) * 3, min(hop * 3, n_seq), w_pass)
        if hop == 1:

            @pl.when(at.y == 0)
            def _():
                o_send.wait_recv()
                o_fan.y(1).start()
                o_fan.core(1).start()

            w_in(at.p, 0).wait()
            w_in(at.p_c, 2).wait()
        if hop == 2:
            loop(0, steps, lambda k: project(k, at.p, at.p_c, False))

    loop((depth - 1) * 3, n_seq, w_pass)
    w_in(at.p_y, 1).start()

    loop(0, n_seq, lambda k: w_fan.from_diagonal(k).wait_recv())
    w_in(at.p_d, 3).start()
    o_fan.from_y(0).wait_recv()
    o_fan.pass_on(0).start()

    @pl.when(at.y == 1)
    def _():
        o_fan.from_y(1).wait_recv()
        o_fan.pass_on(1).start()

    w_in(at.p_y, 1).wait()
    w_in(at.p_d, 3).wait()
    loop(0, steps, lambda k: project(k, at.p_y, at.p_d, True))

    o_local.wait()
    o_fan.from_core(0).wait_recv()
    o_fan.from_diagonal(0).wait_recv()

    @pl.when(at.y == 0)
    def _():
        o_fan.from_core(1).wait_recv()

    @pl.when(at.y == 1)
    def _():
        o_fan.from_diagonal(1).wait_recv()

    for k in (0, 2, 3, 4):
        o_in(k).start()

    @pl.when(at.s < n_seq - 1)
    def _():
        o_in(1).start()
        o_in(1).wait()

    @pl.when(at.s == n_seq - 1)
    def _():
        o_in(5).start()
        o_in(5).wait()

    for k in (0, 2, 3, 4):
        o_in(k).wait()
    o_out = pltpu.make_async_copy(o_near, out_mine, o_in_sems.at[6])
    o_out.start()
    g_go.local().wait()
    half = steps // 2
    for col in (at.x, 1 - at.x):
        if col is not at.x:
            g_go.arrive()
        g_in(col).start()
        g_in(col).wait()
        loop(0, half, lambda k: join_back(col * half + k))

    o_out.wait()
    loop(0, steps, lambda k: p_out(k).wait())
    loop(0, n_seq, lambda i: hid_out(i).wait())
    x_go.sent()
    g_go.sent()

    def w_sent(k):
        w_fan.y(k).wait_send()
        w_fan.core(k).wait_send()
        w_fan.pass_on(k).wait_send()

    loop(0, n_seq, w_sent)

    def seq_sent(hop):
        w_send(hop).wait_send()
        t_send(hop).wait_send()

    loop(1, n_seq, seq_sent)
    for fan in (t_fan, o_fan):
        fan.y(0).wait_send()
        fan.core(0).wait_send()
        fan.pass_on(0).wait_send()

    @pl.when(at.y == 0)
    def _():
        o_send.wait_send()
        o_fan.y(1).wait_send()
        o_fan.core(1).wait_send()

    @pl.when(at.y == 1)
    def _():
        o_fan.pass_on(1).wait_send()


def gather_all(n_dp, n_seq, late, lead, x, g, w, o, tile):
    depth = n_seq // 2
    own, width = o.shape
    block = x.shape[0] * x.shape[1]
    tokens = n_seq * block
    columns = w.shape[2]
    mine = n_dp * (own + lead)
    bf16, f32 = jnp.bfloat16, jnp.float32
    rest, near = pl.BlockSpec(memory_space=pl.ANY), pl.BlockSpec(memory_space=pltpu.VMEM)
    dma = pltpu.SemaphoreType.DMA
    like = lambda lead, ref: jax.ShapeDtypeStruct(lead + ref.shape, ref.dtype)
    return pl.pallas_call(
        functools.partial(gather_kernel, n_seq=n_seq, late=late, lead=lead),
        in_specs=[rest] * 5,
        out_specs=[rest] * 8 + [near],
        out_shape=[
            like((2, depth), x),
            like((2, depth), g),
            jax.ShapeDtypeStruct((n_dp,) + w.shape, w.dtype),
            jax.ShapeDtypeStruct((n_dp, own + late, width), o.dtype),
            like((n_dp, n_seq), tile),
            jax.ShapeDtypeStruct((2, depth, block, width), bf16),
            jax.ShapeDtypeStruct((mine, width), bf16),
            jax.ShapeDtypeStruct((tokens, columns), f32),
            jax.ShapeDtypeStruct((tokens, mine), bf16),
        ],
        scratch_shapes=[
            pltpu.VMEM(x.shape, bf16),
            pltpu.VMEM((2, depth, block, width), bf16),
            pltpu.VMEM((n_dp,) + w.shape, bf16),
            pltpu.VMEM((tokens, columns), f32),
            pltpu.VMEM((2, depth) + g.shape, bf16),
            pltpu.VMEM((mine, width), bf16),
            pltpu.VMEM((n_dp, n_seq) + tile.shape, f32),
            pltpu.VMEM((8, width), f32),
            dma((6, depth)), dma((6, depth)), dma((2, n_seq)), dma((6, n_seq)),
            dma((2,)), dma((6, 2)), dma((2, n_seq)), dma((6, 1)), dma((4,)),
            dma((1,)), dma((n_seq,)), dma((4,)), dma((tokens // (2 * block),)), dma((2,)), dma((7,)),
        ],
        compiler_params=pltpu.CompilerParams(
            collective_id=0, has_side_effects=True, vmem_limit_bytes=56 * 2**20
        ),
        name="gather_all",
    )(x, g, w, o, tile)

def add_rows(out, terms, rows=32):
    count = out.shape[0]

    def some(k):
        at = pl.ds(pl.multiple_of(k * rows, rows), rows)
        total = terms[0][at].astype(jnp.float32)
        for term in terms[1:]:
            total = total + term[at].astype(jnp.float32)
        out[at] = total.astype(out.dtype)

    loop(0, count // rows, some)


def reduce_kernel(
    in_ref, d_proj_ref, joined_ref, hidden_ref, g_ref, w_ref, o_ref,
    normed_ref, small_ref,
    sums, in_sum, out_sum, out_prev, small_sum,
    own_parts, x_got, z_got, in_own, in_core, in_y, out_own, out_core, out_y,
    small_own, small_core, small_y, small_seq,
    d_near, j_near, h_near, g_near, w_near, o_near, b_ref, out_ref,
    load_sems, x_sems, z_sems, in_core_sems, in_y_sems, in_sems, out_sems, small_sems, local_sem,
    w_sems, o_sems,
    *, n_seq, late, first_act, keep, plan,
):
    at = Place(n_seq)
    depth = at.depth
    main = out_own.shape[1] - late
    body, extra = pl.ds(0, main), pl.ds(main, late)
    y, c, z, x, s = at.y, at.c, at.z, at.x, at.s

    loads = [
        pltpu.make_async_copy(d_proj_ref, d_near, load_sems.at[0]),
        pltpu.make_async_copy(joined_ref, j_near, load_sems.at[1]),
        pltpu.make_async_copy(g_ref, g_near, load_sems.at[2]),
    ]
    feats = h_near.shape[4]
    for y_to in range(2):
        first = pl.multiple_of((2 * y_to + c) * feats, feats)
        loads.append(
            pltpu.make_async_copy(
                hidden_ref.at[:, :, :, pl.ds(first, feats)], h_near.at[y_to], load_sems.at[3 + y_to]
            )
        )
    dot = functools.partial(lax.dot_general, preferred_element_type=jnp.float32)
    low = jnp.bfloat16
    block_rows, width = own_parts.shape[2:]
    flat = lambda v: v.reshape(-1, v.shape[-1])

    def w_load(i):
        some = w_near.shape[1]
        return pltpu.make_async_copy(
            w_ref.at[pl.ds(pl.multiple_of(i * some, some), some)],
            w_near.at[lax.rem(i, 2)], w_sems.at[lax.rem(i, 2)],
        )

    def o_load(i):
        some = o_near.shape[2]
        return pltpu.make_async_copy(
            o_ref.at[:, pl.ds(pl.multiple_of(i * some, some), some)],
            o_near.at[lax.rem(i, 2)], o_sems.at[lax.rem(i, 2)],
        )

    def streamed(out, load, count, some, product):
        load(0).start()

        def one(i):
            @pl.when(i + 1 < count)
            def _():
                load(i + 1).start()

            load(i).wait()
            done = product(lax.rem(i, 2)).astype(low)
            columns = pl.ds(pl.multiple_of(i * some, some), some)
            out[:, :, columns] = done.reshape(depth, block_rows, some)

        loop(0, count, one)

    def work(i):
        if i == 5:
            for k in range(depth):
                to_across(0, k).wait_send()
        if i in (0, 7):
            some = w_near.shape[1]
            left = flat(d_near[x if i == 0 else 1 - x])
            streamed(
                own_parts.at[0] if i == 0 else b_ref, w_load, width // some, some,
                lambda k: dot(left, w_near[k], (((1,), (1,)), ((), ()))),
            )
        elif i in (1, 5):
            some = o_near.shape[2]
            left = flat(j_near[x if i == 1 else 1 - x])
            streamed(
                own_parts.at[1] if i == 1 else b_ref, o_load, width // some, some,
                lambda k: dot(left, o_near[k], (((1,), (0,)), ((), ()))),
            )
        elif i < 4:
            y_to = 1 - y if i == 2 else y
            left = flat(h_near[y_to])
            right = flat(d_near[...])
            total = right.shape[1]
            for first in range(0, total, 256):
                some = min(256, total - first)
                done = dot(left, right[:, first : first + some], (((0,), (0,)), ((), ())))
                in_own[y_to, :, :, first : first + some] = done.astype(low).reshape(
                    n_seq, -1, some
                )
        else:
            core = c if i == 4 else 1 - c
            for first in range(0, width, width // 4):
                at_n = slice(first, first + width // 4)
                right = flat(g_near[:, :, :, at_n])
                for y_to in range(2):
                    columns = pl.ds(pl.multiple_of((2 * y_to + core) * main, main), main)
                    done = dot(flat(j_near[:, :, :, columns]), right, (((0,), (0,)), ((), ())))
                    if i == 4:
                        out_own[y_to, body, at_n] = done.astype(low)
                    else:
                        out_ref[y_to * main : (y_to + 1) * main, at_n] = done.astype(low)
                if i == 4:
                    out_own[0, extra, at_n] = dot(
                        flat(j_near[:, :, :, keep : keep + late]), right, (((0,), (0,)), ((), ()))
                    ).astype(low)
            if i == 6:
                out_ref[2 * main :] = out_own[0, extra]

    def in_to_core(y_to, k):
        return remote(
            in_ref.at[y_to, k], in_core.at[y_to, k],
            in_core_sems.at[0, y_to, k], in_core_sems.at[1, y_to, k], at.to_c,
        )

    def out_to_core(y_to):
        return remote(
            out_ref.at[pl.ds(pl.multiple_of(y_to * main, main), main)], out_core.at[y_to, body],
            out_sems.at[0, y_to], out_sems.at[1, y_to], at.to_c,
        )

    extra_to_core = remote(
        out_ref.at[pl.ds(2 * main, late)], out_core.at[0, extra],
        out_sems.at[0, 2], out_sems.at[1, 2], at.to_c,
    )

    def to_across(kind, k):
        return remote(
            b_ref.at[k], x_got.at[kind, k],
            x_sems.at[0, kind, k], x_sems.at[1, kind, k], at.to_x,
        )

    def to_up(kind, k):
        return remote(
            x_got.at[kind, k], z_got.at[kind, k],
            z_sems.at[0, kind, k], z_sems.at[1, kind, k], at.to_up,
        )

    def to_down(kind, k):
        slot = jnp.where(k == z - 1, depth, k)
        return remote(
            x_got.at[kind, k], z_got.at[kind, slot],
            z_sems.at[0, kind, k], z_sems.at[1, kind, slot], at.to_down,
        )

    def from_depth(kind, slot):
        here = z_got.at[kind, slot]
        return remote(here, here, z_sems.at[0, kind, slot], z_sems.at[1, kind, slot], at.to_up)

    def in_to_y(k):
        return remote(
            in_core.at[1 - y, k], in_y.at[k], in_y_sems.at[0, k], in_y_sems.at[1, k], at.to_y
        )

    def in_to_owner(k):
        return remote(
            in_core.at[y, k], in_sum.at[s], in_sems.at[0, k], in_sems.at[1, s], (at.p, k)
        )

    def in_from(k):
        here = in_sum.at[k]
        return remote(here, here, in_sems.at[0, k], in_sems.at[1, k], (at.p, k))

    in_keep = pltpu.make_async_copy(in_core.at[y, s], in_sum.at[s], local_sem.at[0])
    out_to_y = remote(
        out_core.at[1 - y, body], out_y.at[body], out_sems.at[0, 3], out_sems.at[1, 3], at.to_y
    )
    extra_to_y = remote(
        out_core.at[0, extra], out_y.at[extra], out_sems.at[0, 4], out_sems.at[1, 4], at.to_y
    )

    def out_shift(start):
        return remote(
            out_sum.at[pl.ds(start, late)], out_prev,
            out_sems.at[0, 5], out_sems.at[1, 5], (at.p, at.seq(1)),
        )

    small_to_core = remote(small_own, small_core, small_sems.at[0, 0], small_sems.at[1, 0], at.to_c)
    small_to_y = remote(small_core, small_y, small_sems.at[0, 1], small_sems.at[1, 1], at.to_y)

    def small_to(hop):
        to = at.seq(hop)
        first = (at.p * n_seq + to) // 2 * lanes
        return remote(
            small_y.at[:, pl.ds(pl.multiple_of(first, lanes), lanes)], small_seq.at[s],
            small_sems.at[0, 2 + to], small_sems.at[1, 2 + s], (at.p, to),
        )

    def small_from(hop):
        src = at.seq(-hop)
        here = small_seq.at[src]
        return remote(
            here, here, small_sems.at[0, 2 + src], small_sems.at[1, 2 + src], (at.p, src)
        )

    chained, steps = plan
    lanes = small_sum.shape[1]

    def around_z(hop):
        return lax.rem(z + hop, depth)

    def to_depth(kind, k):
        return remote(
            x_got.at[kind, k], z_got.at[kind, z],
            z_sems.at[0, kind, k], z_sems.at[1, kind, z], (at.p, 2 * k + x),
        )

    def turn(i):
        return jnp.where(lax.rem(i, 2) == 0, depth - 1 - i // 2, i // 2)

    def order(kind, i):
        return turn(i) if chained[kind] else around_z(i + 1)

    def across(j):
        to_across(j // depth, order(j // depth, j % depth)).start()

    def straight(kind, i):
        k = around_z(i + 1)
        to_across(kind, k).wait_recv()
        add_rows(x_got.at[kind, k], [x_got.at[kind, k], own_parts.at[kind, k]])
        if i + 1 < depth:
            to_depth(kind, k).start()

    def chain(kind, i):
        k = turn(i)
        to_across(kind, k).wait_recv()
        got, mine = x_got.at[kind, k], own_parts.at[kind, k]
        begins = ((z == 0) & (k > 0)) | ((z == depth - 1) & (k < depth - 1)) | (z == k)

        @pl.when(begins)
        def _():
            add_rows(got, [got, mine])

        @pl.when(jnp.logical_not(begins))
        def _():
            from_depth(kind, k).wait_recv()
            add_rows(got, [got, mine, z_got.at[kind, k]])

        @pl.when(z < k)
        def _():
            to_up(kind, k).start()

        @pl.when(z > k)
        def _():
            to_down(kind, k).start()

    def finish(kind):
        if not chained[kind]:
            others = [around_z(hop) for hop in range(1, depth)]
            for k in others:
                from_depth(kind, k).wait_recv()
            add_rows(
                sums.at[kind], [x_got.at[kind, z]] + [z_got.at[kind, k] for k in others], rows=16
            )
            return
        add_rows(sums.at[kind], [x_got.at[kind, z]], rows=16)

        @pl.when(z > 0)
        def _():
            from_depth(kind, z).wait_recv()
            add_rows(sums.at[kind], [sums.at[kind], z_got.at[kind, z]], rows=16)

        @pl.when(z < depth - 1)
        def _():
            from_depth(kind, depth).wait_recv()
            add_rows(sums.at[kind], [sums.at[kind], z_got.at[kind, depth]], rows=16)

    def to_y_step(hop):
        k = at.seq(hop)
        in_to_core(1 - y, k).wait_recv()
        add_rows(in_core.at[1 - y, k], [in_core.at[1 - y, k], in_own.at[1 - y, k]])
        in_to_y(k).start()

    def owner_step(hop):
        k = at.seq(hop)
        in_to_core(y, k).wait_recv()
        in_to_y(k).wait_recv()
        add_rows(in_core.at[y, k], [in_core.at[y, k], in_own.at[y, k], in_y.at[k]])

        @pl.when(k != s)
        def _():
            in_to_owner(k).start()

        @pl.when(k == s)
        def _():
            in_keep.start()

    def out_y_step():
        out_to_core(1 - y).wait_recv()
        extra_to_core.wait_recv()
        add_rows(out_core.at[1 - y, body], [out_core.at[1 - y, body], out_own.at[1 - y, body]])
        out_to_y.start()

        @pl.when(y == 1)
        def _():
            add_rows(out_core.at[0, extra], [out_core.at[0, extra], out_own.at[0, extra]])
            extra_to_y.start()

    def out_end():
        out_to_core(y).wait_recv()
        out_to_y.wait_recv()
        add_rows(out_sum.at[body], [out_core.at[y, body], out_own.at[y, body], out_y.at[body]])

        @pl.when(y == 0)
        def _():
            extra_to_y.wait_recv()
            add_rows(
                out_sum.at[extra], [out_core.at[0, extra], out_own.at[0, extra], out_y.at[extra]]
            )

            @pl.when(c == 0)
            def _():
                out_shift(keep).start()

            @pl.when((c == 1) & (s == n_seq - 1))
            def _():
                out_shift(main).start()

            @pl.when((c == 1) & (s < n_seq - 1))
            def _():
                out_shift(first_act - late).start()

    def small_step(i):
        if i == 0:
            finish(0)
            small_own[...] = small_ref[...]
            d_hidden = sums[0]
            small_own[0:1, :] = jnp.sum(d_hidden * normed_ref[...], axis=0, keepdims=True)
            small_own[1:2, :] = jnp.sum(d_hidden, axis=0, keepdims=True)
            small_to_core.start()
        elif i == 1:
            small_to_core.wait_recv()
            small_core[...] = small_core[...] + small_own[...]
            small_to_y.start()
        elif i == 2:
            small_to_y.wait()
            small_y[...] = small_core[...] + small_y[...]
            loop(1, n_seq, lambda hop: small_to(hop).start())
        else:
            first = (at.p * n_seq + s) // 2 * lanes
            small_sum[...] = small_y[:, pl.ds(pl.multiple_of(first, lanes), lanes)]

            def small_add(hop):
                small_from(hop).wait_recv()
                small_sum[...] = small_sum[...] + small_seq[at.seq(-hop)]

            loop(1, n_seq, small_add)

    def core_step(i):
        if i == 0:
            loads[0].start()
            loop(0, n_seq, lambda hop: in_to_core(1 - y, at.seq(hop)).start())
            for load in loads[1:]:
                load.start()
        elif i == 1:
            loop(0, n_seq, lambda hop: in_to_core(y, at.seq(hop)).start())
        elif i == 2:
            out_to_core(1 - y).start()
            out_to_core(y).start()
            extra_to_core.start()
        elif i == 3:
            for load in loads[1:]:
                load.wait()
        else:
            loads[0].wait()

    at.meet()
    for what, i in steps:
        if what == 0:
            across(i)
        elif what == 1:
            core_step(i)
        elif what == 2:
            to_y_step(i)
        elif what == 3:
            owner_step(i)
        elif what == 4:
            kind = i // depth
            (chain if chained[kind] else straight)(kind, i % depth)
        elif what == 5:
            small_step(i)
        elif what == 7:
            work(i)
        elif i == 0:
            out_y_step()
        else:
            out_end()
    finish(1)

    @pl.when(y == 0)
    def _():
        out_shift(0).wait()

    def in_last(hop):
        k = at.seq(hop)
        in_from(k).wait_recv()
        in_to_owner(k).wait_send()

    loop(1, n_seq, in_last)
    in_keep.wait()

    def seq_sent(k):
        for y_to in range(2):
            in_to_core(y_to, k).wait_send()
        in_to_y(k).wait_send()

    loop(0, n_seq, seq_sent)
    loop(1, n_seq, lambda hop: small_to(hop).wait_send())
    small_to_core.wait_send()
    for y_to in range(2):
        out_to_core(y_to).wait_send()
    extra_to_core.wait_send()
    out_to_y.wait_send()

    @pl.when(y == 1)
    def _():
        extra_to_y.wait_send()

    for kind in range(2):
        for k in range(depth):
            if kind == 1:
                to_across(kind, k).wait_send()

            @pl.when(z < k)
            def _():
                (to_up if chained[kind] else to_depth)(kind, k).wait_send()

            @pl.when(z > k)
            def _():
                (to_down if chained[kind] else to_depth)(kind, k).wait_send()


def reduce_all(
    plan, n_dp, n_seq, late, first_act, keep, in_sent, d_proj, joined, hidden, g, w, o, normed, small
):
    depth = n_seq // 2
    block = (g.shape[2], g.shape[3])
    in_block = in_sent.shape[2:]
    width = block[1]
    main = joined.shape[-1] // n_dp
    slot = main + late
    bf16, f32 = jnp.bfloat16, jnp.float32
    rest, near = pl.BlockSpec(memory_space=pl.ANY), pl.BlockSpec(memory_space=pltpu.VMEM)
    dma = pltpu.SemaphoreType.DMA
    return pl.pallas_call(
        functools.partial(
            reduce_kernel, n_seq=n_seq, late=late, first_act=first_act, keep=keep, plan=plan
        ),
        in_specs=[rest] * 7 + [near, near],
        out_specs=[near, rest, near, rest, near],
        out_shape=[
            jax.ShapeDtypeStruct((2,) + block, f32),
            jax.ShapeDtypeStruct((n_seq,) + in_block, bf16),
            jax.ShapeDtypeStruct((slot, width), bf16),
            jax.ShapeDtypeStruct((late, width), bf16),
            jax.ShapeDtypeStruct((small.shape[0], 128), f32),
        ],
        scratch_shapes=[
            pltpu.VMEM((2, depth) + block, bf16),
            pltpu.VMEM((2, depth) + block, bf16),
            pltpu.VMEM((2, depth + 1) + block, bf16),
            pltpu.VMEM((2, n_seq) + in_block, bf16),
            pltpu.VMEM((2, n_seq) + in_block, bf16),
            pltpu.VMEM((n_seq,) + in_block, bf16),
            pltpu.VMEM((2, slot, width), bf16),
            pltpu.VMEM((2, slot, width), bf16),
            pltpu.VMEM((slot, width), bf16),
            pltpu.VMEM(small.shape, f32),
            pltpu.VMEM(small.shape, f32),
            pltpu.VMEM(small.shape, f32),
            pltpu.VMEM((n_seq, small.shape[0], 128), f32),
            pltpu.VMEM(d_proj.shape, bf16),
            pltpu.VMEM(joined.shape, bf16),
            pltpu.VMEM((2,) + hidden.shape[:3] + (width // n_dp,), bf16),
            pltpu.VMEM(g.shape, bf16),
            pltpu.VMEM((2, 256, w.shape[1]), bf16),
            pltpu.VMEM((2, o.shape[0], 256), bf16),
            pltpu.VMEM((depth,) + block, bf16),
            pltpu.VMEM((2 * main + late, width), bf16),
            dma((7,)), dma((2, 2, depth)), dma((2, 2, depth + 1)), dma((2, 2, n_seq)), dma((2, n_seq)),
            dma((2, n_seq)), dma((2, 6)), dma((2, 2 + n_seq)), dma((1,)), dma((2,)), dma((2,)),
        ],
        compiler_params=pltpu.CompilerParams(
            collective_id=1, has_side_effects=True, vmem_limit_bytes=60 * 2**20
        ),
        name="reduce_all",
    )(in_sent, d_proj, joined, hidden, g, w, o, normed, small)

def shares(n_seq, width, ffn, att, act):
    stretches, at = [], 0
    for i in range(3):
        stretches.append((i * width, at, att))
        at += att
    for half in range(2):
        first = 3 * width + half * ffn
        for some in act:
            stretches.append((first, at, some))
            at += some
            first += some * n_seq
    return stretches


def share_kernel(w_ref, out_ref, *, stretches):
    for s in range(out_ref.shape[0]):
        parts = [w_ref[:, first + s * some : first + (s + 1) * some] for first, _, some in stretches]
        out_ref[s] = jnp.concatenate(parts, axis=1).astype(out_ref.dtype)


def share_out(weight, n_seq, stretches):
    rows, columns = weight.shape
    step = 16
    return pl.pallas_call(
        functools.partial(share_kernel, stretches=stretches),
        grid=(rows // step,),
        in_specs=[pl.BlockSpec((step, columns), lambda i: (i, 0))],
        out_specs=pl.BlockSpec((n_seq, step, columns // n_seq), lambda i: (0, i, 0)),
        out_shape=jax.ShapeDtypeStruct((n_seq, rows, columns // n_seq), jnp.bfloat16),
        compiler_params=pltpu.CompilerParams(vmem_limit_bytes=56 * 2**20),
        name="share_out",
    )(weight)


def update_kernel(
    sum_ref, w_ref, m_ref, v_ref, a_ref, w_out, v_out, a_out, g_out, *, stretches, rate, decay
):
    n_seq = sum_ref.shape[0]
    for first, at, some in stretches:
        columns = slice(first, first + n_seq * some)
        parts = [sum_ref[s, :, at : at + some].astype(jnp.float32) for s in range(n_seq)]
        gradient = jnp.concatenate(parts, axis=1)
        g_out[:, columns] = gradient
        w_out[:, columns], v_out[:, columns], a_out[:, columns] = adam_update(
            w_ref[:, columns], m_ref[:, columns], v_ref[:, columns], a_ref[:, columns],
            gradient, rate, decay,
        )


def update_in(sums, weight, first, second, average, stretches):
    n_seq, rows, share = sums.shape
    step = 16
    wide = pl.BlockSpec((step, weight.shape[1]), lambda i: (i, 0))
    out = jax.ShapeDtypeStruct(weight.shape, jnp.float32)
    return pl.pallas_call(
        functools.partial(
            update_kernel, stretches=stretches, rate=matrix_rate, decay=weight_decay
        ),
        grid=(rows // step,),
        in_specs=[pl.BlockSpec((n_seq, step, share), lambda i: (0, i, 0))] + [wide] * 4,
        out_specs=[wide] * 4,
        out_shape=[out] * 4,
        compiler_params=pltpu.CompilerParams(vmem_limit_bytes=56 * 2**20),
        name="update_in",
    )(sums, weight, first, second, average)

def split_heads(
    n_dp, n_seq, tokens, cotangent, segment_ids, doc_positions,
    in_weight, in_first, in_second, in_average,
    out_weight, out_first, out_second, out_average,
    small_params, small_first, small_second, small_average,
):
    bf16, f32 = jnp.bfloat16, jnp.float32
    rows, own_tokens, width = tokens.shape
    row_tokens = own_tokens * n_seq
    all_tokens = rows * row_tokens
    head_size = width // HEADS
    ffn = (in_weight.shape[1] - 3 * width) // 2
    in_rows, own = in_weight.shape[0], out_weight.shape[0]
    dp_rows = own * n_seq
    att = width // n_seq
    late = width - dp_rows
    act = [(dp_rows - late) // n_seq, own, own]
    act_all = sum(act)
    lead = att - own
    p, s = lax.axis_index("dp"), lax.axis_index("seq")

    stretches = shares(n_seq, width, ffn, att, act)
    out_low = out_weight.astype(bf16)
    small_low = small_params.astype(bf16).astype(f32).T
    widen = lambda v, n: jnp.pad(v, ((0, n - v.shape[0]), (0, 128 - v.shape[1])))
    tile = jnp.concatenate(
        [
            widen(small_low, 8),
            widen(jnp.concatenate([segment_ids, doc_positions], axis=0).astype(f32), 8),
        ],
        axis=0,
    )
    odd = jnp.concatenate([jnp.zeros_like(tile[:8, :in_rows]), tile[:8, :in_rows]], axis=1)
    tile = jnp.concatenate([jnp.where(s % 2 == 1, odd, tile[:8]), tile[8:]], axis=0)
    _, g_full, in_low, _, tiles, hidden, out_mine, proj, d_joined = gather_all(
        n_dp, n_seq, late, lead, tokens, cotangent, share_out(in_weight, n_seq, stretches), out_low, tile
    )
    g_full, hidden = g_full.reshape(all_tokens, width), hidden.reshape(all_tokens, width)
    in_low = in_low.reshape(n_dp * n_seq * in_rows, 3 * att + 2 * act_all)

    pairs = tiles[:, :, :5].reshape(n_dp, n_seq // 2, 2, 5, 2 * in_rows).sum(axis=2)
    small_low = jnp.transpose(pairs, (2, 0, 1, 3)).reshape(5, width)
    gain = small_low[0]
    bias = lax.dynamic_slice_in_dim(small_low[2:5], s * att, att, 1).reshape(1, 3 * att)
    docs = lax.dynamic_index_in_dim(tiles, p, 0, keepdims=False)[:, 8:, :own_tokens]
    seg_full = jnp.transpose(docs[:, :rows], (1, 0, 2)).reshape(rows, row_tokens)
    pos_full = jnp.transpose(docs[:, rows : 2 * rows], (1, 0, 2)).reshape(rows, row_tokens)
    last = s == n_seq - 1
    keep = att - late

    def normalise(v):
        v = v.astype(f32)
        centered = v - jnp.mean(v, axis=-1, keepdims=True)
        inv_std = lax.rsqrt(jnp.mean(centered * centered, axis=-1, keepdims=True) + norm_eps)
        return centered * inv_std, inv_std

    half_rot = ROT // 2
    inv_freq = rope_base ** (-2.0 * jnp.arange(half_rot, dtype=f32) / ROT)
    angles = pos_full[:, None, :] * inv_freq[:, None]
    cos, sin = jnp.cos(angles), jnp.sin(angles)
    one, zero = jnp.ones((rows, head_size - ROT, row_tokens), f32), jnp.zeros_like(cos)
    rest = 0.0 * one
    rope = jnp.stack(
        [
            jnp.concatenate([cos, cos, one] * 2, axis=1),
            jnp.concatenate([-sin, zero, rest] * 2, axis=1),
            jnp.concatenate([zero, sin, rest] * 2, axis=1),
        ],
        axis=1,
    )
    joined, d_proj, bias_part = middle(
        proj, bias, d_joined, rope, seg_full, n_seq, att, act, head_size
    )

    blocks = lambda v: v.reshape(2, n_seq // 2, rows * own_tokens, v.shape[-1])
    c = p % 2
    def to_core(v):
        some = v.shape[1] // n_dp
        firsts = [(2 * y_to + 1 - c) * some for y_to in range(2)]
        return [lax.dynamic_slice_in_dim(v, first, some, 1) for first in firsts]

    over_tokens = lambda a, b: lax.dot_general(
        a, b, (((0,), (0,)), ((), ())), preferred_element_type=f32
    ).astype(bf16)
    in_sent = over_tokens(jnp.concatenate(to_core(hidden), axis=1), d_proj).reshape(2, n_seq, in_rows, -1)
    normed, inv_std = normalise(tokens.reshape(rows * own_tokens, width))
    small_part = lax.dynamic_update_slice(jnp.zeros((8, width), f32), bias_part[:3], (2, s * att))
    plan = ((1, 1), ((1, 0), (1, 4), (7, 7), (0, 0), (0, 1), (0, 2), (0, 3), (1, 1), (1, 3), (7, 2), (2, 0), (2, 1), (2, 2), (2, 3), (2, 4), (2, 5), (2, 6), (2, 7), (7, 4), (7, 6), (1, 2), (7, 0), (4, 0), (7, 3), (3, 0), (3, 1), (3, 2), (6, 0), (4, 1), (3, 3), (3, 4), (4, 2), (7, 5), (0, 4), (0, 5), (0, 6), (0, 7), (3, 5), (3, 6), (7, 1), (4, 3), (3, 7), (5, 0), (4, 4), (5, 1), (4, 5), (5, 2), (6, 1), (4, 6), (4, 7), (5, 3)))
    sums, in_sum, out_sum, from_prev, small_sum = reduce_all(
        plan, n_dp, n_seq, late, act[0], keep,
        in_sent,
        blocks(d_proj), blocks(joined), blocks(hidden), blocks(g_full), in_low, out_mine,
        normed, small_part,
    )
    d_hidden, branch = sums[0], sums[1]

    output = (tokens.astype(f32) + branch.reshape(tokens.shape)).astype(bf16)
    d_normed = d_hidden * gain
    input_grad = cotangent.astype(f32) + (
        inv_std
        * (
            d_normed
            - jnp.mean(d_normed, axis=-1, keepdims=True)
            - normed * jnp.mean(d_normed * normed, axis=-1, keepdims=True)
        )
    ).reshape(tokens.shape)
    small_grad = lax.dynamic_slice(small_sum, (0, s % 2 * in_rows), (8, in_rows))[:5].T

    count = jnp.where(p == 0, lead * s, jnp.where(p == 1, late - lead * s, 0))
    out_grad = lax.dynamic_slice_in_dim(
        jnp.concatenate([from_prev, out_sum[:own]], axis=0), late - count, own, 0
    ).astype(f32)

    *in_new, in_grad = update_in(
        in_sum, in_weight, in_first, in_second, in_average, stretches
    )
    out_new = adam_update(
        out_weight, out_first, out_second, out_average, out_grad, matrix_rate, weight_decay
    )
    small_new = adam_update(
        small_params, small_first, small_second, small_average, small_grad, small_rate, 0.0
    )
    return (output, input_grad, *in_new, *out_new, *small_new, small_grad, in_grad, out_grad)


def solution(mesh):
    n_dp, n_seq = mesh.shape["dp"], mesh.shape["seq"]

    def choose(*operands):
        own_rows = operands[8].shape[0]
        model_width = operands[0].shape[2]
        if heads_fit(n_dp, n_seq, own_rows, model_width, operands[4].shape[1]):
            return split_heads(n_dp, n_seq, *operands)
        return per_device(*operands)

    return jax.shard_map(
        choose,
        mesh=mesh,
        in_specs=(
            P("dp", "seq", None),
            P("dp", "seq", None),
            P("dp", "seq"),
            P("dp", "seq"),
            P(("dp", "seq"), None),
            P(("dp", "seq"), None),
            P(("dp", "seq"), None),
            P(("dp", "seq"), None),
            P(("dp", "seq"), None),
            P(("dp", "seq"), None),
            P(("dp", "seq"), None),
            P(("dp", "seq"), None),
            P(("dp", "seq"), None),
            P(("dp", "seq"), None),
            P(("dp", "seq"), None),
            P(("dp", "seq"), None),
        ),
        out_specs=(
            P("dp", "seq", None),
            P("dp", "seq", None),
            P(("dp", "seq"), None),
            P(("dp", "seq"), None),
            P(("dp", "seq"), None),
            P(("dp", "seq"), None),
            P(("dp", "seq"), None),
            P(("dp", "seq"), None),
            P(("dp", "seq"), None),
            P(("dp", "seq"), None),
            P(("dp", "seq"), None),
            P(("dp", "seq"), None),
            P(("dp", "seq"), None),
            P(("dp", "seq"), None),
        ),
        check_vma=False,
    )
```
